128 devices in a mesh: stn: 8 (over z, core), chan: 16 (over y, x).
Axes of the slice: x: 4, y: 4, z: 4, core: 2. Of those that a mesh axis runs over, the one named last changes fastest.
Arguments:
- voltages: bfloat16 [2, 1024, 256, 256], P(None, ('stn', 'chan')), may hold values from -6 to 6
- weights: bfloat16 [2, 256, 256, 1024], P(None, ('stn', 'chan')), may hold values from -0.125 to 0.125
- flags: int32 [128, 64], P(('stn', 'chan')), may hold values from 0 to 255
- dm_index: int32 [256], P(('stn', 'chan')), may hold values from 0 to 15
Outputs:
- dedispersed: bfloat16 [2, 256, 65536], P(None, ('stn', 'chan'))
- bandpass: float32 [256, 256], P(('stn', 'chan'))
The draws below stay inside these ranges and needn't reach their ends.
Inputs may be any that keep to these rules, and one draw needn't show every extreme that they name: `flags`: each station group lists 64 channel numbers, repeats allowed.
All inputs are finite; a program needn't handle non-finite values.
Results may differ from the reference program's by a relative error of at most 0.0066.
Values may be sent and summed in bfloat16 or wider, within the bound.
A program may use at most 64 MiB of HBM per device.

```python
import math
import jax
import jax.numpy as jnp
from jax import lax

INPUTS = 1024
CHANNELS = 256
BEAMS = 256
TIME = 256
TAPS = 12
CHIRP = 1024
DMS = 16
GROUP = 8
NFLAG = 64
GROUPS = 128


def plant(entries, key, smallest, largest):
    longest = entries.shape.index(max(entries.shape))
    spots = []
    for shift in (0, 1):
        where = [jax.random.randint(jax.random.fold_in(key, axis), (), 0, length) for axis, length in enumerate(entries.shape)]
        where[longest] = (where[longest] + shift) % entries.shape[longest]
        spots.append(tuple(where))
    return entries.at[spots[0]].set(smallest).at[spots[1]].set(largest)


def level_of(stream_key, extent, cuts, smallest, top_value):
    loudness, own = 1.0, jax.random.fold_in(stream_key, 6)
    for position, blocks in cuts:
        draws = jnp.exp(jax.random.uniform(jax.random.fold_in(own, position), (blocks,), jnp.float32, smallest / len(cuts), top_value / len(cuts)))
        loudness = loudness * jnp.repeat(draws, extent[position] // blocks).reshape([-1 if axis == position else 1 for axis in range(len(extent))])
    return loudness


def scatter_about(key, shape, spread, limit, cuts=(), kind=jnp.bfloat16):
    entries = jax.random.normal(key, shape, jnp.float32) * spread
    if len(cuts) > 0:
        entries = level_of(key, shape, cuts, -0.22, 0.18) * entries
    return jnp.clip(entries, min=-limit, max=limit).astype(kind)


def setup_inputs(seed: int = 0) -> dict:
    key_of = jax.random.split(jax.random.key(seed), 5)
    voltages = scatter_about(key_of[0], (2, INPUTS, CHANNELS, TIME), 1.0, 6.0, ((1, 128),))
    weights = scatter_about(key_of[1], (2, CHANNELS, BEAMS, INPUTS), (2 * INPUTS) ** -0.5, 0.125, ((1, 128),))
    flags = plant(jax.random.randint(key_of[2], (GROUPS, NFLAG), 0, CHANNELS), jax.random.fold_in(key_of[2], 1), 0, CHANNELS - 1).astype(jnp.int32)
    dm_index = plant(jax.random.randint(key_of[3], (BEAMS,), 0, DMS), jax.random.fold_in(key_of[3], 1), 0, DMS - 1).astype(jnp.int32)
    return dict(voltages=voltages, weights=weights, flags=flags, dm_index=dm_index)


def channel_mask(flag_rows, channel_ids):
    hit = jnp.any(flag_rows[:, :, None] == channel_ids[None, None, :], axis=1)
    return jnp.where(hit, 0.0, 1.0).astype(jnp.float32)

def dft_table(order):
    freqs = jnp.arange(CHANNELS, dtype=jnp.int32)
    phase = order[:, None] * freqs[None, :] % CHANNELS
    angle = 2.0 * math.pi / CHANNELS * phase.astype(jnp.float32)
    cosine = jnp.cos(angle) / math.sqrt(CHANNELS)
    sine = jnp.sin(angle) / math.sqrt(CHANNELS)
    upper = jnp.stack([cosine, sine], axis=1)
    lower = jnp.stack([-sine, cosine], axis=1)
    return jnp.stack([upper, lower], axis=0).astype(jnp.bfloat16)

def prototype():
    counter = jnp.arange(TAPS * CHANNELS, dtype=jnp.float32)
    offset = (counter + 0.5) / CHANNELS - TAPS / 2.0
    window = 0.54 + 0.46 * jnp.cos(math.pi * offset / (TAPS / 2.0))
    return (jnp.sinc(offset) * window).reshape(TAPS, CHANNELS)

def chirp_table(dm_value):
    nblock = CHIRP // CHANNELS + 1
    blocks = jnp.arange(nblock, dtype=jnp.int32)[:, None, None]
    inner = jnp.arange(CHANNELS, dtype=jnp.int32)[None, :, None]
    outer = jnp.arange(CHANNELS, dtype=jnp.int32)[None, None, :]
    lag = blocks * CHANNELS + inner - outer
    valid = (lag >= 0) & (lag < CHIRP)
    lagc = jnp.clip(lag, 0, CHIRP - 1)
    phase = (dm_value + 1) * lagc * lagc % (2 * DMS * CHIRP)
    angle = math.pi * phase.astype(jnp.float32) / (DMS * CHIRP)
    real_part = jnp.where(valid, jnp.cos(angle), 0.0) / math.sqrt(CHIRP)
    imag_part = jnp.where(valid, jnp.sin(angle), 0.0) / math.sqrt(CHIRP)
    from_real = jnp.stack([real_part, -imag_part], axis=2)
    from_imag = jnp.stack([imag_part, real_part], axis=2)
    return jnp.stack([from_real, from_imag], axis=1).astype(jnp.bfloat16)

def reference(voltages, weights, flags, dm_index):
    keep = jnp.repeat(channel_mask(flags, jnp.arange(CHANNELS, dtype=jnp.int32)), GROUP, axis=0)

    def beam_channel(chan):
        volt = lax.dynamic_index_in_dim(voltages, chan, axis=2, keepdims=False).astype(jnp.float32)
        mask = lax.dynamic_index_in_dim(keep, chan, axis=1, keepdims=False)
        volt = volt * mask[None, :, None]
        wgt = lax.dynamic_index_in_dim(weights, chan, axis=1, keepdims=False).astype(jnp.float32)
        real_beam = jnp.einsum('bi,it->bt', wgt[0], volt[0]) - jnp.einsum('bi,it->bt', wgt[1], volt[1])
        imag_beam = jnp.einsum('bi,it->bt', wgt[0], volt[1]) + jnp.einsum('bi,it->bt', wgt[1], volt[0])
        return jnp.stack([real_beam, imag_beam], axis=0).astype(jnp.bfloat16)
    beams = lax.map(beam_channel, jnp.arange(CHANNELS, dtype=jnp.int32))
    beams = jnp.transpose(beams, (2, 1, 0, 3))
    table = dft_table(jnp.arange(CHANNELS, dtype=jnp.int32)).astype(jnp.float32)
    taps = prototype()
    nblock = CHIRP // CHANNELS + 1

    def process(items):
        block, dm_value = items
        values = block.astype(jnp.float32)
        power = lax.optimization_barrier(jnp.mean(values[0] * values[0] + values[1] * values[1], axis=1))
        spectra = jnp.einsum('pct,pcqk->qtk', values, table)
        padded = jnp.pad(spectra, ((0, 0), (TAPS - 1, 0), (0, 0)))
        series = jnp.zeros_like(spectra)
        for tap in range(TAPS):
            series = series + taps[tap][None, None, :] * padded[:, TAPS - 1 - tap:TAPS - 1 - tap + TIME, :]
        series = series.astype(jnp.bfloat16).astype(jnp.float32)
        chirp = chirp_table(dm_value).astype(jnp.float32)
        longer = jnp.pad(series, ((0, 0), (0, nblock - 1), (0, 0)))
        result = jnp.zeros_like(series)
        for blk in range(nblock):
            result = result + jnp.einsum('ptu,puqa->qta', longer[:, blk:blk + TIME, :], chirp[blk])
        return (result.reshape(2, TIME * CHANNELS).astype(jnp.bfloat16), power)
    dedispersed, bandpass = lax.map(process, (beams, dm_index))
    return (jnp.transpose(dedispersed, (1, 0, 2)), bandpass)
```

```python
import math
import random

import jax
import jax.numpy as jnp
import numpy as np
from jax import lax
from jax.experimental import pallas as pl
from jax.experimental.pallas import tpu as pltpu
from jax.sharding import PartitionSpec as P

CHANNELS = 256
BEAMS = 256
INPUTS = 1024
TIME = 256
TAPS = 12
CHIRP = 1024
DMS = 16
NBLOCK = CHIRP // CHANNELS + 1
DEVICES = 128
CHAN_AXIS = 16
MESH = pl.DeviceIdType.MESH
BF16 = jnp.bfloat16
F32 = jnp.float32


def dft_rows():
    order = np.arange(CHANNELS)
    angle = 2.0 * math.pi / CHANNELS * (order[:, None] * order[None, :] % CHANNELS)
    cosine = np.cos(angle) / math.sqrt(CHANNELS)
    sine = np.sin(angle) / math.sqrt(CHANNELS)
    return np.block([[cosine, sine], [-sine, cosine]]).astype(np.float32)


def prototype():
    counter = np.arange(TAPS * CHANNELS, dtype=np.float64)
    offset = (counter + 0.5) / CHANNELS - TAPS / 2.0
    window = 0.54 + 0.46 * np.cos(math.pi * offset / (TAPS / 2.0))
    taps = (np.sinc(offset) * window).reshape(TAPS, CHANNELS)
    return np.concatenate([taps, taps], axis=1).astype(np.float32)


def chirp_rows():
    dms = np.arange(DMS, dtype=np.int64)[:, None, None]
    lag = np.arange(NBLOCK)[None, :, None] * CHANNELS + CHANNELS - 1 - np.arange(2 * CHANNELS)[None, None, :]
    valid = (lag >= 0) & (lag < CHIRP)
    lag = np.clip(lag, 0, CHIRP - 1)
    angle = math.pi * ((dms + 1) * lag * lag % (2 * DMS * CHIRP)) / (DMS * CHIRP)
    real = np.where(valid, np.cos(angle), 0.0) / math.sqrt(CHIRP)
    imag = np.where(valid, np.sin(angle), 0.0) / math.sqrt(CHIRP)
    rows = np.concatenate([real, imag, np.zeros((DMS, 6, 2 * CHANNELS))], axis=1)
    return rows.astype(np.float32)


def iota(axis, shape=(256, 256)):
    return lax.broadcasted_iota(jnp.int32, shape, axis)


def ones_where(condition):
    return jnp.where(condition, 1.0, 0.0).astype(BF16)


def dot(a, b):
    return jnp.dot(a, b, preferred_element_type=F32)


def exchange_order():
    steps = [(dz, one, dx) for dz in range(4) for one in range(2) for dx in range(4)]
    random.Random(7).shuffle(steps)
    mixed = []
    for dz, one, dx in steps:
        for step in ((dz, one, dx), (-dz % 4, 1 - one, -dx % 4)):
            if step not in mixed:
                mixed.append(step)
    return mixed


def body(
    volt, wgt, flags, dm, chirps, recv2, tables,
    vin, send, recv, win, toep, chv, flagv, dmv, acc, send2, keep,
    load_sem, table_sem, sent, sent2, recv_sem, recv_sem2, plane_sem,
):
    x = lax.rem(lax.axis_index("chan"), 4)
    y = lax.axis_index("chan") // 4
    z = lax.axis_index("stn") // 2
    core = lax.rem(lax.axis_index("stn"), 2)
    me = lax.axis_index("stn") * CHAN_AXIS + lax.axis_index("chan")

    turn = 1 + 2 * core
    zs = [lax.rem(z + dz * turn, 4) * 2 for dz in range(4)]
    xs = [lax.rem(x + dx * turn, 4) for dx in range(4)]
    ys = [lax.rem(y + dy, 4) * 4 for dy in range(4)]
    cores = (core, 1 - core)
    batches = [(other, lax.rem(y // 2 + k + core, 2)) for other in range(2) for k in range(2)]

    flag_load = pltpu.make_async_copy(flags, flagv, load_sem.at[4])
    flag_load.start()
    volt_loads = [
        pltpu.make_async_copy(volt.at[:, :, cores[other], half], vin.at[:, :, cores[other], half], load_sem.at[n])
        for n, (other, half) in enumerate(batches)
    ]
    for load in volt_loads:
        load.start()

    barrier = pltpu.get_barrier_semaphore()
    greeted = [(zs[dz] + core, ys[0] + x) for dz in range(1, 4)]
    line = list(greeted)
    for other in range(2):
        for dy in range(4):
            for dx in range(4):
                if (other, dy, dx) != (0, 0, 0):
                    greeted.append((zs[0] + cores[other], ys[dy] + xs[dx]))
    for place in greeted:
        pl.semaphore_signal(barrier, inc=1, device_id=place, device_id_type=MESH)

    def send_batch(n, send, landing, sent, recv_sem):
        other, half = batches[n]
        for dz, one, dx in exchange_order():
            stn, yy = zs[dz] + cores[other], half * 2 + one
            chan = yy * 4 + xs[dx]

            def away():
                pltpu.make_async_remote_copy(
                    src_ref=send.at[stn * CHAN_AXIS + chan],
                    dst_ref=landing(me),
                    send_sem=sent,
                    recv_sem=recv_sem.at[other],
                    device_id=(stn, chan),
                    device_id_type=MESH,
                ).start()

            if (other, dz, dx) == (0, 0, 0):
                pl.when(yy != y)(away)

                @pl.when(yy == y)
                def _():
                    pltpu.make_async_copy(send.at[me], landing(me), recv_sem.at[0]).start()
            else:
                away()

    flag_load.wait()
    row, col = iota(0), iota(1)
    hits = ones_where(iota(0, (256, 64)) == flagv[...])
    count = dot(hits, jnp.ones((64, 256), BF16))
    keep_rows = ones_where((count < 0.5) & (row % 16 == col % 16))
    keep[...] = dot(ones_where(iota(1, (16, 256)) // 16 == iota(0, (16, 256))), keep_rows)

    there = (row // 32) * 2 + (row // 8) % 2
    swap = jnp.where((col // 16 == ((row // 16) % 2) * 8 + row % 8) & (col % 16 == there), 1.0, 0.0)

    pl.semaphore_wait(barrier, len(greeted))
    for place in line:
        pl.semaphore_signal(plane_sem, inc=1, device_id=place, device_id_type=MESH)
    loads = [
        pltpu.make_async_copy(source, target, load_sem.at[n])
        for n, (source, target) in enumerate(((wgt, win), (dm, dmv), (chirps, chv)), 5)
    ]
    for n, (other, half) in enumerate(batches):
        volt_loads[n].wait()
        for plane in range(4):
            g = (plane * 2 + cores[other]) * 2 + half
            block = vin[:, plane, cores[other], half].reshape(256, 256)
            mine = (swap * keep[pl.ds(g, 1), :]).astype(BF16)
            send[pl.ds(pl.multiple_of(g * 8, 8), 8)] = dot(mine, block).astype(BF16).reshape(8, 4, 8, 256)
        if n == 0:
            for load in loads:
                load.start()
            pl.semaphore_wait(plane_sem, len(line))
        send_batch(n, send, lambda source: recv.at[:, source], sent, recv_sem)

    for load in loads:
        load.wait()

    def toeplitz(row_of):
        wide = jnp.broadcast_to(row_of, (CHANNELS, 2 * CHANNELS))
        rolled = pltpu.roll(wide, CHANNELS + 1, 1, stride=1, stride_axis=0)
        return rolled[:, :CHANNELS]

    for b in range(2):
        chosen = chv[dmv[b]]
        for blk in range(NBLOCK):
            real = toeplitz(chosen[blk : blk + 1])
            imag = toeplitz(chosen[NBLOCK + blk : NBLOCK + blk + 1])
            upper = jnp.concatenate([real, -imag], axis=1).astype(BF16)
            lower = jnp.concatenate([imag, real], axis=1).astype(BF16)
            toep[b, blk * 512 : blk * 512 + 256, :] = upper
            toep[b, blk * 512 + 256 : blk * 512 + 512, :] = lower
    table_store = pltpu.make_async_copy(toep, tables, table_sem)
    table_store.start()

    for other in range(2):
        half = recv.at[:, pl.ds(0, 64)]
        pltpu.make_async_copy(half, half, recv_sem.at[other]).wait()
        stn_core = lax.rem(core + other, 2)
        for c in range(2):
            real, imag, weight_real, weight_imag = [], [], [], []
            for plane in range(4):
                stn = 2 * plane + stn_core
                sources = pl.ds(pl.multiple_of(stn * 16, 16), 16)
                inputs = pl.ds(pl.multiple_of(stn * 128, 128), 128)
                real.append(recv[c, sources].reshape(128, 256))
                imag.append(recv[2 + c, sources].reshape(128, 256))
                weight_real.append(win[0, c, :, inputs])
                weight_imag.append(win[1, c, :, inputs])
            real, imag = jnp.concatenate(real, axis=0), jnp.concatenate(imag, axis=0)
            both = jnp.concatenate(weight_real + weight_imag, axis=1)
            parts = jnp.concatenate(
                [jnp.concatenate([real, imag], axis=1), jnp.concatenate([-imag, real], axis=1)], axis=0
            )
            if other == 0:
                acc[c] = dot(both, parts)
            else:
                acc[c] += dot(both, parts)

    order = ones_where(
        (col // 128 == row % 2) & ((col // 64) % 2 == (row // 2) % 2) & (col % 64 == (row // 8) * 2 + (row // 4) % 2)
    )
    for m in range(4):
        rows = slice(m * 64, m * 64 + 64)
        block = jnp.concatenate([acc[c, rows, q * 256 : q * 256 + 256] for c in range(2) for q in range(2)], axis=0)
        block = dot(order, block.astype(BF16)).astype(BF16)
        send2[m * 32 : m * 32 + 32] = block.reshape(32, 8, 256)
    for n in range(4):
        send_batch(n, send2, lambda source: recv2.at[source], sent2, recv_sem2)
    table_store.wait()
    blocks = send.at[pl.ds(0, DEVICES - 1)]
    pltpu.make_async_copy(blocks, blocks, sent).wait()
    blocks = send2.at[pl.ds(0, DEVICES - 1)]
    pltpu.make_async_copy(blocks, blocks, sent2).wait()
    for other in range(2):
        half = recv2.at[pl.ds(0, 64)]
        pltpu.make_async_copy(half, half, recv_sem2.at[other]).wait()


def tail(beams, tables, dft, proto, out, band, xv, xs, tv, dftv, protov, padded, even, odd, load_sem):
    loads = [
        pltpu.make_async_copy(source, target, load_sem.at[n])
        for n, (source, target) in enumerate(((beams, xv), (dft, dftv), (proto, protov), (tables, tv)))
    ]
    for load in loads:
        load.start()
    row, col = iota(0), iota(1)
    sort = ones_where(col == ((row % 64) // 2) * 8 + (row // 64) * 2 + row % 2)
    spread = ones_where(col == (row % 8) * 32 + row // 8)
    loads[0].wait()
    for n in range(4):
        block = dot(sort, xv[n * 256 : n * 256 + 256, :]).astype(BF16)
        for k in range(4):
            xs[k // 2, (k % 2) * 256 + n * 64 : (k % 2) * 256 + n * 64 + 64, :] = block[k * 64 : k * 64 + 64]
    loads[1].wait()
    loads[2].wait()
    for b in range(2):
        turned = lax.dot_general(spread, xs[b], (((1,), (1,)), ((), ())), preferred_element_type=F32)
        power = jnp.sum(turned * turned, axis=0, keepdims=True) * (1.0 / TIME)
        band[b : b + 1, :] = power[:, :256] + power[:, 256:]
        spectra = dot(turned.astype(BF16), dftv[...])
        before = pltpu.roll(spectra[168:], 1, 0)
        padded[b, 0:88, :] = jnp.where(iota(0, (88, 512)) % 8 == 0, 0.0, before)
        padded[b, 88:344, :] = spectra
    for b in range(2):
        for n in range(4):
            lanes = slice(n * 128, n * 128 + 128)
            series = protov[0:1, lanes] * padded[b, 88:344, lanes]
            for tap in range(1, TAPS):
                series = series + protov[tap : tap + 1, lanes] * padded[b, 88 - 8 * tap : 344 - 8 * tap, lanes]
            after = pltpu.roll(series[:32], 31, 0)
            after = jnp.where(iota(0, (32, 128)) % 8 == 7, 0.0, after)
            even[b, 0:256, lanes] = series.astype(BF16)
            even[b, 256:288, lanes] = after.astype(BF16)
            odd[b, 0:272, lanes] = jnp.concatenate([series[8:], after[:24]], axis=0).astype(BF16)
    loads[3].wait()
    results = []
    for b in range(2):
        lhs = jnp.concatenate(
            [even[b, 0:256], odd[b, 0:256], even[b, 16:272], odd[b, 16:272], even[b, 32:288]], axis=1
        )
        results.append(dot(lhs, tv[b]).astype(BF16))
    final = ones_where(col == (row % 4) * 64 + ((row // 4) % 8) * 8 + row // 32)
    for j in range(4):
        rows = slice(64 * j, 64 * j + 64)
        block = jnp.concatenate(
            [
                jnp.concatenate([results[b][rows, half * 128 + q * 256 : half * 128 + q * 256 + 128] for q in range(2)], axis=1)
                for half in range(2) for b in range(2)
            ],
            axis=0,
        )
        block = dot(final, block).astype(BF16)
        for q in range(2):
            for k in range(8):
                out[q, 128 * k + 32 * j : 128 * k + 32 * j + 32, :] = block[32 * k : 32 * k + 32, q * 128 : q * 128 + 128]


def on_device(voltages, weights, flags, dm_index):
    hbm = pl.BlockSpec(memory_space=pl.ANY)
    vmem = pl.BlockSpec(memory_space=pltpu.VMEM)
    dma = pltpu.SemaphoreType.DMA
    params = dict(vmem_limit_bytes=62 * 1024 * 1024)
    beams, tables = pl.pallas_call(
        body,
        out_shape=(
            jax.ShapeDtypeStruct((DEVICES, 8, 256), BF16),
            jax.ShapeDtypeStruct((2, NBLOCK * 512, 512), BF16),
        ),
        in_specs=[hbm] * 5,
        out_specs=(hbm, hbm),
        scratch_shapes=[
            pltpu.VMEM((16, 4, 2, 2, 16, 256), BF16),
            pltpu.VMEM((DEVICES, 4, 8, 256), BF16),
            pltpu.VMEM((4, DEVICES, 8, 256), BF16),
            pltpu.VMEM((2, 2, 256, 1024), BF16),
            pltpu.VMEM((2, NBLOCK * 512, 512), BF16),
            pltpu.VMEM((DMS, 16, 512), F32),
            pltpu.VMEM((1, 64), jnp.int32),
            pltpu.SMEM((2,), jnp.int32),
            pltpu.VMEM((2, 256, 512), F32),
            pltpu.VMEM((DEVICES, 8, 256), BF16),
            pltpu.VMEM((16, 256), F32),
            dma((8,)),
            dma,
            dma,
            dma,
            dma((2,)),
            dma((2,)),
            pltpu.SemaphoreType.REGULAR,
        ],
        compiler_params=pltpu.CompilerParams(collective_id=0, has_side_effects=True, **params),
        name="beamform",
    )(
        voltages.reshape(16, 4, 2, 2, 16, TIME),
        weights,
        flags,
        dm_index,
        jnp.asarray(chirp_rows()).astype(BF16).astype(F32),
    )
    dedispersed, bandpass = pl.pallas_call(
        tail,
        out_shape=(
            jax.ShapeDtypeStruct((2, 2 * TIME * 2, 128), BF16),
            jax.ShapeDtypeStruct((2, CHANNELS), F32),
        ),
        in_specs=[hbm] * 4,
        out_specs=(vmem, vmem),
        scratch_shapes=[
            pltpu.VMEM((1024, 256), BF16),
            pltpu.VMEM((2, 512, 256), BF16),
            pltpu.VMEM((2, NBLOCK * 512, 512), BF16),
            pltpu.VMEM((512, 512), BF16),
            pltpu.VMEM((TAPS, 512), F32),
            pltpu.VMEM((2, 344, 512), F32),
            pltpu.VMEM((2, 288, 512), BF16),
            pltpu.VMEM((2, 272, 512), BF16),
            dma((4,)),
        ],
        compiler_params=pltpu.CompilerParams(**params),
        name="synthesis",
    )(
        beams.reshape(1024, 256),
        tables,
        jnp.asarray(dft_rows()).astype(BF16),
        jnp.asarray(prototype()),
    )
    dedispersed = dedispersed.reshape(2, 512, 2, 128).transpose(0, 2, 1, 3).reshape(2, 2, TIME * CHANNELS)
    return dedispersed, bandpass


def solution(mesh):
    return jax.shard_map(
        on_device,
        mesh=mesh,
        in_specs=(
            P(None, ("stn", "chan"), None, None),
            P(None, ("stn", "chan"), None, None),
            P(("stn", "chan"), None),
            P(("stn", "chan")),
        ),
        out_specs=(P(None, ("stn", "chan"), None), P(("stn", "chan"), None)),
        check_vma=False,
    )
```

```python
import math
import random

import jax
import jax.numpy as jnp
import numpy as np
from jax import lax
from jax.experimental import pallas as pl
from jax.experimental.pallas import tpu as pltpu
from jax.sharding import PartitionSpec as P

CHANNELS = 256
BEAMS = 256
INPUTS = 1024
TIME = 256
TAPS = 12
CHIRP = 1024
DMS = 16
NBLOCK = CHIRP // CHANNELS + 1
DEVICES = 128
CHAN_AXIS = 16
PARTS = 2
SPAN = TIME // PARTS
MESH = pl.DeviceIdType.MESH
BF16 = jnp.bfloat16
F32 = jnp.float32


def dft_rows():
    order = np.arange(CHANNELS)
    angle = 2.0 * math.pi / CHANNELS * (order[:, None] * order[None, :] % CHANNELS)
    cosine = np.cos(angle) / math.sqrt(CHANNELS)
    sine = np.sin(angle) / math.sqrt(CHANNELS)
    return np.block([[cosine, sine], [-sine, cosine]]).astype(np.float32)


def prototype():
    counter = np.arange(TAPS * CHANNELS, dtype=np.float64)
    offset = (counter + 0.5) / CHANNELS - TAPS / 2.0
    window = 0.54 + 0.46 * np.cos(math.pi * offset / (TAPS / 2.0))
    taps = (np.sinc(offset) * window).reshape(TAPS, CHANNELS)
    return np.concatenate([taps, taps], axis=1).astype(np.float32)


def chirp_rows():
    dms = np.arange(DMS, dtype=np.int64)[:, None, None]
    lag = np.arange(NBLOCK)[None, :, None] * CHANNELS + CHANNELS - 1 - np.arange(2 * CHANNELS)[None, None, :]
    valid = (lag >= 0) & (lag < CHIRP)
    lag = np.clip(lag, 0, CHIRP - 1)
    angle = math.pi * ((dms + 1) * lag * lag % (2 * DMS * CHIRP)) / (DMS * CHIRP)
    real = np.where(valid, np.cos(angle), 0.0) / math.sqrt(CHIRP)
    imag = np.where(valid, np.sin(angle), 0.0) / math.sqrt(CHIRP)
    rows = np.concatenate([real, imag, np.zeros((DMS, 6, 2 * CHANNELS))], axis=1)
    return rows.astype(np.float32)


def iota(axis, shape=(256, 256)):
    return lax.broadcasted_iota(jnp.int32, shape, axis)


def ones_where(condition):
    return jnp.where(condition, 1.0, 0.0).astype(BF16)


def dot(a, b):
    return jnp.dot(a, b, preferred_element_type=F32)


def exchange_order():
    left = [(dz, dy, dx) for dz in range(4) for dy in range(4) for dx in range(4)]
    random.Random(7).shuffle(left)
    hops, ordered = [0, 0, 0], []
    while left:
        def uneven(step):
            return sum((done + min(d, 4 - d) - len(ordered) - 1) ** 2 for done, d in zip(hops, step))

        best = min(left, key=uneven)
        left.remove(best)
        ordered.append(best)
        hops = [done + min(d, 4 - d) for done, d in zip(hops, best)]
    return ordered


def body(
    volt, wgt, flags, dm, chirps, dft, proto, recv2, tables, dftv, protov,
    vin, give, send, recv, win, chv, flagv, dmv, beams, give2, send2, keep,
    load_sem, plane_sem, given, given2, sent, sent2, sibling_sem, sibling_sem2, recv_sem, recv_sem2,
):
    x = lax.rem(lax.axis_index("chan"), 4)
    y = lax.axis_index("chan") // 4
    z = lax.axis_index("stn") // 2
    core = lax.rem(lax.axis_index("stn"), 2)
    chip = z * CHAN_AXIS + lax.axis_index("chan")
    sibling = (z * 2 + 1 - core, lax.axis_index("chan"))

    turn = 1 + 2 * core
    zs = [lax.rem(z + dz * turn, 4) for dz in range(4)]
    xs = [lax.rem(x + dx * turn, 4) for dx in range(4)]
    ys = [lax.rem(y + dy * turn, 4) * 4 for dy in range(4)]

    flag_load = pltpu.make_async_copy(flags, flagv, load_sem.at[0])
    flag_load.start()
    volt_loads = [
        pltpu.make_async_copy(volt.at[:, :, number], vin.at[:, :, number], load_sem.at[n])
        for n, number in ((1, 1 - core), (2, core))
    ]
    for load in volt_loads:
        load.start()

    barrier = pltpu.get_barrier_semaphore()
    line = [(zs[dz] * 2 + core, ys[0] + x) for dz in range(1, 4)]
    plane = [(z * 2 + core, ys[dy] + xs[dx]) for dy in range(4) for dx in range(4) if (dy, dx) != (0, 0)]
    greeted = [sibling] + line + plane
    for place in greeted:
        pl.semaphore_signal(barrier, inc=1, device_id=place, device_id_type=MESH)

    def hand_over(part, give, send, given, sibling_sem):
        pltpu.make_async_remote_copy(
            src_ref=give.at[part],
            dst_ref=send.at[part, :, core],
            send_sem=given,
            recv_sem=sibling_sem.at[part],
            device_id=sibling,
            device_id_type=MESH,
        ).start()

    def exchange(part, send, landing, sibling_sem, sent, recv_sem):
        share = send.at[part, :, 1 - core]
        pltpu.make_async_copy(share, share, sibling_sem.at[part]).wait()
        pltpu.make_async_copy(send.at[part, chip], landing, recv_sem.at[part]).start()
        for dz, dy, dx in exchange_order():
            if (dz, dy, dx) != (0, 0, 0):
                chan = ys[dy] + xs[dx]
                pltpu.make_async_remote_copy(
                    src_ref=send.at[part, zs[dz] * CHAN_AXIS + chan],
                    dst_ref=landing,
                    send_sem=sent.at[part],
                    recv_sem=recv_sem.at[part],
                    device_id=(zs[dz] * 2 + core, chan),
                    device_id_type=MESH,
                ).start()

    flag_load.wait()
    row, col = iota(0), iota(1)
    hits = ones_where(iota(0, (256, 64)) == flagv[...])
    count = dot(hits, jnp.ones((64, 256), BF16))
    keep_rows = ones_where((count < 0.5) & (row % 16 == col % 16))
    keep[...] = dot(ones_where(iota(1, (16, 256)) // 16 == iota(0, (16, 256))), keep_rows)

    there = (row // 32) * 2 + (row // 8) % 2
    swap = jnp.where((col // 16 == ((row // 16) % 2) * 8 + row % 8) & (col % 16 == there), 1.0, 0.0)

    def sort_out(number):
        for zz in range(4):
            for half in range(2):
                block = vin[:, zz, number, half].reshape(256, 256)
                mine = (swap * keep[pl.ds((zz * 2 + number) * 2 + half, 1), :]).astype(BF16)
                yield slice(zz * 16 + half * 8, zz * 16 + half * 8 + 8), dot(mine, block).astype(BF16).reshape(8, 4, 8, 256)

    volt_loads[0].wait()
    for chips, block in sort_out(1 - core):
        for part in range(PARTS):
            give[part, chips] = block[..., part * SPAN : part * SPAN + SPAN]
    pl.semaphore_wait(barrier, len(greeted))
    for place in line:
        pl.semaphore_signal(plane_sem, inc=1, device_id=place, device_id_type=MESH)
    for part in range(PARTS):
        hand_over(part, give, send, given, sibling_sem)
    volt_loads[1].wait()
    for chips, block in sort_out(core):
        for part in range(PARTS):
            send[part, chips, core] = block[..., part * SPAN : part * SPAN + SPAN]
    loads = [
        pltpu.make_async_copy(source, target, load_sem.at[n])
        for n, (source, target) in enumerate(
            ((wgt, win), (dm, dmv), (chirps, chv), (dft, dftv), (proto, protov)), 3
        )
    ]
    for load in loads:
        load.start()
    pl.semaphore_wait(plane_sem, len(line))
    for part in range(PARTS):
        exchange(part, send, recv.at[part, chip], sibling_sem, sent, recv_sem)
    for load in loads:
        load.wait()

    def toeplitz(n, carry):
        b, block = n // NBLOCK, lax.rem(n, NBLOCK)
        for part in range(2):
            wide = jnp.broadcast_to(chv[dmv[b], pl.ds(part * NBLOCK + block, 1), :], (8, 2 * CHANNELS))
            eight = pltpu.roll(wide, CHANNELS + 1, 1, stride=1, stride_axis=0)
            for k in range(0, CHANNELS, 16):
                both = [pltpu.roll(eight, k + i, 1)[:, :CHANNELS] if k + i else eight[:, :CHANNELS] for i in (0, 8)]
                rows = pl.ds(pl.multiple_of(block * CHANNELS + k, 16), 16)
                tables[b, rows, part * CHANNELS : (part + 1) * CHANNELS] = jnp.concatenate(both, axis=0).astype(BF16)
        return carry

    lax.fori_loop(0, 2 * NBLOCK, toeplitz, 0)

    to_device = lax.rem(core + row // 128, 2) * 16 + (row // 8) % 16
    order = ones_where(
        (col // 128 == row % 2) & ((col // 64) % 2 == (row // 2) % 2) & (col % 64 == to_device * 2 + (row // 4) % 2)
    )
    for part in range(PARTS):
        arrived = recv.at[part]
        pltpu.make_async_copy(arrived, arrived, recv_sem.at[part]).wait()
        for c in range(2):
            both, real, imag = [], [], []
            for number in range(2):
                real.append(recv[part, :, number, c].reshape(512, SPAN))
                imag.append(recv[part, :, number, 2 + c].reshape(512, SPAN))
            for p in range(2):
                for number in range(2):
                    for zz in range(4):
                        inputs = (zz * 2 + number) * 128
                        both.append(win[p, c, :, inputs : inputs + 128])
            parts = jnp.concatenate(
                [
                    jnp.concatenate(real + [-half for half in imag], axis=0),
                    jnp.concatenate(imag + real, axis=0),
                ],
                axis=1,
            )
            beams[c] = dot(jnp.concatenate(both, axis=1), parts).astype(BF16)
        for zz in range(4):
            rows = slice(zz * 64, zz * 64 + 64)
            block = jnp.concatenate([beams[c, rows, q * SPAN : q * SPAN + SPAN] for c in range(2) for q in range(2)], axis=0)
            block = dot(order, block).astype(BF16)
            send2[part, zz * 16 : zz * 16 + 16, core] = block[:128].reshape(16, 8, SPAN)
            give2[part, zz * 16 : zz * 16 + 16] = block[128:].reshape(16, 8, SPAN)
        hand_over(part, give2, send2, given2, sibling_sem2)
        exchange(part, send2, recv2.at[part, chip], sibling_sem2, sent2, recv_sem2)

    for blocks, sem in ((give, given), (give2, given2)):
        pltpu.make_async_copy(blocks, blocks, sem).wait()
    for part in range(PARTS):
        for blocks, sem in ((send.at[part, 0:63], sent), (send2.at[part, 0:63], sent2), (recv2.at[part], recv_sem2)):
            pltpu.make_async_copy(blocks, blocks, sem.at[part]).wait()


def tail(xv, tv, dftv, protov, out, band, xs, padded0, padded1, even0, even1, odd0, odd1):
    row, col = iota(0), iota(1)
    sort = ones_where(col == ((row % 32) // 2 * 2 + (row % 64) // 32) * 8 + (row // 64) * 2 + row % 2)
    spread = ones_where(col == (row % 8) * 32 + row // 8)
    for part in range(PARTS):
        for n in range(4):
            block = dot(sort, xv[part, n * 256 : n * 256 + 256, :]).astype(BF16)
            for k in range(4):
                rows = slice((k % 2) * 256 + n * 64, (k % 2) * 256 + n * 64 + 64)
                xs[k // 2, rows, part * SPAN : part * SPAN + SPAN] = block[k * 64 : k * 64 + 64]
    for b, padded in enumerate((padded0, padded1)):
        turned = lax.dot_general(spread, xs[b], (((1,), (1,)), ((), ())), preferred_element_type=F32)
        power = jnp.sum(turned * turned, axis=0, keepdims=True) * (1.0 / TIME)
        band[b : b + 1, :] = power[:, :256] + power[:, 256:]
        spectra = dot(turned.astype(BF16), dftv[...])
        before = pltpu.roll(spectra[168:], 1, 0)
        padded[0:88, :] = jnp.where(iota(0, (88, 512)) % 8 == 0, 0.0, before)
        padded[88:344, :] = spectra
    results = []
    for b, (padded, even, odd) in enumerate(((padded0, even0, odd0), (padded1, even1, odd1))):
        for n in range(4):
            lanes = slice(n * 128, n * 128 + 128)
            series = protov[0:1, lanes] * padded[88:344, lanes]
            for tap in range(1, TAPS):
                series = series + protov[tap : tap + 1, lanes] * padded[88 - 8 * tap : 344 - 8 * tap, lanes]
            after = pltpu.roll(series[:32], 31, 0)
            after = jnp.where(iota(0, (32, 128)) % 8 == 7, 0.0, after)
            even[0:256, lanes] = series.astype(BF16)
            even[256:288, lanes] = after.astype(BF16)
            odd[0:272, lanes] = jnp.concatenate([series[8:], after[:24]], axis=0).astype(BF16)
        shifted = [even[0:256], odd[0:256], even[16:272], odd[16:272], even[32:288]]
        lhs = jnp.concatenate(
            [jnp.concatenate([block[:, p * 256 : p * 256 + 256] for block in shifted], axis=1) for p in range(2)], axis=0
        )
        product = dot(lhs, tv[b])
        real = product[:256, :256] + product[256:, 256:]
        imag = product[256:, :256] - product[:256, 256:]
        results.append(jnp.concatenate([real, imag], axis=1).astype(BF16))
    final = ones_where(col == (row % 4) * 64 + ((row // 4) % 8) * 8 + row // 32)
    for j in range(4):
        rows = slice(64 * j, 64 * j + 64)
        block = jnp.concatenate(
            [
                jnp.concatenate([results[b][rows, half * 128 + q * 256 : half * 128 + q * 256 + 128] for q in range(2)], axis=1)
                for half in range(2) for b in range(2)
            ],
            axis=0,
        )
        block = dot(final, block).astype(BF16)
        for q in range(2):
            for k in range(8):
                out[q, 128 * k + 32 * j : 128 * k + 32 * j + 32, :] = block[32 * k : 32 * k + 32, q * 128 : q * 128 + 128]


def in_hbm(array):
    return pltpu.with_memory_space_constraint(array, pltpu.HBM)


def on_device(voltages, weights, flags, dm_index):
    hbm = pl.BlockSpec(memory_space=pl.ANY)
    vmem = pl.BlockSpec(memory_space=pltpu.VMEM)
    dma = pltpu.SemaphoreType.DMA
    params = dict(vmem_limit_bytes=24 * 1024 * 1024)
    beams, tables, dft, proto = pl.pallas_call(
        body,
        out_shape=(
            jax.ShapeDtypeStruct((PARTS, 64, 2, 8, SPAN), BF16),
            jax.ShapeDtypeStruct((2, NBLOCK * CHANNELS, 512), BF16),
            jax.ShapeDtypeStruct((512, 512), BF16),
            jax.ShapeDtypeStruct((TAPS, 512), F32),
        ),
        in_specs=[hbm] * 7,
        out_specs=(vmem,) * 4,
        scratch_shapes=[
            pltpu.VMEM((16, 4, 2, 2, 16, 256), BF16),
            pltpu.VMEM((PARTS, 64, 4, 8, SPAN), BF16),
            pltpu.VMEM((PARTS, 64, 2, 4, 8, SPAN), BF16),
            pltpu.VMEM((PARTS, 64, 2, 4, 8, SPAN), BF16),
            pltpu.VMEM((2, 2, 256, 1024), BF16),
            pltpu.VMEM((DMS, 16, 512), F32),
            pltpu.VMEM((1, 64), jnp.int32),
            pltpu.SMEM((2,), jnp.int32),
            pltpu.VMEM((2, 256, 2 * SPAN), BF16),
            pltpu.VMEM((PARTS, 64, 8, SPAN), BF16),
            pltpu.VMEM((PARTS, 64, 2, 8, SPAN), BF16),
            pltpu.VMEM((16, 256), F32),
            dma((8,)),
            pltpu.SemaphoreType.REGULAR,
            dma,
            dma,
            *[dma((PARTS,)) for _ in range(6)],
        ],
        compiler_params=pltpu.CompilerParams(collective_id=0, has_side_effects=True, **params),
        name="beamform",
    )(
        in_hbm(voltages.reshape(16, 4, 2, 2, 16, TIME)),
        in_hbm(weights),
        in_hbm(flags),
        in_hbm(dm_index),
        in_hbm(jnp.asarray(chirp_rows()).astype(BF16).astype(F32)),
        in_hbm(jnp.asarray(dft_rows()).astype(BF16)),
        in_hbm(jnp.asarray(prototype())),
    )
    dedispersed, bandpass = pl.pallas_call(
        tail,
        out_shape=(
            jax.ShapeDtypeStruct((2, 2 * TIME * 2, 128), BF16),
            jax.ShapeDtypeStruct((2, CHANNELS), F32),
        ),
        in_specs=[vmem] * 4,
        out_specs=(vmem, vmem),
        scratch_shapes=[
            pltpu.VMEM((2, 512, 256), BF16),
            *[pltpu.VMEM((344, 512), F32) for _ in range(2)],
            *[pltpu.VMEM((288, 512), BF16) for _ in range(2)],
            *[pltpu.VMEM((272, 512), BF16) for _ in range(2)],
        ],
        compiler_params=pltpu.CompilerParams(**params),
        name="synthesis",
    )(
        beams.reshape(PARTS, 1024, SPAN),
        tables,
        dft,
        proto,
    )
    dedispersed = dedispersed.reshape(2, 512, 2, 128).transpose(0, 2, 1, 3).reshape(2, 2, TIME * CHANNELS)
    return dedispersed, bandpass


def solution(mesh):
    return jax.shard_map(
        on_device,
        mesh=mesh,
        in_specs=(
            P(None, ("stn", "chan"), None, None),
            P(None, ("stn", "chan"), None, None),
            P(("stn", "chan"), None),
            P(("stn", "chan")),
        ),
        out_specs=(P(None, ("stn", "chan"), None), P(("stn", "chan"), None)),
        check_vma=False,
    )
```

```python
import math
import random

import jax
import jax.numpy as jnp
import numpy as np
from jax import lax
from jax.experimental import pallas as pl
from jax.experimental.pallas import tpu as pltpu
from jax.sharding import PartitionSpec as P

CHANNELS = 256
BEAMS = 256
INPUTS = 1024
TIME = 256
TAPS = 12
CHIRP = 1024
DMS = 16
NBLOCK = CHIRP // CHANNELS + 1
DEVICES = 128
CHAN_AXIS = 16
PARTS = 2
SPAN = TIME // PARTS
MESH = pl.DeviceIdType.MESH
BF16 = jnp.bfloat16
F32 = jnp.float32


def dft_rows():
    order = np.arange(CHANNELS)
    angle = 2.0 * math.pi / CHANNELS * (order[:, None] * order[None, :] % CHANNELS)
    cosine = np.cos(angle) / math.sqrt(CHANNELS)
    sine = np.sin(angle) / math.sqrt(CHANNELS)
    return np.block([[cosine, sine], [-sine, cosine]]).astype(np.float32)


def prototype():
    counter = np.arange(TAPS * CHANNELS, dtype=np.float64)
    offset = (counter + 0.5) / CHANNELS - TAPS / 2.0
    window = 0.54 + 0.46 * np.cos(math.pi * offset / (TAPS / 2.0))
    taps = (np.sinc(offset) * window).reshape(TAPS, CHANNELS)
    return np.concatenate([taps, taps], axis=1).astype(np.float32)


def chirp_rows():
    dms = np.arange(DMS, dtype=np.int64)[:, None, None]
    lag = np.arange(NBLOCK)[None, :, None] * CHANNELS + CHANNELS - 1 - np.arange(2 * CHANNELS)[None, None, :]
    valid = (lag >= 0) & (lag < CHIRP)
    lag = np.clip(lag, 0, CHIRP - 1)
    angle = math.pi * ((dms + 1) * lag * lag % (2 * DMS * CHIRP)) / (DMS * CHIRP)
    real = np.where(valid, np.cos(angle), 0.0) / math.sqrt(CHIRP)
    imag = np.where(valid, np.sin(angle), 0.0) / math.sqrt(CHIRP)
    rows = np.concatenate([real, imag, np.zeros((DMS, 6, 2 * CHANNELS))], axis=1)
    return rows.astype(np.float32)


def iota(axis, shape=(256, 256)):
    return lax.broadcasted_iota(jnp.int32, shape, axis)


def ones_where(condition):
    return jnp.where(condition, 1.0, 0.0).astype(BF16)


def dot(a, b):
    return jnp.dot(a, b, preferred_element_type=F32)


def exchange_order():
    left = [(dz, dy, dx) for dz in range(4) for dy in range(4) for dx in range(4)]
    random.Random(7).shuffle(left)
    hops, ordered = [0, 0, 0], []
    while left:
        def uneven(step):
            return sum((done + min(d, 4 - d) - len(ordered) - 1) ** 2 for done, d in zip(hops, step))

        best = min(left, key=uneven)
        left.remove(best)
        ordered.append(best)
        hops = [done + min(d, 4 - d) for done, d in zip(hops, best)]
    return ordered


def body(
    volt, wgt, flags, dm, chirps, dft, proto, recv2, tables, dftv, protov,
    vin, give, send, recv, win, chv, flagv, dmv, beams, give2, send2, keep,
    load_sem, plane_sem, given, given2, sent, sent2, sibling_sem, sibling_sem2, recv_sem, recv_sem2, pack_sem, packs_sent, relays_sent, *stages,
):
    x = lax.rem(lax.axis_index("chan"), 4)
    y = lax.axis_index("chan") // 4
    z = lax.axis_index("stn") // 2
    core = lax.rem(lax.axis_index("stn"), 2)
    chip = z * CHAN_AXIS + lax.axis_index("chan")
    sibling = (z * 2 + 1 - core, lax.axis_index("chan"))

    turn = 1 + 2 * core
    zs = [lax.rem(z + dz * turn, 4) for dz in range(4)]
    xs = [lax.rem(x + dx * turn, 4) for dx in range(4)]
    ys = [lax.rem(y + dy * turn, 4) * 4 for dy in range(4)]

    flag_load = pltpu.make_async_copy(flags, flagv, load_sem.at[0])
    flag_load.start()
    volt_loads = [
        pltpu.make_async_copy(volt.at[:, :, number], vin.at[:, :, number], load_sem.at[n])
        for n, number in ((1, 1 - core), (2, core))
    ]
    for load in volt_loads:
        load.start()

    barrier = pltpu.get_barrier_semaphore()
    line = [(zs[dz] * 2 + core, ys[0] + x) for dz in range(1, 4)]
    plane = [(z * 2 + core, ys[dy] + xs[dx]) for dy in range(4) for dx in range(4) if (dy, dx) != (0, 0)]
    greeted = [sibling] + line + plane
    for peer in greeted:
        pl.semaphore_signal(barrier, inc=1, device_id=peer, device_id_type=MESH)

    def hand_over(part, give, send, given, sibling_sem):
        pltpu.make_async_remote_copy(
            src_ref=give.at[part],
            dst_ref=send.at[part, :, :, :, core] if len(send.shape) == 8 else send.at[part, :, core],
            send_sem=given,
            recv_sem=sibling_sem.at[part],
            device_id=sibling,
            device_id_type=MESH,
        ).start()

    def exchange(part, send, landing, sibling_sem, sent, recv_sem):
        share = send.at[part, :, 1 - core]
        pltpu.make_async_copy(share, share, sibling_sem.at[part]).wait()
        pltpu.make_async_copy(send.at[part, chip], landing, recv_sem.at[part]).start()
        for dz, dy, dx in exchange_order():
            if (dz, dy, dx) != (0, 0, 0):
                chan = ys[dy] + xs[dx]
                pltpu.make_async_remote_copy(
                    src_ref=send.at[part, zs[dz] * CHAN_AXIS + chan],
                    dst_ref=landing,
                    send_sem=sent.at[part],
                    recv_sem=recv_sem.at[part],
                    device_id=(zs[dz] * 2 + core, chan),
                    device_id_type=MESH,
                ).start()

    by_z, by_x, by_y, by_xz, by_yz, by_xy, by_xyz = stages

    def place(steps):
        dz, dy, dx = steps
        return zs[dz % 4] * 2 + core, ys[dy % 4] + xs[dx % 4]

    def packs(part):
        near = (-1, 0, 1)
        listed = []
        for m in range(3):
            listed.append(((3, m, slice(0, 3)), by_z.at[part, m], (1, 0, 0), [(1, m - 1, d) for d in near]))
            listed.append(((m, slice(0, 3), 3), by_x.at[part, m], (0, 0, 1), [(m - 1, d, 1) for d in near]))
            listed.append(((m, 3, slice(0, 3)), by_y.at[part, m], (0, 1, 0), [(m - 1, 1, d) for d in near]))
        listed.append(((3, slice(0, 3), 3), by_xz.at[part], (1, 0, 1), [(1, d, 1) for d in near]))
        listed.append(((3, 3, slice(0, 3)), by_yz.at[part], (1, 1, 0), [(1, 1, d) for d in near]))
        for m in range(3):
            listed.append(((m, 3, 3), by_xy.at[part, m], (0, 1, 1), [(m - 1, 1, 1)]))
        listed.append(((3, 3, 3), by_xyz.at[part], (1, 1, 1), [(1, 1, 1)]))
        return [(15 * part + n, *pack) for n, pack in enumerate(listed)]

    def send_packs(part):
        share = send.at[part, :, :, :, 1 - core]
        pltpu.make_async_copy(share, share, sibling_sem.at[part]).wait()
        for n, at, stage, steps, _ in packs(part):
            pltpu.make_async_remote_copy(
                src_ref=send.at[part, at[0], at[1], at[2]],
                dst_ref=stage,
                send_sem=packs_sent,
                recv_sem=pack_sem.at[n],
                device_id=place(steps),
                device_id_type=MESH,
            ).start()

    def send_direct(part):
        pltpu.make_async_copy(send.at[part, 1, 1, 1], recv.at[part, chip], recv_sem.at[part]).start()
        for steps in exchange_order():
            if 2 not in steps and steps != (0, 0, 0):
                at = [(d + 1) % 4 for d in steps]
                pltpu.make_async_remote_copy(
                    src_ref=send.at[part, at[0], at[1], at[2]],
                    dst_ref=recv.at[part, chip],
                    send_sem=sent.at[part],
                    recv_sem=recv_sem.at[part],
                    device_id=place(steps),
                    device_id_type=MESH,
                ).start()

    def relay_packs(part):
        for n, _, stage, steps, onward in packs(part):
            pltpu.make_async_copy(stage, stage, pack_sem.at[n]).wait()
            dz, dy, dx = (-d % 4 for d in steps)
            origin = zs[dz] * CHAN_AXIS + ys[dy] + xs[dx]
            for m, further in enumerate(onward):
                pltpu.make_async_remote_copy(
                    src_ref=stage.at[m] if len(onward) > 1 else stage,
                    dst_ref=recv.at[part, origin],
                    send_sem=relays_sent,
                    recv_sem=recv_sem.at[part],
                    device_id=place(further),
                    device_id_type=MESH,
                ).start()

    flag_load.wait()
    row, col = iota(0), iota(1)
    hits = ones_where(iota(0, (256, 64)) == flagv[...])
    count = dot(hits, jnp.ones((64, 256), BF16))
    keep_rows = ones_where((count < 0.5) & (row % 16 == col % 16))
    keep[...] = dot(ones_where(iota(1, (16, 256)) // 16 == iota(0, (16, 256))), keep_rows)

    def sort_out(number):
        way = 1 + 2 * number
        there = (row // 128) * 8 + ((x + (row // 32 + 3) % 4 * way) % 4) * 2 + (row // 8) % 2
        swap = jnp.where((col // 16 == ((row // 16) % 2) * 8 + row % 8) & (col % 16 == there), 1.0, 0.0)
        for zz in range(4):
            for half in range(2):
                block = vin[:, zz, number, half].reshape(256, 256)
                mine = (swap * keep[pl.ds((zz * 2 + number) * 2 + half, 1), :]).astype(BF16)
                sorted_block = dot(mine, block).astype(BF16)
                for one in range(2):
                    mz = lax.rem((zz + 4 - z) * way + 1, 4)
                    my = lax.rem((half * 2 + one + 4 - y) * way + 1, 4)
                    yield mz, my, sorted_block[one * 128 : one * 128 + 128].reshape(4, 4, 8, 256)

    volt_loads[0].wait()
    for mz, my, block in sort_out(1 - core):
        for part in range(PARTS):
            give[part, mz, my] = block[..., part * SPAN : part * SPAN + SPAN]
    pl.semaphore_wait(barrier, len(greeted))
    for peer in line:
        pl.semaphore_signal(plane_sem, inc=1, device_id=peer, device_id_type=MESH)
    for part in range(PARTS):
        hand_over(part, give, send, given, sibling_sem)
    volt_loads[1].wait()
    for mz, my, block in sort_out(core):
        for part in range(PARTS):
            send[part, mz, my, :, core] = block[..., part * SPAN : part * SPAN + SPAN]
    loads = [
        pltpu.make_async_copy(source, target, load_sem.at[n])
        for n, (source, target) in enumerate(
            ((wgt, win), (dm, dmv), (chirps, chv), (dft, dftv), (proto, protov)), 3
        )
    ]
    for load in loads:
        load.start()
    pl.semaphore_wait(plane_sem, len(line))
    send_packs(0)
    send_direct(0)
    send_packs(1)
    relay_packs(0)
    send_direct(1)
    relay_packs(1)
    for load in loads:
        load.wait()

    def toeplitz(n, carry):
        b, block = n // NBLOCK, lax.rem(n, NBLOCK)
        for part in range(2):
            wide = jnp.broadcast_to(chv[dmv[b], pl.ds(part * NBLOCK + block, 1), :], (8, 2 * CHANNELS))
            eight = pltpu.roll(wide, CHANNELS + 1, 1, stride=1, stride_axis=0)
            for k in range(0, CHANNELS, 16):
                both = [pltpu.roll(eight, k + i, 1)[:, :CHANNELS] if k + i else eight[:, :CHANNELS] for i in (0, 8)]
                rows = pl.ds(pl.multiple_of(block * CHANNELS + k, 16), 16)
                tables[b, rows, part * CHANNELS : (part + 1) * CHANNELS] = jnp.concatenate(both, axis=0).astype(BF16)
        return carry

    lax.fori_loop(0, 2 * NBLOCK, toeplitz, 0)

    to_device = lax.rem(core + row // 128, 2) * 16 + (row // 8) % 16
    order = ones_where(
        (col // 128 == row % 2) & ((col // 64) % 2 == (row // 2) % 2) & (col % 64 == to_device * 2 + (row // 4) % 2)
    )
    for part in range(PARTS):
        arrived = recv.at[part]
        pltpu.make_async_copy(arrived, arrived, recv_sem.at[part]).wait()
        for c in range(2):
            both, real, imag = [], [], []
            for number in range(2):
                real.append(recv[part, :, number, c].reshape(512, SPAN))
                imag.append(recv[part, :, number, 2 + c].reshape(512, SPAN))
            for p in range(2):
                for number in range(2):
                    for zz in range(4):
                        inputs = (zz * 2 + number) * 128
                        both.append(win[p, c, :, inputs : inputs + 128])
            parts = jnp.concatenate(
                [
                    jnp.concatenate(real + [-half for half in imag], axis=0),
                    jnp.concatenate(imag + real, axis=0),
                ],
                axis=1,
            )
            beams[c] = dot(jnp.concatenate(both, axis=1), parts).astype(BF16)
        for zz in range(4):
            rows = slice(zz * 64, zz * 64 + 64)
            block = jnp.concatenate([beams[c, rows, q * SPAN : q * SPAN + SPAN] for c in range(2) for q in range(2)], axis=0)
            block = dot(order, block).astype(BF16)
            send2[part, zz * 16 : zz * 16 + 16, core] = block[:128].reshape(16, 8, SPAN)
            give2[part, zz * 16 : zz * 16 + 16] = block[128:].reshape(16, 8, SPAN)
        hand_over(part, give2, send2, given2, sibling_sem2)
        exchange(part, send2, recv2.at[part, chip], sibling_sem2, sent2, recv_sem2)

    for blocks, sem in ((give, given), (give2, given2)):
        pltpu.make_async_copy(blocks, blocks, sem).wait()
    for sem in (packs_sent, relays_sent):
        for part in range(PARTS):
            blocks = recv.at[part, 0:37]
            pltpu.make_async_copy(blocks, blocks, sem).wait()
    for part in range(PARTS):
        for blocks, sem in ((recv.at[part, 0:26], sent), (send2.at[part, 0:63], sent2), (recv2.at[part], recv_sem2)):
            pltpu.make_async_copy(blocks, blocks, sem.at[part]).wait()


def tail(xv, tv, dftv, protov, out, band, xs, padded0, padded1, even0, even1, odd0, odd1):
    row, col = iota(0), iota(1)
    sort = ones_where(col == ((row % 32) // 2 * 2 + (row % 64) // 32) * 8 + (row // 64) * 2 + row % 2)
    spread = ones_where(col == (row % 8) * 32 + row // 8)
    for part in range(PARTS):
        for n in range(4):
            block = dot(sort, xv[part, n * 256 : n * 256 + 256, :]).astype(BF16)
            for k in range(4):
                rows = slice((k % 2) * 256 + n * 64, (k % 2) * 256 + n * 64 + 64)
                xs[k // 2, rows, part * SPAN : part * SPAN + SPAN] = block[k * 64 : k * 64 + 64]
    for b, padded in enumerate((padded0, padded1)):
        turned = lax.dot_general(spread, xs[b], (((1,), (1,)), ((), ())), preferred_element_type=F32)
        power = jnp.sum(turned * turned, axis=0, keepdims=True) * (1.0 / TIME)
        band[b : b + 1, :] = power[:, :256] + power[:, 256:]
        spectra = dot(turned.astype(BF16), dftv[...])
        before = pltpu.roll(spectra[168:], 1, 0)
        padded[0:88, :] = jnp.where(iota(0, (88, 512)) % 8 == 0, 0.0, before)
        padded[88:344, :] = spectra
    results = []
    for b, (padded, even, odd) in enumerate(((padded0, even0, odd0), (padded1, even1, odd1))):
        for n in range(4):
            lanes = slice(n * 128, n * 128 + 128)
            series = protov[0:1, lanes] * padded[88:344, lanes]
            for tap in range(1, TAPS):
                series = series + protov[tap : tap + 1, lanes] * padded[88 - 8 * tap : 344 - 8 * tap, lanes]
            after = pltpu.roll(series[:32], 31, 0)
            after = jnp.where(iota(0, (32, 128)) % 8 == 7, 0.0, after)
            even[0:256, lanes] = series.astype(BF16)
            even[256:288, lanes] = after.astype(BF16)
            odd[0:272, lanes] = jnp.concatenate([series[8:], after[:24]], axis=0).astype(BF16)
        shifted = [even[0:256], odd[0:256], even[16:272], odd[16:272], even[32:288]]
        lhs = jnp.concatenate(
            [jnp.concatenate([block[:, p * 256 : p * 256 + 256] for block in shifted], axis=1) for p in range(2)], axis=0
        )
        product = dot(lhs, tv[b])
        real = product[:256, :256] + product[256:, 256:]
        imag = product[256:, :256] - product[:256, 256:]
        results.append(jnp.concatenate([real, imag], axis=1).astype(BF16))
    final = ones_where(col == (row % 4) * 64 + ((row // 4) % 8) * 8 + row // 32)
    for j in range(4):
        rows = slice(64 * j, 64 * j + 64)
        block = jnp.concatenate(
            [
                jnp.concatenate([results[b][rows, half * 128 + q * 256 : half * 128 + q * 256 + 128] for q in range(2)], axis=1)
                for half in range(2) for b in range(2)
            ],
            axis=0,
        )
        block = dot(final, block).astype(BF16)
        for q in range(2):
            for k in range(8):
                out[q, 128 * k + 32 * j : 128 * k + 32 * j + 32, :] = block[32 * k : 32 * k + 32, q * 128 : q * 128 + 128]


def in_hbm(array):
    return pltpu.with_memory_space_constraint(array, pltpu.HBM)


def on_device(voltages, weights, flags, dm_index):
    hbm = pl.BlockSpec(memory_space=pl.ANY)
    vmem = pl.BlockSpec(memory_space=pltpu.VMEM)
    dma = pltpu.SemaphoreType.DMA
    params = dict(vmem_limit_bytes=24 * 1024 * 1024)
    beams, tables, dft, proto = pl.pallas_call(
        body,
        out_shape=(
            jax.ShapeDtypeStruct((PARTS, 64, 2, 8, SPAN), BF16),
            jax.ShapeDtypeStruct((2, NBLOCK * CHANNELS, 512), BF16),
            jax.ShapeDtypeStruct((512, 512), BF16),
            jax.ShapeDtypeStruct((TAPS, 512), F32),
        ),
        in_specs=[hbm] * 7,
        out_specs=(vmem,) * 4,
        scratch_shapes=[
            pltpu.VMEM((16, 4, 2, 2, 16, 256), BF16),
            pltpu.VMEM((PARTS, 4, 4, 4, 4, 8, SPAN), BF16),
            pltpu.VMEM((PARTS, 4, 4, 4, 2, 4, 8, SPAN), BF16),
            pltpu.VMEM((PARTS, 64, 2, 4, 8, SPAN), BF16),
            pltpu.VMEM((2, 2, 256, 1024), BF16),
            pltpu.VMEM((DMS, 16, 512), F32),
            pltpu.VMEM((1, 64), jnp.int32),
            pltpu.SMEM((2,), jnp.int32),
            pltpu.VMEM((2, 256, 2 * SPAN), BF16),
            pltpu.VMEM((PARTS, 64, 8, SPAN), BF16),
            pltpu.VMEM((PARTS, 64, 2, 8, SPAN), BF16),
            pltpu.VMEM((16, 256), F32),
            dma((8,)),
            pltpu.SemaphoreType.REGULAR,
            dma,
            dma,
            *[dma((PARTS,)) for _ in range(6)],
            dma((30,)),
            dma,
            dma,
            *[
                pltpu.VMEM((PARTS,) + shape + (2, 4, 8, SPAN), BF16)
                for shape in [(3, 3), (3, 3), (3, 3), (3,), (3,), (3,), ()]
            ],
        ],
        compiler_params=pltpu.CompilerParams(collective_id=0, has_side_effects=True, **params),
        name="beamform",
    )(
        in_hbm(voltages.reshape(16, 4, 2, 2, 16, TIME)),
        in_hbm(weights),
        in_hbm(flags),
        in_hbm(dm_index),
        in_hbm(jnp.asarray(chirp_rows()).astype(BF16).astype(F32)),
        in_hbm(jnp.asarray(dft_rows()).astype(BF16)),
        in_hbm(jnp.asarray(prototype())),
    )
    dedispersed, bandpass = pl.pallas_call(
        tail,
        out_shape=(
            jax.ShapeDtypeStruct((2, 2 * TIME * 2, 128), BF16),
            jax.ShapeDtypeStruct((2, CHANNELS), F32),
        ),
        in_specs=[vmem] * 4,
        out_specs=(vmem, vmem),
        scratch_shapes=[
            pltpu.VMEM((2, 512, 256), BF16),
            *[pltpu.VMEM((344, 512), F32) for _ in range(2)],
            *[pltpu.VMEM((288, 512), BF16) for _ in range(2)],
            *[pltpu.VMEM((272, 512), BF16) for _ in range(2)],
        ],
        compiler_params=pltpu.CompilerParams(**params),
        name="synthesis",
    )(
        beams.reshape(PARTS, 1024, SPAN),
        tables,
        dft,
        proto,
    )
    dedispersed = dedispersed.reshape(2, 512, 2, 128).transpose(0, 2, 1, 3).reshape(2, 2, TIME * CHANNELS)
    return dedispersed, bandpass


def solution(mesh):
    return jax.shard_map(
        on_device,
        mesh=mesh,
        in_specs=(
            P(None, ("stn", "chan"), None, None),
            P(None, ("stn", "chan"), None, None),
            P(("stn", "chan"), None),
            P(("stn", "chan")),
        ),
        out_specs=(P(None, ("stn", "chan"), None), P(("stn", "chan"), None)),
        check_vma=False,
    )
```

```python
import math
import random

import jax
import jax.numpy as jnp
import numpy as np
from jax import lax
from jax.experimental import pallas as pl
from jax.experimental.pallas import tpu as pltpu
from jax.sharding import PartitionSpec as P

CHANNELS = 256
BEAMS = 256
INPUTS = 1024
TIME = 256
TAPS = 12
CHIRP = 1024
DMS = 16
NBLOCK = CHIRP // CHANNELS + 1
DEVICES = 128
CHAN_AXIS = 16
PARTS = 2
SPAN = TIME // PARTS
MESH = pl.DeviceIdType.MESH
BF16 = jnp.bfloat16
F32 = jnp.float32


def dft_rows():
    order = np.arange(CHANNELS)
    angle = 2.0 * math.pi / CHANNELS * (order[:, None] * order[None, :] % CHANNELS)
    cosine = np.cos(angle) / math.sqrt(CHANNELS)
    sine = np.sin(angle) / math.sqrt(CHANNELS)
    return np.block([[cosine, sine], [-sine, cosine]]).astype(np.float32)


def prototype():
    counter = np.arange(TAPS * CHANNELS, dtype=np.float64)
    offset = (counter + 0.5) / CHANNELS - TAPS / 2.0
    window = 0.54 + 0.46 * np.cos(math.pi * offset / (TAPS / 2.0))
    taps = (np.sinc(offset) * window).reshape(TAPS, CHANNELS)
    return np.concatenate([taps, taps], axis=1).astype(np.float32)


def chirp_rows():
    dms = np.arange(DMS, dtype=np.int64)[:, None, None]
    lag = np.arange(NBLOCK)[None, :, None] * CHANNELS + CHANNELS - 1 - np.arange(2 * CHANNELS)[None, None, :]
    valid = (lag >= 0) & (lag < CHIRP)
    lag = np.clip(lag, 0, CHIRP - 1)
    angle = math.pi * ((dms + 1) * lag * lag % (2 * DMS * CHIRP)) / (DMS * CHIRP)
    real = np.where(valid, np.cos(angle), 0.0) / math.sqrt(CHIRP)
    imag = np.where(valid, np.sin(angle), 0.0) / math.sqrt(CHIRP)
    rows = np.concatenate([real, imag, np.zeros((DMS, 6, 2 * CHANNELS))], axis=1)
    return rows.astype(np.float32)


def iota(axis, shape=(256, 256)):
    return lax.broadcasted_iota(jnp.int32, shape, axis)


def ones_where(condition):
    return jnp.where(condition, 1.0, 0.0).astype(BF16)


def dot(a, b):
    return jnp.dot(a, b, preferred_element_type=F32)


def exchange_order():
    left = [(dz, dy, dx) for dz in range(4) for dy in range(4) for dx in range(4)]
    random.Random(7).shuffle(left)
    hops, ordered = [0, 0, 0], []
    while left:
        def uneven(step):
            return sum((done + min(d, 4 - d) - len(ordered) - 1) ** 2 for done, d in zip(hops, step))

        best = min(left, key=uneven)
        left.remove(best)
        ordered.append(best)
        hops = [done + min(d, 4 - d) for done, d in zip(hops, best)]
    return ordered


def body(
    volt, wgt, flags, dm, chirps, dft, proto, recv2, tables, dftv, protov, series0, last0, power0,
    vin, give, send, recv, win, chv, flagv, dmv, beams, give2, send2, keep, ordered, padded,
    load_sem, plane_sem, given, given2, sent, sent2, sibling_sem, sibling_sem2, recv_sem, recv_sem2, pack_sem, packs_sent, relays_sent, *stages,
):
    x = lax.rem(lax.axis_index("chan"), 4)
    y = lax.axis_index("chan") // 4
    z = lax.axis_index("stn") // 2
    core = lax.rem(lax.axis_index("stn"), 2)
    chip = z * CHAN_AXIS + lax.axis_index("chan")
    sibling = (z * 2 + 1 - core, lax.axis_index("chan"))

    turn = 1 + 2 * core
    zs = [lax.rem(z + dz * turn, 4) for dz in range(4)]
    xs = [lax.rem(x + dx * turn, 4) for dx in range(4)]
    ys = [lax.rem(y + dy * turn, 4) * 4 for dy in range(4)]

    flag_load = pltpu.make_async_copy(flags, flagv, load_sem.at[0])
    flag_load.start()
    volt_loads = [
        pltpu.make_async_copy(volt.at[:, :, number], vin.at[:, :, number], load_sem.at[n])
        for n, number in ((1, 1 - core), (2, core))
    ]
    for load in volt_loads:
        load.start()

    barrier = pltpu.get_barrier_semaphore()
    line = [(zs[dz] * 2 + core, ys[0] + x) for dz in range(1, 4)]
    plane = [(z * 2 + core, ys[dy] + xs[dx]) for dy in range(4) for dx in range(4) if (dy, dx) != (0, 0)]
    greeted = [sibling] + line + plane
    for peer in greeted:
        pl.semaphore_signal(barrier, inc=1, device_id=peer, device_id_type=MESH)

    def hand_over(part, give, send, given, sibling_sem):
        pltpu.make_async_remote_copy(
            src_ref=give.at[part],
            dst_ref=send.at[part, :, :, :, core] if len(send.shape) == 8 else send.at[part, :, core],
            send_sem=given,
            recv_sem=sibling_sem.at[part],
            device_id=sibling,
            device_id_type=MESH,
        ).start()

    def exchange(part, send, landing, sibling_sem, sent, recv_sem):
        share = send.at[part, :, 1 - core]
        pltpu.make_async_copy(share, share, sibling_sem.at[part]).wait()
        pltpu.make_async_copy(send.at[part, chip], landing, recv_sem.at[part]).start()
        for dz, dy, dx in exchange_order():
            if (dz, dy, dx) != (0, 0, 0):
                chan = ys[dy] + xs[dx]
                pltpu.make_async_remote_copy(
                    src_ref=send.at[part, zs[dz] * CHAN_AXIS + chan],
                    dst_ref=landing,
                    send_sem=sent.at[part],
                    recv_sem=recv_sem.at[part],
                    device_id=(zs[dz] * 2 + core, chan),
                    device_id_type=MESH,
                ).start()

    by_z, by_x, by_y, by_xz, by_yz, by_xy, by_xyz = stages

    def place(steps):
        dz, dy, dx = steps
        return zs[dz % 4] * 2 + core, ys[dy % 4] + xs[dx % 4]

    def packs(part):
        near = (-1, 0, 1)
        listed = []
        for m in range(3):
            listed.append(((3, m, slice(0, 3)), by_z.at[part, m], (1, 0, 0), [(1, m - 1, d) for d in near]))
            listed.append(((m, slice(0, 3), 3), by_x.at[part, m], (0, 0, 1), [(m - 1, d, 1) for d in near]))
            listed.append(((m, 3, slice(0, 3)), by_y.at[part, m], (0, 1, 0), [(m - 1, 1, d) for d in near]))
        listed.append(((3, slice(0, 3), 3), by_xz.at[part], (1, 0, 1), [(1, d, 1) for d in near]))
        listed.append(((3, 3, slice(0, 3)), by_yz.at[part], (1, 1, 0), [(1, 1, d) for d in near]))
        for m in range(3):
            listed.append(((m, 3, 3), by_xy.at[part, m], (0, 1, 1), [(m - 1, 1, 1)]))
        listed.append(((3, 3, 3), by_xyz.at[part], (1, 1, 1), [(1, 1, 1)]))
        return [(15 * part + n, *pack) for n, pack in enumerate(listed)]

    def send_packs(part):
        share = send.at[part, :, :, :, 1 - core]
        pltpu.make_async_copy(share, share, sibling_sem.at[part]).wait()
        for n, at, stage, steps, _ in packs(part):
            pltpu.make_async_remote_copy(
                src_ref=send.at[part, at[0], at[1], at[2]],
                dst_ref=stage,
                send_sem=packs_sent,
                recv_sem=pack_sem.at[n],
                device_id=place(steps),
                device_id_type=MESH,
            ).start()

    def send_direct(part):
        pltpu.make_async_copy(send.at[part, 1, 1, 1], recv.at[part, chip], recv_sem.at[part]).start()
        for steps in exchange_order():
            if 2 not in steps and steps != (0, 0, 0):
                at = [(d + 1) % 4 for d in steps]
                pltpu.make_async_remote_copy(
                    src_ref=send.at[part, at[0], at[1], at[2]],
                    dst_ref=recv.at[part, chip],
                    send_sem=sent.at[part],
                    recv_sem=recv_sem.at[part],
                    device_id=place(steps),
                    device_id_type=MESH,
                ).start()

    def relay_packs(part):
        for n, _, stage, steps, onward in packs(part):
            pltpu.make_async_copy(stage, stage, pack_sem.at[n]).wait()
            dz, dy, dx = (-d % 4 for d in steps)
            origin = zs[dz] * CHAN_AXIS + ys[dy] + xs[dx]
            for m, further in enumerate(onward):
                pltpu.make_async_remote_copy(
                    src_ref=stage.at[m] if len(onward) > 1 else stage,
                    dst_ref=recv.at[part, origin],
                    send_sem=relays_sent,
                    recv_sem=recv_sem.at[part],
                    device_id=place(further),
                    device_id_type=MESH,
                ).start()

    flag_load.wait()
    row, col = iota(0), iota(1)
    hits = ones_where(iota(0, (256, 64)) == flagv[...])
    count = dot(hits, jnp.ones((64, 256), BF16))
    keep_rows = ones_where((count < 0.5) & (row % 16 == col % 16))
    keep[...] = dot(ones_where(iota(1, (16, 256)) // 16 == iota(0, (16, 256))), keep_rows)

    def sort_out(number):
        way = 1 + 2 * number
        there = (row // 128) * 8 + ((x + (row // 32 + 3) % 4 * way) % 4) * 2 + (row // 8) % 2
        swap = jnp.where((col // 16 == ((row // 16) % 2) * 8 + row % 8) & (col % 16 == there), 1.0, 0.0)
        for zz in range(4):
            for half in range(2):
                block = vin[:, zz, number, half].reshape(256, 256)
                mine = (swap * keep[pl.ds((zz * 2 + number) * 2 + half, 1), :]).astype(BF16)
                sorted_block = dot(mine, block).astype(BF16)
                for one in range(2):
                    mz = lax.rem((zz + 4 - z) * way + 1, 4)
                    my = lax.rem((half * 2 + one + 4 - y) * way + 1, 4)
                    yield mz, my, sorted_block[one * 128 : one * 128 + 128].reshape(4, 4, 8, 256)

    volt_loads[0].wait()
    for mz, my, block in sort_out(1 - core):
        for part in range(PARTS):
            give[part, mz, my] = block[..., part * SPAN : part * SPAN + SPAN]
    pl.semaphore_wait(barrier, len(greeted))
    for peer in line:
        pl.semaphore_signal(plane_sem, inc=1, device_id=peer, device_id_type=MESH)
    for part in range(PARTS):
        hand_over(part, give, send, given, sibling_sem)
    volt_loads[1].wait()
    for mz, my, block in sort_out(core):
        for part in range(PARTS):
            send[part, mz, my, :, core] = block[..., part * SPAN : part * SPAN + SPAN]
    loads = [
        pltpu.make_async_copy(source, target, load_sem.at[n])
        for n, (source, target) in enumerate(
            ((wgt, win), (dm, dmv), (chirps, chv), (dft, dftv), (proto, protov)), 3
        )
    ]
    for load in loads:
        load.start()
    pl.semaphore_wait(plane_sem, len(line))
    send_packs(0)
    send_direct(0)
    send_packs(1)
    relay_packs(0)
    send_direct(1)
    relay_packs(1)
    for load in loads:
        load.wait()

    def toeplitz(n, carry):
        b, block = n // NBLOCK, lax.rem(n, NBLOCK)
        for part in range(2):
            wide = jnp.broadcast_to(chv[dmv[b], pl.ds(part * NBLOCK + block, 1), :], (8, 2 * CHANNELS))
            eight = pltpu.roll(wide, CHANNELS + 1, 1, stride=1, stride_axis=0)
            for k in range(0, CHANNELS, 16):
                both = [pltpu.roll(eight, k + i, 1)[:, :CHANNELS] if k + i else eight[:, :CHANNELS] for i in (0, 8)]
                rows = pl.ds(pl.multiple_of(block * CHANNELS + k, 16), 16)
                tables[b, rows, part * CHANNELS : (part + 1) * CHANNELS] = jnp.concatenate(both, axis=0).astype(BF16)
        return carry

    lax.fori_loop(0, 2 * NBLOCK, toeplitz, 0)

    to_device = lax.rem(core + row // 128, 2) * 16 + (row // 8) % 16
    order = ones_where(
        (col // 128 == row % 2) & ((col // 64) % 2 == (row // 2) % 2) & (col % 64 == to_device * 2 + (row // 4) % 2)
    )
    for part in range(PARTS):
        arrived = recv.at[part]
        pltpu.make_async_copy(arrived, arrived, recv_sem.at[part]).wait()
        for c in range(2):
            both, real, imag = [], [], []
            for number in range(2):
                real.append(recv[part, :, number, c].reshape(512, SPAN))
                imag.append(recv[part, :, number, 2 + c].reshape(512, SPAN))
            for p in range(2):
                for number in range(2):
                    for zz in range(4):
                        inputs = (zz * 2 + number) * 128
                        both.append(win[p, c, :, inputs : inputs + 128])
            parts = jnp.concatenate(
                [
                    jnp.concatenate(real + [-half for half in imag], axis=0),
                    jnp.concatenate(imag + real, axis=0),
                ],
                axis=1,
            )
            beams[c] = dot(jnp.concatenate(both, axis=1), parts).astype(BF16)
        for zz in range(4):
            rows = slice(zz * 64, zz * 64 + 64)
            block = jnp.concatenate([beams[c, rows, q * SPAN : q * SPAN + SPAN] for c in range(2) for q in range(2)], axis=0)
            block = dot(order, block).astype(BF16)
            send2[part, zz * 16 : zz * 16 + 16, core] = block[:128].reshape(16, 8, SPAN)
            give2[part, zz * 16 : zz * 16 + 16] = block[128:].reshape(16, 8, SPAN)
        hand_over(part, give2, send2, given2, sibling_sem2)
        exchange(part, send2, recv2.at[part, chip], sibling_sem2, sent2, recv_sem2)

    arrived = recv2.at[0]
    pltpu.make_async_copy(arrived, arrived, recv_sem2.at[0]).wait()
    for b, power, last in front(
        lambda n: recv2[0, n * 16 : n * 16 + 16].reshape(256, SPAN), lambda b: 0.0, dftv, protov, ordered, padded
    ):
        power0[b : b + 1, :] = power
        last0[b] = last
    for b in range(2):
        for n in range(4):
            lanes, series = synthesise(b, n, protov, padded)
            series0[b, :, lanes] = series

    for blocks, sem in ((give, given), (give2, given2)):
        pltpu.make_async_copy(blocks, blocks, sem).wait()
    for sem in (packs_sent, relays_sent):
        for part in range(PARTS):
            blocks = recv.at[part, 0:37]
            pltpu.make_async_copy(blocks, blocks, sem).wait()
    for part in range(PARTS):
        for blocks, sem in ((recv.at[part, 0:26], sent), (send2.at[part, 0:63], sent2)):
            pltpu.make_async_copy(blocks, blocks, sem.at[part]).wait()
    arrived = recv2.at[1]
    pltpu.make_async_copy(arrived, arrived, recv_sem2.at[1]).wait()


def front(chunk, before_first, dftv, protov, xs, padded):
    row, col = iota(0), iota(1)
    sort = ones_where(col == ((row % 32) // 2 * 2 + (row % 64) // 32) * 8 + (row // 64) * 2 + row % 2)
    spread = ones_where(iota(1, (SPAN, SPAN)) == (iota(0, (SPAN, SPAN)) % 8) * 16 + iota(0, (SPAN, SPAN)) // 8)
    for n in range(4):
        block = dot(sort, chunk(n)).astype(BF16)
        for k in range(4):
            xs[k // 2, (k % 2) * 256 + n * 64 : (k % 2) * 256 + n * 64 + 64, :] = block[k * 64 : k * 64 + 64]
    for b in range(2):
        turned = lax.dot_general(spread, xs[b], (((1,), (1,)), ((), ())), preferred_element_type=F32)
        power = jnp.sum(turned * turned, axis=0, keepdims=True)
        spectra = dot(turned.astype(BF16), dftv[...])
        last = spectra[SPAN - 88 :]
        first = iota(0, (88, 512)) % 8 == 0
        padded[b, 0:88, :] = jnp.where(first, before_first(b), pltpu.roll(last, 1, 0))
        padded[b, 88 : 88 + SPAN, :] = spectra
        yield b, power, pltpu.roll(last, 81, 0)


def synthesise(b, n, protov, padded):
    lanes = slice(n * 128, n * 128 + 128)
    series = protov[0:1, lanes] * padded[b, 88 : 88 + SPAN, lanes]
    for tap in range(1, TAPS):
        series = series + protov[tap : tap + 1, lanes] * padded[b, 88 - 8 * tap : 88 - 8 * tap + SPAN, lanes]
    return lanes, series


def tail(
    xv, tv, dftv, protov, series0, last0, power0, out, band,
    xs, padded, even00, even01, even10, even11, odd00, odd01, odd10, odd11, outv, bandv, out_sem,
):
    band_copy = pltpu.make_async_copy(bandv, band, out_sem.at[2])
    for b, power, _ in front(lambda n: xv[1, n * 256 : n * 256 + 256, :], lambda b: last0[b], dftv, protov, xs, padded):
        power = (power + power0[b : b + 1, :]) * (1.0 / TIME)
        bandv[b : b + 1, :] = power[:, :256] + power[:, 256:]
    band_copy.start()
    results = []
    final_lane = iota(0, (32, 128)) % 8 == 7
    for b, evens, odds in ((0, (even00, even01), (odd00, odd01)), (1, (even10, even11), (odd10, odd11))):
        for n in range(4):
            lanes, series1 = synthesise(b, n, protov, padded)
            both = (series0[b, :, lanes], series1)
            following = (pltpu.roll(series1[:32], 7, 0), 0.0)
            for series, follow, even, odd in zip(both, following, evens, odds):
                after = jnp.where(final_lane, follow, pltpu.roll(series[:32], 31, 0))
                even[0:SPAN, lanes] = series.astype(BF16)
                even[SPAN : SPAN + 32, lanes] = after.astype(BF16)
                odd[0 : SPAN + 16, lanes] = jnp.concatenate([series[8:], after[:24]], axis=0).astype(BF16)
        shifted = [
            [even[0:SPAN], odd[0:SPAN], even[16 : 16 + SPAN], odd[16 : 16 + SPAN], even[32 : 32 + SPAN]]
            for even, odd in zip(evens, odds)
        ]
        lhs = jnp.concatenate(
            [
                jnp.concatenate([block[:, p * 256 : p * 256 + 256] for block in blocks], axis=1)
                for p in range(2) for blocks in shifted
            ],
            axis=0,
        )
        product = dot(lhs, tv[b])
        real = product[:256, :256] + product[256:, 256:]
        imag = product[256:, :256] - product[:256, 256:]
        results.append(jnp.concatenate([real, imag], axis=1).astype(BF16))
    row, col = iota(0), iota(1)
    final = ones_where(col == (row % 4) * 64 + ((row // 4) % 8) * 8 + row // 32)
    copies = []
    for h in range(2):
        for j in range(2):
            rows = slice(128 * h + 64 * j, 128 * h + 64 * j + 64)
            block = jnp.concatenate(
                [
                    jnp.concatenate([results[b][rows, half * 128 + q * 256 : half * 128 + q * 256 + 128] for q in range(2)], axis=1)
                    for half in range(2) for b in range(2)
                ],
                axis=0,
            )
            block = dot(final, block).astype(BF16)
            for q in range(2):
                for k in range(8):
                    start = 512 * h + 64 * k + 32 * j
                    outv[q, start : start + 32, :] = block[32 * k : 32 * k + 32, q * 128 : q * 128 + 128]
        done = pl.ds(512 * h, 512)
        copies.append(pltpu.make_async_copy(outv.at[:, done], out.at[:, done], out_sem.at[h]))
        copies[-1].start()
    for copy in copies + [band_copy]:
        copy.wait()


def in_hbm(array):
    return pltpu.with_memory_space_constraint(array, pltpu.HBM)


def on_device(voltages, weights, flags, dm_index):
    hbm = pl.BlockSpec(memory_space=pl.ANY)
    vmem = pl.BlockSpec(memory_space=pltpu.VMEM)
    dma = pltpu.SemaphoreType.DMA
    params = dict(vmem_limit_bytes=24 * 1024 * 1024)
    beams, tables, dft, proto, series0, last0, power0 = pl.pallas_call(
        body,
        out_shape=(
            jax.ShapeDtypeStruct((PARTS, 64, 2, 8, SPAN), BF16),
            jax.ShapeDtypeStruct((2, NBLOCK * CHANNELS, 512), BF16),
            jax.ShapeDtypeStruct((512, 512), BF16),
            jax.ShapeDtypeStruct((TAPS, 512), F32),
            jax.ShapeDtypeStruct((2, SPAN, 512), F32),
            jax.ShapeDtypeStruct((2, 88, 512), F32),
            jax.ShapeDtypeStruct((2, 512), F32),
        ),
        in_specs=[hbm] * 7,
        out_specs=(vmem,) * 7,
        scratch_shapes=[
            pltpu.VMEM((16, 4, 2, 2, 16, 256), BF16),
            pltpu.VMEM((PARTS, 4, 4, 4, 4, 8, SPAN), BF16),
            pltpu.VMEM((PARTS, 4, 4, 4, 2, 4, 8, SPAN), BF16),
            pltpu.VMEM((PARTS, 64, 2, 4, 8, SPAN), BF16),
            pltpu.VMEM((2, 2, 256, 1024), BF16),
            pltpu.VMEM((DMS, 16, 512), F32),
            pltpu.VMEM((1, 64), jnp.int32),
            pltpu.SMEM((2,), jnp.int32),
            pltpu.VMEM((2, 256, 2 * SPAN), BF16),
            pltpu.VMEM((PARTS, 64, 8, SPAN), BF16),
            pltpu.VMEM((PARTS, 64, 2, 8, SPAN), BF16),
            pltpu.VMEM((16, 256), F32),
            pltpu.VMEM((2, 512, SPAN), BF16),
            pltpu.VMEM((2, 88 + SPAN, 512), F32),
            dma((8,)),
            pltpu.SemaphoreType.REGULAR,
            dma,
            dma,
            *[dma((PARTS,)) for _ in range(6)],
            dma((30,)),
            dma,
            dma,
            *[
                pltpu.VMEM((PARTS,) + shape + (2, 4, 8, SPAN), BF16)
                for shape in [(3, 3), (3, 3), (3, 3), (3,), (3,), (3,), ()]
            ],
        ],
        compiler_params=pltpu.CompilerParams(collective_id=0, has_side_effects=True, **params),
        name="beamform",
    )(
        in_hbm(voltages.reshape(16, 4, 2, 2, 16, TIME)),
        in_hbm(weights),
        in_hbm(flags),
        in_hbm(dm_index),
        in_hbm(jnp.asarray(chirp_rows()).astype(BF16).astype(F32)),
        in_hbm(jnp.asarray(dft_rows()).astype(BF16)),
        in_hbm(jnp.asarray(prototype())),
    )
    dedispersed, bandpass = pl.pallas_call(
        tail,
        out_shape=(
            jax.ShapeDtypeStruct((2, 2 * TIME * 2, 128), BF16),
            jax.ShapeDtypeStruct((2, CHANNELS), F32),
        ),
        in_specs=[vmem] * 7,
        out_specs=(hbm, hbm),
        scratch_shapes=[
            pltpu.VMEM((2, 512, SPAN), BF16),
            pltpu.VMEM((2, 88 + SPAN, 512), F32),
            *[pltpu.VMEM((SPAN + 32, 512), BF16) for _ in range(4)],
            *[pltpu.VMEM((SPAN + 16, 512), BF16) for _ in range(4)],
            pltpu.VMEM((2, 2 * TIME * 2, 128), BF16),
            pltpu.VMEM((2, CHANNELS), F32),
            dma((3,)),
        ],
        compiler_params=pltpu.CompilerParams(**params),
        name="synthesis",
    )(
        beams.reshape(PARTS, 1024, SPAN),
        tables,
        dft,
        proto,
        series0,
        last0,
        power0,
    )
    dedispersed = dedispersed.reshape(2, 512, 2, 128).transpose(0, 2, 1, 3).reshape(2, 2, TIME * CHANNELS)
    return dedispersed, bandpass


def solution(mesh):
    return jax.shard_map(
        on_device,
        mesh=mesh,
        in_specs=(
            P(None, ("stn", "chan"), None, None),
            P(None, ("stn", "chan"), None, None),
            P(("stn", "chan"), None),
            P(("stn", "chan")),
        ),
        out_specs=(P(None, ("stn", "chan"), None), P(("stn", "chan"), None)),
        check_vma=False,
    )
```

```python
import math
import random

import jax
import jax.numpy as jnp
import numpy as np
from jax import lax
from jax.experimental import pallas as pl
from jax.experimental.pallas import tpu as pltpu
from jax.sharding import PartitionSpec as P

CHANNELS = 256
BEAMS = 256
INPUTS = 1024
TIME = 256
TAPS = 12
CHIRP = 1024
DMS = 16
NBLOCK = CHIRP // CHANNELS + 1
DEVICES = 128
CHAN_AXIS = 16
PARTS = 2
SPAN = TIME // PARTS
MESH = pl.DeviceIdType.MESH
BF16 = jnp.bfloat16
F32 = jnp.float32


def dft_rows():
    order = np.arange(CHANNELS)
    angle = 2.0 * math.pi / CHANNELS * (order[:, None] * order[None, :] % CHANNELS)
    cosine = np.cos(angle) / math.sqrt(CHANNELS)
    sine = np.sin(angle) / math.sqrt(CHANNELS)
    return np.block([[cosine, sine], [-sine, cosine]]).astype(np.float32)


def prototype():
    counter = np.arange(TAPS * CHANNELS, dtype=np.float64)
    offset = (counter + 0.5) / CHANNELS - TAPS / 2.0
    window = 0.54 + 0.46 * np.cos(math.pi * offset / (TAPS / 2.0))
    taps = (np.sinc(offset) * window).reshape(TAPS, CHANNELS)
    return np.concatenate([taps, taps], axis=1).astype(np.float32)


def chirp_rows():
    dms = np.arange(DMS, dtype=np.int64)[:, None, None]
    lag = np.arange(NBLOCK)[None, :, None] * CHANNELS + CHANNELS - 1 - np.arange(2 * CHANNELS)[None, None, :]
    valid = (lag >= 0) & (lag < CHIRP)
    lag = np.clip(lag, 0, CHIRP - 1)
    angle = math.pi * ((dms + 1) * lag * lag % (2 * DMS * CHIRP)) / (DMS * CHIRP)
    real = np.where(valid, np.cos(angle), 0.0) / math.sqrt(CHIRP)
    imag = np.where(valid, np.sin(angle), 0.0) / math.sqrt(CHIRP)
    rows = np.concatenate([real, imag, np.zeros((DMS, 6, 2 * CHANNELS))], axis=1)
    return rows.astype(np.float32)


def iota(axis, shape=(256, 256)):
    return lax.broadcasted_iota(jnp.int32, shape, axis)


def ones_where(condition):
    return jnp.where(condition, 1.0, 0.0).astype(BF16)


def dot(a, b):
    return jnp.dot(a, b, preferred_element_type=F32)


def exchange_order():
    left = [(dz, dy, dx) for dz in range(4) for dy in range(4) for dx in range(4)]
    random.Random(7).shuffle(left)
    hops, ordered = [0, 0, 0], []
    while left:
        def uneven(step):
            return sum((done + min(d, 4 - d) - len(ordered) - 1) ** 2 for done, d in zip(hops, step))

        best = min(left, key=uneven)
        left.remove(best)
        ordered.append(best)
        hops = [done + min(d, 4 - d) for done, d in zip(hops, best)]
    return ordered


def body(
    volt, wgt, flags, dm, chirps, dft, proto, recv2, tables, dftv, protov, series0, last0, power0,
    vin, give, send, recv, win, chv, flagv, dmv, beams, give2, send2, keep, ordered, padded, acc,
    load_sem, plane_sem, given, given2, sent, sent2, sibling_sem, sibling_sem2, recv_sem, recv_sem2, pack_sem, packs_sent, relays_sent, *stages,
):
    x = lax.rem(lax.axis_index("chan"), 4)
    y = lax.axis_index("chan") // 4
    z = lax.axis_index("stn") // 2
    core = lax.rem(lax.axis_index("stn"), 2)
    chip = z * CHAN_AXIS + lax.axis_index("chan")
    sibling = (z * 2 + 1 - core, lax.axis_index("chan"))

    turn = 1 + 2 * core
    zs = [lax.rem(z + dz * turn, 4) for dz in range(4)]
    xs = [lax.rem(x + dx * turn, 4) for dx in range(4)]
    ys = [lax.rem(y + dy * turn, 4) * 4 for dy in range(4)]

    flag_load = pltpu.make_async_copy(flags, flagv, load_sem.at[0])
    flag_load.start()
    volt_loads = [
        pltpu.make_async_copy(volt.at[:, :, number], vin.at[:, :, number], load_sem.at[n])
        for n, number in ((1, 1 - core), (2, core))
    ]
    for load in volt_loads:
        load.start()

    barrier = pltpu.get_barrier_semaphore()
    line = [(zs[dz] * 2 + core, ys[0] + x) for dz in range(1, 4)]
    plane = [(z * 2 + core, ys[dy] + xs[dx]) for dy in range(4) for dx in range(4) if (dy, dx) != (0, 0)]
    greeted = [sibling] + line + plane
    for peer in greeted:
        pl.semaphore_signal(barrier, inc=1, device_id=peer, device_id_type=MESH)

    def hand_over(part, give, send, given, sibling_sem):
        pltpu.make_async_remote_copy(
            src_ref=give.at[part],
            dst_ref=send.at[part, :, :, :, core] if len(send.shape) == 8 else send.at[part, :, core],
            send_sem=given,
            recv_sem=sibling_sem.at[part],
            device_id=sibling,
            device_id_type=MESH,
        ).start()

    def exchange(part, send, landing, sibling_sem, sent, recv_sem):
        share = send.at[part, :, 1 - core]
        pltpu.make_async_copy(share, share, sibling_sem.at[part]).wait()
        pltpu.make_async_copy(send.at[part, chip], landing, recv_sem.at[part]).start()
        for dz, dy, dx in exchange_order():
            if (dz, dy, dx) != (0, 0, 0):
                chan = ys[dy] + xs[dx]
                pltpu.make_async_remote_copy(
                    src_ref=send.at[part, zs[dz] * CHAN_AXIS + chan],
                    dst_ref=landing,
                    send_sem=sent.at[part],
                    recv_sem=recv_sem.at[part],
                    device_id=(zs[dz] * 2 + core, chan),
                    device_id_type=MESH,
                ).start()

    by_z, by_x, by_y, by_xz, by_yz, by_xy, by_xyz = stages

    def place(steps):
        dz, dy, dx = steps
        return zs[dz % 4] * 2 + core, ys[dy % 4] + xs[dx % 4]

    def packs(part):
        near = (-1, 0, 1)
        listed = []
        for m in range(3):
            listed.append(((3, m, slice(0, 3)), by_z.at[part, m], (1, 0, 0), [(1, m - 1, d) for d in near]))
            listed.append(((m, slice(0, 3), 3), by_x.at[part, m], (0, 0, 1), [(m - 1, d, 1) for d in near]))
            listed.append(((m, 3, slice(0, 3)), by_y.at[part, m], (0, 1, 0), [(m - 1, 1, d) for d in near]))
            listed.append(((m, 3, 3), by_xy.at[part, m], (0, 1, 1), [(m - 1, 1, 1)]))
        listed.append(((3, slice(0, 3), 3), by_xz.at[part], (1, 0, 1), [(1, d, 1) for d in near]))
        listed.append(((3, 3, slice(0, 3)), by_yz.at[part], (1, 1, 0), [(1, 1, d) for d in near]))
        listed.append(((3, 3, 3), by_xyz.at[part], (1, 1, 1), [(1, 1, 1)]))
        return [(15 * part + n, *pack) for n, pack in enumerate(listed)]

    def send_packs(part):
        share = send.at[part, :, :, :, 1 - core]
        pltpu.make_async_copy(share, share, sibling_sem.at[part]).wait()
        for n, at, stage, steps, _ in packs(part):
            pltpu.make_async_remote_copy(
                src_ref=send.at[part, at[0], at[1], at[2]],
                dst_ref=stage,
                send_sem=packs_sent,
                recv_sem=pack_sem.at[n],
                device_id=place(steps),
                device_id_type=MESH,
            ).start()

    def send_direct(part):
        pltpu.make_async_copy(send.at[part, 1, 1, 1], recv.at[part, chip], recv_sem.at[part, 0]).start()
        for steps in exchange_order():
            if 2 not in steps and steps != (0, 0, 0):
                at = [(d + 1) % 4 for d in steps]
                pltpu.make_async_remote_copy(
                    src_ref=send.at[part, at[0], at[1], at[2]],
                    dst_ref=recv.at[part, chip],
                    send_sem=sent.at[part],
                    recv_sem=recv_sem.at[part, steps[0]],
                    device_id=place(steps),
                    device_id_type=MESH,
                ).start()

    def relay_packs(part):
        for n, _, stage, steps, onward in packs(part):
            pltpu.make_async_copy(stage, stage, pack_sem.at[n]).wait()
            dz, dy, dx = (-d % 4 for d in steps)
            origin = zs[dz] * CHAN_AXIS + ys[dy] + xs[dx]
            for m, further in enumerate(onward):
                pltpu.make_async_remote_copy(
                    src_ref=stage.at[m] if len(onward) > 1 else stage,
                    dst_ref=recv.at[part, origin],
                    send_sem=relays_sent,
                    recv_sem=recv_sem.at[part, (steps[0] + further[0]) % 4],
                    device_id=place(further),
                    device_id_type=MESH,
                ).start()

    flag_load.wait()
    row, col = iota(0), iota(1)
    hits = ones_where(iota(0, (256, 64)) == flagv[...])
    count = dot(hits, jnp.ones((64, 256), BF16))
    keep_rows = ones_where((count < 0.5) & (row % 16 == col % 16))
    keep[...] = dot(ones_where(iota(1, (16, 256)) // 16 == iota(0, (16, 256))), keep_rows)

    def sort_out(number):
        way = 1 + 2 * number
        there = (row // 128) * 8 + ((x + (row // 32 + 3) % 4 * way) % 4) * 2 + (row // 8) % 2
        swap = jnp.where((col // 16 == ((row // 16) % 2) * 8 + row % 8) & (col % 16 == there), 1.0, 0.0)
        for zz in range(4):
            for half in range(2):
                block = vin[:, zz, number, half].reshape(256, 256)
                mine = (swap * keep[pl.ds((zz * 2 + number) * 2 + half, 1), :]).astype(BF16)
                sorted_block = dot(mine, block).astype(BF16)
                for one in range(2):
                    mz = lax.rem((zz + 4 - z) * way + 1, 4)
                    my = lax.rem((half * 2 + one + 4 - y) * way + 1, 4)
                    yield mz, my, sorted_block[one * 128 : one * 128 + 128].reshape(4, 4, 8, 256)

    volt_loads[0].wait()
    for mz, my, block in sort_out(1 - core):
        for part in range(PARTS):
            give[part, mz, my] = block[..., part * SPAN : part * SPAN + SPAN]
    pl.semaphore_wait(barrier, len(greeted))
    for peer in line:
        pl.semaphore_signal(plane_sem, inc=1, device_id=peer, device_id_type=MESH)
    for part in range(PARTS):
        hand_over(part, give, send, given, sibling_sem)
    volt_loads[1].wait()
    for mz, my, block in sort_out(core):
        for part in range(PARTS):
            send[part, mz, my, :, core] = block[..., part * SPAN : part * SPAN + SPAN]
    loads = [
        pltpu.make_async_copy(source, target, load_sem.at[n])
        for n, (source, target) in enumerate(
            ((wgt, win), (dm, dmv), (chirps, chv), (dft, dftv), (proto, protov)), 3
        )
    ]
    for load in loads:
        load.start()
    pl.semaphore_wait(plane_sem, len(line))
    send_packs(0)
    send_direct(0)
    send_packs(1)
    relay_packs(0)
    send_direct(1)
    relay_packs(1)
    for load in loads:
        load.wait()

    def toeplitz(n, carry):
        b, block = n // NBLOCK, lax.rem(n, NBLOCK)
        for part in range(2):
            wide = jnp.broadcast_to(chv[dmv[b], pl.ds(part * NBLOCK + block, 1), :], (8, 2 * CHANNELS))
            eight = pltpu.roll(wide, CHANNELS + 1, 1, stride=1, stride_axis=0)
            for k in range(0, CHANNELS, 16):
                both = [pltpu.roll(eight, k + i, 1)[:, :CHANNELS] if k + i else eight[:, :CHANNELS] for i in (0, 8)]
                rows = pl.ds(pl.multiple_of(block * CHANNELS + k, 16), 16)
                tables[b, rows, part * CHANNELS : (part + 1) * CHANNELS] = jnp.concatenate(both, axis=0).astype(BF16)
        return carry

    lax.fori_loop(0, 2 * NBLOCK, toeplitz, 0)

    to_device = lax.rem(core + row // 128, 2) * 16 + (row // 8) % 16
    order = ones_where(
        (col // 128 == row % 2) & ((col // 64) % 2 == (row // 2) % 2) & (col % 64 == to_device * 2 + (row // 4) % 2)
    )
    for part in range(PARTS):
        for n, dz in enumerate((3, 0, 1, 2)):
            source = zs[-dz % 4]
            arrived = recv.at[part, pl.ds(pl.multiple_of(source * 16, 16), 16)]
            pltpu.make_async_copy(arrived, arrived, recv_sem.at[part, dz]).wait()
            for c in range(2):
                real, imag, weight_real, weight_imag = [], [], [], []
                for number in range(2):
                    chips = pl.ds(pl.multiple_of(source * 16, 16), 16)
                    inputs = pl.ds(pl.multiple_of((source * 2 + number) * 128, 128), 128)
                    real.append(recv[part, chips, number, c].reshape(128, SPAN))
                    imag.append(recv[part, chips, number, 2 + c].reshape(128, SPAN))
                    weight_real.append(win[0, c, :, inputs])
                    weight_imag.append(win[1, c, :, inputs])
                parts = jnp.concatenate(
                    [
                        jnp.concatenate(real + [-half for half in imag], axis=0),
                        jnp.concatenate(imag + real, axis=0),
                    ],
                    axis=1,
                )
                product = dot(jnp.concatenate(weight_real + weight_imag, axis=1), parts)
                if n == 0:
                    acc[c] = product
                elif n < 3:
                    acc[c] += product
                else:
                    beams[c] = (acc[c] + product).astype(BF16)
        for zz in range(4):
            rows = slice(zz * 64, zz * 64 + 64)
            block = jnp.concatenate([beams[c, rows, q * SPAN : q * SPAN + SPAN] for c in range(2) for q in range(2)], axis=0)
            block = dot(order, block).astype(BF16)
            send2[part, zz * 16 : zz * 16 + 16, core] = block[:128].reshape(16, 8, SPAN)
            give2[part, zz * 16 : zz * 16 + 16] = block[128:].reshape(16, 8, SPAN)
        hand_over(part, give2, send2, given2, sibling_sem2)
        exchange(part, send2, recv2.at[part, chip], sibling_sem2, sent2, recv_sem2)

    arrived = recv2.at[0]
    pltpu.make_async_copy(arrived, arrived, recv_sem2.at[0]).wait()
    for b, power, last in front(
        lambda n: recv2[0, n * 16 : n * 16 + 16].reshape(256, SPAN), lambda b: 0.0, dftv, protov, ordered, padded
    ):
        power0[b : b + 1, :] = power
        last0[b] = last
    for b in range(2):
        for n in range(4):
            lanes, series = synthesise(b, n, protov, padded)
            series0[b, :, lanes] = series

    for blocks, sem in ((give, given), (give2, given2)):
        pltpu.make_async_copy(blocks, blocks, sem).wait()
    for sem in (packs_sent, relays_sent):
        for part in range(PARTS):
            blocks = recv.at[part, 0:37]
            pltpu.make_async_copy(blocks, blocks, sem).wait()
    for part in range(PARTS):
        for blocks, sem in ((recv.at[part, 0:26], sent), (send2.at[part, 0:63], sent2)):
            pltpu.make_async_copy(blocks, blocks, sem.at[part]).wait()
    arrived = recv2.at[1]
    pltpu.make_async_copy(arrived, arrived, recv_sem2.at[1]).wait()


def front(chunk, before_first, dftv, protov, xs, padded):
    row, col = iota(0), iota(1)
    sort = ones_where(col == ((row % 32) // 2 * 2 + (row % 64) // 32) * 8 + (row // 64) * 2 + row % 2)
    spread = ones_where(iota(1, (SPAN, SPAN)) == (iota(0, (SPAN, SPAN)) % 8) * 16 + iota(0, (SPAN, SPAN)) // 8)
    for n in range(4):
        block = dot(sort, chunk(n)).astype(BF16)
        for k in range(4):
            xs[k // 2, (k % 2) * 256 + n * 64 : (k % 2) * 256 + n * 64 + 64, :] = block[k * 64 : k * 64 + 64]
    for b in range(2):
        turned = lax.dot_general(spread, xs[b], (((1,), (1,)), ((), ())), preferred_element_type=F32)
        power = jnp.sum(turned * turned, axis=0, keepdims=True)
        spectra = dot(turned.astype(BF16), dftv[...])
        last = spectra[SPAN - 88 :]
        first = iota(0, (88, 512)) % 8 == 0
        padded[b, 0:88, :] = jnp.where(first, before_first(b), pltpu.roll(last, 1, 0))
        padded[b, 88 : 88 + SPAN, :] = spectra
        yield b, power, pltpu.roll(last, 81, 0)


def synthesise(b, n, protov, padded):
    lanes = slice(n * 128, n * 128 + 128)
    series = protov[0:1, lanes] * padded[b, 88 : 88 + SPAN, lanes]
    for tap in range(1, TAPS):
        series = series + protov[tap : tap + 1, lanes] * padded[b, 88 - 8 * tap : 88 - 8 * tap + SPAN, lanes]
    return lanes, series


def tail(
    xv, tv, dftv, protov, series0, last0, power0, out, band,
    xs, padded, even00, even01, even10, even11, odd00, odd01, odd10, odd11, outv, bandv, out_sem,
):
    band_copy = pltpu.make_async_copy(bandv, band, out_sem.at[2])
    for b, power, _ in front(lambda n: xv[1, n * 256 : n * 256 + 256, :], lambda b: last0[b], dftv, protov, xs, padded):
        power = (power + power0[b : b + 1, :]) * (1.0 / TIME)
        bandv[b : b + 1, :] = power[:, :256] + power[:, 256:]
    band_copy.start()
    results = []
    final_lane = iota(0, (32, 128)) % 8 == 7
    for b, evens, odds in ((0, (even00, even01), (odd00, odd01)), (1, (even10, even11), (odd10, odd11))):
        for n in range(4):
            lanes, series1 = synthesise(b, n, protov, padded)
            both = (series0[b, :, lanes], series1)
            following = (pltpu.roll(series1[:32], 7, 0), 0.0)
            for series, follow, even, odd in zip(both, following, evens, odds):
                after = jnp.where(final_lane, follow, pltpu.roll(series[:32], 31, 0))
                even[0:SPAN, lanes] = series.astype(BF16)
                even[SPAN : SPAN + 32, lanes] = after.astype(BF16)
                odd[0 : SPAN + 16, lanes] = jnp.concatenate([series[8:], after[:24]], axis=0).astype(BF16)
        shifted = [
            [even[0:SPAN], odd[0:SPAN], even[16 : 16 + SPAN], odd[16 : 16 + SPAN], even[32 : 32 + SPAN]]
            for even, odd in zip(evens, odds)
        ]
        lhs = jnp.concatenate(
            [
                jnp.concatenate([block[:, p * 256 : p * 256 + 256] for block in blocks], axis=1)
                for p in range(2) for blocks in shifted
            ],
            axis=0,
        )
        product = dot(lhs, tv[b])
        real = product[:256, :256] + product[256:, 256:]
        imag = product[256:, :256] - product[:256, 256:]
        results.append(jnp.concatenate([real, imag], axis=1).astype(BF16))
    row, col = iota(0), iota(1)
    final = ones_where(col == (row % 4) * 64 + ((row // 4) % 8) * 8 + row // 32)
    copies = []
    for h in range(2):
        for j in range(2):
            rows = slice(128 * h + 64 * j, 128 * h + 64 * j + 64)
            block = jnp.concatenate(
                [
                    jnp.concatenate([results[b][rows, half * 128 + q * 256 : half * 128 + q * 256 + 128] for q in range(2)], axis=1)
                    for half in range(2) for b in range(2)
                ],
                axis=0,
            )
            block = dot(final, block).astype(BF16)
            for q in range(2):
                for k in range(8):
                    start = 512 * h + 64 * k + 32 * j
                    outv[q, start : start + 32, :] = block[32 * k : 32 * k + 32, q * 128 : q * 128 + 128]
        done = pl.ds(512 * h, 512)
        copies.append(pltpu.make_async_copy(outv.at[:, done], out.at[:, done], out_sem.at[h]))
        copies[-1].start()
    for copy in copies + [band_copy]:
        copy.wait()


def in_hbm(array):
    return pltpu.with_memory_space_constraint(array, pltpu.HBM)


def on_device(voltages, weights, flags, dm_index):
    hbm = pl.BlockSpec(memory_space=pl.ANY)
    vmem = pl.BlockSpec(memory_space=pltpu.VMEM)
    dma = pltpu.SemaphoreType.DMA
    params = dict(vmem_limit_bytes=24 * 1024 * 1024)
    beams, tables, dft, proto, series0, last0, power0 = pl.pallas_call(
        body,
        out_shape=(
            jax.ShapeDtypeStruct((PARTS, 64, 2, 8, SPAN), BF16),
            jax.ShapeDtypeStruct((2, NBLOCK * CHANNELS, 512), BF16),
            jax.ShapeDtypeStruct((512, 512), BF16),
            jax.ShapeDtypeStruct((TAPS, 512), F32),
            jax.ShapeDtypeStruct((2, SPAN, 512), F32),
            jax.ShapeDtypeStruct((2, 88, 512), F32),
            jax.ShapeDtypeStruct((2, 512), F32),
        ),
        in_specs=[hbm] * 7,
        out_specs=(vmem,) * 7,
        scratch_shapes=[
            pltpu.VMEM((16, 4, 2, 2, 16, 256), BF16),
            pltpu.VMEM((PARTS, 4, 4, 4, 4, 8, SPAN), BF16),
            pltpu.VMEM((PARTS, 4, 4, 4, 2, 4, 8, SPAN), BF16),
            pltpu.VMEM((PARTS, 64, 2, 4, 8, SPAN), BF16),
            pltpu.VMEM((2, 2, 256, 1024), BF16),
            pltpu.VMEM((DMS, 16, 512), F32),
            pltpu.VMEM((1, 64), jnp.int32),
            pltpu.SMEM((2,), jnp.int32),
            pltpu.VMEM((2, 256, 2 * SPAN), BF16),
            pltpu.VMEM((PARTS, 64, 8, SPAN), BF16),
            pltpu.VMEM((PARTS, 64, 2, 8, SPAN), BF16),
            pltpu.VMEM((16, 256), F32),
            pltpu.VMEM((2, 512, SPAN), BF16),
            pltpu.VMEM((2, 88 + SPAN, 512), F32),
            pltpu.VMEM((2, 256, 2 * SPAN), F32),
            dma((8,)),
            pltpu.SemaphoreType.REGULAR,
            dma,
            dma,
            *[dma((PARTS,)) for _ in range(4)],
            dma((PARTS, 4)),
            dma((PARTS,)),
            dma((30,)),
            dma,
            dma,
            *[
                pltpu.VMEM((PARTS,) + shape + (2, 4, 8, SPAN), BF16)
                for shape in [(3, 3), (3, 3), (3, 3), (3,), (3,), (3,), ()]
            ],
        ],
        compiler_params=pltpu.CompilerParams(collective_id=0, has_side_effects=True, **params),
        name="beamform",
    )(
        in_hbm(voltages.reshape(16, 4, 2, 2, 16, TIME)),
        in_hbm(weights),
        in_hbm(flags),
        in_hbm(dm_index),
        in_hbm(jnp.asarray(chirp_rows()).astype(BF16).astype(F32)),
        in_hbm(jnp.asarray(dft_rows()).astype(BF16)),
        in_hbm(jnp.asarray(prototype())),
    )
    dedispersed, bandpass = pl.pallas_call(
        tail,
        out_shape=(
            jax.ShapeDtypeStruct((2, 2 * TIME * 2, 128), BF16),
            jax.ShapeDtypeStruct((2, CHANNELS), F32),
        ),
        in_specs=[vmem] * 7,
        out_specs=(hbm, hbm),
        scratch_shapes=[
            pltpu.VMEM((2, 512, SPAN), BF16),
            pltpu.VMEM((2, 88 + SPAN, 512), F32),
            *[pltpu.VMEM((SPAN + 32, 512), BF16) for _ in range(4)],
            *[pltpu.VMEM((SPAN + 16, 512), BF16) for _ in range(4)],
            pltpu.VMEM((2, 2 * TIME * 2, 128), BF16),
            pltpu.VMEM((2, CHANNELS), F32),
            dma((3,)),
        ],
        compiler_params=pltpu.CompilerParams(**params),
        name="synthesis",
    )(
        beams.reshape(PARTS, 1024, SPAN),
        tables,
        dft,
        proto,
        series0,
        last0,
        power0,
    )
    dedispersed = dedispersed.reshape(2, 512, 2, 128).transpose(0, 2, 1, 3).reshape(2, 2, TIME * CHANNELS)
    return dedispersed, bandpass


def solution(mesh):
    return jax.shard_map(
        on_device,
        mesh=mesh,
        in_specs=(
            P(None, ("stn", "chan"), None, None),
            P(None, ("stn", "chan"), None, None),
            P(("stn", "chan"), None),
            P(("stn", "chan")),
        ),
        out_specs=(P(None, ("stn", "chan"), None), P(("stn", "chan"), None)),
        check_vma=False,
    )
```

```python
import math
import random

import jax
import jax.numpy as jnp
import numpy as np
from jax import lax
from jax.experimental import pallas as pl
from jax.experimental.pallas import tpu as pltpu
from jax.sharding import PartitionSpec as P

CHANNELS = 256
BEAMS = 256
INPUTS = 1024
TIME = 256
TAPS = 12
CHIRP = 1024
DMS = 16
NBLOCK = CHIRP // CHANNELS + 1
DEVICES = 128
CHAN_AXIS = 16
PARTS = 2
SPAN = TIME // PARTS
MESH = pl.DeviceIdType.MESH
BF16 = jnp.bfloat16
F32 = jnp.float32


def dft_rows():
    order = np.arange(CHANNELS)
    angle = 2.0 * math.pi / CHANNELS * (order[:, None] * order[None, :] % CHANNELS)
    cosine = np.cos(angle) / math.sqrt(CHANNELS)
    sine = np.sin(angle) / math.sqrt(CHANNELS)
    return np.block([[cosine, sine], [-sine, cosine]]).astype(np.float32)


def prototype():
    counter = np.arange(TAPS * CHANNELS, dtype=np.float64)
    offset = (counter + 0.5) / CHANNELS - TAPS / 2.0
    window = 0.54 + 0.46 * np.cos(math.pi * offset / (TAPS / 2.0))
    taps = (np.sinc(offset) * window).reshape(TAPS, CHANNELS)
    return np.concatenate([taps, taps], axis=1).astype(np.float32)


def chirp_rows():
    dms = np.arange(DMS, dtype=np.int64)[:, None, None]
    lag = np.arange(NBLOCK)[None, :, None] * CHANNELS + CHANNELS - 1 - np.arange(2 * CHANNELS)[None, None, :]
    valid = (lag >= 0) & (lag < CHIRP)
    lag = np.clip(lag, 0, CHIRP - 1)
    angle = math.pi * ((dms + 1) * lag * lag % (2 * DMS * CHIRP)) / (DMS * CHIRP)
    real = np.where(valid, np.cos(angle), 0.0) / math.sqrt(CHIRP)
    imag = np.where(valid, np.sin(angle), 0.0) / math.sqrt(CHIRP)
    rows = np.concatenate([real, imag, np.zeros((DMS, 6, 2 * CHANNELS))], axis=1)
    return rows.astype(np.float32)


def iota(axis, shape=(256, 256)):
    return lax.broadcasted_iota(jnp.int32, shape, axis)


def ones_where(condition):
    return jnp.where(condition, 1.0, 0.0).astype(BF16)


def dot(a, b):
    return jnp.dot(a, b, preferred_element_type=F32)


def exchange_order(far_first=False):
    left = [(dz, dy, dx) for dz in range(4) for dy in range(4) for dx in range(4)]
    random.Random(7).shuffle(left)
    hops, ordered = [0, 0, 0], []
    while left:
        def uneven(step):
            return sum((done + min(d, 4 - d) - len(ordered) - 1) ** 2 for done, d in zip(hops, step))

        best = min(left, key=uneven)
        left.remove(best)
        ordered.append(best)
        hops = [done + min(d, 4 - d) for done, d in zip(hops, best)]
    return sorted(ordered, key=lambda step: -sum(min(d, 4 - d) for d in step)) if far_first else ordered


def body(
    volt, wgt, flags, dm, chirps, dft, proto, recv2, tables, dftv, protov, series0, last0, power0,
    vin, give, send, recv, win, chv, flagv, dmv, beams, give2, send2, keep, ordered, padded, acc,
    load_sem, plane_sem, given, given2, sent, sent2, sibling_sem, sibling_sem2, recv_sem, recv_sem2, pack_sem, packs_sent, relays_sent, *stages,
):
    x = lax.rem(lax.axis_index("chan"), 4)
    y = lax.axis_index("chan") // 4
    z = lax.axis_index("stn") // 2
    core = lax.rem(lax.axis_index("stn"), 2)
    chip = z * CHAN_AXIS + lax.axis_index("chan")
    sibling = (z * 2 + 1 - core, lax.axis_index("chan"))

    turn = 1 + 2 * core
    zs = [lax.rem(z + dz * turn, 4) for dz in range(4)]
    xs = [lax.rem(x + dx * turn, 4) for dx in range(4)]
    ys = [lax.rem(y + dy * turn, 4) * 4 for dy in range(4)]

    flag_load = pltpu.make_async_copy(flags, flagv, load_sem.at[0])
    flag_load.start()
    volt_loads = [
        pltpu.make_async_copy(volt.at[:, :, number], vin.at[:, :, number], load_sem.at[n])
        for n, number in ((1, 1 - core), (2, core))
    ]
    for load in volt_loads:
        load.start()

    barrier = pltpu.get_barrier_semaphore()
    line = [(zs[dz] * 2 + core, ys[0] + x) for dz in range(1, 4)]
    plane = [(z * 2 + core, ys[dy] + xs[dx]) for dy in range(4) for dx in range(4) if (dy, dx) != (0, 0)]
    greeted = [sibling] + line + plane
    for peer in greeted:
        pl.semaphore_signal(barrier, inc=1, device_id=peer, device_id_type=MESH)

    def hand_over(give, share, given, sibling_sem):
        pltpu.make_async_remote_copy(
            src_ref=give, dst_ref=share, send_sem=given, recv_sem=sibling_sem, device_id=sibling, device_id_type=MESH
        ).start()

    by_z, by_x, by_y, by_xz, by_yz, by_xy, by_xyz = stages

    def place(steps):
        dz, dy, dx = steps
        return zs[dz % 4] * 2 + core, ys[dy % 4] + xs[dx % 4]

    def packs(part):
        near = (-1, 0, 1)
        listed = []
        for m in range(3):
            listed.append(((3, m, slice(0, 3)), by_z.at[part, m], (1, 0, 0), [(1, m - 1, d) for d in near]))
            listed.append(((m, slice(0, 3), 3), by_x.at[part, m], (0, 0, 1), [(m - 1, d, 1) for d in near]))
            listed.append(((m, 3, slice(0, 3)), by_y.at[part, m], (0, 1, 0), [(m - 1, 1, d) for d in near]))
            listed.append(((m, 3, 3), by_xy.at[part, m], (0, 1, 1), [(m - 1, 1, 1)]))
        listed.append(((3, slice(0, 3), 3), by_xz.at[part], (1, 0, 1), [(1, d, 1) for d in near]))
        listed.append(((3, 3, slice(0, 3)), by_yz.at[part], (1, 1, 0), [(1, 1, d) for d in near]))
        listed.append(((3, 3, 3), by_xyz.at[part], (1, 1, 1), [(1, 1, 1)]))
        return [(15 * part + n, *pack) for n, pack in enumerate(listed)]

    def send_packs(part):
        share = send.at[part, :, :, :, 1 - core]
        pltpu.make_async_copy(share, share, sibling_sem.at[part]).wait()
        for n, at, stage, steps, _ in packs(part):
            pltpu.make_async_remote_copy(
                src_ref=send.at[part, at[0], at[1], at[2]],
                dst_ref=stage,
                send_sem=packs_sent,
                recv_sem=pack_sem.at[n],
                device_id=place(steps),
                device_id_type=MESH,
            ).start()

    def send_direct(part):
        pltpu.make_async_copy(send.at[part, 1, 1, 1], recv.at[part, chip], recv_sem.at[part, 0]).start()
        for steps in exchange_order():
            if 2 not in steps and steps != (0, 0, 0):
                at = [(d + 1) % 4 for d in steps]
                pltpu.make_async_remote_copy(
                    src_ref=send.at[part, at[0], at[1], at[2]],
                    dst_ref=recv.at[part, chip],
                    send_sem=sent.at[part],
                    recv_sem=recv_sem.at[part, steps[0]],
                    device_id=place(steps),
                    device_id_type=MESH,
                ).start()

    def relay_packs(part):
        for n, _, stage, steps, onward in packs(part):
            pltpu.make_async_copy(stage, stage, pack_sem.at[n]).wait()
            dz, dy, dx = (-d % 4 for d in steps)
            origin = zs[dz] * CHAN_AXIS + ys[dy] + xs[dx]
            for m, further in enumerate(onward):
                pltpu.make_async_remote_copy(
                    src_ref=stage.at[m] if len(onward) > 1 else stage,
                    dst_ref=recv.at[part, origin],
                    send_sem=relays_sent,
                    recv_sem=recv_sem.at[part, (steps[0] + further[0]) % 4],
                    device_id=place(further),
                    device_id_type=MESH,
                ).start()

    flag_load.wait()
    row, col = iota(0), iota(1)
    hits = ones_where(iota(0, (256, 64)) == flagv[...])
    count = dot(hits, jnp.ones((64, 256), BF16))
    keep_rows = ones_where((count < 0.5) & (row % 16 == col % 16))
    keep[...] = dot(ones_where(iota(1, (16, 256)) // 16 == iota(0, (16, 256))), keep_rows)

    def sort_out(number):
        way = 1 + 2 * number
        there = (row // 128) * 8 + ((x + (row // 32 + 3) % 4 * way) % 4) * 2 + (row // 8) % 2
        swap = jnp.where((col // 16 == ((row // 16) % 2) * 8 + row % 8) & (col % 16 == there), 1.0, 0.0)
        for zz in range(4):
            for half in range(2):
                block = vin[:, zz, number, half].reshape(256, 256)
                mine = (swap * keep[pl.ds((zz * 2 + number) * 2 + half, 1), :]).astype(BF16)
                sorted_block = dot(mine, block).astype(BF16)
                for one in range(2):
                    mz = lax.rem((zz + 4 - z) * way + 1, 4)
                    my = lax.rem((half * 2 + one + 4 - y) * way + 1, 4)
                    yield mz, my, sorted_block[one * 128 : one * 128 + 128].reshape(4, 4, 8, 256)

    volt_loads[0].wait()
    for mz, my, block in sort_out(1 - core):
        for part in range(PARTS):
            give[part, mz, my] = block[..., part * SPAN : part * SPAN + SPAN]
    pl.semaphore_wait(barrier, len(greeted))
    for peer in line:
        pl.semaphore_signal(plane_sem, inc=1, device_id=peer, device_id_type=MESH)
    for part in range(PARTS):
        hand_over(give.at[part], send.at[part, :, :, :, core], given, sibling_sem.at[part])
    volt_loads[1].wait()
    for mz, my, block in sort_out(core):
        for part in range(PARTS):
            send[part, mz, my, :, core] = block[..., part * SPAN : part * SPAN + SPAN]
    loads = [
        pltpu.make_async_copy(source, target, load_sem.at[n])
        for n, (source, target) in enumerate(
            ((wgt, win), (dm, dmv), (chirps, chv), (dft, dftv), (proto, protov)), 3
        )
    ]
    for load in loads:
        load.start()
    pl.semaphore_wait(plane_sem, len(line))
    send_packs(0)
    send_direct(0)
    send_packs(1)
    relay_packs(0)
    send_direct(1)
    relay_packs(1)
    for load in loads:
        load.wait()

    def toeplitz(n, carry):
        b, block = n // NBLOCK, lax.rem(n, NBLOCK)
        for part in range(2):
            wide = jnp.broadcast_to(chv[dmv[b], pl.ds(part * NBLOCK + block, 1), :], (8, 2 * CHANNELS))
            eight = pltpu.roll(wide, CHANNELS + 1, 1, stride=1, stride_axis=0)
            for k in range(0, CHANNELS, 16):
                both = [pltpu.roll(eight, k + i, 1)[:, :CHANNELS] if k + i else eight[:, :CHANNELS] for i in (0, 8)]
                rows = pl.ds(pl.multiple_of(block * CHANNELS + k, 16), 16)
                tables[b, rows, part * CHANNELS : (part + 1) * CHANNELS] = jnp.concatenate(both, axis=0).astype(BF16)
        return carry

    lax.fori_loop(0, 2 * NBLOCK, toeplitz, 0)

    to_device = lax.rem(core + row // 128, 2) * 16 + (row // 8) % 16
    order = ones_where(
        (col // 128 == row % 2) & ((col // 64) % 2 == (row // 2) % 2) & (col % 64 == to_device * 2 + (row // 4) % 2)
    )
    for part in range(PARTS):
        for n, dz in enumerate((3, 0, 1, 2)):
            source = zs[-dz % 4]
            arrived = recv.at[part, pl.ds(pl.multiple_of(source * 16, 16), 16)]
            pltpu.make_async_copy(arrived, arrived, recv_sem.at[part, dz]).wait()
            for c in range(2):
                real, imag, weight_real, weight_imag = [], [], [], []
                for number in range(2):
                    chips = pl.ds(pl.multiple_of(source * 16, 16), 16)
                    inputs = pl.ds(pl.multiple_of((source * 2 + number) * 128, 128), 128)
                    real.append(recv[part, chips, number, c].reshape(128, SPAN))
                    imag.append(recv[part, chips, number, 2 + c].reshape(128, SPAN))
                    weight_real.append(win[0, c, :, inputs])
                    weight_imag.append(win[1, c, :, inputs])
                parts = jnp.concatenate(
                    [
                        jnp.concatenate(real + [-half for half in imag], axis=0),
                        jnp.concatenate(imag + real, axis=0),
                    ],
                    axis=1,
                )
                product = dot(jnp.concatenate(weight_real + weight_imag, axis=1), parts)
                if n == 0:
                    acc[c] = product
                elif n < 3:
                    acc[c] += product
                else:
                    beams[c] = (acc[c] + product).astype(BF16)
        for dz in (0, 2, 1, 3):
            rows = pl.ds(pl.multiple_of(zs[dz] * 64, 64), 64)
            chips = pl.ds(pl.multiple_of(zs[dz] * 16, 16), 16)
            block = jnp.concatenate([beams[c, rows, q * SPAN : q * SPAN + SPAN] for c in range(2) for q in range(2)], axis=0)
            block = dot(order, block).astype(BF16)
            give2[part, chips] = block[128:].reshape(16, 8, SPAN)
            hand_over(give2.at[part, chips], send2.at[part, chips, core], given2, sibling_sem2.at[part, -dz % 4])
            send2[part, chips, core] = block[:128].reshape(16, 8, SPAN)
        for dz in (0, 2, 1, 3):
            chips = pl.ds(pl.multiple_of(zs[dz] * 16, 16), 16)
            share = send2.at[part, chips, 1 - core]
            pltpu.make_async_copy(share, share, sibling_sem2.at[part, dz]).wait()
            if dz == 0:
                pltpu.make_async_copy(send2.at[part, chip], recv2.at[part, chip], recv_sem2.at[part]).start()
            for steps in exchange_order(far_first=True):
                if steps[0] == dz and steps != (0, 0, 0):
                    stn, chan = place(steps)
                    pltpu.make_async_remote_copy(
                        src_ref=send2.at[part, zs[dz] * CHAN_AXIS + chan],
                        dst_ref=recv2.at[part, chip],
                        send_sem=sent2.at[part],
                        recv_sem=recv_sem2.at[part],
                        device_id=(stn, chan),
                        device_id_type=MESH,
                    ).start()

    arrived = recv2.at[0]
    pltpu.make_async_copy(arrived, arrived, recv_sem2.at[0]).wait()
    for b, power, last in front(
        lambda n: recv2[0, n * 16 : n * 16 + 16].reshape(256, SPAN), lambda b: 0.0, dftv, protov, ordered, padded
    ):
        power0[b : b + 1, :] = power
        last0[b] = last
    for b in range(2):
        for n in range(4):
            lanes, series = synthesise(b, n, protov, padded)
            series0[b, :, lanes] = series

    for blocks, sem in ((give, given), (give2, given2)):
        pltpu.make_async_copy(blocks, blocks, sem).wait()
    for sem in (packs_sent, relays_sent):
        for part in range(PARTS):
            blocks = recv.at[part, 0:37]
            pltpu.make_async_copy(blocks, blocks, sem).wait()
    for part in range(PARTS):
        for blocks, sem in ((recv.at[part, 0:26], sent), (send2.at[part, 0:63], sent2)):
            pltpu.make_async_copy(blocks, blocks, sem.at[part]).wait()
    arrived = recv2.at[1]
    pltpu.make_async_copy(arrived, arrived, recv_sem2.at[1]).wait()


def front(chunk, before_first, dftv, protov, xs, padded):
    row, col = iota(0), iota(1)
    sort = ones_where(col == ((row % 32) // 2 * 2 + (row % 64) // 32) * 8 + (row // 64) * 2 + row % 2)
    spread = ones_where(iota(1, (SPAN, SPAN)) == (iota(0, (SPAN, SPAN)) % 8) * 16 + iota(0, (SPAN, SPAN)) // 8)
    for n in range(4):
        block = dot(sort, chunk(n)).astype(BF16)
        for k in range(4):
            xs[k // 2, (k % 2) * 256 + n * 64 : (k % 2) * 256 + n * 64 + 64, :] = block[k * 64 : k * 64 + 64]
    for b in range(2):
        turned = lax.dot_general(spread, xs[b], (((1,), (1,)), ((), ())), preferred_element_type=F32)
        power = jnp.sum(turned * turned, axis=0, keepdims=True)
        spectra = dot(turned.astype(BF16), dftv[...])
        last = spectra[SPAN - 88 :]
        first = iota(0, (88, 512)) % 8 == 0
        padded[b, 0:88, :] = jnp.where(first, before_first(b), pltpu.roll(last, 1, 0))
        padded[b, 88 : 88 + SPAN, :] = spectra
        yield b, power, pltpu.roll(last, 81, 0)


def synthesise(b, n, protov, padded):
    lanes = slice(n * 128, n * 128 + 128)
    series = protov[0:1, lanes] * padded[b, 88 : 88 + SPAN, lanes]
    for tap in range(1, TAPS):
        series = series + protov[tap : tap + 1, lanes] * padded[b, 88 - 8 * tap : 88 - 8 * tap + SPAN, lanes]
    return lanes, series


def tail(
    xv, tv, dftv, protov, series0, last0, power0, out, band,
    xs, padded, even00, even01, even10, even11, odd00, odd01, odd10, odd11, outv, bandv, out_sem,
):
    band_copy = pltpu.make_async_copy(bandv, band, out_sem.at[2])
    for b, power, _ in front(lambda n: xv[1, n * 256 : n * 256 + 256, :], lambda b: last0[b], dftv, protov, xs, padded):
        power = (power + power0[b : b + 1, :]) * (1.0 / TIME)
        bandv[b : b + 1, :] = power[:, :256] + power[:, 256:]
    band_copy.start()
    results = []
    final_lane = iota(0, (32, 128)) % 8 == 7
    for b, evens, odds in ((0, (even00, even01), (odd00, odd01)), (1, (even10, even11), (odd10, odd11))):
        for n in range(4):
            lanes, series1 = synthesise(b, n, protov, padded)
            both = (series0[b, :, lanes], series1)
            following = (pltpu.roll(series1[:32], 7, 0), 0.0)
            for series, follow, even, odd in zip(both, following, evens, odds):
                after = jnp.where(final_lane, follow, pltpu.roll(series[:32], 31, 0))
                even[0:SPAN, lanes] = series.astype(BF16)
                even[SPAN : SPAN + 32, lanes] = after.astype(BF16)
                odd[0 : SPAN + 16, lanes] = jnp.concatenate([series[8:], after[:24]], axis=0).astype(BF16)
        shifted = [
            [even[0:SPAN], odd[0:SPAN], even[16 : 16 + SPAN], odd[16 : 16 + SPAN], even[32 : 32 + SPAN]]
            for even, odd in zip(evens, odds)
        ]
        lhs = jnp.concatenate(
            [
                jnp.concatenate([block[:, p * 256 : p * 256 + 256] for block in blocks], axis=1)
                for p in range(2) for blocks in shifted
            ],
            axis=0,
        )
        product = dot(lhs, tv[b])
        real = product[:256, :256] + product[256:, 256:]
        imag = product[256:, :256] - product[:256, 256:]
        results.append(jnp.concatenate([real, imag], axis=1).astype(BF16))
    row, col = iota(0), iota(1)
    final = ones_where(col == (row % 4) * 64 + ((row // 4) % 8) * 8 + row // 32)
    copies = []
    for h in range(2):
        for j in range(2):
            rows = slice(128 * h + 64 * j, 128 * h + 64 * j + 64)
            block = jnp.concatenate(
                [
                    jnp.concatenate([results[b][rows, half * 128 + q * 256 : half * 128 + q * 256 + 128] for q in range(2)], axis=1)
                    for half in range(2) for b in range(2)
                ],
                axis=0,
            )
            block = dot(final, block).astype(BF16)
            for q in range(2):
                for k in range(8):
                    start = 512 * h + 64 * k + 32 * j
                    outv[q, start : start + 32, :] = block[32 * k : 32 * k + 32, q * 128 : q * 128 + 128]
        done = pl.ds(512 * h, 512)
        copies.append(pltpu.make_async_copy(outv.at[:, done], out.at[:, done], out_sem.at[h]))
        copies[-1].start()
    for copy in copies + [band_copy]:
        copy.wait()


def in_hbm(array):
    return pltpu.with_memory_space_constraint(array, pltpu.HBM)


def on_device(voltages, weights, flags, dm_index):
    hbm = pl.BlockSpec(memory_space=pl.ANY)
    vmem = pl.BlockSpec(memory_space=pltpu.VMEM)
    dma = pltpu.SemaphoreType.DMA
    params = dict(vmem_limit_bytes=24 * 1024 * 1024)
    beams, tables, dft, proto, series0, last0, power0 = pl.pallas_call(
        body,
        out_shape=(
            jax.ShapeDtypeStruct((PARTS, 64, 2, 8, SPAN), BF16),
            jax.ShapeDtypeStruct((2, NBLOCK * CHANNELS, 512), BF16),
            jax.ShapeDtypeStruct((512, 512), BF16),
            jax.ShapeDtypeStruct((TAPS, 512), F32),
            jax.ShapeDtypeStruct((2, SPAN, 512), F32),
            jax.ShapeDtypeStruct((2, 88, 512), F32),
            jax.ShapeDtypeStruct((2, 512), F32),
        ),
        in_specs=[hbm] * 7,
        out_specs=(vmem,) * 7,
        scratch_shapes=[
            pltpu.VMEM((16, 4, 2, 2, 16, 256), BF16),
            pltpu.VMEM((PARTS, 4, 4, 4, 4, 8, SPAN), BF16),
            pltpu.VMEM((PARTS, 4, 4, 4, 2, 4, 8, SPAN), BF16),
            pltpu.VMEM((PARTS, 64, 2, 4, 8, SPAN), BF16),
            pltpu.VMEM((2, 2, 256, 1024), BF16),
            pltpu.VMEM((DMS, 16, 512), F32),
            pltpu.VMEM((1, 64), jnp.int32),
            pltpu.SMEM((2,), jnp.int32),
            pltpu.VMEM((2, 256, 2 * SPAN), BF16),
            pltpu.VMEM((PARTS, 64, 8, SPAN), BF16),
            pltpu.VMEM((PARTS, 64, 2, 8, SPAN), BF16),
            pltpu.VMEM((16, 256), F32),
            pltpu.VMEM((2, 512, SPAN), BF16),
            pltpu.VMEM((2, 88 + SPAN, 512), F32),
            pltpu.VMEM((2, 256, 2 * SPAN), F32),
            dma((8,)),
            pltpu.SemaphoreType.REGULAR,
            dma,
            dma,
            *[dma((PARTS,)) for _ in range(3)],
            dma((PARTS, 4)),
            dma((PARTS, 4)),
            dma((PARTS,)),
            dma((30,)),
            dma,
            dma,
            *[
                pltpu.VMEM((PARTS,) + shape + (2, 4, 8, SPAN), BF16)
                for shape in [(3, 3), (3, 3), (3, 3), (3,), (3,), (3,), ()]
            ],
        ],
        compiler_params=pltpu.CompilerParams(collective_id=0, has_side_effects=True, **params),
        name="beamform",
    )(
        in_hbm(voltages.reshape(16, 4, 2, 2, 16, TIME)),
        in_hbm(weights),
        in_hbm(flags),
        in_hbm(dm_index),
        in_hbm(jnp.asarray(chirp_rows()).astype(BF16).astype(F32)),
        in_hbm(jnp.asarray(dft_rows()).astype(BF16)),
        in_hbm(jnp.asarray(prototype())),
    )
    dedispersed, bandpass = pl.pallas_call(
        tail,
        out_shape=(
            jax.ShapeDtypeStruct((2, 2 * TIME * 2, 128), BF16),
            jax.ShapeDtypeStruct((2, CHANNELS), F32),
        ),
        in_specs=[vmem] * 7,
        out_specs=(hbm, hbm),
        scratch_shapes=[
            pltpu.VMEM((2, 512, SPAN), BF16),
            pltpu.VMEM((2, 88 + SPAN, 512), F32),
            *[pltpu.VMEM((SPAN + 32, 512), BF16) for _ in range(4)],
            *[pltpu.VMEM((SPAN + 16, 512), BF16) for _ in range(4)],
            pltpu.VMEM((2, 2 * TIME * 2, 128), BF16),
            pltpu.VMEM((2, CHANNELS), F32),
            dma((3,)),
        ],
        compiler_params=pltpu.CompilerParams(**params),
        name="synthesis",
    )(
        beams.reshape(PARTS, 1024, SPAN),
        tables,
        dft,
        proto,
        series0,
        last0,
        power0,
    )
    dedispersed = dedispersed.reshape(2, 512, 2, 128).transpose(0, 2, 1, 3).reshape(2, 2, TIME * CHANNELS)
    return dedispersed, bandpass


def solution(mesh):
    return jax.shard_map(
        on_device,
        mesh=mesh,
        in_specs=(
            P(None, ("stn", "chan"), None, None),
            P(None, ("stn", "chan"), None, None),
            P(("stn", "chan"), None),
            P(("stn", "chan")),
        ),
        out_specs=(P(None, ("stn", "chan"), None), P(("stn", "chan"), None)),
        check_vma=False,
    )
```

```python
import math
import random

import jax
import jax.numpy as jnp
import numpy as np
from jax import lax
from jax.experimental import pallas as pl
from jax.experimental.pallas import tpu as pltpu
from jax.sharding import PartitionSpec as P

CHANNELS = 256
BEAMS = 256
INPUTS = 1024
TIME = 256
TAPS = 12
CHIRP = 1024
DMS = 16
NBLOCK = CHIRP // CHANNELS + 1
DEVICES = 128
CHAN_AXIS = 16
PARTS = 2
SPAN = TIME // PARTS
MESH = pl.DeviceIdType.MESH
BF16 = jnp.bfloat16
F32 = jnp.float32


def dft_rows():
    order = np.arange(CHANNELS)
    angle = 2.0 * math.pi / CHANNELS * (order[:, None] * order[None, :] % CHANNELS)
    cosine = np.cos(angle) / math.sqrt(CHANNELS)
    sine = np.sin(angle) / math.sqrt(CHANNELS)
    return np.block([[cosine, sine], [-sine, cosine]]).astype(np.float32)


def prototype():
    counter = np.arange(TAPS * CHANNELS, dtype=np.float64)
    offset = (counter + 0.5) / CHANNELS - TAPS / 2.0
    window = 0.54 + 0.46 * np.cos(math.pi * offset / (TAPS / 2.0))
    taps = (np.sinc(offset) * window).reshape(TAPS, CHANNELS)
    return np.concatenate([taps, taps], axis=1).astype(np.float32)


def chirp_rows():
    dms = np.arange(DMS, dtype=np.int64)[:, None, None]
    lag = np.arange(NBLOCK)[None, :, None] * CHANNELS + CHANNELS - 1 - np.arange(2 * CHANNELS)[None, None, :]
    valid = (lag >= 0) & (lag < CHIRP)
    lag = np.clip(lag, 0, CHIRP - 1)
    angle = math.pi * ((dms + 1) * lag * lag % (2 * DMS * CHIRP)) / (DMS * CHIRP)
    real = np.where(valid, np.cos(angle), 0.0) / math.sqrt(CHIRP)
    imag = np.where(valid, np.sin(angle), 0.0) / math.sqrt(CHIRP)
    rows = np.concatenate([real, imag, np.zeros((DMS, 6, 2 * CHANNELS))], axis=1)
    return rows.astype(np.float32)


def iota(axis, shape=(256, 256)):
    return lax.broadcasted_iota(jnp.int32, shape, axis)


def ones_where(condition):
    return jnp.where(condition, 1.0, 0.0).astype(BF16)


def dot(a, b):
    return jnp.dot(a, b, preferred_element_type=F32)


def exchange_order():
    left = [(dz, dy, dx) for dz in range(4) for dy in range(4) for dx in range(4)]
    random.Random(7).shuffle(left)
    hops, ordered = [0, 0, 0], []
    while left:
        def uneven(step):
            return sum((done + min(d, 4 - d) - len(ordered) - 1) ** 2 for done, d in zip(hops, step))

        best = min(left, key=uneven)
        left.remove(best)
        ordered.append(best)
        hops = [done + min(d, 4 - d) for done, d in zip(hops, best)]
    return ordered


def body(
    volt, wgt, flags, dm, chirps, dft, proto, recv2, tables, dftv, protov, product0, last0, power0,
    vin, give, send, recv, win, chv, flagv, dmv, beams, give2, send2, keep, ordered, padded, even, odd, acc,
    load_sem, plane_sem, given, given2, sent, sent2, sibling_sem, sibling_sem2, recv_sem, recv_sem2, pack_sem, packs_sent, relays_sent, *stages,
):
    x = lax.rem(lax.axis_index("chan"), 4)
    y = lax.axis_index("chan") // 4
    z = lax.axis_index("stn") // 2
    core = lax.rem(lax.axis_index("stn"), 2)
    chip = z * CHAN_AXIS + lax.axis_index("chan")
    sibling = (z * 2 + 1 - core, lax.axis_index("chan"))

    turn = 1 + 2 * core
    zs = [lax.rem(z + dz * turn, 4) for dz in range(4)]
    xs = [lax.rem(x + dx * turn, 4) for dx in range(4)]
    ys = [lax.rem(y + dy * turn, 4) * 4 for dy in range(4)]

    flag_load = pltpu.make_async_copy(flags, flagv, load_sem.at[0])
    flag_load.start()
    volt_loads = [
        pltpu.make_async_copy(volt.at[:, :, number], vin.at[:, :, number], load_sem.at[n])
        for n, number in ((1, 1 - core), (2, core))
    ]
    for load in volt_loads:
        load.start()

    barrier = pltpu.get_barrier_semaphore()
    line = [(zs[dz] * 2 + core, ys[0] + x) for dz in range(1, 4)]
    plane = [(z * 2 + core, ys[dy] + xs[dx]) for dy in range(4) for dx in range(4) if (dy, dx) != (0, 0)]
    greeted = [sibling] + line + plane
    for peer in greeted:
        pl.semaphore_signal(barrier, inc=1, device_id=peer, device_id_type=MESH)

    def hand_over(part, give, send, given, sibling_sem):
        pltpu.make_async_remote_copy(
            src_ref=give.at[part],
            dst_ref=send.at[part, :, :, :, core] if len(send.shape) == 8 else send.at[part, :, core],
            send_sem=given,
            recv_sem=sibling_sem.at[part],
            device_id=sibling,
            device_id_type=MESH,
        ).start()

    def exchange(part, send, landing, sibling_sem, sent, recv_sem):
        share = send.at[part, :, 1 - core]
        pltpu.make_async_copy(share, share, sibling_sem.at[part]).wait()
        pltpu.make_async_copy(send.at[part, chip], landing, recv_sem.at[part]).start()
        for dz, dy, dx in exchange_order():
            if (dz, dy, dx) != (0, 0, 0):
                chan = ys[dy] + xs[dx]
                pltpu.make_async_remote_copy(
                    src_ref=send.at[part, zs[dz] * CHAN_AXIS + chan],
                    dst_ref=landing,
                    send_sem=sent.at[part],
                    recv_sem=recv_sem.at[part],
                    device_id=(zs[dz] * 2 + core, chan),
                    device_id_type=MESH,
                ).start()

    by_z, by_x, by_y, by_xz, by_yz, by_xy, by_xyz = stages

    def place(steps):
        dz, dy, dx = steps
        return zs[dz % 4] * 2 + core, ys[dy % 4] + xs[dx % 4]

    def packs(part):
        near = (-1, 0, 1)
        listed = []
        for m in range(3):
            listed.append(((3, m, slice(0, 3)), by_z.at[part, m], (1, 0, 0), [(1, m - 1, d) for d in near]))
            listed.append(((m, slice(0, 3), 3), by_x.at[part, m], (0, 0, 1), [(m - 1, d, 1) for d in near]))
            listed.append(((m, 3, slice(0, 3)), by_y.at[part, m], (0, 1, 0), [(m - 1, 1, d) for d in near]))
            listed.append(((m, 3, 3), by_xy.at[part, m], (0, 1, 1), [(m - 1, 1, 1)]))
        listed.append(((3, slice(0, 3), 3), by_xz.at[part], (1, 0, 1), [(1, d, 1) for d in near]))
        listed.append(((3, 3, slice(0, 3)), by_yz.at[part], (1, 1, 0), [(1, 1, d) for d in near]))
        listed.append(((3, 3, 3), by_xyz.at[part], (1, 1, 1), [(1, 1, 1)]))
        return [(15 * part + n, *pack) for n, pack in enumerate(listed)]

    def send_packs(part):
        share = send.at[part, :, :, :, 1 - core]
        pltpu.make_async_copy(share, share, sibling_sem.at[part]).wait()
        for n, at, stage, steps, _ in packs(part):
            pltpu.make_async_remote_copy(
                src_ref=send.at[part, at[0], at[1], at[2]],
                dst_ref=stage,
                send_sem=packs_sent,
                recv_sem=pack_sem.at[n],
                device_id=place(steps),
                device_id_type=MESH,
            ).start()

    def send_direct(part):
        pltpu.make_async_copy(send.at[part, 1, 1, 1], recv.at[part, chip], recv_sem.at[part, 0]).start()
        for steps in exchange_order():
            if 2 not in steps and steps != (0, 0, 0):
                at = [(d + 1) % 4 for d in steps]
                pltpu.make_async_remote_copy(
                    src_ref=send.at[part, at[0], at[1], at[2]],
                    dst_ref=recv.at[part, chip],
                    send_sem=sent.at[part],
                    recv_sem=recv_sem.at[part, steps[0]],
                    device_id=place(steps),
                    device_id_type=MESH,
                ).start()

    def relay_packs(part):
        for n, _, stage, steps, onward in packs(part):
            pltpu.make_async_copy(stage, stage, pack_sem.at[n]).wait()
            dz, dy, dx = (-d % 4 for d in steps)
            origin = zs[dz] * CHAN_AXIS + ys[dy] + xs[dx]
            for m, further in enumerate(onward):
                pltpu.make_async_remote_copy(
                    src_ref=stage.at[m] if len(onward) > 1 else stage,
                    dst_ref=recv.at[part, origin],
                    send_sem=relays_sent,
                    recv_sem=recv_sem.at[part, (steps[0] + further[0]) % 4],
                    device_id=place(further),
                    device_id_type=MESH,
                ).start()

    flag_load.wait()
    row, col = iota(0), iota(1)
    hits = ones_where(iota(0, (256, 64)) == flagv[...])
    count = dot(hits, jnp.ones((64, 256), BF16))
    keep_rows = ones_where((count < 0.5) & (row % 16 == col % 16))
    keep[...] = dot(ones_where(iota(1, (16, 256)) // 16 == iota(0, (16, 256))), keep_rows)

    def sort_out(number):
        way = 1 + 2 * number
        there = (row // 128) * 8 + ((x + (row // 32 + 3) % 4 * way) % 4) * 2 + (row // 8) % 2
        swap = jnp.where((col // 16 == ((row // 16) % 2) * 8 + row % 8) & (col % 16 == there), 1.0, 0.0)
        for zz in range(4):
            for half in range(2):
                block = vin[:, zz, number, half].reshape(256, 256)
                mine = (swap * keep[pl.ds((zz * 2 + number) * 2 + half, 1), :]).astype(BF16)
                sorted_block = dot(mine, block).astype(BF16)
                for one in range(2):
                    mz = lax.rem((zz + 4 - z) * way + 1, 4)
                    my = lax.rem((half * 2 + one + 4 - y) * way + 1, 4)
                    yield mz, my, sorted_block[one * 128 : one * 128 + 128].reshape(4, 4, 8, 256)

    volt_loads[0].wait()
    for n, (mz, my, block) in enumerate(sort_out(1 - core)):
        if n == 8:
            pl.semaphore_wait(barrier, len(greeted))
            for peer in line:
                pl.semaphore_signal(plane_sem, inc=1, device_id=peer, device_id_type=MESH)
        for part in range(PARTS):
            give[part, mz, my] = block[..., part * SPAN : part * SPAN + SPAN]
    for part in range(PARTS):
        hand_over(part, give, send, given, sibling_sem)
    volt_loads[1].wait()
    for mz, my, block in sort_out(core):
        for part in range(PARTS):
            send[part, mz, my, :, core] = block[..., part * SPAN : part * SPAN + SPAN]
    loads = [
        pltpu.make_async_copy(source, target, load_sem.at[n])
        for n, (source, target) in enumerate(
            ((wgt, win), (dm, dmv), (chirps, chv), (dft, dftv), (proto, protov)), 3
        )
    ]
    for load in loads:
        load.start()
    pl.semaphore_wait(plane_sem, len(line))
    send_packs(0)
    send_direct(0)
    send_packs(1)
    relay_packs(0)
    send_direct(1)
    relay_packs(1)
    for load in loads:
        load.wait()

    def toeplitz(n, carry):
        b, block = n // NBLOCK, lax.rem(n, NBLOCK)
        for part in range(2):
            wide = jnp.broadcast_to(chv[dmv[b], pl.ds(part * NBLOCK + block, 1), :], (8, 2 * CHANNELS))
            eight = pltpu.roll(wide, CHANNELS + 1, 1, stride=1, stride_axis=0)
            for k in range(0, CHANNELS, 16):
                both = [pltpu.roll(eight, k + i, 1)[:, :CHANNELS] if k + i else eight[:, :CHANNELS] for i in (0, 8)]
                rows = pl.ds(pl.multiple_of(block * CHANNELS + k, 16), 16)
                tables[b, rows, part * CHANNELS : (part + 1) * CHANNELS] = jnp.concatenate(both, axis=0).astype(BF16)
        return carry

    lax.fori_loop(0, 2 * NBLOCK, toeplitz, 0)

    to_device = lax.rem(core + row // 128, 2) * 16 + (row // 8) % 16
    order = ones_where(
        (col // 128 == row % 2) & ((col // 64) % 2 == (row // 2) % 2) & (col % 64 == to_device * 2 + (row // 4) % 2)
    )
    for part in range(PARTS):
        for n, dz in enumerate((3, 0, 1, 2)):
            source = zs[-dz % 4]
            arrived = recv.at[part, pl.ds(pl.multiple_of(source * 16, 16), 16)]
            pltpu.make_async_copy(arrived, arrived, recv_sem.at[part, dz]).wait()
            for c in range(2):
                real, imag, weight_real, weight_imag = [], [], [], []
                for number in range(2):
                    chips = pl.ds(pl.multiple_of(source * 16, 16), 16)
                    inputs = pl.ds(pl.multiple_of((source * 2 + number) * 128, 128), 128)
                    real.append(recv[part, chips, number, c].reshape(128, SPAN))
                    imag.append(recv[part, chips, number, 2 + c].reshape(128, SPAN))
                    weight_real.append(win[0, c, :, inputs])
                    weight_imag.append(win[1, c, :, inputs])
                parts = jnp.concatenate(
                    [
                        jnp.concatenate(real + [-half for half in imag], axis=0),
                        jnp.concatenate(imag + real, axis=0),
                    ],
                    axis=1,
                )
                product = dot(jnp.concatenate(weight_real + weight_imag, axis=1), parts)
                if n == 0:
                    acc[c] = product
                elif n < 3:
                    acc[c] += product
                else:
                    beams[c] = (acc[c] + product).astype(BF16)
        for zz in range(4):
            rows = slice(zz * 64, zz * 64 + 64)
            block = jnp.concatenate([beams[c, rows, q * SPAN : q * SPAN + SPAN] for c in range(2) for q in range(2)], axis=0)
            block = dot(order, block).astype(BF16)
            send2[part, zz * 16 : zz * 16 + 16, core] = block[:128].reshape(16, 8, SPAN)
            give2[part, zz * 16 : zz * 16 + 16] = block[128:].reshape(16, 8, SPAN)
        hand_over(part, give2, send2, given2, sibling_sem2)
        exchange(part, send2, recv2.at[part, chip], sibling_sem2, sent2, recv_sem2)

    arrived = recv2.at[0]
    pltpu.make_async_copy(arrived, arrived, recv_sem2.at[0]).wait()
    for b, power, last in front(
        lambda n: recv2[0, n * 16 : n * 16 + 16].reshape(256, SPAN), lambda b: 0.0, dftv, protov, ordered, padded
    ):
        power0[b : b + 1, :] = power
        last0[b] = last
    for b in range(2):
        for n in range(4):
            lanes, series = synthesise(b, n, protov, padded)
            store_shifted(series, lanes, even, odd)
        product0[b] = chirped(stacked_shifts(even, odd), tables[b])

    for blocks, sem in ((give, given), (give2, given2)):
        pltpu.make_async_copy(blocks, blocks, sem).wait()
    for sem in (packs_sent, relays_sent):
        for part in range(PARTS):
            blocks = recv.at[part, 0:37]
            pltpu.make_async_copy(blocks, blocks, sem).wait()
    for part in range(PARTS):
        for blocks, sem in ((recv.at[part, 0:26], sent), (send2.at[part, 0:63], sent2)):
            pltpu.make_async_copy(blocks, blocks, sem.at[part]).wait()
    arrived = recv2.at[1]
    pltpu.make_async_copy(arrived, arrived, recv_sem2.at[1]).wait()


def front(chunk, before_first, dftv, protov, xs, padded):
    row, col = iota(0), iota(1)
    sort = ones_where(col == ((row % 32) // 2 * 2 + (row % 64) // 32) * 8 + (row // 64) * 2 + row % 2)
    spread = ones_where(iota(1, (SPAN, SPAN)) == (iota(0, (SPAN, SPAN)) % 8) * 16 + iota(0, (SPAN, SPAN)) // 8)
    for n in range(4):
        block = dot(sort, chunk(n)).astype(BF16)
        for k in range(4):
            xs[k // 2, (k % 2) * 256 + n * 64 : (k % 2) * 256 + n * 64 + 64, :] = block[k * 64 : k * 64 + 64]
    for b in range(2):
        turned = lax.dot_general(spread, xs[b], (((1,), (1,)), ((), ())), preferred_element_type=F32)
        power = jnp.sum(turned * turned, axis=0, keepdims=True)
        spectra = dot(turned.astype(BF16), dftv[...])
        last = spectra[SPAN - 88 :]
        first = iota(0, (88, 512)) % 8 == 0
        padded[b, 0:88, :] = jnp.where(first, before_first(b), pltpu.roll(last, 1, 0))
        padded[b, 88 : 88 + SPAN, :] = spectra
        yield b, power, pltpu.roll(last, 81, 0)


def synthesise(b, n, protov, padded):
    lanes = slice(n * 128, n * 128 + 128)
    series = protov[0:1, lanes] * padded[b, 88 : 88 + SPAN, lanes]
    for tap in range(1, TAPS):
        series = series + protov[tap : tap + 1, lanes] * padded[b, 88 - 8 * tap : 88 - 8 * tap + SPAN, lanes]
    return lanes, series


def store_shifted(series, lanes, even, odd):
    after = jnp.where(iota(0, (32, 128)) % 8 == 7, 0.0, pltpu.roll(series[:32], 31, 0))
    even[0:SPAN, lanes] = series.astype(BF16)
    even[SPAN : SPAN + 32, lanes] = after.astype(BF16)
    odd[0 : SPAN + 16, lanes] = jnp.concatenate([series[8:], after[:24]], axis=0).astype(BF16)


def stacked_shifts(even, odd):
    shifted = [even[0:SPAN], odd[0:SPAN], even[16 : 16 + SPAN], odd[16 : 16 + SPAN], even[32 : 32 + SPAN]]
    return [jnp.concatenate([block[:, p * 256 : p * 256 + 256] for block in shifted], axis=1) for p in range(2)]


def chirped(parts, table):
    product = dot(jnp.concatenate(parts, axis=0), table)
    rows = product.shape[0] // 2
    real = product[:rows, :256] + product[rows:, 256:]
    imag = product[rows:, :256] - product[:rows, 256:]
    return jnp.concatenate([real, imag], axis=1)


def tail(
    xv, tv, dftv, protov, product0, last0, power0, out, band,
    xs, padded, even0, even1, odd0, odd1, over0, over1, outv, bandv, out_sem,
):
    band_copy = pltpu.make_async_copy(bandv, band, out_sem.at[2])
    for b, power, _ in front(lambda n: xv[1, n * 256 : n * 256 + 256, :], lambda b: last0[b], dftv, protov, xs, padded):
        power = (power + power0[b : b + 1, :]) * (1.0 / TIME)
        bandv[b : b + 1, :] = power[:, :256] + power[:, 256:]
    band_copy.start()
    results = []
    for b, (even, odd, over) in enumerate(((even0, odd0, over0), (even1, odd1, over1))):
        for n in range(4):
            lanes, series = synthesise(b, n, protov, padded)
            store_shifted(series, lanes, even, odd)
            over_edge = jnp.where(iota(0, (32, 128)) % 8 == 7, pltpu.roll(series[:32], 7, 0), 0.0)
            for blk in range(NBLOCK):
                seen = [over_edge[: 8 * blk]] if blk else []
                unseen = [jnp.zeros((32 - 8 * blk, 128), F32)] if blk < 4 else []
                over[blk, :, lanes] = jnp.concatenate(unseen + seen, axis=0).astype(BF16)
        edges = [
            jnp.concatenate([over[blk, :, p * 256 : p * 256 + 256] for blk in range(NBLOCK)], axis=1) for p in range(2)
        ]
        parts = [jnp.concatenate(pair, axis=0) for pair in zip(stacked_shifts(even, odd), edges)]
        product = chirped(parts, tv[b])
        results.append(
            jnp.concatenate([product0[b, :96], product0[b, 96:] + product[SPAN:], product[:SPAN]], axis=0).astype(BF16)
        )
    row, col = iota(0), iota(1)
    final = ones_where(col == (row % 4) * 64 + ((row // 4) % 8) * 8 + row // 32)
    copies = []
    for h in range(2):
        for j in range(2):
            rows = slice(128 * h + 64 * j, 128 * h + 64 * j + 64)
            block = jnp.concatenate(
                [
                    jnp.concatenate([results[b][rows, half * 128 + q * 256 : half * 128 + q * 256 + 128] for q in range(2)], axis=1)
                    for half in range(2) for b in range(2)
                ],
                axis=0,
            )
            block = dot(final, block).astype(BF16)
            for q in range(2):
                for k in range(8):
                    start = 512 * h + 64 * k + 32 * j
                    outv[q, start : start + 32, :] = block[32 * k : 32 * k + 32, q * 128 : q * 128 + 128]
        done = pl.ds(512 * h, 512)
        copies.append(pltpu.make_async_copy(outv.at[:, done], out.at[:, done], out_sem.at[h]))
        copies[-1].start()
    for copy in copies + [band_copy]:
        copy.wait()


def in_hbm(array):
    return pltpu.with_memory_space_constraint(array, pltpu.HBM)


def on_device(voltages, weights, flags, dm_index):
    hbm = pl.BlockSpec(memory_space=pl.ANY)
    vmem = pl.BlockSpec(memory_space=pltpu.VMEM)
    dma = pltpu.SemaphoreType.DMA
    params = dict(vmem_limit_bytes=24 * 1024 * 1024)
    beams, tables, dft, proto, product0, last0, power0 = pl.pallas_call(
        body,
        out_shape=(
            jax.ShapeDtypeStruct((PARTS, 64, 2, 8, SPAN), BF16),
            jax.ShapeDtypeStruct((2, NBLOCK * CHANNELS, 512), BF16),
            jax.ShapeDtypeStruct((512, 512), BF16),
            jax.ShapeDtypeStruct((TAPS, 512), F32),
            jax.ShapeDtypeStruct((2, SPAN, 512), F32),
            jax.ShapeDtypeStruct((2, 88, 512), F32),
            jax.ShapeDtypeStruct((2, 512), F32),
        ),
        in_specs=[hbm] * 7,
        out_specs=(vmem,) * 7,
        scratch_shapes=[
            pltpu.VMEM((16, 4, 2, 2, 16, 256), BF16),
            pltpu.VMEM((PARTS, 4, 4, 4, 4, 8, SPAN), BF16),
            pltpu.VMEM((PARTS, 4, 4, 4, 2, 4, 8, SPAN), BF16),
            pltpu.VMEM((PARTS, 64, 2, 4, 8, SPAN), BF16),
            pltpu.VMEM((2, 2, 256, 1024), BF16),
            pltpu.VMEM((DMS, 16, 512), F32),
            pltpu.VMEM((1, 64), jnp.int32),
            pltpu.SMEM((2,), jnp.int32),
            pltpu.VMEM((2, 256, 2 * SPAN), BF16),
            pltpu.VMEM((PARTS, 64, 8, SPAN), BF16),
            pltpu.VMEM((PARTS, 64, 2, 8, SPAN), BF16),
            pltpu.VMEM((16, 256), F32),
            pltpu.VMEM((2, 512, SPAN), BF16),
            pltpu.VMEM((2, 88 + SPAN, 512), F32),
            pltpu.VMEM((SPAN + 32, 512), BF16),
            pltpu.VMEM((SPAN + 16, 512), BF16),
            pltpu.VMEM((2, 256, 2 * SPAN), F32),
            dma((8,)),
            pltpu.SemaphoreType.REGULAR,
            dma,
            dma,
            *[dma((PARTS,)) for _ in range(4)],
            dma((PARTS, 4)),
            dma((PARTS,)),
            dma((30,)),
            dma,
            dma,
            *[
                pltpu.VMEM((PARTS,) + shape + (2, 4, 8, SPAN), BF16)
                for shape in [(3, 3), (3, 3), (3, 3), (3,), (3,), (3,), ()]
            ],
        ],
        compiler_params=pltpu.CompilerParams(collective_id=0, has_side_effects=True, **params),
        name="beamform",
    )(
        in_hbm(voltages.reshape(16, 4, 2, 2, 16, TIME)),
        in_hbm(weights),
        in_hbm(flags),
        in_hbm(dm_index),
        in_hbm(jnp.asarray(chirp_rows()).astype(BF16).astype(F32)),
        in_hbm(jnp.asarray(dft_rows()).astype(BF16)),
        in_hbm(jnp.asarray(prototype())),
    )
    dedispersed, bandpass = pl.pallas_call(
        tail,
        out_shape=(
            jax.ShapeDtypeStruct((2, 2 * TIME * 2, 128), BF16),
            jax.ShapeDtypeStruct((2, CHANNELS), F32),
        ),
        in_specs=[vmem] * 7,
        out_specs=(hbm, hbm),
        scratch_shapes=[
            pltpu.VMEM((2, 512, SPAN), BF16),
            pltpu.VMEM((2, 88 + SPAN, 512), F32),
            *[pltpu.VMEM((SPAN + 32, 512), BF16) for _ in range(2)],
            *[pltpu.VMEM((SPAN + 16, 512), BF16) for _ in range(2)],
            *[pltpu.VMEM((NBLOCK, 32, 512), BF16) for _ in range(2)],
            pltpu.VMEM((2, 2 * TIME * 2, 128), BF16),
            pltpu.VMEM((2, CHANNELS), F32),
            dma((3,)),
        ],
        compiler_params=pltpu.CompilerParams(**params),
        name="synthesis",
    )(
        beams.reshape(PARTS, 1024, SPAN),
        tables,
        dft,
        proto,
        product0,
        last0,
        power0,
    )
    dedispersed = dedispersed.reshape(2, 512, 2, 128).transpose(0, 2, 1, 3).reshape(2, 2, TIME * CHANNELS)
    return dedispersed, bandpass


def solution(mesh):
    return jax.shard_map(
        on_device,
        mesh=mesh,
        in_specs=(
            P(None, ("stn", "chan"), None, None),
            P(None, ("stn", "chan"), None, None),
            P(("stn", "chan"), None),
            P(("stn", "chan")),
        ),
        out_specs=(P(None, ("stn", "chan"), None), P(("stn", "chan"), None)),
        check_vma=False,
    )
```

```python
import math
import random

import jax
import jax.numpy as jnp
import numpy as np
from jax import lax
from jax.experimental import pallas as pl
from jax.experimental.pallas import tpu as pltpu
from jax.sharding import PartitionSpec as P

CHANNELS = 256
BEAMS = 256
INPUTS = 1024
TIME = 256
TAPS = 12
CHIRP = 1024
DMS = 16
NBLOCK = CHIRP // CHANNELS + 1
DEVICES = 128
CHAN_AXIS = 16
PARTS = 2
SPAN = TIME // PARTS
MESH = pl.DeviceIdType.MESH
BF16 = jnp.bfloat16
F32 = jnp.float32


def dft_rows():
    order = np.arange(CHANNELS)
    angle = 2.0 * math.pi / CHANNELS * (order[:, None] * order[None, :] % CHANNELS)
    cosine = np.cos(angle) / math.sqrt(CHANNELS)
    sine = np.sin(angle) / math.sqrt(CHANNELS)
    return np.block([[cosine, sine], [-sine, cosine]]).astype(np.float32)


def prototype():
    counter = np.arange(TAPS * CHANNELS, dtype=np.float64)
    offset = (counter + 0.5) / CHANNELS - TAPS / 2.0
    window = 0.54 + 0.46 * np.cos(math.pi * offset / (TAPS / 2.0))
    taps = (np.sinc(offset) * window).reshape(TAPS, CHANNELS)
    return np.concatenate([taps, taps], axis=1).astype(np.float32)


def chirp_rows():
    dms = np.arange(DMS, dtype=np.int64)[:, None, None]
    lag = np.arange(NBLOCK)[None, :, None] * CHANNELS + CHANNELS - 1 - np.arange(2 * CHANNELS)[None, None, :]
    valid = (lag >= 0) & (lag < CHIRP)
    lag = np.clip(lag, 0, CHIRP - 1)
    angle = math.pi * ((dms + 1) * lag * lag % (2 * DMS * CHIRP)) / (DMS * CHIRP)
    real = np.where(valid, np.cos(angle), 0.0) / math.sqrt(CHIRP)
    imag = np.where(valid, np.sin(angle), 0.0) / math.sqrt(CHIRP)
    rows = np.concatenate([real, imag, np.zeros((DMS, 6, 2 * CHANNELS))], axis=1)
    return rows.astype(np.float32)


def iota(axis, shape=(256, 256)):
    return lax.broadcasted_iota(jnp.int32, shape, axis)


def ones_where(condition):
    return jnp.where(condition, 1.0, 0.0).astype(BF16)


def dot(a, b):
    return jnp.dot(a, b, preferred_element_type=F32)


def exchange_order():
    left = [(dz, dy, dx) for dz in range(4) for dy in range(4) for dx in range(4)]
    random.Random(7).shuffle(left)
    hops, ordered = [0, 0, 0], []
    while left:
        def uneven(step):
            return sum((done + min(d, 4 - d) - len(ordered) - 1) ** 2 for done, d in zip(hops, step))

        best = min(left, key=uneven)
        left.remove(best)
        ordered.append(best)
        hops = [done + min(d, 4 - d) for done, d in zip(hops, best)]
    return ordered


def body(
    volt, wgt, flags, dm, chirps, dft, proto, recv2, tables, dftv, protov, product0, last0, power0,
    vin, give, send, recv, win, chv, flagv, dmv, beams, give2, send2, keep, ordered, padded, even, odd, acc,
    load_sem, plane_sem, given, given2, sent, sent2, sibling_sem, sibling_sem2, recv_sem, recv_sem2, pack_sem, packs_sent, relays_sent, *stages,
):
    x = lax.rem(lax.axis_index("chan"), 4)
    y = lax.axis_index("chan") // 4
    z = lax.axis_index("stn") // 2
    core = lax.rem(lax.axis_index("stn"), 2)
    chip = z * CHAN_AXIS + lax.axis_index("chan")
    sibling = (z * 2 + 1 - core, lax.axis_index("chan"))

    turn = 1 + 2 * core
    zs = [lax.rem(z + dz * turn, 4) for dz in range(4)]
    xs = [lax.rem(x + dx * turn, 4) for dx in range(4)]
    ys = [lax.rem(y + dy * turn, 4) * 4 for dy in range(4)]

    flag_load = pltpu.make_async_copy(flags, flagv, load_sem.at[0])
    flag_load.start()
    volt_loads = [
        pltpu.make_async_copy(volt.at[:, :, number], vin.at[:, :, number], load_sem.at[n])
        for n, number in ((1, 1 - core), (2, core))
    ]
    for load in volt_loads:
        load.start()

    barrier = pltpu.get_barrier_semaphore()
    line = [(zs[dz] * 2 + core, ys[0] + x) for dz in range(1, 4)]
    plane = [(z * 2 + core, ys[dy] + xs[dx]) for dy in range(4) for dx in range(4) if (dy, dx) != (0, 0)]
    greeted = [sibling] + line + plane
    for peer in greeted:
        pl.semaphore_signal(barrier, inc=1, device_id=peer, device_id_type=MESH)

    def hand_over(part, give, send, given, sibling_sem):
        pltpu.make_async_remote_copy(
            src_ref=give.at[part],
            dst_ref=send.at[part, :, :, :, core] if len(send.shape) == 8 else send.at[part, :, core],
            send_sem=given,
            recv_sem=sibling_sem.at[part],
            device_id=sibling,
            device_id_type=MESH,
        ).start()

    def exchange(part, send, landing, sibling_sem, sent, recv_sem):
        share = send.at[part, :, 1 - core]
        pltpu.make_async_copy(share, share, sibling_sem.at[part]).wait()
        pltpu.make_async_copy(send.at[part, chip], landing, recv_sem.at[part]).start()
        for dz, dy, dx in exchange_order():
            if (dz, dy, dx) != (0, 0, 0):
                chan = ys[dy] + xs[dx]
                pltpu.make_async_remote_copy(
                    src_ref=send.at[part, zs[dz] * CHAN_AXIS + chan],
                    dst_ref=landing,
                    send_sem=sent.at[part],
                    recv_sem=recv_sem.at[part],
                    device_id=(zs[dz] * 2 + core, chan),
                    device_id_type=MESH,
                ).start()

    by_z, by_x, by_y, by_xz, by_yz, by_xy, by_xyz = stages

    def place(steps):
        dz, dy, dx = steps
        return zs[dz % 4] * 2 + core, ys[dy % 4] + xs[dx % 4]

    def packs(part):
        near = (-1, 0, 1)
        listed = []
        for m in range(3):
            listed.append(((3, m, slice(0, 3)), by_z.at[part, m], (1, 0, 0), [(1, m - 1, d) for d in near]))
            listed.append(((m, slice(0, 3), 3), by_x.at[part, m], (0, 0, 1), [(m - 1, d, 1) for d in near]))
            listed.append(((m, 3, slice(0, 3)), by_y.at[part, m], (0, 1, 0), [(m - 1, 1, d) for d in near]))
            listed.append(((m, 3, 3), by_xy.at[part, m], (0, 1, 1), [(m - 1, 1, 1)]))
        listed.append(((3, slice(0, 3), 3), by_xz.at[part], (1, 0, 1), [(1, d, 1) for d in near]))
        listed.append(((3, 3, slice(0, 3)), by_yz.at[part], (1, 1, 0), [(1, 1, d) for d in near]))
        listed.append(((3, 3, 3), by_xyz.at[part], (1, 1, 1), [(1, 1, 1)]))
        return [(15 * part + n, *pack) for n, pack in enumerate(listed)]

    def send_packs(part):
        share = send.at[part, :, :, :, 1 - core]
        pltpu.make_async_copy(share, share, sibling_sem.at[part]).wait()
        for n, at, stage, steps, _ in packs(part):
            pltpu.make_async_remote_copy(
                src_ref=send.at[part, at[0], at[1], at[2]],
                dst_ref=stage,
                send_sem=packs_sent,
                recv_sem=pack_sem.at[n],
                device_id=place(steps),
                device_id_type=MESH,
            ).start()

    def send_direct(part):
        pltpu.make_async_copy(send.at[part, 1, 1, 1], recv.at[part, chip], recv_sem.at[part, 0]).start()
        for steps in exchange_order():
            if 2 not in steps and steps != (0, 0, 0):
                at = [(d + 1) % 4 for d in steps]
                pltpu.make_async_remote_copy(
                    src_ref=send.at[part, at[0], at[1], at[2]],
                    dst_ref=recv.at[part, chip],
                    send_sem=sent.at[part],
                    recv_sem=recv_sem.at[part, steps[0]],
                    device_id=place(steps),
                    device_id_type=MESH,
                ).start()

    def relay_packs(part):
        for n, _, stage, steps, onward in packs(part):
            pltpu.make_async_copy(stage, stage, pack_sem.at[n]).wait()
            dz, dy, dx = (-d % 4 for d in steps)
            origin = zs[dz] * CHAN_AXIS + ys[dy] + xs[dx]
            for m, further in enumerate(onward):
                pltpu.make_async_remote_copy(
                    src_ref=stage.at[m] if len(onward) > 1 else stage,
                    dst_ref=recv.at[part, origin],
                    send_sem=relays_sent,
                    recv_sem=recv_sem.at[part, (steps[0] + further[0]) % 4],
                    device_id=place(further),
                    device_id_type=MESH,
                ).start()

    flag_load.wait()
    row, col = iota(0), iota(1)
    hits = ones_where(iota(0, (256, 64)) == flagv[...])
    count = dot(hits, jnp.ones((64, 256), BF16))
    keep_rows = ones_where((count < 0.5) & (row % 16 == col % 16))
    keep[...] = dot(ones_where(iota(1, (16, 256)) // 16 == iota(0, (16, 256))), keep_rows)

    def sort_out(number):
        way = 1 + 2 * number
        there = (row // 128) * 8 + ((x + (row // 32 + 3) % 4 * way) % 4) * 2 + (row // 8) % 2
        swap = jnp.where((col // 16 == ((row // 16) % 2) * 8 + row % 8) & (col % 16 == there), 1.0, 0.0)
        for zz in range(4):
            for half in range(2):
                block = vin[:, zz, number, half].reshape(256, 256)
                mine = (swap * keep[pl.ds((zz * 2 + number) * 2 + half, 1), :]).astype(BF16)
                sorted_block = dot(mine, block).astype(BF16)
                for one in range(2):
                    mz = lax.rem((zz + 4 - z) * way + 1, 4)
                    my = lax.rem((half * 2 + one + 4 - y) * way + 1, 4)
                    yield mz, my, sorted_block[one * 128 : one * 128 + 128].reshape(4, 4, 8, 256)

    volt_loads[0].wait()
    for mz, my, block in sort_out(1 - core):
        for part in range(PARTS):
            give[part, mz, my] = block[..., part * SPAN : part * SPAN + SPAN]
    pl.semaphore_wait(barrier, len(greeted))
    for peer in line:
        pl.semaphore_signal(plane_sem, inc=1, device_id=peer, device_id_type=MESH)
    for part in range(PARTS):
        hand_over(part, give, send, given, sibling_sem)
    volt_loads[1].wait()
    for mz, my, block in sort_out(core):
        for part in range(PARTS):
            send[part, mz, my, :, core] = block[..., part * SPAN : part * SPAN + SPAN]
    loads = [
        pltpu.make_async_copy(source, target, load_sem.at[n])
        for n, (source, target) in enumerate(
            ((wgt, win), (dm, dmv), (chirps, chv), (dft, dftv), (proto, protov)), 3
        )
    ]
    for load in loads:
        load.start()
    pl.semaphore_wait(plane_sem, len(line))
    send_packs(0)
    send_direct(0)
    send_packs(1)
    relay_packs(0)
    send_direct(1)
    relay_packs(1)
    for load in loads:
        load.wait()

    def toeplitz(n, carry):
        b, block = n // NBLOCK, lax.rem(n, NBLOCK)
        for part in range(2):
            wide = jnp.broadcast_to(chv[dmv[b], pl.ds(part * NBLOCK + block, 1), :], (8, 2 * CHANNELS))
            eight = pltpu.roll(wide, CHANNELS + 1, 1, stride=1, stride_axis=0)
            for k in range(0, CHANNELS, 16):
                both = [pltpu.roll(eight, k + i, 1)[:, :CHANNELS] if k + i else eight[:, :CHANNELS] for i in (0, 8)]
                rows = pl.ds(pl.multiple_of(block * CHANNELS + k, 16), 16)
                tables[b, rows, part * CHANNELS : (part + 1) * CHANNELS] = jnp.concatenate(both, axis=0).astype(BF16)
        return carry

    lax.fori_loop(0, 2 * NBLOCK, toeplitz, 0)

    to_device = lax.rem(core + row // 128, 2) * 16 + (row // 8) % 16
    order = ones_where(
        (col // 128 == row % 2) & ((col // 64) % 2 == (row // 2) % 2) & (col % 64 == to_device * 2 + (row // 4) % 2)
    )
    for part in range(PARTS):
        for n, dz in enumerate((3, 0, 1, 2)):
            source = zs[-dz % 4]
            arrived = recv.at[part, pl.ds(pl.multiple_of(source * 16, 16), 16)]
            pltpu.make_async_copy(arrived, arrived, recv_sem.at[part, dz]).wait()
            for c in range(2):
                real, imag, weight_real, weight_imag = [], [], [], []
                for number in range(2):
                    chips = pl.ds(pl.multiple_of(source * 16, 16), 16)
                    inputs = pl.ds(pl.multiple_of((source * 2 + number) * 128, 128), 128)
                    real.append(recv[part, chips, number, c].reshape(128, SPAN))
                    imag.append(recv[part, chips, number, 2 + c].reshape(128, SPAN))
                    weight_real.append(win[0, c, :, inputs])
                    weight_imag.append(win[1, c, :, inputs])
                parts = jnp.concatenate(
                    [
                        jnp.concatenate(real + [-half for half in imag], axis=0),
                        jnp.concatenate(imag + real, axis=0),
                    ],
                    axis=1,
                )
                product = dot(jnp.concatenate(weight_real + weight_imag, axis=1), parts)
                if n == 0:
                    acc[c] = product
                elif n < 3:
                    acc[c] += product
                else:
                    beams[c] = (acc[c] + product).astype(BF16)
        for zz in range(4):
            rows = slice(zz * 64, zz * 64 + 64)
            block = jnp.concatenate([beams[c, rows, q * SPAN : q * SPAN + SPAN] for c in range(2) for q in range(2)], axis=0)
            block = dot(order, block).astype(BF16)
            send2[part, zz * 16 : zz * 16 + 16, core] = block[:128].reshape(16, 8, SPAN)
            give2[part, zz * 16 : zz * 16 + 16] = block[128:].reshape(16, 8, SPAN)
        hand_over(part, give2, send2, given2, sibling_sem2)
        exchange(part, send2, recv2.at[part, chip], sibling_sem2, sent2, recv_sem2)

    arrived = recv2.at[0]
    pltpu.make_async_copy(arrived, arrived, recv_sem2.at[0]).wait()
    for b, power, last in front(
        lambda n: recv2[0, n * 16 : n * 16 + 16].reshape(256, SPAN), lambda b: 0.0, dftv, protov, ordered, padded
    ):
        power0[b : b + 1, :] = power
        last0[b] = last
    for b in range(2):
        for n in range(4):
            lanes, series = synthesise(b, n, protov, padded)
            store_shifted(series, lanes, even, odd)
        product0[b] = chirped(stacked_shifts(even, odd), tables[b])

    for blocks, sem in ((give, given), (give2, given2)):
        pltpu.make_async_copy(blocks, blocks, sem).wait()
    for sem in (packs_sent, relays_sent):
        for part in range(PARTS):
            blocks = recv.at[part, 0:37]
            pltpu.make_async_copy(blocks, blocks, sem).wait()
    for part in range(PARTS):
        for blocks, sem in ((recv.at[part, 0:26], sent), (send2.at[part, 0:63], sent2)):
            pltpu.make_async_copy(blocks, blocks, sem.at[part]).wait()
    arrived = recv2.at[1]
    pltpu.make_async_copy(arrived, arrived, recv_sem2.at[1]).wait()


def front(chunk, before_first, dftv, protov, xs, padded):
    row, col = iota(0), iota(1)
    sort = ones_where(col == ((row % 32) // 2 * 2 + (row % 64) // 32) * 8 + (row // 64) * 2 + row % 2)
    spread = ones_where(iota(1, (SPAN, SPAN)) == (iota(0, (SPAN, SPAN)) % 8) * 16 + iota(0, (SPAN, SPAN)) // 8)
    for n in range(4):
        block = dot(sort, chunk(n)).astype(BF16)
        for k in range(4):
            xs[k // 2, (k % 2) * 256 + n * 64 : (k % 2) * 256 + n * 64 + 64, :] = block[k * 64 : k * 64 + 64]
    for b in range(2):
        turned = lax.dot_general(spread, xs[b], (((1,), (1,)), ((), ())), preferred_element_type=F32)
        power = jnp.sum(turned * turned, axis=0, keepdims=True)
        spectra = dot(turned.astype(BF16), dftv[...])
        last = spectra[SPAN - 88 :]
        first = iota(0, (88, 512)) % 8 == 0
        padded[b, 0:88, :] = jnp.where(first, before_first(b), pltpu.roll(last, 1, 0))
        padded[b, 88 : 88 + SPAN, :] = spectra
        yield b, power, pltpu.roll(last, 81, 0)


def synthesise(b, n, protov, padded):
    lanes = slice(n * 128, n * 128 + 128)
    series = protov[0:1, lanes] * padded[b, 88 : 88 + SPAN, lanes]
    for tap in range(1, TAPS):
        series = series + protov[tap : tap + 1, lanes] * padded[b, 88 - 8 * tap : 88 - 8 * tap + SPAN, lanes]
    return lanes, series


def store_shifted(series, lanes, even, odd):
    after = jnp.where(iota(0, (32, 128)) % 8 == 7, 0.0, pltpu.roll(series[:32], 31, 0))
    even[0:SPAN, lanes] = series.astype(BF16)
    even[SPAN : SPAN + 32, lanes] = after.astype(BF16)
    odd[0 : SPAN + 16, lanes] = jnp.concatenate([series[8:], after[:24]], axis=0).astype(BF16)


def stacked_shifts(even, odd):
    shifted = [even[0:SPAN], odd[0:SPAN], even[16 : 16 + SPAN], odd[16 : 16 + SPAN], even[32 : 32 + SPAN]]
    return [jnp.concatenate([block[:, p * 256 : p * 256 + 256] for block in shifted], axis=1) for p in range(2)]


def chirped(parts, table):
    product = dot(jnp.concatenate(parts, axis=0), table)
    rows = product.shape[0] // 2
    real = product[:rows, :256] + product[rows:, 256:]
    imag = product[rows:, :256] - product[:rows, 256:]
    return jnp.concatenate([real, imag], axis=1)


def tail(
    xv, tv, dftv, protov, product0, last0, power0, out, band,
    xs, padded, even0, even1, odd0, odd1, over0, over1, outv, bandv, out_sem,
):
    band_copy = pltpu.make_async_copy(bandv, band, out_sem.at[2])
    for b, power, _ in front(lambda n: xv[1, n * 256 : n * 256 + 256, :], lambda b: last0[b], dftv, protov, xs, padded):
        power = (power + power0[b : b + 1, :]) * (1.0 / TIME)
        bandv[b : b + 1, :] = power[:, :256] + power[:, 256:]
    band_copy.start()
    results = []
    for b, (even, odd, over) in enumerate(((even0, odd0, over0), (even1, odd1, over1))):
        for n in range(4):
            lanes, series = synthesise(b, n, protov, padded)
            store_shifted(series, lanes, even, odd)
            over_edge = jnp.where(iota(0, (32, 128)) % 8 == 7, pltpu.roll(series[:32], 7, 0), 0.0)
            for blk in range(NBLOCK):
                seen = [over_edge[: 8 * blk]] if blk else []
                unseen = [jnp.zeros((32 - 8 * blk, 128), F32)] if blk < 4 else []
                over[blk, :, lanes] = jnp.concatenate(unseen + seen, axis=0).astype(BF16)
        edges = [
            jnp.concatenate([over[blk, :, p * 256 : p * 256 + 256] for blk in range(NBLOCK)], axis=1) for p in range(2)
        ]
        parts = [jnp.concatenate(pair, axis=0) for pair in zip(stacked_shifts(even, odd), edges)]
        product = chirped(parts, tv[b])
        results.append(
            jnp.concatenate([product0[b, :96], product0[b, 96:] + product[SPAN:], product[:SPAN]], axis=0).astype(BF16)
        )
    row, col = iota(0), iota(1)
    final = ones_where(col == (row % 4) * 64 + ((row // 4) % 8) * 8 + row // 32)
    copies = []
    for h in range(2):
        for j in range(2):
            rows = slice(128 * h + 64 * j, 128 * h + 64 * j + 64)
            block = jnp.concatenate(
                [
                    jnp.concatenate([results[b][rows, half * 128 + q * 256 : half * 128 + q * 256 + 128] for q in range(2)], axis=1)
                    for half in range(2) for b in range(2)
                ],
                axis=0,
            )
            block = dot(final, block).astype(BF16)
            for q in range(2):
                for k in range(8):
                    start = 512 * h + 64 * k + 32 * j
                    outv[q, start : start + 32, :] = block[32 * k : 32 * k + 32, q * 128 : q * 128 + 128]
        done = pl.ds(512 * h, 512)
        copies.append(pltpu.make_async_copy(outv.at[:, done], out.at[:, done], out_sem.at[h]))
        copies[-1].start()
    for copy in copies + [band_copy]:
        copy.wait()


def in_hbm(array):
    return pltpu.with_memory_space_constraint(array, pltpu.HBM)


def on_device(voltages, weights, flags, dm_index):
    hbm = pl.BlockSpec(memory_space=pl.ANY)
    vmem = pl.BlockSpec(memory_space=pltpu.VMEM)
    dma = pltpu.SemaphoreType.DMA
    params = dict(vmem_limit_bytes=24 * 1024 * 1024)
    beams, tables, dft, proto, product0, last0, power0 = pl.pallas_call(
        body,
        out_shape=(
            jax.ShapeDtypeStruct((PARTS, 64, 2, 8, SPAN), BF16),
            jax.ShapeDtypeStruct((2, NBLOCK * CHANNELS, 512), BF16),
            jax.ShapeDtypeStruct((512, 512), BF16),
            jax.ShapeDtypeStruct((TAPS, 512), F32),
            jax.ShapeDtypeStruct((2, SPAN, 512), F32),
            jax.ShapeDtypeStruct((2, 88, 512), F32),
            jax.ShapeDtypeStruct((2, 512), F32),
        ),
        in_specs=[hbm] * 7,
        out_specs=(vmem,) * 7,
        scratch_shapes=[
            pltpu.VMEM((16, 4, 2, 2, 16, 256), BF16),
            pltpu.VMEM((PARTS, 4, 4, 4, 4, 8, SPAN), BF16),
            pltpu.VMEM((PARTS, 4, 4, 4, 2, 4, 8, SPAN), BF16),
            pltpu.VMEM((PARTS, 64, 2, 4, 8, SPAN), BF16),
            pltpu.VMEM((2, 2, 256, 1024), BF16),
            pltpu.VMEM((DMS, 16, 512), F32),
            pltpu.VMEM((1, 64), jnp.int32),
            pltpu.SMEM((2,), jnp.int32),
            pltpu.VMEM((2, 256, 2 * SPAN), BF16),
            pltpu.VMEM((PARTS, 64, 8, SPAN), BF16),
            pltpu.VMEM((PARTS, 64, 2, 8, SPAN), BF16),
            pltpu.VMEM((16, 256), F32),
            pltpu.VMEM((2, 512, SPAN), BF16),
            pltpu.VMEM((2, 88 + SPAN, 512), F32),
            pltpu.VMEM((SPAN + 32, 512), BF16),
            pltpu.VMEM((SPAN + 16, 512), BF16),
            pltpu.VMEM((2, 256, 2 * SPAN), F32),
            dma((8,)),
            pltpu.SemaphoreType.REGULAR,
            dma,
            dma,
            *[dma((PARTS,)) for _ in range(4)],
            dma((PARTS, 4)),
            dma((PARTS,)),
            dma((30,)),
            dma,
            dma,
            *[
                pltpu.VMEM((PARTS,) + shape + (2, 4, 8, SPAN), BF16)
                for shape in [(3, 3), (3, 3), (3, 3), (3,), (3,), (3,), ()]
            ],
        ],
        compiler_params=pltpu.CompilerParams(collective_id=0, has_side_effects=True, **params),
        name="beamform",
    )(
        in_hbm(voltages.reshape(16, 4, 2, 2, 16, TIME)),
        in_hbm(weights),
        in_hbm(flags),
        in_hbm(dm_index),
        in_hbm(jnp.asarray(chirp_rows()).astype(BF16).astype(F32)),
        in_hbm(jnp.asarray(dft_rows()).astype(BF16)),
        in_hbm(jnp.asarray(prototype())),
    )
    dedispersed, bandpass = pl.pallas_call(
        tail,
        out_shape=(
            jax.ShapeDtypeStruct((2, 2 * TIME * 2, 128), BF16),
            jax.ShapeDtypeStruct((2, CHANNELS), F32),
        ),
        in_specs=[vmem] * 7,
        out_specs=(hbm, hbm),
        scratch_shapes=[
            pltpu.VMEM((2, 512, SPAN), BF16),
            pltpu.VMEM((2, 88 + SPAN, 512), F32),
            *[pltpu.VMEM((SPAN + 32, 512), BF16) for _ in range(2)],
            *[pltpu.VMEM((SPAN + 16, 512), BF16) for _ in range(2)],
            *[pltpu.VMEM((NBLOCK, 32, 512), BF16) for _ in range(2)],
            pltpu.VMEM((2, 2 * TIME * 2, 128), BF16),
            pltpu.VMEM((2, CHANNELS), F32),
            dma((3,)),
        ],
        compiler_params=pltpu.CompilerParams(**params),
        name="synthesis",
    )(
        beams.reshape(PARTS, 1024, SPAN),
        tables,
        dft,
        proto,
        product0,
        last0,
        power0,
    )
    dedispersed = dedispersed.reshape(2, 512, 2, 128).transpose(0, 2, 1, 3).reshape(2, 2, TIME * CHANNELS)
    return dedispersed, bandpass


def solution(mesh):
    return jax.shard_map(
        on_device,
        mesh=mesh,
        in_specs=(
            P(None, ("stn", "chan"), None, None),
            P(None, ("stn", "chan"), None, None),
            P(("stn", "chan"), None),
            P(("stn", "chan")),
        ),
        out_specs=(P(None, ("stn", "chan"), None), P(("stn", "chan"), None)),
        check_vma=False,
    )
```

```python
import math
import random

import jax
import jax.numpy as jnp
import numpy as np
from jax import lax
from jax.experimental import pallas as pl
from jax.experimental.pallas import tpu as pltpu
from jax.sharding import PartitionSpec as P

CHANNELS = 256
BEAMS = 256
INPUTS = 1024
TIME = 256
TAPS = 12
CHIRP = 1024
DMS = 16
NBLOCK = CHIRP // CHANNELS + 1
DEVICES = 128
CHAN_AXIS = 16
PARTS = 2
SPAN = TIME // PARTS
MESH = pl.DeviceIdType.MESH
BF16 = jnp.bfloat16
F32 = jnp.float32


def dft_rows():
    order = np.arange(CHANNELS)
    angle = 2.0 * math.pi / CHANNELS * (order[:, None] * order[None, :] % CHANNELS)
    cosine = np.cos(angle) / math.sqrt(CHANNELS)
    sine = np.sin(angle) / math.sqrt(CHANNELS)
    return np.block([[cosine, sine], [-sine, cosine]]).astype(np.float32)


def prototype():
    counter = np.arange(TAPS * CHANNELS, dtype=np.float64)
    offset = (counter + 0.5) / CHANNELS - TAPS / 2.0
    window = 0.54 + 0.46 * np.cos(math.pi * offset / (TAPS / 2.0))
    taps = (np.sinc(offset) * window).reshape(TAPS, CHANNELS)
    return np.concatenate([taps, taps], axis=1).astype(np.float32)


def chirp_rows():
    dms = np.arange(DMS, dtype=np.int64)[:, None, None]
    lag = np.arange(NBLOCK)[None, :, None] * CHANNELS + CHANNELS - 1 - np.arange(2 * CHANNELS)[None, None, :]
    valid = (lag >= 0) & (lag < CHIRP)
    lag = np.clip(lag, 0, CHIRP - 1)
    angle = math.pi * ((dms + 1) * lag * lag % (2 * DMS * CHIRP)) / (DMS * CHIRP)
    real = np.where(valid, np.cos(angle), 0.0) / math.sqrt(CHIRP)
    imag = np.where(valid, np.sin(angle), 0.0) / math.sqrt(CHIRP)
    rows = np.concatenate([real, imag, np.zeros((DMS, 6, 2 * CHANNELS))], axis=1)
    return rows.astype(np.float32)


def iota(axis, shape=(256, 256)):
    return lax.broadcasted_iota(jnp.int32, shape, axis)


def ones_where(condition):
    return jnp.where(condition, 1.0, 0.0).astype(BF16)


def dot(a, b):
    return jnp.dot(a, b, preferred_element_type=F32)


def exchange_order():
    left = [(dz, dy, dx) for dz in range(4) for dy in range(4) for dx in range(4)]
    random.Random(7).shuffle(left)
    hops, ordered = [0, 0, 0], []
    while left:
        def uneven(step):
            return sum((done + min(d, 4 - d) - len(ordered) - 1) ** 2 for done, d in zip(hops, step))

        best = min(left, key=uneven)
        left.remove(best)
        ordered.append(best)
        hops = [done + min(d, 4 - d) for done, d in zip(hops, best)]
    return ordered


def body(
    volt, wgt, flags, dm, chirps, dft, proto, recv2, tables, dftv, protov, product0, last0, power0,
    vin, give, send, recv, win, chv, flagv, dmv, beams, give2, send2, keep, ordered, padded, even, odd, acc,
    load_sem, plane_sem, given, given2, sent, sent2, sibling_sem, sibling_sem2, recv_sem, recv_sem2, pack_sem, packs_sent, relays_sent, *stages,
):
    x = lax.rem(lax.axis_index("chan"), 4)
    y = lax.axis_index("chan") // 4
    z = lax.axis_index("stn") // 2
    core = lax.rem(lax.axis_index("stn"), 2)
    chip = z * CHAN_AXIS + lax.axis_index("chan")
    sibling = (z * 2 + 1 - core, lax.axis_index("chan"))

    turn = 1 + 2 * core
    zs = [lax.rem(z + dz * turn, 4) for dz in range(4)]
    xs = [lax.rem(x + dx * turn, 4) for dx in range(4)]
    ys = [lax.rem(y + dy * turn, 4) * 4 for dy in range(4)]

    flag_load = pltpu.make_async_copy(flags, flagv, load_sem.at[0])
    flag_load.start()
    volt_loads = [
        pltpu.make_async_copy(volt.at[:, :, number], vin.at[:, :, number], load_sem.at[n])
        for n, number in ((1, 1 - core), (2, core))
    ]
    for load in volt_loads:
        load.start()

    barrier = pltpu.get_barrier_semaphore()
    line = [(zs[dz] * 2 + core, ys[0] + x) for dz in range(1, 4)]
    plane = [(z * 2 + core, ys[dy] + xs[dx]) for dy in range(4) for dx in range(4) if (dy, dx) != (0, 0)]
    greeted = [sibling] + line + plane
    for peer in greeted:
        pl.semaphore_signal(barrier, inc=1, device_id=peer, device_id_type=MESH)

    def hand_over(part, give, send, given, sibling_sem):
        pltpu.make_async_remote_copy(
            src_ref=give.at[part],
            dst_ref=send.at[part, :, :, :, core] if len(send.shape) == 8 else send.at[part, :, core],
            send_sem=given,
            recv_sem=sibling_sem.at[part],
            device_id=sibling,
            device_id_type=MESH,
        ).start()

    def exchange(part, send, landing, sibling_sem, sent, recv_sem):
        share = send.at[part, :, 1 - core]
        pltpu.make_async_copy(share, share, sibling_sem.at[part]).wait()
        pltpu.make_async_copy(send.at[part, chip], landing, recv_sem.at[part]).start()
        for dz, dy, dx in exchange_order():
            if (dz, dy, dx) != (0, 0, 0):
                chan = ys[dy] + xs[dx]
                pltpu.make_async_remote_copy(
                    src_ref=send.at[part, zs[dz] * CHAN_AXIS + chan],
                    dst_ref=landing,
                    send_sem=sent.at[part],
                    recv_sem=recv_sem.at[part],
                    device_id=(zs[dz] * 2 + core, chan),
                    device_id_type=MESH,
                ).start()

    by_z, by_x, by_y, by_xz, by_yz, by_xy, by_xyz = stages

    def place(steps):
        dz, dy, dx = steps
        return zs[dz % 4] * 2 + core, ys[dy % 4] + xs[dx % 4]

    def packs(part):
        near = (-1, 0, 1)
        listed = []
        for m in range(3):
            listed.append(((3, m, slice(0, 3)), by_z.at[part, m], (1, 0, 0), [(1, m - 1, d) for d in near]))
            listed.append(((m, slice(0, 3), 3), by_x.at[part, m], (0, 0, 1), [(m - 1, d, 1) for d in near]))
            listed.append(((m, 3, slice(0, 3)), by_y.at[part, m], (0, 1, 0), [(m - 1, 1, d) for d in near]))
            listed.append(((m, 3, 3), by_xy.at[part, m], (0, 1, 1), [(m - 1, 1, 1)]))
        listed.append(((3, slice(0, 3), 3), by_xz.at[part], (1, 0, 1), [(1, d, 1) for d in near]))
        listed.append(((3, 3, slice(0, 3)), by_yz.at[part], (1, 1, 0), [(1, 1, d) for d in near]))
        listed.append(((3, 3, 3), by_xyz.at[part], (1, 1, 1), [(1, 1, 1)]))
        return [(15 * part + n, *pack) for n, pack in enumerate(listed)]

    def send_packs(part):
        share = send.at[part, :, :, :, 1 - core]
        pltpu.make_async_copy(share, share, sibling_sem.at[part]).wait()
        for n, at, stage, steps, _ in packs(part):
            pltpu.make_async_remote_copy(
                src_ref=send.at[part, at[0], at[1], at[2]],
                dst_ref=stage,
                send_sem=packs_sent,
                recv_sem=pack_sem.at[n],
                device_id=place(steps),
                device_id_type=MESH,
            ).start()

    def send_direct(part):
        pltpu.make_async_copy(send.at[part, 1, 1, 1], recv.at[part, chip], recv_sem.at[part, 0]).start()
        for steps in exchange_order():
            if 2 not in steps and steps != (0, 0, 0):
                at = [(d + 1) % 4 for d in steps]
                pltpu.make_async_remote_copy(
                    src_ref=send.at[part, at[0], at[1], at[2]],
                    dst_ref=recv.at[part, chip],
                    send_sem=sent.at[part],
                    recv_sem=recv_sem.at[part, steps[0]],
                    device_id=place(steps),
                    device_id_type=MESH,
                ).start()

    def relay_packs(part):
        for n, _, stage, steps, onward in packs(part):
            pltpu.make_async_copy(stage, stage, pack_sem.at[n]).wait()
            dz, dy, dx = (-d % 4 for d in steps)
            origin = zs[dz] * CHAN_AXIS + ys[dy] + xs[dx]
            for m, further in enumerate(onward):
                pltpu.make_async_remote_copy(
                    src_ref=stage.at[m] if len(onward) > 1 else stage,
                    dst_ref=recv.at[part, origin],
                    send_sem=relays_sent,
                    recv_sem=recv_sem.at[part, (steps[0] + further[0]) % 4],
                    device_id=place(further),
                    device_id_type=MESH,
                ).start()

    flag_load.wait()
    row, col = iota(0), iota(1)
    hits = ones_where(iota(0, (256, 64)) == flagv[...])
    count = dot(hits, jnp.ones((64, 256), BF16))
    keep_rows = ones_where((count < 0.5) & (row % 16 == col % 16))
    keep[...] = dot(ones_where(iota(1, (16, 256)) // 16 == iota(0, (16, 256))), keep_rows)

    def sort_out(number):
        way = 1 + 2 * number
        there = (row // 128) * 8 + ((x + (row // 32 + 3) % 4 * way) % 4) * 2 + (row // 8) % 2
        swap = jnp.where((col // 16 == ((row // 16) % 2) * 8 + row % 8) & (col % 16 == there), 1.0, 0.0)
        for zz in range(4):
            for half in range(2):
                block = vin[:, zz, number, half].reshape(256, 256)
                mine = (swap * keep[pl.ds((zz * 2 + number) * 2 + half, 1), :]).astype(BF16)
                sorted_block = dot(mine, block).astype(BF16)
                for one in range(2):
                    mz = lax.rem((zz + 4 - z) * way + 1, 4)
                    my = lax.rem((half * 2 + one + 4 - y) * way + 1, 4)
                    yield mz, my, sorted_block[one * 128 : one * 128 + 128].reshape(4, 4, 8, 256)

    volt_loads[0].wait()
    for mz, my, block in sort_out(1 - core):
        for part in range(PARTS):
            give[part, mz, my] = block[..., part * SPAN : part * SPAN + SPAN]
    pl.semaphore_wait(barrier, len(greeted))
    for peer in line:
        pl.semaphore_signal(plane_sem, inc=1, device_id=peer, device_id_type=MESH)
    for part in range(PARTS):
        hand_over(part, give, send, given, sibling_sem)
    volt_loads[1].wait()
    for mz, my, block in sort_out(core):
        for part in range(PARTS):
            send[part, mz, my, :, core] = block[..., part * SPAN : part * SPAN + SPAN]
    loads = [
        pltpu.make_async_copy(source, target, load_sem.at[n])
        for n, (source, target) in enumerate(
            ((wgt, win), (dm, dmv), (chirps, chv), (dft, dftv), (proto, protov)), 3
        )
    ]
    for load in loads:
        load.start()
    pl.semaphore_wait(plane_sem, len(line))
    send_packs(0)
    send_direct(0)
    send_packs(1)
    relay_packs(0)
    send_direct(1)
    relay_packs(1)
    for load in loads:
        load.wait()

    def toeplitz(n, carry):
        b, block = n // NBLOCK, lax.rem(n, NBLOCK)
        for part in range(2):
            wide = jnp.broadcast_to(chv[dmv[b], pl.ds(part * NBLOCK + block, 1), :], (8, 2 * CHANNELS))
            eight = pltpu.roll(wide, CHANNELS + 1, 1, stride=1, stride_axis=0)
            for k in range(0, CHANNELS, 16):
                both = [pltpu.roll(eight, k + i, 1)[:, :CHANNELS] if k + i else eight[:, :CHANNELS] for i in (0, 8)]
                rows = pl.ds(pl.multiple_of(block * CHANNELS + k, 16), 16)
                tables[b, rows, part * CHANNELS : (part + 1) * CHANNELS] = jnp.concatenate(both, axis=0).astype(BF16)
        return carry

    lax.fori_loop(0, 2 * NBLOCK, toeplitz, 0)

    to_device = lax.rem(core + row // 128, 2) * 16 + (row // 8) % 16
    order = ones_where(
        (col // 128 == row % 2) & ((col // 64) % 2 == (row // 2) % 2) & (col % 64 == to_device * 2 + (row // 4) % 2)
    )
    for part in range(PARTS):
        for n, dz in enumerate((3, 0, 1, 2)):
            source = zs[-dz % 4]
            arrived = recv.at[part, pl.ds(pl.multiple_of(source * 16, 16), 16)]
            pltpu.make_async_copy(arrived, arrived, recv_sem.at[part, dz]).wait()
            for c in range(2):
                real, imag, weight_real, weight_imag = [], [], [], []
                for number in range(2):
                    chips = pl.ds(pl.multiple_of(source * 16, 16), 16)
                    inputs = pl.ds(pl.multiple_of((source * 2 + number) * 128, 128), 128)
                    real.append(recv[part, chips, number, c].reshape(128, SPAN))
                    imag.append(recv[part, chips, number, 2 + c].reshape(128, SPAN))
                    weight_real.append(win[0, c, :, inputs])
                    weight_imag.append(win[1, c, :, inputs])
                parts = jnp.concatenate(
                    [
                        jnp.concatenate(real + [-half for half in imag], axis=0),
                        jnp.concatenate(imag + real, axis=0),
                    ],
                    axis=1,
                )
                product = dot(jnp.concatenate(weight_real + weight_imag, axis=1), parts)
                if n == 0:
                    acc[c] = product
                elif n < 3:
                    acc[c] += product
                else:
                    beams[c] = (acc[c] + product).astype(BF16)
        for zz in range(4):
            rows = slice(zz * 64, zz * 64 + 64)
            block = jnp.concatenate([beams[c, rows, q * SPAN : q * SPAN + SPAN] for c in range(2) for q in range(2)], axis=0)
            block = dot(order, block).astype(BF16)
            send2[part, zz * 16 : zz * 16 + 16, core] = block[:128].reshape(16, 8, SPAN)
            give2[part, zz * 16 : zz * 16 + 16] = block[128:].reshape(16, 8, SPAN)
        hand_over(part, give2, send2, given2, sibling_sem2)
        if part == 1:
            arrived = recv2.at[0]
            pltpu.make_async_copy(arrived, arrived, recv_sem2.at[0]).wait()
            for b, power, last in front(
                lambda n: recv2[0, n * 16 : n * 16 + 16].reshape(256, SPAN), lambda b: 0.0, dftv, protov, ordered, padded
            ):
                power0[b : b + 1, :] = power
                last0[b] = last
        exchange(part, send2, recv2.at[part, chip], sibling_sem2, sent2, recv_sem2)

    for b in range(2):
        for n in range(4):
            lanes, series = synthesise(b, n, protov, padded)
            store_shifted(series, lanes, even, odd)
        product0[b] = chirped(stacked_shifts(even, odd), tables[b])

    for blocks, sem in ((give, given), (give2, given2)):
        pltpu.make_async_copy(blocks, blocks, sem).wait()
    for sem in (packs_sent, relays_sent):
        for part in range(PARTS):
            blocks = recv.at[part, 0:37]
            pltpu.make_async_copy(blocks, blocks, sem).wait()
    for part in range(PARTS):
        for blocks, sem in ((recv.at[part, 0:26], sent), (send2.at[part, 0:63], sent2)):
            pltpu.make_async_copy(blocks, blocks, sem.at[part]).wait()
    arrived = recv2.at[1]
    pltpu.make_async_copy(arrived, arrived, recv_sem2.at[1]).wait()


def front(chunk, before_first, dftv, protov, xs, padded):
    row, col = iota(0), iota(1)
    sort = ones_where(col == ((row % 32) // 2 * 2 + (row % 64) // 32) * 8 + (row // 64) * 2 + row % 2)
    spread = ones_where(iota(1, (SPAN, SPAN)) == (iota(0, (SPAN, SPAN)) % 8) * 16 + iota(0, (SPAN, SPAN)) // 8)
    for n in range(4):
        block = dot(sort, chunk(n)).astype(BF16)
        for k in range(4):
            xs[k // 2, (k % 2) * 256 + n * 64 : (k % 2) * 256 + n * 64 + 64, :] = block[k * 64 : k * 64 + 64]
    for b in range(2):
        turned = lax.dot_general(spread, xs[b], (((1,), (1,)), ((), ())), preferred_element_type=F32)
        power = jnp.sum(turned * turned, axis=0, keepdims=True)
        spectra = dot(turned.astype(BF16), dftv[...])
        last = spectra[SPAN - 88 :]
        first = iota(0, (88, 512)) % 8 == 0
        padded[b, 0:88, :] = jnp.where(first, before_first(b), pltpu.roll(last, 1, 0))
        padded[b, 88 : 88 + SPAN, :] = spectra
        yield b, power, pltpu.roll(last, 81, 0)


def synthesise(b, n, protov, padded):
    lanes = slice(n * 128, n * 128 + 128)
    series = protov[0:1, lanes] * padded[b, 88 : 88 + SPAN, lanes]
    for tap in range(1, TAPS):
        series = series + protov[tap : tap + 1, lanes] * padded[b, 88 - 8 * tap : 88 - 8 * tap + SPAN, lanes]
    return lanes, series


def store_shifted(series, lanes, even, odd):
    after = jnp.where(iota(0, (32, 128)) % 8 == 7, 0.0, pltpu.roll(series[:32], 31, 0))
    even[0:SPAN, lanes] = series.astype(BF16)
    even[SPAN : SPAN + 32, lanes] = after.astype(BF16)
    odd[0 : SPAN + 16, lanes] = jnp.concatenate([series[8:], after[:24]], axis=0).astype(BF16)


def stacked_shifts(even, odd):
    shifted = [even[0:SPAN], odd[0:SPAN], even[16 : 16 + SPAN], odd[16 : 16 + SPAN], even[32 : 32 + SPAN]]
    return [jnp.concatenate([block[:, p * 256 : p * 256 + 256] for block in shifted], axis=1) for p in range(2)]


def chirped(parts, table):
    product = dot(jnp.concatenate(parts, axis=0), table)
    rows = product.shape[0] // 2
    real = product[:rows, :256] + product[rows:, 256:]
    imag = product[rows:, :256] - product[:rows, 256:]
    return jnp.concatenate([real, imag], axis=1)


def tail(
    xv, tv, dftv, protov, product0, last0, power0, out, band,
    xs, padded, even0, even1, odd0, odd1, over0, over1, outv, bandv, out_sem,
):
    band_copy = pltpu.make_async_copy(bandv, band, out_sem.at[2])
    for b, power, _ in front(lambda n: xv[1, n * 256 : n * 256 + 256, :], lambda b: last0[b], dftv, protov, xs, padded):
        power = (power + power0[b : b + 1, :]) * (1.0 / TIME)
        bandv[b : b + 1, :] = power[:, :256] + power[:, 256:]
    band_copy.start()
    results = []
    for b, (even, odd, over) in enumerate(((even0, odd0, over0), (even1, odd1, over1))):
        for n in range(4):
            lanes, series = synthesise(b, n, protov, padded)
            store_shifted(series, lanes, even, odd)
            over_edge = jnp.where(iota(0, (32, 128)) % 8 == 7, pltpu.roll(series[:32], 7, 0), 0.0)
            for blk in range(NBLOCK):
                seen = [over_edge[: 8 * blk]] if blk else []
                unseen = [jnp.zeros((32 - 8 * blk, 128), F32)] if blk < 4 else []
                over[blk, :, lanes] = jnp.concatenate(unseen + seen, axis=0).astype(BF16)
        edges = [
            jnp.concatenate([over[blk, :, p * 256 : p * 256 + 256] for blk in range(NBLOCK)], axis=1) for p in range(2)
        ]
        parts = [jnp.concatenate(pair, axis=0) for pair in zip(stacked_shifts(even, odd), edges)]
        product = chirped(parts, tv[b])
        results.append(
            jnp.concatenate([product0[b, :96], product0[b, 96:] + product[SPAN:], product[:SPAN]], axis=0).astype(BF16)
        )
    row, col = iota(0), iota(1)
    final = ones_where(col == (row % 4) * 64 + ((row // 4) % 8) * 8 + row // 32)
    copies = []
    for h in range(2):
        for j in range(2):
            rows = slice(128 * h + 64 * j, 128 * h + 64 * j + 64)
            block = jnp.concatenate(
                [
                    jnp.concatenate([results[b][rows, half * 128 + q * 256 : half * 128 + q * 256 + 128] for q in range(2)], axis=1)
                    for half in range(2) for b in range(2)
                ],
                axis=0,
            )
            block = dot(final, block).astype(BF16)
            for q in range(2):
                for k in range(8):
                    start = 512 * h + 64 * k + 32 * j
                    outv[q, start : start + 32, :] = block[32 * k : 32 * k + 32, q * 128 : q * 128 + 128]
        done = pl.ds(512 * h, 512)
        copies.append(pltpu.make_async_copy(outv.at[:, done], out.at[:, done], out_sem.at[h]))
        copies[-1].start()
    for copy in copies + [band_copy]:
        copy.wait()


def in_hbm(array):
    return pltpu.with_memory_space_constraint(array, pltpu.HBM)


def on_device(voltages, weights, flags, dm_index):
    hbm = pl.BlockSpec(memory_space=pl.ANY)
    vmem = pl.BlockSpec(memory_space=pltpu.VMEM)
    dma = pltpu.SemaphoreType.DMA
    params = dict(vmem_limit_bytes=24 * 1024 * 1024)
    beams, tables, dft, proto, product0, last0, power0 = pl.pallas_call(
        body,
        out_shape=(
            jax.ShapeDtypeStruct((PARTS, 64, 2, 8, SPAN), BF16),
            jax.ShapeDtypeStruct((2, NBLOCK * CHANNELS, 512), BF16),
            jax.ShapeDtypeStruct((512, 512), BF16),
            jax.ShapeDtypeStruct((TAPS, 512), F32),
            jax.ShapeDtypeStruct((2, SPAN, 512), F32),
            jax.ShapeDtypeStruct((2, 88, 512), F32),
            jax.ShapeDtypeStruct((2, 512), F32),
        ),
        in_specs=[hbm] * 7,
        out_specs=(vmem,) * 7,
        scratch_shapes=[
            pltpu.VMEM((16, 4, 2, 2, 16, 256), BF16),
            pltpu.VMEM((PARTS, 4, 4, 4, 4, 8, SPAN), BF16),
            pltpu.VMEM((PARTS, 4, 4, 4, 2, 4, 8, SPAN), BF16),
            pltpu.VMEM((PARTS, 64, 2, 4, 8, SPAN), BF16),
            pltpu.VMEM((2, 2, 256, 1024), BF16),
            pltpu.VMEM((DMS, 16, 512), F32),
            pltpu.VMEM((1, 64), jnp.int32),
            pltpu.SMEM((2,), jnp.int32),
            pltpu.VMEM((2, 256, 2 * SPAN), BF16),
            pltpu.VMEM((PARTS, 64, 8, SPAN), BF16),
            pltpu.VMEM((PARTS, 64, 2, 8, SPAN), BF16),
            pltpu.VMEM((16, 256), F32),
            pltpu.VMEM((2, 512, SPAN), BF16),
            pltpu.VMEM((2, 88 + SPAN, 512), F32),
            pltpu.VMEM((SPAN + 32, 512), BF16),
            pltpu.VMEM((SPAN + 16, 512), BF16),
            pltpu.VMEM((2, 256, 2 * SPAN), F32),
            dma((8,)),
            pltpu.SemaphoreType.REGULAR,
            dma,
            dma,
            *[dma((PARTS,)) for _ in range(4)],
            dma((PARTS, 4)),
            dma((PARTS,)),
            dma((30,)),
            dma,
            dma,
            *[
                pltpu.VMEM((PARTS,) + shape + (2, 4, 8, SPAN), BF16)
                for shape in [(3, 3), (3, 3), (3, 3), (3,), (3,), (3,), ()]
            ],
        ],
        compiler_params=pltpu.CompilerParams(collective_id=0, has_side_effects=True, **params),
        name="beamform",
    )(
        in_hbm(voltages.reshape(16, 4, 2, 2, 16, TIME)),
        in_hbm(weights),
        in_hbm(flags),
        in_hbm(dm_index),
        in_hbm(jnp.asarray(chirp_rows()).astype(BF16).astype(F32)),
        in_hbm(jnp.asarray(dft_rows()).astype(BF16)),
        in_hbm(jnp.asarray(prototype())),
    )
    dedispersed, bandpass = pl.pallas_call(
        tail,
        out_shape=(
            jax.ShapeDtypeStruct((2, 2 * TIME * 2, 128), BF16),
            jax.ShapeDtypeStruct((2, CHANNELS), F32),
        ),
        in_specs=[vmem] * 7,
        out_specs=(hbm, hbm),
        scratch_shapes=[
            pltpu.VMEM((2, 512, SPAN), BF16),
            pltpu.VMEM((2, 88 + SPAN, 512), F32),
            *[pltpu.VMEM((SPAN + 32, 512), BF16) for _ in range(2)],
            *[pltpu.VMEM((SPAN + 16, 512), BF16) for _ in range(2)],
            *[pltpu.VMEM((NBLOCK, 32, 512), BF16) for _ in range(2)],
            pltpu.VMEM((2, 2 * TIME * 2, 128), BF16),
            pltpu.VMEM((2, CHANNELS), F32),
            dma((3,)),
        ],
        compiler_params=pltpu.CompilerParams(**params),
        name="synthesis",
    )(
        beams.reshape(PARTS, 1024, SPAN),
        tables,
        dft,
        proto,
        product0,
        last0,
        power0,
    )
    dedispersed = dedispersed.reshape(2, 512, 2, 128).transpose(0, 2, 1, 3).reshape(2, 2, TIME * CHANNELS)
    return dedispersed, bandpass


def solution(mesh):
    return jax.shard_map(
        on_device,
        mesh=mesh,
        in_specs=(
            P(None, ("stn", "chan"), None, None),
            P(None, ("stn", "chan"), None, None),
            P(("stn", "chan"), None),
            P(("stn", "chan")),
        ),
        out_specs=(P(None, ("stn", "chan"), None), P(("stn", "chan"), None)),
        check_vma=False,
    )
```

```python
import math
import random

import jax
import jax.numpy as jnp
import numpy as np
from jax import lax
from jax.experimental import pallas as pl
from jax.experimental.pallas import tpu as pltpu
from jax.sharding import PartitionSpec as P

CHANNELS = 256
BEAMS = 256
INPUTS = 1024
TIME = 256
TAPS = 12
CHIRP = 1024
DMS = 16
NBLOCK = CHIRP // CHANNELS + 1
DEVICES = 128
CHAN_AXIS = 16
PARTS = 2
SPAN = TIME // PARTS
MESH = pl.DeviceIdType.MESH
BF16 = jnp.bfloat16
F32 = jnp.float32


def dft_rows():
    order = np.arange(CHANNELS)
    angle = 2.0 * math.pi / CHANNELS * (order[:, None] * order[None, :] % CHANNELS)
    cosine = np.cos(angle) / math.sqrt(CHANNELS)
    sine = np.sin(angle) / math.sqrt(CHANNELS)
    return np.block([[cosine, sine], [-sine, cosine]]).astype(np.float32)


def prototype():
    counter = np.arange(TAPS * CHANNELS, dtype=np.float64)
    offset = (counter + 0.5) / CHANNELS - TAPS / 2.0
    window = 0.54 + 0.46 * np.cos(math.pi * offset / (TAPS / 2.0))
    taps = (np.sinc(offset) * window).reshape(TAPS, CHANNELS)
    return np.concatenate([taps, taps], axis=1).astype(np.float32)


def chirp_rows():
    dms = np.arange(DMS, dtype=np.int64)[:, None, None]
    lag = np.arange(NBLOCK)[None, :, None] * CHANNELS + CHANNELS - 1 - np.arange(2 * CHANNELS)[None, None, :]
    valid = (lag >= 0) & (lag < CHIRP)
    lag = np.clip(lag, 0, CHIRP - 1)
    angle = math.pi * ((dms + 1) * lag * lag % (2 * DMS * CHIRP)) / (DMS * CHIRP)
    real = np.where(valid, np.cos(angle), 0.0) / math.sqrt(CHIRP)
    imag = np.where(valid, np.sin(angle), 0.0) / math.sqrt(CHIRP)
    rows = np.concatenate([real, imag, np.zeros((DMS, 6, 2 * CHANNELS))], axis=1)
    return rows.astype(np.float32)


def iota(axis, shape=(256, 256)):
    return lax.broadcasted_iota(jnp.int32, shape, axis)


def ones_where(condition):
    return jnp.where(condition, 1.0, 0.0).astype(BF16)


def dot(a, b):
    return jnp.dot(a, b, preferred_element_type=F32)


def exchange_order():
    left = [(dz, dy, dx) for dz in range(4) for dy in range(4) for dx in range(4)]
    random.Random(7).shuffle(left)
    hops, ordered = [0, 0, 0], []
    while left:
        def uneven(step):
            return sum((done + min(d, 4 - d) - len(ordered) - 1) ** 2 for done, d in zip(hops, step))

        best = min(left, key=uneven)
        left.remove(best)
        ordered.append(best)
        hops = [done + min(d, 4 - d) for done, d in zip(hops, best)]
    return ordered


def body(
    volt, wgt, flags, dm, chirps, dft, proto, recv2, tables, dftv, protov, product0, last0, power0,
    vin, give, send, recv, win, chv, flagv, dmv, beams, give2, send2, keep, ordered, padded, even, odd, acc,
    load_sem, plane_sem, given, given2, sent, sent2, sibling_sem, sibling_sem2, recv_sem, recv_sem2, pack_sem, packs_sent, relays_sent, *stages,
):
    x = lax.rem(lax.axis_index("chan"), 4)
    y = lax.axis_index("chan") // 4
    z = lax.axis_index("stn") // 2
    core = lax.rem(lax.axis_index("stn"), 2)
    chip = z * CHAN_AXIS + lax.axis_index("chan")
    sibling = (z * 2 + 1 - core, lax.axis_index("chan"))

    turn = 1 + 2 * core
    zs = [lax.rem(z + dz * turn, 4) for dz in range(4)]
    xs = [lax.rem(x + dx * turn, 4) for dx in range(4)]
    ys = [lax.rem(y + dy * turn, 4) * 4 for dy in range(4)]

    flag_load = pltpu.make_async_copy(flags, flagv, load_sem.at[0])
    flag_load.start()
    volt_loads = [
        pltpu.make_async_copy(volt.at[:, :, number], vin.at[:, :, number], load_sem.at[n])
        for n, number in ((1, 1 - core), (2, core))
    ]
    for load in volt_loads:
        load.start()

    barrier = pltpu.get_barrier_semaphore()
    line = [(zs[dz] * 2 + core, ys[0] + x) for dz in range(1, 4)]
    plane = [(z * 2 + core, ys[dy] + xs[dx]) for dy in range(4) for dx in range(4) if (dy, dx) != (0, 0)]
    greeted = [sibling] + line + plane
    for peer in greeted:
        pl.semaphore_signal(barrier, inc=1, device_id=peer, device_id_type=MESH)

    def hand_over(part, give, send, given, sibling_sem):
        pltpu.make_async_remote_copy(
            src_ref=give.at[part],
            dst_ref=send.at[part, :, :, :, core] if len(send.shape) == 8 else send.at[part, :, core],
            send_sem=given,
            recv_sem=sibling_sem.at[part],
            device_id=sibling,
            device_id_type=MESH,
        ).start()

    def exchange(part, send, landing, sibling_sem, sent, recv_sem):
        share = send.at[part, :, 1 - core]
        pltpu.make_async_copy(share, share, sibling_sem.at[part]).wait()
        pltpu.make_async_copy(send.at[part, chip], landing, recv_sem.at[part]).start()
        for dz, dy, dx in exchange_order():
            if (dz, dy, dx) != (0, 0, 0):
                chan = ys[dy] + xs[dx]
                pltpu.make_async_remote_copy(
                    src_ref=send.at[part, zs[dz] * CHAN_AXIS + chan],
                    dst_ref=landing,
                    send_sem=sent.at[part],
                    recv_sem=recv_sem.at[part],
                    device_id=(zs[dz] * 2 + core, chan),
                    device_id_type=MESH,
                ).start()

    by_z, by_x, by_y, by_xz, by_yz, by_xy, by_xyz = stages

    def place(steps):
        dz, dy, dx = steps
        return zs[dz % 4] * 2 + core, ys[dy % 4] + xs[dx % 4]

    def packs(part):
        near = (-1, 0, 1)
        listed = []
        for m in range(3):
            listed.append(((3, m, slice(0, 3)), by_z.at[part, m], (1, 0, 0), [(1, m - 1, d) for d in near]))
            listed.append(((m, slice(0, 3), 3), by_x.at[part, m], (0, 0, 1), [(m - 1, d, 1) for d in near]))
            listed.append(((m, 3, slice(0, 3)), by_y.at[part, m], (0, 1, 0), [(m - 1, 1, d) for d in near]))
            listed.append(((m, 3, 3), by_xy.at[part, m], (0, 1, 1), [(m - 1, 1, 1)]))
        listed.append(((3, slice(0, 3), 3), by_xz.at[part], (1, 0, 1), [(1, d, 1) for d in near]))
        listed.append(((3, 3, slice(0, 3)), by_yz.at[part], (1, 1, 0), [(1, 1, d) for d in near]))
        listed.append(((3, 3, 3), by_xyz.at[part], (1, 1, 1), [(1, 1, 1)]))
        return [(15 * part + n, *pack) for n, pack in enumerate(listed)]

    def send_packs(part):
        share = send.at[part, :, :, :, 1 - core]
        pltpu.make_async_copy(share, share, sibling_sem.at[part]).wait()
        for n, at, stage, steps, _ in packs(part):
            pltpu.make_async_remote_copy(
                src_ref=send.at[part, at[0], at[1], at[2]],
                dst_ref=stage,
                send_sem=packs_sent,
                recv_sem=pack_sem.at[n],
                device_id=place(steps),
                device_id_type=MESH,
            ).start()

    def send_direct(part):
        pltpu.make_async_copy(send.at[part, 1, 1, 1], recv.at[part, chip], recv_sem.at[part, 0]).start()
        for steps in exchange_order():
            if 2 not in steps and steps != (0, 0, 0):
                at = [(d + 1) % 4 for d in steps]
                pltpu.make_async_remote_copy(
                    src_ref=send.at[part, at[0], at[1], at[2]],
                    dst_ref=recv.at[part, chip],
                    send_sem=sent.at[part],
                    recv_sem=recv_sem.at[part, steps[0]],
                    device_id=place(steps),
                    device_id_type=MESH,
                ).start()

    def relay_packs(part):
        for n, _, stage, steps, onward in packs(part):
            pltpu.make_async_copy(stage, stage, pack_sem.at[n]).wait()
            dz, dy, dx = (-d % 4 for d in steps)
            origin = zs[dz] * CHAN_AXIS + ys[dy] + xs[dx]
            for m, further in enumerate(onward):
                pltpu.make_async_remote_copy(
                    src_ref=stage.at[m] if len(onward) > 1 else stage,
                    dst_ref=recv.at[part, origin],
                    send_sem=relays_sent,
                    recv_sem=recv_sem.at[part, (steps[0] + further[0]) % 4],
                    device_id=place(further),
                    device_id_type=MESH,
                ).start()

    flag_load.wait()
    row, col = iota(0), iota(1)
    hits = ones_where(iota(0, (256, 64)) == flagv[...])
    count = dot(hits, jnp.ones((64, 256), BF16))
    keep_rows = ones_where((count < 0.5) & (row % 16 == col % 16))
    keep[...] = dot(ones_where(iota(1, (16, 256)) // 16 == iota(0, (16, 256))), keep_rows)

    def sort_out(number):
        way = 1 + 2 * number
        there = (row // 128) * 8 + ((x + (row // 32 + 3) % 4 * way) % 4) * 2 + (row // 8) % 2
        swap = jnp.where((col // 16 == ((row // 16) % 2) * 8 + row % 8) & (col % 16 == there), 1.0, 0.0)
        for zz in range(4):
            for half in range(2):
                block = vin[:, zz, number, half].reshape(256, 256)
                mine = (swap * keep[pl.ds((zz * 2 + number) * 2 + half, 1), :]).astype(BF16)
                sorted_block = dot(mine, block).astype(BF16)
                for one in range(2):
                    mz = lax.rem((zz + 4 - z) * way + 1, 4)
                    my = lax.rem((half * 2 + one + 4 - y) * way + 1, 4)
                    yield mz, my, sorted_block[one * 128 : one * 128 + 128].reshape(4, 4, 8, 256)

    volt_loads[0].wait()
    for mz, my, block in sort_out(1 - core):
        for part in range(PARTS):
            give[part, mz, my] = block[..., part * SPAN : part * SPAN + SPAN]
    pl.semaphore_wait(barrier, len(greeted))
    for peer in line:
        pl.semaphore_signal(plane_sem, inc=1, device_id=peer, device_id_type=MESH)
    for part in range(PARTS):
        hand_over(part, give, send, given, sibling_sem)
    volt_loads[1].wait()
    for mz, my, block in sort_out(core):
        for part in range(PARTS):
            send[part, mz, my, :, core] = block[..., part * SPAN : part * SPAN + SPAN]
    loads = [
        pltpu.make_async_copy(source, target, load_sem.at[n])
        for n, (source, target) in enumerate(
            ((wgt, win), (dm, dmv), (chirps, chv), (dft, dftv), (proto, protov)), 3
        )
    ]
    for load in loads:
        load.start()
    pl.semaphore_wait(plane_sem, len(line))
    send_packs(0)
    send_direct(0)
    relay_packs(0)
    send_packs(1)
    send_direct(1)
    for load in loads:
        load.wait()

    def toeplitz(n, carry):
        b, block = n // NBLOCK, lax.rem(n, NBLOCK)
        for part in range(2):
            wide = jnp.broadcast_to(chv[dmv[b], pl.ds(part * NBLOCK + block, 1), :], (8, 2 * CHANNELS))
            eight = pltpu.roll(wide, CHANNELS + 1, 1, stride=1, stride_axis=0)
            for k in range(0, CHANNELS, 16):
                both = [pltpu.roll(eight, k + i, 1)[:, :CHANNELS] if k + i else eight[:, :CHANNELS] for i in (0, 8)]
                rows = pl.ds(pl.multiple_of(block * CHANNELS + k, 16), 16)
                tables[b, rows, part * CHANNELS : (part + 1) * CHANNELS] = jnp.concatenate(both, axis=0).astype(BF16)
        return carry

    lax.fori_loop(0, 2 * NBLOCK, toeplitz, 0)

    to_device = lax.rem(core + row // 128, 2) * 16 + (row // 8) % 16
    order = ones_where(
        (col // 128 == row % 2) & ((col // 64) % 2 == (row // 2) % 2) & (col % 64 == to_device * 2 + (row // 4) % 2)
    )
    for part in range(PARTS):
        for n, dz in enumerate((3, 0, 1, 2)):
            source = zs[-dz % 4]
            arrived = recv.at[part, pl.ds(pl.multiple_of(source * 16, 16), 16)]
            pltpu.make_async_copy(arrived, arrived, recv_sem.at[part, dz]).wait()
            for c in range(2):
                real, imag, weight_real, weight_imag = [], [], [], []
                for number in range(2):
                    chips = pl.ds(pl.multiple_of(source * 16, 16), 16)
                    inputs = pl.ds(pl.multiple_of((source * 2 + number) * 128, 128), 128)
                    real.append(recv[part, chips, number, c].reshape(128, SPAN))
                    imag.append(recv[part, chips, number, 2 + c].reshape(128, SPAN))
                    weight_real.append(win[0, c, :, inputs])
                    weight_imag.append(win[1, c, :, inputs])
                parts = jnp.concatenate(
                    [
                        jnp.concatenate(real + [-half for half in imag], axis=0),
                        jnp.concatenate(imag + real, axis=0),
                    ],
                    axis=1,
                )
                product = dot(jnp.concatenate(weight_real + weight_imag, axis=1), parts)
                if n == 0:
                    acc[c] = product
                elif n < 3:
                    acc[c] += product
                else:
                    beams[c] = (acc[c] + product).astype(BF16)
        for zz in range(4):
            rows = slice(zz * 64, zz * 64 + 64)
            block = jnp.concatenate([beams[c, rows, q * SPAN : q * SPAN + SPAN] for c in range(2) for q in range(2)], axis=0)
            block = dot(order, block).astype(BF16)
            send2[part, zz * 16 : zz * 16 + 16, core] = block[:128].reshape(16, 8, SPAN)
            give2[part, zz * 16 : zz * 16 + 16] = block[128:].reshape(16, 8, SPAN)
        hand_over(part, give2, send2, given2, sibling_sem2)
        if part == 0:
            relay_packs(1)
        exchange(part, send2, recv2.at[part, chip], sibling_sem2, sent2, recv_sem2)

    arrived = recv2.at[0]
    pltpu.make_async_copy(arrived, arrived, recv_sem2.at[0]).wait()
    for b, power, last in front(
        lambda n: recv2[0, n * 16 : n * 16 + 16].reshape(256, SPAN), lambda b: 0.0, dftv, protov, ordered, padded
    ):
        power0[b : b + 1, :] = power
        last0[b] = last
    for b in range(2):
        for n in range(4):
            lanes, series = synthesise(b, n, protov, padded)
            store_shifted(series, lanes, even, odd)
        product0[b] = chirped(stacked_shifts(even, odd), tables[b])

    for blocks, sem in ((give, given), (give2, given2)):
        pltpu.make_async_copy(blocks, blocks, sem).wait()
    for sem in (packs_sent, relays_sent):
        for part in range(PARTS):
            blocks = recv.at[part, 0:37]
            pltpu.make_async_copy(blocks, blocks, sem).wait()
    for part in range(PARTS):
        for blocks, sem in ((recv.at[part, 0:26], sent), (send2.at[part, 0:63], sent2)):
            pltpu.make_async_copy(blocks, blocks, sem.at[part]).wait()
    arrived = recv2.at[1]
    pltpu.make_async_copy(arrived, arrived, recv_sem2.at[1]).wait()


def front(chunk, before_first, dftv, protov, xs, padded):
    row, col = iota(0), iota(1)
    sort = ones_where(col == ((row % 32) // 2 * 2 + (row % 64) // 32) * 8 + (row // 64) * 2 + row % 2)
    spread = ones_where(iota(1, (SPAN, SPAN)) == (iota(0, (SPAN, SPAN)) % 8) * 16 + iota(0, (SPAN, SPAN)) // 8)
    for n in range(4):
        block = dot(sort, chunk(n)).astype(BF16)
        for k in range(4):
            xs[k // 2, (k % 2) * 256 + n * 64 : (k % 2) * 256 + n * 64 + 64, :] = block[k * 64 : k * 64 + 64]
    for b in range(2):
        turned = lax.dot_general(spread, xs[b], (((1,), (1,)), ((), ())), preferred_element_type=F32)
        power = jnp.sum(turned * turned, axis=0, keepdims=True)
        spectra = dot(turned.astype(BF16), dftv[...])
        last = spectra[SPAN - 88 :]
        first = iota(0, (88, 512)) % 8 == 0
        padded[b, 0:88, :] = jnp.where(first, before_first(b), pltpu.roll(last, 1, 0))
        padded[b, 88 : 88 + SPAN, :] = spectra
        yield b, power, pltpu.roll(last, 81, 0)


def synthesise(b, n, protov, padded):
    lanes = slice(n * 128, n * 128 + 128)
    series = protov[0:1, lanes] * padded[b, 88 : 88 + SPAN, lanes]
    for tap in range(1, TAPS):
        series = series + protov[tap : tap + 1, lanes] * padded[b, 88 - 8 * tap : 88 - 8 * tap + SPAN, lanes]
    return lanes, series


def store_shifted(series, lanes, even, odd):
    after = jnp.where(iota(0, (32, 128)) % 8 == 7, 0.0, pltpu.roll(series[:32], 31, 0))
    even[0:SPAN, lanes] = series.astype(BF16)
    even[SPAN : SPAN + 32, lanes] = after.astype(BF16)
    odd[0 : SPAN + 16, lanes] = jnp.concatenate([series[8:], after[:24]], axis=0).astype(BF16)


def stacked_shifts(even, odd):
    shifted = [even[0:SPAN], odd[0:SPAN], even[16 : 16 + SPAN], odd[16 : 16 + SPAN], even[32 : 32 + SPAN]]
    return [jnp.concatenate([block[:, p * 256 : p * 256 + 256] for block in shifted], axis=1) for p in range(2)]


def chirped(parts, table):
    product = dot(jnp.concatenate(parts, axis=0), table)
    rows = product.shape[0] // 2
    real = product[:rows, :256] + product[rows:, 256:]
    imag = product[rows:, :256] - product[:rows, 256:]
    return jnp.concatenate([real, imag], axis=1)


def tail(
    xv, tv, dftv, protov, product0, last0, power0, out, band,
    xs, padded, even0, even1, odd0, odd1, over0, over1, outv, bandv, out_sem,
):
    band_copy = pltpu.make_async_copy(bandv, band, out_sem.at[2])
    for b, power, _ in front(lambda n: xv[1, n * 256 : n * 256 + 256, :], lambda b: last0[b], dftv, protov, xs, padded):
        power = (power + power0[b : b + 1, :]) * (1.0 / TIME)
        bandv[b : b + 1, :] = power[:, :256] + power[:, 256:]
    band_copy.start()
    results = []
    for b, (even, odd, over) in enumerate(((even0, odd0, over0), (even1, odd1, over1))):
        for n in range(4):
            lanes, series = synthesise(b, n, protov, padded)
            store_shifted(series, lanes, even, odd)
            over_edge = jnp.where(iota(0, (32, 128)) % 8 == 7, pltpu.roll(series[:32], 7, 0), 0.0)
            for blk in range(NBLOCK):
                seen = [over_edge[: 8 * blk]] if blk else []
                unseen = [jnp.zeros((32 - 8 * blk, 128), F32)] if blk < 4 else []
                over[blk, :, lanes] = jnp.concatenate(unseen + seen, axis=0).astype(BF16)
        edges = [
            jnp.concatenate([over[blk, :, p * 256 : p * 256 + 256] for blk in range(NBLOCK)], axis=1) for p in range(2)
        ]
        parts = [jnp.concatenate(pair, axis=0) for pair in zip(stacked_shifts(even, odd), edges)]
        product = chirped(parts, tv[b])
        results.append(
            jnp.concatenate([product0[b, :96], product0[b, 96:] + product[SPAN:], product[:SPAN]], axis=0).astype(BF16)
        )
    row, col = iota(0), iota(1)
    final = ones_where(col == (row % 4) * 64 + ((row // 4) % 8) * 8 + row // 32)
    copies = []
    for h in range(2):
        for j in range(2):
            rows = slice(128 * h + 64 * j, 128 * h + 64 * j + 64)
            block = jnp.concatenate(
                [
                    jnp.concatenate([results[b][rows, half * 128 + q * 256 : half * 128 + q * 256 + 128] for q in range(2)], axis=1)
                    for half in range(2) for b in range(2)
                ],
                axis=0,
            )
            block = dot(final, block).astype(BF16)
            for q in range(2):
                for k in range(8):
                    start = 512 * h + 64 * k + 32 * j
                    outv[q, start : start + 32, :] = block[32 * k : 32 * k + 32, q * 128 : q * 128 + 128]
        done = pl.ds(512 * h, 512)
        copies.append(pltpu.make_async_copy(outv.at[:, done], out.at[:, done], out_sem.at[h]))
        copies[-1].start()
    for copy in copies + [band_copy]:
        copy.wait()


def in_hbm(array):
    return pltpu.with_memory_space_constraint(array, pltpu.HBM)


def on_device(voltages, weights, flags, dm_index):
    hbm = pl.BlockSpec(memory_space=pl.ANY)
    vmem = pl.BlockSpec(memory_space=pltpu.VMEM)
    dma = pltpu.SemaphoreType.DMA
    params = dict(vmem_limit_bytes=24 * 1024 * 1024)
    beams, tables, dft, proto, product0, last0, power0 = pl.pallas_call(
        body,
        out_shape=(
            jax.ShapeDtypeStruct((PARTS, 64, 2, 8, SPAN), BF16),
            jax.ShapeDtypeStruct((2, NBLOCK * CHANNELS, 512), BF16),
            jax.ShapeDtypeStruct((512, 512), BF16),
            jax.ShapeDtypeStruct((TAPS, 512), F32),
            jax.ShapeDtypeStruct((2, SPAN, 512), F32),
            jax.ShapeDtypeStruct((2, 88, 512), F32),
            jax.ShapeDtypeStruct((2, 512), F32),
        ),
        in_specs=[hbm] * 7,
        out_specs=(vmem,) * 7,
        scratch_shapes=[
            pltpu.VMEM((16, 4, 2, 2, 16, 256), BF16),
            pltpu.VMEM((PARTS, 4, 4, 4, 4, 8, SPAN), BF16),
            pltpu.VMEM((PARTS, 4, 4, 4, 2, 4, 8, SPAN), BF16),
            pltpu.VMEM((PARTS, 64, 2, 4, 8, SPAN), BF16),
            pltpu.VMEM((2, 2, 256, 1024), BF16),
            pltpu.VMEM((DMS, 16, 512), F32),
            pltpu.VMEM((1, 64), jnp.int32),
            pltpu.SMEM((2,), jnp.int32),
            pltpu.VMEM((2, 256, 2 * SPAN), BF16),
            pltpu.VMEM((PARTS, 64, 8, SPAN), BF16),
            pltpu.VMEM((PARTS, 64, 2, 8, SPAN), BF16),
            pltpu.VMEM((16, 256), F32),
            pltpu.VMEM((2, 512, SPAN), BF16),
            pltpu.VMEM((2, 88 + SPAN, 512), F32),
            pltpu.VMEM((SPAN + 32, 512), BF16),
            pltpu.VMEM((SPAN + 16, 512), BF16),
            pltpu.VMEM((2, 256, 2 * SPAN), F32),
            dma((8,)),
            pltpu.SemaphoreType.REGULAR,
            dma,
            dma,
            *[dma((PARTS,)) for _ in range(4)],
            dma((PARTS, 4)),
            dma((PARTS,)),
            dma((30,)),
            dma,
            dma,
            *[
                pltpu.VMEM((PARTS,) + shape + (2, 4, 8, SPAN), BF16)
                for shape in [(3, 3), (3, 3), (3, 3), (3,), (3,), (3,), ()]
            ],
        ],
        compiler_params=pltpu.CompilerParams(collective_id=0, has_side_effects=True, **params),
        name="beamform",
    )(
        in_hbm(voltages.reshape(16, 4, 2, 2, 16, TIME)),
        in_hbm(weights),
        in_hbm(flags),
        in_hbm(dm_index),
        in_hbm(jnp.asarray(chirp_rows()).astype(BF16).astype(F32)),
        in_hbm(jnp.asarray(dft_rows()).astype(BF16)),
        in_hbm(jnp.asarray(prototype())),
    )
    dedispersed, bandpass = pl.pallas_call(
        tail,
        out_shape=(
            jax.ShapeDtypeStruct((2, 2 * TIME * 2, 128), BF16),
            jax.ShapeDtypeStruct((2, CHANNELS), F32),
        ),
        in_specs=[vmem] * 7,
        out_specs=(hbm, hbm),
        scratch_shapes=[
            pltpu.VMEM((2, 512, SPAN), BF16),
            pltpu.VMEM((2, 88 + SPAN, 512), F32),
            *[pltpu.VMEM((SPAN + 32, 512), BF16) for _ in range(2)],
            *[pltpu.VMEM((SPAN + 16, 512), BF16) for _ in range(2)],
            *[pltpu.VMEM((NBLOCK, 32, 512), BF16) for _ in range(2)],
            pltpu.VMEM((2, 2 * TIME * 2, 128), BF16),
            pltpu.VMEM((2, CHANNELS), F32),
            dma((3,)),
        ],
        compiler_params=pltpu.CompilerParams(**params),
        name="synthesis",
    )(
        beams.reshape(PARTS, 1024, SPAN),
        tables,
        dft,
        proto,
        product0,
        last0,
        power0,
    )
    dedispersed = dedispersed.reshape(2, 512, 2, 128).transpose(0, 2, 1, 3).reshape(2, 2, TIME * CHANNELS)
    return dedispersed, bandpass


def solution(mesh):
    return jax.shard_map(
        on_device,
        mesh=mesh,
        in_specs=(
            P(None, ("stn", "chan"), None, None),
            P(None, ("stn", "chan"), None, None),
            P(("stn", "chan"), None),
            P(("stn", "chan")),
        ),
        out_specs=(P(None, ("stn", "chan"), None), P(("stn", "chan"), None)),
        check_vma=False,
    )
```

```python
import math
import random

import jax
import jax.numpy as jnp
import numpy as np
from jax import lax
from jax.experimental import pallas as pl
from jax.experimental.pallas import tpu as pltpu
from jax.sharding import PartitionSpec as P

CHANNELS = 256
BEAMS = 256
INPUTS = 1024
TIME = 256
TAPS = 12
CHIRP = 1024
DMS = 16
NBLOCK = CHIRP // CHANNELS + 1
DEVICES = 128
CHAN_AXIS = 16
PARTS = 2
SPAN = TIME // PARTS
MESH = pl.DeviceIdType.MESH
BF16 = jnp.bfloat16
F32 = jnp.float32


def dft_rows():
    order = np.arange(CHANNELS)
    angle = 2.0 * math.pi / CHANNELS * (order[:, None] * order[None, :] % CHANNELS)
    cosine = np.cos(angle) / math.sqrt(CHANNELS)
    sine = np.sin(angle) / math.sqrt(CHANNELS)
    return np.block([[cosine, sine], [-sine, cosine]]).astype(np.float32)


def prototype():
    counter = np.arange(TAPS * CHANNELS, dtype=np.float64)
    offset = (counter + 0.5) / CHANNELS - TAPS / 2.0
    window = 0.54 + 0.46 * np.cos(math.pi * offset / (TAPS / 2.0))
    taps = (np.sinc(offset) * window).reshape(TAPS, CHANNELS)
    return np.concatenate([taps, taps], axis=1).astype(np.float32)


def chirp_rows():
    dms = np.arange(DMS, dtype=np.int64)[:, None, None]
    lag = np.arange(NBLOCK)[None, :, None] * CHANNELS + CHANNELS - 1 - np.arange(2 * CHANNELS)[None, None, :]
    valid = (lag >= 0) & (lag < CHIRP)
    lag = np.clip(lag, 0, CHIRP - 1)
    angle = math.pi * ((dms + 1) * lag * lag % (2 * DMS * CHIRP)) / (DMS * CHIRP)
    real = np.where(valid, np.cos(angle), 0.0) / math.sqrt(CHIRP)
    imag = np.where(valid, np.sin(angle), 0.0) / math.sqrt(CHIRP)
    rows = np.concatenate([real, imag, np.zeros((DMS, 6, 2 * CHANNELS))], axis=1)
    return rows.astype(np.float32)


def iota(axis, shape=(256, 256)):
    return lax.broadcasted_iota(jnp.int32, shape, axis)


def ones_where(condition):
    return jnp.where(condition, 1.0, 0.0).astype(BF16)


def dot(a, b):
    return jnp.dot(a, b, preferred_element_type=F32)


def exchange_order():
    left = [(dz, dy, dx) for dz in range(4) for dy in range(4) for dx in range(4)]
    random.Random(7).shuffle(left)
    hops, ordered = [0, 0, 0], []
    while left:
        def uneven(step):
            return sum((done + min(d, 4 - d) - len(ordered) - 1) ** 2 for done, d in zip(hops, step))

        best = min(left, key=uneven)
        left.remove(best)
        ordered.append(best)
        hops = [done + min(d, 4 - d) for done, d in zip(hops, best)]
    return ordered


def body(
    volt, wgt, flags, dm, chirps, dft, proto, recv2, tables, dftv, protov, product0, last0, power0,
    vin, give, send, recv, win, chv, flagv, dmv, beams, give2, send2, keep, ordered, padded, even, odd, acc,
    load_sem, plane_sem, given, given2, sent, sent2, sibling_sem, sibling_sem2, recv_sem, recv_sem2, pack_sem, packs_sent, relays_sent, *stages,
):
    x = lax.rem(lax.axis_index("chan"), 4)
    y = lax.axis_index("chan") // 4
    z = lax.axis_index("stn") // 2
    core = lax.rem(lax.axis_index("stn"), 2)
    chip = z * CHAN_AXIS + lax.axis_index("chan")
    sibling = (z * 2 + 1 - core, lax.axis_index("chan"))

    turn = 1 + 2 * core
    zs = [lax.rem(z + dz * turn, 4) for dz in range(4)]
    xs = [lax.rem(x + dx * turn, 4) for dx in range(4)]
    ys = [lax.rem(y + dy * turn, 4) * 4 for dy in range(4)]

    flag_load = pltpu.make_async_copy(flags, flagv, load_sem.at[0])
    flag_load.start()
    volt_loads = [
        pltpu.make_async_copy(volt.at[:, :, number], vin.at[:, :, number], load_sem.at[n])
        for n, number in ((1, 1 - core), (2, core))
    ]
    for load in volt_loads:
        load.start()

    barrier = pltpu.get_barrier_semaphore()
    line = [(zs[dz] * 2 + core, ys[0] + x) for dz in range(1, 4)]
    plane = [(z * 2 + core, ys[dy] + xs[dx]) for dy in range(4) for dx in range(4) if (dy, dx) != (0, 0)]
    greeted = [sibling] + line + plane
    for peer in greeted:
        pl.semaphore_signal(barrier, inc=1, device_id=peer, device_id_type=MESH)

    def hand_over(part, give, send, given, sibling_sem):
        pltpu.make_async_remote_copy(
            src_ref=give.at[part],
            dst_ref=send.at[part, :, :, :, core] if len(send.shape) == 8 else send.at[part, :, core],
            send_sem=given,
            recv_sem=sibling_sem.at[part],
            device_id=sibling,
            device_id_type=MESH,
        ).start()

    def exchange(part, send, landing, sibling_sem, sent, recv_sem):
        share = send.at[part, :, 1 - core]
        pltpu.make_async_copy(share, share, sibling_sem.at[part]).wait()
        pltpu.make_async_copy(send.at[part, chip], landing, recv_sem.at[part]).start()
        for dz, dy, dx in exchange_order():
            if (dz, dy, dx) != (0, 0, 0):
                chan = ys[dy] + xs[dx]
                pltpu.make_async_remote_copy(
                    src_ref=send.at[part, zs[dz] * CHAN_AXIS + chan],
                    dst_ref=landing,
                    send_sem=sent.at[part],
                    recv_sem=recv_sem.at[part],
                    device_id=(zs[dz] * 2 + core, chan),
                    device_id_type=MESH,
                ).start()

    by_z, by_x, by_y, by_xz, by_yz, by_xy, by_xyz = stages

    def place(steps):
        dz, dy, dx = steps
        return zs[dz % 4] * 2 + core, ys[dy % 4] + xs[dx % 4]

    def packs(part):
        near = (-1, 0, 1)
        listed = []
        for m in range(3):
            listed.append(((3, m, slice(0, 3)), by_z.at[part, m], (1, 0, 0), [(1, m - 1, d) for d in near]))
            listed.append(((m, slice(0, 3), 3), by_x.at[part, m], (0, 0, 1), [(m - 1, d, 1) for d in near]))
            listed.append(((m, 3, slice(0, 3)), by_y.at[part, m], (0, 1, 0), [(m - 1, 1, d) for d in near]))
            listed.append(((m, 3, 3), by_xy.at[part, m], (0, 1, 1), [(m - 1, 1, 1)]))
        listed.append(((3, slice(0, 3), 3), by_xz.at[part], (1, 0, 1), [(1, d, 1) for d in near]))
        listed.append(((3, 3, slice(0, 3)), by_yz.at[part], (1, 1, 0), [(1, 1, d) for d in near]))
        listed.append(((3, 3, 3), by_xyz.at[part], (1, 1, 1), [(1, 1, 1)]))
        return [(15 * part + n, *pack) for n, pack in enumerate(listed)]

    def send_packs(part):
        share = send.at[part, :, :, :, 1 - core]
        pltpu.make_async_copy(share, share, sibling_sem.at[part]).wait()
        for n, at, stage, steps, _ in packs(part):
            pltpu.make_async_remote_copy(
                src_ref=send.at[part, at[0], at[1], at[2]],
                dst_ref=stage,
                send_sem=packs_sent,
                recv_sem=pack_sem.at[n],
                device_id=place(steps),
                device_id_type=MESH,
            ).start()

    def send_direct(part):
        pltpu.make_async_copy(send.at[part, 1, 1, 1], recv.at[part, chip], recv_sem.at[part, 0]).start()
        for steps in exchange_order():
            if 2 not in steps and steps != (0, 0, 0):
                at = [(d + 1) % 4 for d in steps]
                pltpu.make_async_remote_copy(
                    src_ref=send.at[part, at[0], at[1], at[2]],
                    dst_ref=recv.at[part, chip],
                    send_sem=sent.at[part],
                    recv_sem=recv_sem.at[part, steps[0]],
                    device_id=place(steps),
                    device_id_type=MESH,
                ).start()

    def relay_packs(part):
        for n, _, stage, steps, onward in packs(part):
            pltpu.make_async_copy(stage, stage, pack_sem.at[n]).wait()
            dz, dy, dx = (-d % 4 for d in steps)
            origin = zs[dz] * CHAN_AXIS + ys[dy] + xs[dx]
            for m, further in enumerate(onward):
                pltpu.make_async_remote_copy(
                    src_ref=stage.at[m] if len(onward) > 1 else stage,
                    dst_ref=recv.at[part, origin],
                    send_sem=relays_sent,
                    recv_sem=recv_sem.at[part, (steps[0] + further[0]) % 4],
                    device_id=place(further),
                    device_id_type=MESH,
                ).start()

    flag_load.wait()
    row, col = iota(0), iota(1)
    hits = ones_where(iota(0, (256, 64)) == flagv[...])
    count = dot(hits, jnp.ones((64, 256), BF16))
    keep_rows = ones_where((count < 0.5) & (row % 16 == col % 16))
    keep[...] = dot(ones_where(iota(1, (16, 256)) // 16 == iota(0, (16, 256))), keep_rows)

    def sort_out(number):
        way = 1 + 2 * number
        there = (row // 128) * 8 + ((x + (row // 32 + 3) % 4 * way) % 4) * 2 + (row // 8) % 2
        swap = jnp.where((col // 16 == ((row // 16) % 2) * 8 + row % 8) & (col % 16 == there), 1.0, 0.0)
        for zz in range(4):
            for half in range(2):
                block = vin[:, zz, number, half].reshape(256, 256)
                mine = (swap * keep[pl.ds((zz * 2 + number) * 2 + half, 1), :]).astype(BF16)
                sorted_block = dot(mine, block).astype(BF16)
                for one in range(2):
                    mz = lax.rem((zz + 4 - z) * way + 1, 4)
                    my = lax.rem((half * 2 + one + 4 - y) * way + 1, 4)
                    yield mz, my, sorted_block[one * 128 : one * 128 + 128].reshape(4, 4, 8, 256)

    volt_loads[0].wait()
    for mz, my, block in sort_out(1 - core):
        for part in range(PARTS):
            give[part, mz, my] = block[..., part * SPAN : part * SPAN + SPAN]
    pl.semaphore_wait(barrier, len(greeted))
    for peer in line:
        pl.semaphore_signal(plane_sem, inc=1, device_id=peer, device_id_type=MESH)
    for part in range(PARTS):
        hand_over(part, give, send, given, sibling_sem)
    volt_loads[1].wait()
    for mz, my, block in sort_out(core):
        for part in range(PARTS):
            send[part, mz, my, :, core] = block[..., part * SPAN : part * SPAN + SPAN]
    loads = [
        pltpu.make_async_copy(source, target, load_sem.at[n])
        for n, (source, target) in enumerate(
            ((wgt, win), (dm, dmv), (chirps, chv), (dft, dftv), (proto, protov)), 3
        )
    ]
    for load in loads:
        load.start()
    pl.semaphore_wait(plane_sem, len(line))
    send_packs(0)
    send_direct(0)
    send_packs(1)
    relay_packs(0)
    send_direct(1)
    relay_packs(1)
    for load in loads:
        load.wait()

    def toeplitz(n, carry):
        b, block = n // NBLOCK, lax.rem(n, NBLOCK)
        for part in range(2):
            wide = jnp.broadcast_to(chv[dmv[b], pl.ds(part * NBLOCK + block, 1), :], (8, 2 * CHANNELS))
            eight = pltpu.roll(wide, CHANNELS + 1, 1, stride=1, stride_axis=0)
            for k in range(0, CHANNELS, 16):
                both = [pltpu.roll(eight, k + i, 1)[:, :CHANNELS] if k + i else eight[:, :CHANNELS] for i in (0, 8)]
                rows = pl.ds(pl.multiple_of(block * CHANNELS + k, 16), 16)
                tables[b, rows, part * CHANNELS : (part + 1) * CHANNELS] = jnp.concatenate(both, axis=0).astype(BF16)
        return carry

    lax.fori_loop(0, 2 * NBLOCK, toeplitz, 0)

    to_device = lax.rem(core + row // 128, 2) * 16 + (row // 8) % 16
    order = ones_where(
        (col // 128 == row % 2) & ((col // 64) % 2 == (row // 2) % 2) & (col % 64 == to_device * 2 + (row // 4) % 2)
    )
    for part in range(PARTS):
        for n, dz in enumerate((3, 0, 1, 2)):
            source = zs[-dz % 4]
            arrived = recv.at[part, pl.ds(pl.multiple_of(source * 16, 16), 16)]
            pltpu.make_async_copy(arrived, arrived, recv_sem.at[part, dz]).wait()
            for c in range(2):
                real, imag, weight_real, weight_imag = [], [], [], []
                for number in range(2):
                    chips = pl.ds(pl.multiple_of(source * 16, 16), 16)
                    inputs = pl.ds(pl.multiple_of((source * 2 + number) * 128, 128), 128)
                    real.append(recv[part, chips, number, c].reshape(128, SPAN))
                    imag.append(recv[part, chips, number, 2 + c].reshape(128, SPAN))
                    weight_real.append(win[0, c, :, inputs])
                    weight_imag.append(win[1, c, :, inputs])
                parts = jnp.concatenate(
                    [
                        jnp.concatenate(real + [-half for half in imag], axis=0),
                        jnp.concatenate(imag + real, axis=0),
                    ],
                    axis=1,
                )
                product = dot(jnp.concatenate(weight_real + weight_imag, axis=1), parts)
                if n == 0:
                    acc[c] = product
                elif n < 3:
                    acc[c] += product
                else:
                    beams[c] = (acc[c] + product).astype(BF16)
        for zz in range(4):
            rows = slice(zz * 64, zz * 64 + 64)
            block = jnp.concatenate([beams[c, rows, q * SPAN : q * SPAN + SPAN] for c in range(2) for q in range(2)], axis=0)
            block = dot(order, block).astype(BF16)
            send2[part, zz * 16 : zz * 16 + 16, core] = block[:128].reshape(16, 8, SPAN)
            give2[part, zz * 16 : zz * 16 + 16] = block[128:].reshape(16, 8, SPAN)
        hand_over(part, give2, send2, given2, sibling_sem2)
    for part in range(PARTS):
        exchange(part, send2, recv2.at[part, chip], sibling_sem2, sent2, recv_sem2)

    arrived = recv2.at[0]
    pltpu.make_async_copy(arrived, arrived, recv_sem2.at[0]).wait()
    for b, power, last in front(
        lambda n: recv2[0, n * 16 : n * 16 + 16].reshape(256, SPAN), lambda b: 0.0, dftv, protov, ordered, padded
    ):
        power0[b : b + 1, :] = power
        last0[b] = last
    for b in range(2):
        for n in range(4):
            lanes, series = synthesise(b, n, protov, padded)
            store_shifted(series, lanes, even, odd)
        product0[b] = chirped(stacked_shifts(even, odd), tables[b])

    for blocks, sem in ((give, given), (give2, given2)):
        pltpu.make_async_copy(blocks, blocks, sem).wait()
    for sem in (packs_sent, relays_sent):
        for part in range(PARTS):
            blocks = recv.at[part, 0:37]
            pltpu.make_async_copy(blocks, blocks, sem).wait()
    for part in range(PARTS):
        for blocks, sem in ((recv.at[part, 0:26], sent), (send2.at[part, 0:63], sent2)):
            pltpu.make_async_copy(blocks, blocks, sem.at[part]).wait()
    arrived = recv2.at[1]
    pltpu.make_async_copy(arrived, arrived, recv_sem2.at[1]).wait()


def front(chunk, before_first, dftv, protov, xs, padded):
    row, col = iota(0), iota(1)
    sort = ones_where(col == ((row % 32) // 2 * 2 + (row % 64) // 32) * 8 + (row // 64) * 2 + row % 2)
    spread = ones_where(iota(1, (SPAN, SPAN)) == (iota(0, (SPAN, SPAN)) % 8) * 16 + iota(0, (SPAN, SPAN)) // 8)
    for n in range(4):
        block = dot(sort, chunk(n)).astype(BF16)
        for k in range(4):
            xs[k // 2, (k % 2) * 256 + n * 64 : (k % 2) * 256 + n * 64 + 64, :] = block[k * 64 : k * 64 + 64]
    for b in range(2):
        turned = lax.dot_general(spread, xs[b], (((1,), (1,)), ((), ())), preferred_element_type=F32)
        power = jnp.sum(turned * turned, axis=0, keepdims=True)
        spectra = dot(turned.astype(BF16), dftv[...])
        last = spectra[SPAN - 88 :]
        first = iota(0, (88, 512)) % 8 == 0
        padded[b, 0:88, :] = jnp.where(first, before_first(b), pltpu.roll(last, 1, 0))
        padded[b, 88 : 88 + SPAN, :] = spectra
        yield b, power, pltpu.roll(last, 81, 0)


def synthesise(b, n, protov, padded):
    lanes = slice(n * 128, n * 128 + 128)
    series = protov[0:1, lanes] * padded[b, 88 : 88 + SPAN, lanes]
    for tap in range(1, TAPS):
        series = series + protov[tap : tap + 1, lanes] * padded[b, 88 - 8 * tap : 88 - 8 * tap + SPAN, lanes]
    return lanes, series


def store_shifted(series, lanes, even, odd):
    after = jnp.where(iota(0, (32, 128)) % 8 == 7, 0.0, pltpu.roll(series[:32], 31, 0))
    even[0:SPAN, lanes] = series.astype(BF16)
    even[SPAN : SPAN + 32, lanes] = after.astype(BF16)
    odd[0 : SPAN + 16, lanes] = jnp.concatenate([series[8:], after[:24]], axis=0).astype(BF16)


def stacked_shifts(even, odd):
    shifted = [even[0:SPAN], odd[0:SPAN], even[16 : 16 + SPAN], odd[16 : 16 + SPAN], even[32 : 32 + SPAN]]
    return [jnp.concatenate([block[:, p * 256 : p * 256 + 256] for block in shifted], axis=1) for p in range(2)]


def chirped(parts, table):
    product = dot(jnp.concatenate(parts, axis=0), table)
    rows = product.shape[0] // 2
    real = product[:rows, :256] + product[rows:, 256:]
    imag = product[rows:, :256] - product[:rows, 256:]
    return jnp.concatenate([real, imag], axis=1)


def tail(
    xv, tv, dftv, protov, product0, last0, power0, out, band,
    xs, padded, even0, even1, odd0, odd1, over0, over1, outv, bandv, out_sem,
):
    band_copy = pltpu.make_async_copy(bandv, band, out_sem.at[2])
    for b, power, _ in front(lambda n: xv[1, n * 256 : n * 256 + 256, :], lambda b: last0[b], dftv, protov, xs, padded):
        power = (power + power0[b : b + 1, :]) * (1.0 / TIME)
        bandv[b : b + 1, :] = power[:, :256] + power[:, 256:]
    band_copy.start()
    results = []
    for b, (even, odd, over) in enumerate(((even0, odd0, over0), (even1, odd1, over1))):
        for n in range(4):
            lanes, series = synthesise(b, n, protov, padded)
            store_shifted(series, lanes, even, odd)
            over_edge = jnp.where(iota(0, (32, 128)) % 8 == 7, pltpu.roll(series[:32], 7, 0), 0.0)
            for blk in range(NBLOCK):
                seen = [over_edge[: 8 * blk]] if blk else []
                unseen = [jnp.zeros((32 - 8 * blk, 128), F32)] if blk < 4 else []
                over[blk, :, lanes] = jnp.concatenate(unseen + seen, axis=0).astype(BF16)
        edges = [
            jnp.concatenate([over[blk, :, p * 256 : p * 256 + 256] for blk in range(NBLOCK)], axis=1) for p in range(2)
        ]
        parts = [jnp.concatenate(pair, axis=0) for pair in zip(stacked_shifts(even, odd), edges)]
        product = chirped(parts, tv[b])
        results.append(
            jnp.concatenate([product0[b, :96], product0[b, 96:] + product[SPAN:], product[:SPAN]], axis=0).astype(BF16)
        )
    row, col = iota(0), iota(1)
    final = ones_where(col == (row % 4) * 64 + ((row // 4) % 8) * 8 + row // 32)
    copies = []
    for h in range(2):
        for j in range(2):
            rows = slice(128 * h + 64 * j, 128 * h + 64 * j + 64)
            block = jnp.concatenate(
                [
                    jnp.concatenate([results[b][rows, half * 128 + q * 256 : half * 128 + q * 256 + 128] for q in range(2)], axis=1)
                    for half in range(2) for b in range(2)
                ],
                axis=0,
            )
            block = dot(final, block).astype(BF16)
            for q in range(2):
                for k in range(8):
                    start = 512 * h + 64 * k + 32 * j
                    outv[q, start : start + 32, :] = block[32 * k : 32 * k + 32, q * 128 : q * 128 + 128]
        done = pl.ds(512 * h, 512)
        copies.append(pltpu.make_async_copy(outv.at[:, done], out.at[:, done], out_sem.at[h]))
        copies[-1].start()
    for copy in copies + [band_copy]:
        copy.wait()


def in_hbm(array):
    return pltpu.with_memory_space_constraint(array, pltpu.HBM)


def on_device(voltages, weights, flags, dm_index):
    hbm = pl.BlockSpec(memory_space=pl.ANY)
    vmem = pl.BlockSpec(memory_space=pltpu.VMEM)
    dma = pltpu.SemaphoreType.DMA
    params = dict(vmem_limit_bytes=24 * 1024 * 1024)
    beams, tables, dft, proto, product0, last0, power0 = pl.pallas_call(
        body,
        out_shape=(
            jax.ShapeDtypeStruct((PARTS, 64, 2, 8, SPAN), BF16),
            jax.ShapeDtypeStruct((2, NBLOCK * CHANNELS, 512), BF16),
            jax.ShapeDtypeStruct((512, 512), BF16),
            jax.ShapeDtypeStruct((TAPS, 512), F32),
            jax.ShapeDtypeStruct((2, SPAN, 512), F32),
            jax.ShapeDtypeStruct((2, 88, 512), F32),
            jax.ShapeDtypeStruct((2, 512), F32),
        ),
        in_specs=[hbm] * 7,
        out_specs=(vmem,) * 7,
        scratch_shapes=[
            pltpu.VMEM((16, 4, 2, 2, 16, 256), BF16),
            pltpu.VMEM((PARTS, 4, 4, 4, 4, 8, SPAN), BF16),
            pltpu.VMEM((PARTS, 4, 4, 4, 2, 4, 8, SPAN), BF16),
            pltpu.VMEM((PARTS, 64, 2, 4, 8, SPAN), BF16),
            pltpu.VMEM((2, 2, 256, 1024), BF16),
            pltpu.VMEM((DMS, 16, 512), F32),
            pltpu.VMEM((1, 64), jnp.int32),
            pltpu.SMEM((2,), jnp.int32),
            pltpu.VMEM((2, 256, 2 * SPAN), BF16),
            pltpu.VMEM((PARTS, 64, 8, SPAN), BF16),
            pltpu.VMEM((PARTS, 64, 2, 8, SPAN), BF16),
            pltpu.VMEM((16, 256), F32),
            pltpu.VMEM((2, 512, SPAN), BF16),
            pltpu.VMEM((2, 88 + SPAN, 512), F32),
            pltpu.VMEM((SPAN + 32, 512), BF16),
            pltpu.VMEM((SPAN + 16, 512), BF16),
            pltpu.VMEM((2, 256, 2 * SPAN), F32),
            dma((8,)),
            pltpu.SemaphoreType.REGULAR,
            dma,
            dma,
            *[dma((PARTS,)) for _ in range(4)],
            dma((PARTS, 4)),
            dma((PARTS,)),
            dma((30,)),
            dma,
            dma,
            *[
                pltpu.VMEM((PARTS,) + shape + (2, 4, 8, SPAN), BF16)
                for shape in [(3, 3), (3, 3), (3, 3), (3,), (3,), (3,), ()]
            ],
        ],
        compiler_params=pltpu.CompilerParams(collective_id=0, has_side_effects=True, **params),
        name="beamform",
    )(
        in_hbm(voltages.reshape(16, 4, 2, 2, 16, TIME)),
        in_hbm(weights),
        in_hbm(flags),
        in_hbm(dm_index),
        in_hbm(jnp.asarray(chirp_rows()).astype(BF16).astype(F32)),
        in_hbm(jnp.asarray(dft_rows()).astype(BF16)),
        in_hbm(jnp.asarray(prototype())),
    )
    dedispersed, bandpass = pl.pallas_call(
        tail,
        out_shape=(
            jax.ShapeDtypeStruct((2, 2 * TIME * 2, 128), BF16),
            jax.ShapeDtypeStruct((2, CHANNELS), F32),
        ),
        in_specs=[vmem] * 7,
        out_specs=(hbm, hbm),
        scratch_shapes=[
            pltpu.VMEM((2, 512, SPAN), BF16),
            pltpu.VMEM((2, 88 + SPAN, 512), F32),
            *[pltpu.VMEM((SPAN + 32, 512), BF16) for _ in range(2)],
            *[pltpu.VMEM((SPAN + 16, 512), BF16) for _ in range(2)],
            *[pltpu.VMEM((NBLOCK, 32, 512), BF16) for _ in range(2)],
            pltpu.VMEM((2, 2 * TIME * 2, 128), BF16),
            pltpu.VMEM((2, CHANNELS), F32),
            dma((3,)),
        ],
        compiler_params=pltpu.CompilerParams(**params),
        name="synthesis",
    )(
        beams.reshape(PARTS, 1024, SPAN),
        tables,
        dft,
        proto,
        product0,
        last0,
        power0,
    )
    dedispersed = dedispersed.reshape(2, 512, 2, 128).transpose(0, 2, 1, 3).reshape(2, 2, TIME * CHANNELS)
    return dedispersed, bandpass


def solution(mesh):
    return jax.shard_map(
        on_device,
        mesh=mesh,
        in_specs=(
            P(None, ("stn", "chan"), None, None),
            P(None, ("stn", "chan"), None, None),
            P(("stn", "chan"), None),
            P(("stn", "chan")),
        ),
        out_specs=(P(None, ("stn", "chan"), None), P(("stn", "chan"), None)),
        check_vma=False,
    )
```

```python
import math
import random

import jax
import jax.numpy as jnp
import numpy as np
from jax import lax
from jax.experimental import pallas as pl
from jax.experimental.pallas import tpu as pltpu
from jax.sharding import PartitionSpec as P

CHANNELS = 256
BEAMS = 256
INPUTS = 1024
TIME = 256
TAPS = 12
CHIRP = 1024
DMS = 16
NBLOCK = CHIRP // CHANNELS + 1
DEVICES = 128
CHAN_AXIS = 16
PARTS = 2
SPAN = TIME // PARTS
MESH = pl.DeviceIdType.MESH
BF16 = jnp.bfloat16
F32 = jnp.float32


def dft_rows():
    order = np.arange(CHANNELS)
    angle = 2.0 * math.pi / CHANNELS * (order[:, None] * order[None, :] % CHANNELS)
    cosine = np.cos(angle) / math.sqrt(CHANNELS)
    sine = np.sin(angle) / math.sqrt(CHANNELS)
    return np.block([[cosine, sine], [-sine, cosine]]).astype(np.float32)


def prototype():
    counter = np.arange(TAPS * CHANNELS, dtype=np.float64)
    offset = (counter + 0.5) / CHANNELS - TAPS / 2.0
    window = 0.54 + 0.46 * np.cos(math.pi * offset / (TAPS / 2.0))
    taps = (np.sinc(offset) * window).reshape(TAPS, CHANNELS)
    return np.concatenate([taps, taps], axis=1).astype(np.float32)


def chirp_rows():
    dms = np.arange(DMS, dtype=np.int64)[:, None, None]
    lag = np.arange(NBLOCK)[None, :, None] * CHANNELS + CHANNELS - 1 - np.arange(2 * CHANNELS)[None, None, :]
    valid = (lag >= 0) & (lag < CHIRP)
    lag = np.clip(lag, 0, CHIRP - 1)
    angle = math.pi * ((dms + 1) * lag * lag % (2 * DMS * CHIRP)) / (DMS * CHIRP)
    real = np.where(valid, np.cos(angle), 0.0) / math.sqrt(CHIRP)
    imag = np.where(valid, np.sin(angle), 0.0) / math.sqrt(CHIRP)
    rows = np.concatenate([real, imag, np.zeros((DMS, 6, 2 * CHANNELS))], axis=1)
    return rows.astype(np.float32)


def iota(axis, shape=(256, 256)):
    return lax.broadcasted_iota(jnp.int32, shape, axis)


def ones_where(condition):
    return jnp.where(condition, 1.0, 0.0).astype(BF16)


def dot(a, b):
    return jnp.dot(a, b, preferred_element_type=F32)


def exchange_order():
    left = [(dz, dy, dx) for dz in range(4) for dy in range(4) for dx in range(4)]
    random.Random(7).shuffle(left)
    hops, ordered = [0, 0, 0], []
    while left:
        def uneven(step):
            return sum((done + min(d, 4 - d) - len(ordered) - 1) ** 2 for done, d in zip(hops, step))

        best = min(left, key=uneven)
        left.remove(best)
        ordered.append(best)
        hops = [done + min(d, 4 - d) for done, d in zip(hops, best)]
    return ordered


def body(
    volt, wgt, flags, dm, chirps, dft, proto, recv2, tables, dftv, protov, product0, last0, power0,
    vin, give, send, recv, win, chv, flagv, dmv, beams, give2, send2, keep, ordered, padded, even, odd, acc,
    load_sem, plane_sem, given, given2, sent, sent2, sibling_sem, sibling_sem2, recv_sem, recv_sem2, pack_sem, packs_sent, relays_sent, *stages,
):
    x = lax.rem(lax.axis_index("chan"), 4)
    y = lax.axis_index("chan") // 4
    z = lax.axis_index("stn") // 2
    core = lax.rem(lax.axis_index("stn"), 2)
    chip = z * CHAN_AXIS + lax.axis_index("chan")
    sibling = (z * 2 + 1 - core, lax.axis_index("chan"))

    turn = 1 + 2 * core
    zs = [lax.rem(z + dz * turn, 4) for dz in range(4)]
    xs = [lax.rem(x + dx * turn, 4) for dx in range(4)]
    ys = [lax.rem(y + dy * turn, 4) * 4 for dy in range(4)]

    flag_load = pltpu.make_async_copy(flags, flagv, load_sem.at[0])
    flag_load.start()
    volt_loads = [
        pltpu.make_async_copy(volt.at[:, :, number], vin.at[:, :, number], load_sem.at[n])
        for n, number in ((1, 1 - core), (2, core))
    ]
    for load in volt_loads:
        load.start()

    barrier = pltpu.get_barrier_semaphore()
    line = [(zs[dz] * 2 + core, ys[0] + x) for dz in range(1, 4)]
    plane = [(z * 2 + core, ys[dy] + xs[dx]) for dy in range(4) for dx in range(4) if (dy, dx) != (0, 0)]
    greeted = [sibling] + line + plane
    for peer in greeted:
        pl.semaphore_signal(barrier, inc=1, device_id=peer, device_id_type=MESH)

    def hand_over(part, give, send, given, sibling_sem):
        pltpu.make_async_remote_copy(
            src_ref=give.at[part],
            dst_ref=send.at[part, :, :, :, core] if len(send.shape) == 8 else send.at[part, :, core],
            send_sem=given,
            recv_sem=sibling_sem.at[part],
            device_id=sibling,
            device_id_type=MESH,
        ).start()

    def exchange(part, send, landing, sibling_sem, sent, recv_sem):
        share = send.at[part, :, 1 - core]
        pltpu.make_async_copy(share, share, sibling_sem.at[part]).wait()
        pltpu.make_async_copy(send.at[part, chip], landing, recv_sem.at[part]).start()
        for dz, dy, dx in exchange_order():
            if (dz, dy, dx) != (0, 0, 0):
                chan = ys[dy] + xs[dx]
                pltpu.make_async_remote_copy(
                    src_ref=send.at[part, zs[dz] * CHAN_AXIS + chan],
                    dst_ref=landing,
                    send_sem=sent.at[part],
                    recv_sem=recv_sem.at[part],
                    device_id=(zs[dz] * 2 + core, chan),
                    device_id_type=MESH,
                ).start()

    by_z, by_x, by_y, by_xz, by_yz, by_xy, by_xyz = stages

    def place(steps):
        dz, dy, dx = steps
        return zs[dz % 4] * 2 + core, ys[dy % 4] + xs[dx % 4]

    def packs(part):
        near = (-1, 0, 1)
        listed = []
        for m in range(3):
            listed.append(((3, m, slice(0, 3)), by_z.at[part, m], (1, 0, 0), [(1, m - 1, d) for d in near]))
            listed.append(((m, slice(0, 3), 3), by_x.at[part, m], (0, 0, 1), [(m - 1, d, 1) for d in near]))
            listed.append(((m, 3, slice(0, 3)), by_y.at[part, m], (0, 1, 0), [(m - 1, 1, d) for d in near]))
            listed.append(((m, 3, 3), by_xy.at[part, m], (0, 1, 1), [(m - 1, 1, 1)]))
        listed.append(((3, slice(0, 3), 3), by_xz.at[part], (1, 0, 1), [(1, d, 1) for d in near]))
        listed.append(((3, 3, slice(0, 3)), by_yz.at[part], (1, 1, 0), [(1, 1, d) for d in near]))
        listed.append(((3, 3, 3), by_xyz.at[part], (1, 1, 1), [(1, 1, 1)]))
        return [(15 * part + n, *pack) for n, pack in enumerate(listed)]

    def send_packs(part):
        share = send.at[part, :, :, :, 1 - core]
        pltpu.make_async_copy(share, share, sibling_sem.at[part]).wait()
        for n, at, stage, steps, _ in packs(part):
            pltpu.make_async_remote_copy(
                src_ref=send.at[part, at[0], at[1], at[2]],
                dst_ref=stage,
                send_sem=packs_sent,
                recv_sem=pack_sem.at[n],
                device_id=place(steps),
                device_id_type=MESH,
            ).start()

    def send_direct(part):
        pltpu.make_async_copy(send.at[part, 1, 1, 1], recv.at[part, chip], recv_sem.at[part, 0]).start()
        for steps in exchange_order():
            if 2 not in steps and steps != (0, 0, 0):
                at = [(d + 1) % 4 for d in steps]
                pltpu.make_async_remote_copy(
                    src_ref=send.at[part, at[0], at[1], at[2]],
                    dst_ref=recv.at[part, chip],
                    send_sem=sent.at[part],
                    recv_sem=recv_sem.at[part, steps[0]],
                    device_id=place(steps),
                    device_id_type=MESH,
                ).start()

    def relay_packs(part):
        for n, _, stage, steps, onward in packs(part):
            pltpu.make_async_copy(stage, stage, pack_sem.at[n]).wait()
            dz, dy, dx = (-d % 4 for d in steps)
            origin = zs[dz] * CHAN_AXIS + ys[dy] + xs[dx]
            for m, further in enumerate(onward):
                pltpu.make_async_remote_copy(
                    src_ref=stage.at[m] if len(onward) > 1 else stage,
                    dst_ref=recv.at[part, origin],
                    send_sem=relays_sent,
                    recv_sem=recv_sem.at[part, (steps[0] + further[0]) % 4],
                    device_id=place(further),
                    device_id_type=MESH,
                ).start()

    flag_load.wait()
    row, col = iota(0), iota(1)
    hits = ones_where(iota(0, (256, 64)) == flagv[...])
    count = dot(hits, jnp.ones((64, 256), BF16))
    keep_rows = ones_where((count < 0.5) & (row % 16 == col % 16))
    keep[...] = dot(ones_where(iota(1, (16, 256)) // 16 == iota(0, (16, 256))), keep_rows)

    def sort_out(number):
        way = 1 + 2 * number
        there = (row // 128) * 8 + ((x + (row // 32 + 3) % 4 * way) % 4) * 2 + (row // 8) % 2
        swap = jnp.where((col // 16 == ((row // 16) % 2) * 8 + row % 8) & (col % 16 == there), 1.0, 0.0)
        for zz in range(4):
            for half in range(2):
                block = vin[:, zz, number, half].reshape(256, 256)
                mine = (swap * keep[pl.ds((zz * 2 + number) * 2 + half, 1), :]).astype(BF16)
                sorted_block = dot(mine, block).astype(BF16)
                for one in range(2):
                    mz = lax.rem((zz + 4 - z) * way + 1, 4)
                    my = lax.rem((half * 2 + one + 4 - y) * way + 1, 4)
                    yield mz, my, sorted_block[one * 128 : one * 128 + 128].reshape(4, 4, 8, 256)

    volt_loads[0].wait()
    for mz, my, block in sort_out(1 - core):
        for part in range(PARTS):
            give[part, mz, my] = block[..., part * SPAN : part * SPAN + SPAN]
    pl.semaphore_wait(barrier, len(greeted))
    for peer in line:
        pl.semaphore_signal(plane_sem, inc=1, device_id=peer, device_id_type=MESH)
    for part in range(PARTS):
        hand_over(part, give, send, given, sibling_sem)
    volt_loads[1].wait()
    for mz, my, block in sort_out(core):
        for part in range(PARTS):
            send[part, mz, my, :, core] = block[..., part * SPAN : part * SPAN + SPAN]
    loads = [
        pltpu.make_async_copy(source, target, load_sem.at[n])
        for n, (source, target) in enumerate(
            ((wgt, win), (dm, dmv), (chirps, chv), (dft, dftv), (proto, protov)), 3
        )
    ]
    for load in loads:
        load.start()
    pl.semaphore_wait(plane_sem, len(line))
    send_packs(0)
    send_direct(0)
    send_packs(1)
    relay_packs(0)
    send_direct(1)
    relay_packs(1)
    for load in loads:
        load.wait()

    def toeplitz(n, carry):
        b, block = n // NBLOCK, lax.rem(n, NBLOCK)
        for part in range(2):
            wide = jnp.broadcast_to(chv[dmv[b], pl.ds(part * NBLOCK + block, 1), :], (8, 2 * CHANNELS))
            eight = pltpu.roll(wide, CHANNELS + 1, 1, stride=1, stride_axis=0)
            for k in range(0, CHANNELS, 16):
                both = [pltpu.roll(eight, k + i, 1)[:, :CHANNELS] if k + i else eight[:, :CHANNELS] for i in (0, 8)]
                rows = pl.ds(pl.multiple_of(block * CHANNELS + k, 16), 16)
                tables[b, rows, part * CHANNELS : (part + 1) * CHANNELS] = jnp.concatenate(both, axis=0).astype(BF16)
        return carry


    to_device = lax.rem(core + row // 128, 2) * 16 + (row // 8) % 16
    order = ones_where(
        (col // 128 == row % 2) & ((col // 64) % 2 == (row // 2) % 2) & (col % 64 == to_device * 2 + (row // 4) % 2)
    )
    for part in range(PARTS):
        for n, dz in enumerate((3, 0, 1, 2)):
            source = zs[-dz % 4]
            arrived = recv.at[part, pl.ds(pl.multiple_of(source * 16, 16), 16)]
            pltpu.make_async_copy(arrived, arrived, recv_sem.at[part, dz]).wait()
            for c in range(2):
                real, imag, weight_real, weight_imag = [], [], [], []
                for number in range(2):
                    chips = pl.ds(pl.multiple_of(source * 16, 16), 16)
                    inputs = pl.ds(pl.multiple_of((source * 2 + number) * 128, 128), 128)
                    real.append(recv[part, chips, number, c].reshape(128, SPAN))
                    imag.append(recv[part, chips, number, 2 + c].reshape(128, SPAN))
                    weight_real.append(win[0, c, :, inputs])
                    weight_imag.append(win[1, c, :, inputs])
                parts = jnp.concatenate(
                    [
                        jnp.concatenate(real + [-half for half in imag], axis=0),
                        jnp.concatenate(imag + real, axis=0),
                    ],
                    axis=1,
                )
                product = dot(jnp.concatenate(weight_real + weight_imag, axis=1), parts)
                if n == 0:
                    acc[c] = product
                elif n < 3:
                    acc[c] += product
                else:
                    beams[c] = (acc[c] + product).astype(BF16)
        for zz in range(4):
            rows = slice(zz * 64, zz * 64 + 64)
            block = jnp.concatenate([beams[c, rows, q * SPAN : q * SPAN + SPAN] for c in range(2) for q in range(2)], axis=0)
            block = dot(order, block).astype(BF16)
            send2[part, zz * 16 : zz * 16 + 16, core] = block[:128].reshape(16, 8, SPAN)
            give2[part, zz * 16 : zz * 16 + 16] = block[128:].reshape(16, 8, SPAN)
        hand_over(part, give2, send2, given2, sibling_sem2)
        if part == 0:
            lax.fori_loop(0, 2 * NBLOCK, toeplitz, 0)
        exchange(part, send2, recv2.at[part, chip], sibling_sem2, sent2, recv_sem2)

    arrived = recv2.at[0]
    pltpu.make_async_copy(arrived, arrived, recv_sem2.at[0]).wait()
    for b, power, last in front(
        lambda n: recv2[0, n * 16 : n * 16 + 16].reshape(256, SPAN), lambda b: 0.0, dftv, protov, ordered, padded
    ):
        power0[b : b + 1, :] = power
        last0[b] = last
    for b in range(2):
        for n in range(4):
            lanes, series = synthesise(b, n, protov, padded)
            store_shifted(series, lanes, even, odd)
        product0[b] = chirped(stacked_shifts(even, odd), tables[b])

    for blocks, sem in ((give, given), (give2, given2)):
        pltpu.make_async_copy(blocks, blocks, sem).wait()
    for sem in (packs_sent, relays_sent):
        for part in range(PARTS):
            blocks = recv.at[part, 0:37]
            pltpu.make_async_copy(blocks, blocks, sem).wait()
    for part in range(PARTS):
        for blocks, sem in ((recv.at[part, 0:26], sent), (send2.at[part, 0:63], sent2)):
            pltpu.make_async_copy(blocks, blocks, sem.at[part]).wait()
    arrived = recv2.at[1]
    pltpu.make_async_copy(arrived, arrived, recv_sem2.at[1]).wait()


def front(chunk, before_first, dftv, protov, xs, padded):
    row, col = iota(0), iota(1)
    sort = ones_where(col == ((row % 32) // 2 * 2 + (row % 64) // 32) * 8 + (row // 64) * 2 + row % 2)
    spread = ones_where(iota(1, (SPAN, SPAN)) == (iota(0, (SPAN, SPAN)) % 8) * 16 + iota(0, (SPAN, SPAN)) // 8)
    for n in range(4):
        block = dot(sort, chunk(n)).astype(BF16)
        for k in range(4):
            xs[k // 2, (k % 2) * 256 + n * 64 : (k % 2) * 256 + n * 64 + 64, :] = block[k * 64 : k * 64 + 64]
    for b in range(2):
        turned = lax.dot_general(spread, xs[b], (((1,), (1,)), ((), ())), preferred_element_type=F32)
        power = jnp.sum(turned * turned, axis=0, keepdims=True)
        spectra = dot(turned.astype(BF16), dftv[...])
        last = spectra[SPAN - 88 :]
        first = iota(0, (88, 512)) % 8 == 0
        padded[b, 0:88, :] = jnp.where(first, before_first(b), pltpu.roll(last, 1, 0))
        padded[b, 88 : 88 + SPAN, :] = spectra
        yield b, power, pltpu.roll(last, 81, 0)


def synthesise(b, n, protov, padded):
    lanes = slice(n * 128, n * 128 + 128)
    series = protov[0:1, lanes] * padded[b, 88 : 88 + SPAN, lanes]
    for tap in range(1, TAPS):
        series = series + protov[tap : tap + 1, lanes] * padded[b, 88 - 8 * tap : 88 - 8 * tap + SPAN, lanes]
    return lanes, series


def store_shifted(series, lanes, even, odd):
    after = jnp.where(iota(0, (32, 128)) % 8 == 7, 0.0, pltpu.roll(series[:32], 31, 0))
    even[0:SPAN, lanes] = series.astype(BF16)
    even[SPAN : SPAN + 32, lanes] = after.astype(BF16)
    odd[0 : SPAN + 16, lanes] = jnp.concatenate([series[8:], after[:24]], axis=0).astype(BF16)


def stacked_shifts(even, odd):
    shifted = [even[0:SPAN], odd[0:SPAN], even[16 : 16 + SPAN], odd[16 : 16 + SPAN], even[32 : 32 + SPAN]]
    return [jnp.concatenate([block[:, p * 256 : p * 256 + 256] for block in shifted], axis=1) for p in range(2)]


def chirped(parts, table):
    product = dot(jnp.concatenate(parts, axis=0), table)
    rows = product.shape[0] // 2
    real = product[:rows, :256] + product[rows:, 256:]
    imag = product[rows:, :256] - product[:rows, 256:]
    return jnp.concatenate([real, imag], axis=1)


def tail(
    xv, tv, dftv, protov, product0, last0, power0, out, band,
    xs, padded, even0, even1, odd0, odd1, over0, over1, outv, bandv, out_sem,
):
    band_copy = pltpu.make_async_copy(bandv, band, out_sem.at[2])
    for b, power, _ in front(lambda n: xv[1, n * 256 : n * 256 + 256, :], lambda b: last0[b], dftv, protov, xs, padded):
        power = (power + power0[b : b + 1, :]) * (1.0 / TIME)
        bandv[b : b + 1, :] = power[:, :256] + power[:, 256:]
    band_copy.start()
    results = []
    for b, (even, odd, over) in enumerate(((even0, odd0, over0), (even1, odd1, over1))):
        for n in range(4):
            lanes, series = synthesise(b, n, protov, padded)
            store_shifted(series, lanes, even, odd)
            over_edge = jnp.where(iota(0, (32, 128)) % 8 == 7, pltpu.roll(series[:32], 7, 0), 0.0)
            for blk in range(NBLOCK):
                seen = [over_edge[: 8 * blk]] if blk else []
                unseen = [jnp.zeros((32 - 8 * blk, 128), F32)] if blk < 4 else []
                over[blk, :, lanes] = jnp.concatenate(unseen + seen, axis=0).astype(BF16)
        edges = [
            jnp.concatenate([over[blk, :, p * 256 : p * 256 + 256] for blk in range(NBLOCK)], axis=1) for p in range(2)
        ]
        parts = [jnp.concatenate(pair, axis=0) for pair in zip(stacked_shifts(even, odd), edges)]
        product = chirped(parts, tv[b])
        results.append(
            jnp.concatenate([product0[b, :96], product0[b, 96:] + product[SPAN:], product[:SPAN]], axis=0).astype(BF16)
        )
    row, col = iota(0), iota(1)
    final = ones_where(col == (row % 4) * 64 + ((row // 4) % 8) * 8 + row // 32)
    copies = []
    for h in range(2):
        for j in range(2):
            rows = slice(128 * h + 64 * j, 128 * h + 64 * j + 64)
            block = jnp.concatenate(
                [
                    jnp.concatenate([results[b][rows, half * 128 + q * 256 : half * 128 + q * 256 + 128] for q in range(2)], axis=1)
                    for half in range(2) for b in range(2)
                ],
                axis=0,
            )
            block = dot(final, block).astype(BF16)
            for q in range(2):
                for k in range(8):
                    start = 512 * h + 64 * k + 32 * j
                    outv[q, start : start + 32, :] = block[32 * k : 32 * k + 32, q * 128 : q * 128 + 128]
        done = pl.ds(512 * h, 512)
        copies.append(pltpu.make_async_copy(outv.at[:, done], out.at[:, done], out_sem.at[h]))
        copies[-1].start()
    for copy in copies + [band_copy]:
        copy.wait()


def in_hbm(array):
    return pltpu.with_memory_space_constraint(array, pltpu.HBM)


def on_device(voltages, weights, flags, dm_index):
    hbm = pl.BlockSpec(memory_space=pl.ANY)
    vmem = pl.BlockSpec(memory_space=pltpu.VMEM)
    dma = pltpu.SemaphoreType.DMA
    params = dict(vmem_limit_bytes=24 * 1024 * 1024)
    beams, tables, dft, proto, product0, last0, power0 = pl.pallas_call(
        body,
        out_shape=(
            jax.ShapeDtypeStruct((PARTS, 64, 2, 8, SPAN), BF16),
            jax.ShapeDtypeStruct((2, NBLOCK * CHANNELS, 512), BF16),
            jax.ShapeDtypeStruct((512, 512), BF16),
            jax.ShapeDtypeStruct((TAPS, 512), F32),
            jax.ShapeDtypeStruct((2, SPAN, 512), F32),
            jax.ShapeDtypeStruct((2, 88, 512), F32),
            jax.ShapeDtypeStruct((2, 512), F32),
        ),
        in_specs=[hbm] * 7,
        out_specs=(vmem,) * 7,
        scratch_shapes=[
            pltpu.VMEM((16, 4, 2, 2, 16, 256), BF16),
            pltpu.VMEM((PARTS, 4, 4, 4, 4, 8, SPAN), BF16),
            pltpu.VMEM((PARTS, 4, 4, 4, 2, 4, 8, SPAN), BF16),
            pltpu.VMEM((PARTS, 64, 2, 4, 8, SPAN), BF16),
            pltpu.VMEM((2, 2, 256, 1024), BF16),
            pltpu.VMEM((DMS, 16, 512), F32),
            pltpu.VMEM((1, 64), jnp.int32),
            pltpu.SMEM((2,), jnp.int32),
            pltpu.VMEM((2, 256, 2 * SPAN), BF16),
            pltpu.VMEM((PARTS, 64, 8, SPAN), BF16),
            pltpu.VMEM((PARTS, 64, 2, 8, SPAN), BF16),
            pltpu.VMEM((16, 256), F32),
            pltpu.VMEM((2, 512, SPAN), BF16),
            pltpu.VMEM((2, 88 + SPAN, 512), F32),
            pltpu.VMEM((SPAN + 32, 512), BF16),
            pltpu.VMEM((SPAN + 16, 512), BF16),
            pltpu.VMEM((2, 256, 2 * SPAN), F32),
            dma((8,)),
            pltpu.SemaphoreType.REGULAR,
            dma,
            dma,
            *[dma((PARTS,)) for _ in range(4)],
            dma((PARTS, 4)),
            dma((PARTS,)),
            dma((30,)),
            dma,
            dma,
            *[
                pltpu.VMEM((PARTS,) + shape + (2, 4, 8, SPAN), BF16)
                for shape in [(3, 3), (3, 3), (3, 3), (3,), (3,), (3,), ()]
            ],
        ],
        compiler_params=pltpu.CompilerParams(collective_id=0, has_side_effects=True, **params),
        name="beamform",
    )(
        in_hbm(voltages.reshape(16, 4, 2, 2, 16, TIME)),
        in_hbm(weights),
        in_hbm(flags),
        in_hbm(dm_index),
        in_hbm(jnp.asarray(chirp_rows()).astype(BF16).astype(F32)),
        in_hbm(jnp.asarray(dft_rows()).astype(BF16)),
        in_hbm(jnp.asarray(prototype())),
    )
    dedispersed, bandpass = pl.pallas_call(
        tail,
        out_shape=(
            jax.ShapeDtypeStruct((2, 2 * TIME * 2, 128), BF16),
            jax.ShapeDtypeStruct((2, CHANNELS), F32),
        ),
        in_specs=[vmem] * 7,
        out_specs=(hbm, hbm),
        scratch_shapes=[
            pltpu.VMEM((2, 512, SPAN), BF16),
            pltpu.VMEM((2, 88 + SPAN, 512), F32),
            *[pltpu.VMEM((SPAN + 32, 512), BF16) for _ in range(2)],
            *[pltpu.VMEM((SPAN + 16, 512), BF16) for _ in range(2)],
            *[pltpu.VMEM((NBLOCK, 32, 512), BF16) for _ in range(2)],
            pltpu.VMEM((2, 2 * TIME * 2, 128), BF16),
            pltpu.VMEM((2, CHANNELS), F32),
            dma((3,)),
        ],
        compiler_params=pltpu.CompilerParams(**params),
        name="synthesis",
    )(
        beams.reshape(PARTS, 1024, SPAN),
        tables,
        dft,
        proto,
        product0,
        last0,
        power0,
    )
    dedispersed = dedispersed.reshape(2, 512, 2, 128).transpose(0, 2, 1, 3).reshape(2, 2, TIME * CHANNELS)
    return dedispersed, bandpass


def solution(mesh):
    return jax.shard_map(
        on_device,
        mesh=mesh,
        in_specs=(
            P(None, ("stn", "chan"), None, None),
            P(None, ("stn", "chan"), None, None),
            P(("stn", "chan"), None),
            P(("stn", "chan")),
        ),
        out_specs=(P(None, ("stn", "chan"), None), P(("stn", "chan"), None)),
        check_vma=False,
    )
```

```python
import math
import random

import jax
import jax.numpy as jnp
import numpy as np
from jax import lax
from jax.experimental import pallas as pl
from jax.experimental.pallas import tpu as pltpu
from jax.sharding import PartitionSpec as P

CHANNELS = 256
BEAMS = 256
INPUTS = 1024
TIME = 256
TAPS = 12
CHIRP = 1024
DMS = 16
NBLOCK = CHIRP // CHANNELS + 1
DEVICES = 128
CHAN_AXIS = 16
PARTS = 2
SPAN = TIME // PARTS
MESH = pl.DeviceIdType.MESH
BF16 = jnp.bfloat16
F32 = jnp.float32


def dft_rows():
    order = np.arange(CHANNELS)
    angle = 2.0 * math.pi / CHANNELS * (order[:, None] * order[None, :] % CHANNELS)
    cosine = np.cos(angle) / math.sqrt(CHANNELS)
    sine = np.sin(angle) / math.sqrt(CHANNELS)
    return np.block([[cosine, sine], [-sine, cosine]]).astype(np.float32)


def prototype():
    counter = np.arange(TAPS * CHANNELS, dtype=np.float64)
    offset = (counter + 0.5) / CHANNELS - TAPS / 2.0
    window = 0.54 + 0.46 * np.cos(math.pi * offset / (TAPS / 2.0))
    taps = (np.sinc(offset) * window).reshape(TAPS, CHANNELS)
    return np.concatenate([taps, taps], axis=1).astype(np.float32)


def chirp_rows():
    dms = np.arange(DMS, dtype=np.int64)[:, None, None]
    lag = np.arange(NBLOCK)[None, :, None] * CHANNELS + CHANNELS - 1 - np.arange(2 * CHANNELS)[None, None, :]
    valid = (lag >= 0) & (lag < CHIRP)
    lag = np.clip(lag, 0, CHIRP - 1)
    angle = math.pi * ((dms + 1) * lag * lag % (2 * DMS * CHIRP)) / (DMS * CHIRP)
    real = np.where(valid, np.cos(angle), 0.0) / math.sqrt(CHIRP)
    imag = np.where(valid, np.sin(angle), 0.0) / math.sqrt(CHIRP)
    rows = np.concatenate([real, imag, np.zeros((DMS, 6, 2 * CHANNELS))], axis=1)
    return rows.astype(np.float32)


def iota(axis, shape=(256, 256)):
    return lax.broadcasted_iota(jnp.int32, shape, axis)


def ones_where(condition):
    return jnp.where(condition, 1.0, 0.0).astype(BF16)


def dot(a, b):
    return jnp.dot(a, b, preferred_element_type=F32)


def exchange_order():
    left = [(dz, dy, dx) for dz in range(4) for dy in range(4) for dx in range(4)]
    random.Random(7).shuffle(left)
    hops, ordered = [0, 0, 0], []
    while left:
        def uneven(step):
            return sum((done + min(d, 4 - d) - len(ordered) - 1) ** 2 for done, d in zip(hops, step))

        best = min(left, key=uneven)
        left.remove(best)
        ordered.append(best)
        hops = [done + min(d, 4 - d) for done, d in zip(hops, best)]
    return ordered


def body(
    volt, wgt, flags, dm, chirps, dft, proto, recv2, tables, dftv, protov, product0, last0, power0,
    vin, give, send, recv, win, chv, flagv, dmv, beams, give2, send2, keep, ordered, padded, even, odd, acc,
    load_sem, plane_sem, given, given2, sent, sent2, sibling_sem, sibling_sem2, recv_sem, recv_sem2, pack_sem, packs_sent, relays_sent, *stages,
):
    x = lax.rem(lax.axis_index("chan"), 4)
    y = lax.axis_index("chan") // 4
    z = lax.axis_index("stn") // 2
    core = lax.rem(lax.axis_index("stn"), 2)
    chip = z * CHAN_AXIS + lax.axis_index("chan")
    sibling = (z * 2 + 1 - core, lax.axis_index("chan"))

    turn = 1 + 2 * core
    zs = [lax.rem(z + dz * turn, 4) for dz in range(4)]
    xs = [lax.rem(x + dx * turn, 4) for dx in range(4)]
    ys = [lax.rem(y + dy * turn, 4) * 4 for dy in range(4)]

    flag_load = pltpu.make_async_copy(flags, flagv, load_sem.at[0])
    flag_load.start()
    volt_loads = [
        pltpu.make_async_copy(volt.at[:, :, number], vin.at[:, :, number], load_sem.at[n])
        for n, number in ((1, 1 - core), (2, core))
    ]
    for load in volt_loads:
        load.start()

    barrier = pltpu.get_barrier_semaphore()
    line = [(zs[dz] * 2 + core, ys[0] + x) for dz in range(1, 4)]
    plane = [(z * 2 + core, ys[dy] + xs[dx]) for dy in range(4) for dx in range(4) if (dy, dx) != (0, 0)]
    greeted = [sibling] + line + plane
    for peer in greeted:
        pl.semaphore_signal(barrier, inc=1, device_id=peer, device_id_type=MESH)

    def hand_over(part, give, send, given, sibling_sem):
        pltpu.make_async_remote_copy(
            src_ref=give.at[part],
            dst_ref=send.at[part, :, :, :, core] if len(send.shape) == 8 else send.at[part, :, core],
            send_sem=given,
            recv_sem=sibling_sem.at[part],
            device_id=sibling,
            device_id_type=MESH,
        ).start()

    def exchange(part, send, landing, sibling_sem, sent, recv_sem):
        share = send.at[part, :, 1 - core]
        pltpu.make_async_copy(share, share, sibling_sem.at[part]).wait()
        pltpu.make_async_copy(send.at[part, chip], landing, recv_sem.at[part]).start()
        for dz, dy, dx in exchange_order():
            if (dz, dy, dx) != (0, 0, 0):
                chan = ys[dy] + xs[dx]
                pltpu.make_async_remote_copy(
                    src_ref=send.at[part, zs[dz] * CHAN_AXIS + chan],
                    dst_ref=landing,
                    send_sem=sent.at[part],
                    recv_sem=recv_sem.at[part],
                    device_id=(zs[dz] * 2 + core, chan),
                    device_id_type=MESH,
                ).start()

    by_z, by_x, by_y, by_xz, by_yz, by_xy, by_xyz = stages

    def place(steps):
        dz, dy, dx = steps
        return zs[dz % 4] * 2 + core, ys[dy % 4] + xs[dx % 4]

    def packs(part):
        near = (-1, 0, 1)
        listed = []
        for m in range(3):
            listed.append(((3, m, slice(0, 3)), by_z.at[part, m], (1, 0, 0), [(1, m - 1, d) for d in near]))
            listed.append(((m, slice(0, 3), 3), by_x.at[part, m], (0, 0, 1), [(m - 1, d, 1) for d in near]))
            listed.append(((m, 3, slice(0, 3)), by_y.at[part, m], (0, 1, 0), [(m - 1, 1, d) for d in near]))
            listed.append(((m, 3, 3), by_xy.at[part, m], (0, 1, 1), [(m - 1, 1, 1)]))
        listed.append(((3, slice(0, 3), 3), by_xz.at[part], (1, 0, 1), [(1, d, 1) for d in near]))
        listed.append(((3, 3, slice(0, 3)), by_yz.at[part], (1, 1, 0), [(1, 1, d) for d in near]))
        listed.append(((3, 3, 3), by_xyz.at[part], (1, 1, 1), [(1, 1, 1)]))
        return [(15 * part + n, *pack) for n, pack in enumerate(listed)]

    def send_packs(part):
        share = send.at[part, :, :, :, 1 - core]
        pltpu.make_async_copy(share, share, sibling_sem.at[part]).wait()
        for n, at, stage, steps, _ in packs(part):
            pltpu.make_async_remote_copy(
                src_ref=send.at[part, at[0], at[1], at[2]],
                dst_ref=stage,
                send_sem=packs_sent,
                recv_sem=pack_sem.at[n],
                device_id=place(steps),
                device_id_type=MESH,
            ).start()

    def send_direct(part):
        pltpu.make_async_copy(send.at[part, 1, 1, 1], recv.at[part, chip], recv_sem.at[part, 0]).start()
        for steps in exchange_order():
            if 2 not in steps and steps != (0, 0, 0):
                at = [(d + 1) % 4 for d in steps]
                pltpu.make_async_remote_copy(
                    src_ref=send.at[part, at[0], at[1], at[2]],
                    dst_ref=recv.at[part, chip],
                    send_sem=sent.at[part],
                    recv_sem=recv_sem.at[part, steps[0]],
                    device_id=place(steps),
                    device_id_type=MESH,
                ).start()

    def relay_packs(part, some=slice(None)):
        for n, _, stage, steps, onward in packs(part)[some]:
            pltpu.make_async_copy(stage, stage, pack_sem.at[n]).wait()
            dz, dy, dx = (-d % 4 for d in steps)
            origin = zs[dz] * CHAN_AXIS + ys[dy] + xs[dx]
            for m, further in enumerate(onward):
                pltpu.make_async_remote_copy(
                    src_ref=stage.at[m] if len(onward) > 1 else stage,
                    dst_ref=recv.at[part, origin],
                    send_sem=relays_sent,
                    recv_sem=recv_sem.at[part, (steps[0] + further[0]) % 4],
                    device_id=place(further),
                    device_id_type=MESH,
                ).start()

    flag_load.wait()
    row, col = iota(0), iota(1)
    hits = ones_where(iota(0, (256, 64)) == flagv[...])
    count = dot(hits, jnp.ones((64, 256), BF16))
    keep_rows = ones_where((count < 0.5) & (row % 16 == col % 16))
    keep[...] = dot(ones_where(iota(1, (16, 256)) // 16 == iota(0, (16, 256))), keep_rows)

    def sort_out(number):
        way = 1 + 2 * number
        there = (row // 128) * 8 + ((x + (row // 32 + 3) % 4 * way) % 4) * 2 + (row // 8) % 2
        swap = jnp.where((col // 16 == ((row // 16) % 2) * 8 + row % 8) & (col % 16 == there), 1.0, 0.0)
        for zz in range(4):
            for half in range(2):
                block = vin[:, zz, number, half].reshape(256, 256)
                mine = (swap * keep[pl.ds((zz * 2 + number) * 2 + half, 1), :]).astype(BF16)
                sorted_block = dot(mine, block).astype(BF16)
                for one in range(2):
                    mz = lax.rem((zz + 4 - z) * way + 1, 4)
                    my = lax.rem((half * 2 + one + 4 - y) * way + 1, 4)
                    yield mz, my, sorted_block[one * 128 : one * 128 + 128].reshape(4, 4, 8, 256)

    volt_loads[0].wait()
    for mz, my, block in sort_out(1 - core):
        for part in range(PARTS):
            give[part, mz, my] = block[..., part * SPAN : part * SPAN + SPAN]
    pl.semaphore_wait(barrier, len(greeted))
    for peer in line:
        pl.semaphore_signal(plane_sem, inc=1, device_id=peer, device_id_type=MESH)
    for part in range(PARTS):
        hand_over(part, give, send, given, sibling_sem)
    volt_loads[1].wait()
    for mz, my, block in sort_out(core):
        for part in range(PARTS):
            send[part, mz, my, :, core] = block[..., part * SPAN : part * SPAN + SPAN]
    loads = [
        pltpu.make_async_copy(source, target, load_sem.at[n])
        for n, (source, target) in enumerate(
            ((wgt, win), (dm, dmv), (chirps, chv), (dft, dftv), (proto, protov)), 3
        )
    ]
    for load in loads:
        load.start()
    pl.semaphore_wait(plane_sem, len(line))
    send_packs(0)
    send_direct(0)
    send_packs(1)
    relay_packs(0)
    send_direct(1)
    relay_packs(1, slice(0, 8))
    for load in loads:
        load.wait()

    def toeplitz(n, carry):
        b, block = n // NBLOCK, lax.rem(n, NBLOCK)
        for part in range(2):
            wide = jnp.broadcast_to(chv[dmv[b], pl.ds(part * NBLOCK + block, 1), :], (8, 2 * CHANNELS))
            eight = pltpu.roll(wide, CHANNELS + 1, 1, stride=1, stride_axis=0)
            for k in range(0, CHANNELS, 16):
                both = [pltpu.roll(eight, k + i, 1)[:, :CHANNELS] if k + i else eight[:, :CHANNELS] for i in (0, 8)]
                rows = pl.ds(pl.multiple_of(block * CHANNELS + k, 16), 16)
                tables[b, rows, part * CHANNELS : (part + 1) * CHANNELS] = jnp.concatenate(both, axis=0).astype(BF16)
        return carry


    to_device = lax.rem(core + row // 128, 2) * 16 + (row // 8) % 16
    order = ones_where(
        (col // 128 == row % 2) & ((col // 64) % 2 == (row // 2) % 2) & (col % 64 == to_device * 2 + (row // 4) % 2)
    )
    for part in range(PARTS):
        for n, dz in enumerate((3, 0, 1, 2)):
            source = zs[-dz % 4]
            arrived = recv.at[part, pl.ds(pl.multiple_of(source * 16, 16), 16)]
            pltpu.make_async_copy(arrived, arrived, recv_sem.at[part, dz]).wait()
            for c in range(2):
                real, imag, weight_real, weight_imag = [], [], [], []
                for number in range(2):
                    chips = pl.ds(pl.multiple_of(source * 16, 16), 16)
                    inputs = pl.ds(pl.multiple_of((source * 2 + number) * 128, 128), 128)
                    real.append(recv[part, chips, number, c].reshape(128, SPAN))
                    imag.append(recv[part, chips, number, 2 + c].reshape(128, SPAN))
                    weight_real.append(win[0, c, :, inputs])
                    weight_imag.append(win[1, c, :, inputs])
                parts = jnp.concatenate(
                    [
                        jnp.concatenate(real + [-half for half in imag], axis=0),
                        jnp.concatenate(imag + real, axis=0),
                    ],
                    axis=1,
                )
                product = dot(jnp.concatenate(weight_real + weight_imag, axis=1), parts)
                if n == 0:
                    acc[c] = product
                elif n < 3:
                    acc[c] += product
                else:
                    beams[c] = (acc[c] + product).astype(BF16)
        for zz in range(4):
            rows = slice(zz * 64, zz * 64 + 64)
            block = jnp.concatenate([beams[c, rows, q * SPAN : q * SPAN + SPAN] for c in range(2) for q in range(2)], axis=0)
            block = dot(order, block).astype(BF16)
            send2[part, zz * 16 : zz * 16 + 16, core] = block[:128].reshape(16, 8, SPAN)
            give2[part, zz * 16 : zz * 16 + 16] = block[128:].reshape(16, 8, SPAN)
        hand_over(part, give2, send2, given2, sibling_sem2)
        if part == 0:
            relay_packs(1, slice(8, None))
        else:
            lax.fori_loop(0, 2 * NBLOCK, toeplitz, 0)
        exchange(part, send2, recv2.at[part, chip], sibling_sem2, sent2, recv_sem2)

    arrived = recv2.at[0]
    pltpu.make_async_copy(arrived, arrived, recv_sem2.at[0]).wait()
    for b, power, last in front(
        lambda n: recv2[0, n * 16 : n * 16 + 16].reshape(256, SPAN), lambda b: 0.0, dftv, protov, ordered, padded
    ):
        power0[b : b + 1, :] = power
        last0[b] = last
    for b in range(2):
        for n in range(4):
            lanes, series = synthesise(b, n, protov, padded)
            store_shifted(series, lanes, even, odd)
        product0[b] = chirped(stacked_shifts(even, odd), tables[b])

    for blocks, sem in ((give, given), (give2, given2)):
        pltpu.make_async_copy(blocks, blocks, sem).wait()
    for sem in (packs_sent, relays_sent):
        for part in range(PARTS):
            blocks = recv.at[part, 0:37]
            pltpu.make_async_copy(blocks, blocks, sem).wait()
    for part in range(PARTS):
        for blocks, sem in ((recv.at[part, 0:26], sent), (send2.at[part, 0:63], sent2)):
            pltpu.make_async_copy(blocks, blocks, sem.at[part]).wait()
    arrived = recv2.at[1]
    pltpu.make_async_copy(arrived, arrived, recv_sem2.at[1]).wait()


def front(chunk, before_first, dftv, protov, xs, padded):
    row, col = iota(0), iota(1)
    sort = ones_where(col == ((row % 32) // 2 * 2 + (row % 64) // 32) * 8 + (row // 64) * 2 + row % 2)
    spread = ones_where(iota(1, (SPAN, SPAN)) == (iota(0, (SPAN, SPAN)) % 8) * 16 + iota(0, (SPAN, SPAN)) // 8)
    for n in range(4):
        block = dot(sort, chunk(n)).astype(BF16)
        for k in range(4):
            xs[k // 2, (k % 2) * 256 + n * 64 : (k % 2) * 256 + n * 64 + 64, :] = block[k * 64 : k * 64 + 64]
    for b in range(2):
        turned = lax.dot_general(spread, xs[b], (((1,), (1,)), ((), ())), preferred_element_type=F32)
        power = jnp.sum(turned * turned, axis=0, keepdims=True)
        spectra = dot(turned.astype(BF16), dftv[...])
        last = spectra[SPAN - 88 :]
        first = iota(0, (88, 512)) % 8 == 0
        padded[b, 0:88, :] = jnp.where(first, before_first(b), pltpu.roll(last, 1, 0))
        padded[b, 88 : 88 + SPAN, :] = spectra
        yield b, power, pltpu.roll(last, 81, 0)


def synthesise(b, n, protov, padded):
    lanes = slice(n * 128, n * 128 + 128)
    series = protov[0:1, lanes] * padded[b, 88 : 88 + SPAN, lanes]
    for tap in range(1, TAPS):
        series = series + protov[tap : tap + 1, lanes] * padded[b, 88 - 8 * tap : 88 - 8 * tap + SPAN, lanes]
    return lanes, series


def store_shifted(series, lanes, even, odd):
    after = jnp.where(iota(0, (32, 128)) % 8 == 7, 0.0, pltpu.roll(series[:32], 31, 0))
    even[0:SPAN, lanes] = series.astype(BF16)
    even[SPAN : SPAN + 32, lanes] = after.astype(BF16)
    odd[0 : SPAN + 16, lanes] = jnp.concatenate([series[8:], after[:24]], axis=0).astype(BF16)


def stacked_shifts(even, odd):
    shifted = [even[0:SPAN], odd[0:SPAN], even[16 : 16 + SPAN], odd[16 : 16 + SPAN], even[32 : 32 + SPAN]]
    return [jnp.concatenate([block[:, p * 256 : p * 256 + 256] for block in shifted], axis=1) for p in range(2)]


def chirped(parts, table):
    product = dot(jnp.concatenate(parts, axis=0), table)
    rows = product.shape[0] // 2
    real = product[:rows, :256] + product[rows:, 256:]
    imag = product[rows:, :256] - product[:rows, 256:]
    return jnp.concatenate([real, imag], axis=1)


def tail(
    xv, tv, dftv, protov, product0, last0, power0, out, band,
    xs, padded, even0, even1, odd0, odd1, over0, over1, outv, bandv, out_sem,
):
    band_copy = pltpu.make_async_copy(bandv, band, out_sem.at[2])
    for b, power, _ in front(lambda n: xv[1, n * 256 : n * 256 + 256, :], lambda b: last0[b], dftv, protov, xs, padded):
        power = (power + power0[b : b + 1, :]) * (1.0 / TIME)
        bandv[b : b + 1, :] = power[:, :256] + power[:, 256:]
    band_copy.start()
    results = []
    for b, (even, odd, over) in enumerate(((even0, odd0, over0), (even1, odd1, over1))):
        for n in range(4):
            lanes, series = synthesise(b, n, protov, padded)
            store_shifted(series, lanes, even, odd)
            over_edge = jnp.where(iota(0, (32, 128)) % 8 == 7, pltpu.roll(series[:32], 7, 0), 0.0)
            for blk in range(NBLOCK):
                seen = [over_edge[: 8 * blk]] if blk else []
                unseen = [jnp.zeros((32 - 8 * blk, 128), F32)] if blk < 4 else []
                over[blk, :, lanes] = jnp.concatenate(unseen + seen, axis=0).astype(BF16)
        edges = [
            jnp.concatenate([over[blk, :, p * 256 : p * 256 + 256] for blk in range(NBLOCK)], axis=1) for p in range(2)
        ]
        parts = [jnp.concatenate(pair, axis=0) for pair in zip(stacked_shifts(even, odd), edges)]
        product = chirped(parts, tv[b])
        results.append(
            jnp.concatenate([product0[b, :96], product0[b, 96:] + product[SPAN:], product[:SPAN]], axis=0).astype(BF16)
        )
    row, col = iota(0), iota(1)
    final = ones_where(col == (row % 4) * 64 + ((row // 4) % 8) * 8 + row // 32)
    copies = []
    for h in range(2):
        for j in range(2):
            rows = slice(128 * h + 64 * j, 128 * h + 64 * j + 64)
            block = jnp.concatenate(
                [
                    jnp.concatenate([results[b][rows, half * 128 + q * 256 : half * 128 + q * 256 + 128] for q in range(2)], axis=1)
                    for half in range(2) for b in range(2)
                ],
                axis=0,
            )
            block = dot(final, block).astype(BF16)
            for q in range(2):
                for k in range(8):
                    start = 512 * h + 64 * k + 32 * j
                    outv[q, start : start + 32, :] = block[32 * k : 32 * k + 32, q * 128 : q * 128 + 128]
        done = pl.ds(512 * h, 512)
        copies.append(pltpu.make_async_copy(outv.at[:, done], out.at[:, done], out_sem.at[h]))
        copies[-1].start()
    for copy in copies + [band_copy]:
        copy.wait()


def in_hbm(array):
    return pltpu.with_memory_space_constraint(array, pltpu.HBM)


def on_device(voltages, weights, flags, dm_index):
    hbm = pl.BlockSpec(memory_space=pl.ANY)
    vmem = pl.BlockSpec(memory_space=pltpu.VMEM)
    dma = pltpu.SemaphoreType.DMA
    params = dict(vmem_limit_bytes=24 * 1024 * 1024)
    beams, tables, dft, proto, product0, last0, power0 = pl.pallas_call(
        body,
        out_shape=(
            jax.ShapeDtypeStruct((PARTS, 64, 2, 8, SPAN), BF16),
            jax.ShapeDtypeStruct((2, NBLOCK * CHANNELS, 512), BF16),
            jax.ShapeDtypeStruct((512, 512), BF16),
            jax.ShapeDtypeStruct((TAPS, 512), F32),
            jax.ShapeDtypeStruct((2, SPAN, 512), F32),
            jax.ShapeDtypeStruct((2, 88, 512), F32),
            jax.ShapeDtypeStruct((2, 512), F32),
        ),
        in_specs=[hbm] * 7,
        out_specs=(vmem,) * 7,
        scratch_shapes=[
            pltpu.VMEM((16, 4, 2, 2, 16, 256), BF16),
            pltpu.VMEM((PARTS, 4, 4, 4, 4, 8, SPAN), BF16),
            pltpu.VMEM((PARTS, 4, 4, 4, 2, 4, 8, SPAN), BF16),
            pltpu.VMEM((PARTS, 64, 2, 4, 8, SPAN), BF16),
            pltpu.VMEM((2, 2, 256, 1024), BF16),
            pltpu.VMEM((DMS, 16, 512), F32),
            pltpu.VMEM((1, 64), jnp.int32),
            pltpu.SMEM((2,), jnp.int32),
            pltpu.VMEM((2, 256, 2 * SPAN), BF16),
            pltpu.VMEM((PARTS, 64, 8, SPAN), BF16),
            pltpu.VMEM((PARTS, 64, 2, 8, SPAN), BF16),
            pltpu.VMEM((16, 256), F32),
            pltpu.VMEM((2, 512, SPAN), BF16),
            pltpu.VMEM((2, 88 + SPAN, 512), F32),
            pltpu.VMEM((SPAN + 32, 512), BF16),
            pltpu.VMEM((SPAN + 16, 512), BF16),
            pltpu.VMEM((2, 256, 2 * SPAN), F32),
            dma((8,)),
            pltpu.SemaphoreType.REGULAR,
            dma,
            dma,
            *[dma((PARTS,)) for _ in range(4)],
            dma((PARTS, 4)),
            dma((PARTS,)),
            dma((30,)),
            dma,
            dma,
            *[
                pltpu.VMEM((PARTS,) + shape + (2, 4, 8, SPAN), BF16)
                for shape in [(3, 3), (3, 3), (3, 3), (3,), (3,), (3,), ()]
            ],
        ],
        compiler_params=pltpu.CompilerParams(collective_id=0, has_side_effects=True, **params),
        name="beamform",
    )(
        in_hbm(voltages.reshape(16, 4, 2, 2, 16, TIME)),
        in_hbm(weights),
        in_hbm(flags),
        in_hbm(dm_index),
        in_hbm(jnp.asarray(chirp_rows()).astype(BF16).astype(F32)),
        in_hbm(jnp.asarray(dft_rows()).astype(BF16)),
        in_hbm(jnp.asarray(prototype())),
    )
    dedispersed, bandpass = pl.pallas_call(
        tail,
        out_shape=(
            jax.ShapeDtypeStruct((2, 2 * TIME * 2, 128), BF16),
            jax.ShapeDtypeStruct((2, CHANNELS), F32),
        ),
        in_specs=[vmem] * 7,
        out_specs=(hbm, hbm),
        scratch_shapes=[
            pltpu.VMEM((2, 512, SPAN), BF16),
            pltpu.VMEM((2, 88 + SPAN, 512), F32),
            *[pltpu.VMEM((SPAN + 32, 512), BF16) for _ in range(2)],
            *[pltpu.VMEM((SPAN + 16, 512), BF16) for _ in range(2)],
            *[pltpu.VMEM((NBLOCK, 32, 512), BF16) for _ in range(2)],
            pltpu.VMEM((2, 2 * TIME * 2, 128), BF16),
            pltpu.VMEM((2, CHANNELS), F32),
            dma((3,)),
        ],
        compiler_params=pltpu.CompilerParams(**params),
        name="synthesis",
    )(
        beams.reshape(PARTS, 1024, SPAN),
        tables,
        dft,
        proto,
        product0,
        last0,
        power0,
    )
    dedispersed = dedispersed.reshape(2, 512, 2, 128).transpose(0, 2, 1, 3).reshape(2, 2, TIME * CHANNELS)
    return dedispersed, bandpass


def solution(mesh):
    return jax.shard_map(
        on_device,
        mesh=mesh,
        in_specs=(
            P(None, ("stn", "chan"), None, None),
            P(None, ("stn", "chan"), None, None),
            P(("stn", "chan"), None),
            P(("stn", "chan")),
        ),
        out_specs=(P(None, ("stn", "chan"), None), P(("stn", "chan"), None)),
        check_vma=False,
    )
```

```python
import math
import random

import jax
import jax.numpy as jnp
import numpy as np
from jax import lax
from jax.experimental import pallas as pl
from jax.experimental.pallas import tpu as pltpu
from jax.sharding import PartitionSpec as P

CHANNELS = 256
BEAMS = 256
INPUTS = 1024
TIME = 256
TAPS = 12
CHIRP = 1024
DMS = 16
NBLOCK = CHIRP // CHANNELS + 1
DEVICES = 128
CHAN_AXIS = 16
PARTS = 2
SPAN = TIME // PARTS
MESH = pl.DeviceIdType.MESH
BF16 = jnp.bfloat16
F32 = jnp.float32


def dft_rows():
    order = np.arange(CHANNELS)
    angle = 2.0 * math.pi / CHANNELS * (order[:, None] * order[None, :] % CHANNELS)
    cosine = np.cos(angle) / math.sqrt(CHANNELS)
    sine = np.sin(angle) / math.sqrt(CHANNELS)
    return np.block([[cosine, sine], [-sine, cosine]]).astype(np.float32)


def prototype():
    counter = np.arange(TAPS * CHANNELS, dtype=np.float64)
    offset = (counter + 0.5) / CHANNELS - TAPS / 2.0
    window = 0.54 + 0.46 * np.cos(math.pi * offset / (TAPS / 2.0))
    taps = (np.sinc(offset) * window).reshape(TAPS, CHANNELS)
    return np.concatenate([taps, taps], axis=1).astype(np.float32)


def chirp_rows():
    dms = np.arange(DMS, dtype=np.int64)[:, None, None]
    lag = np.arange(NBLOCK)[None, :, None] * CHANNELS + CHANNELS - 1 - np.arange(2 * CHANNELS)[None, None, :]
    valid = (lag >= 0) & (lag < CHIRP)
    lag = np.clip(lag, 0, CHIRP - 1)
    angle = math.pi * ((dms + 1) * lag * lag % (2 * DMS * CHIRP)) / (DMS * CHIRP)
    real = np.where(valid, np.cos(angle), 0.0) / math.sqrt(CHIRP)
    imag = np.where(valid, np.sin(angle), 0.0) / math.sqrt(CHIRP)
    rows = np.concatenate([real, imag, np.zeros((DMS, 6, 2 * CHANNELS))], axis=1)
    return rows.astype(np.float32)


def iota(axis, shape=(256, 256)):
    return lax.broadcasted_iota(jnp.int32, shape, axis)


def ones_where(condition):
    return jnp.where(condition, 1.0, 0.0).astype(BF16)


def dot(a, b):
    return jnp.dot(a, b, preferred_element_type=F32)


def exchange_order():
    left = [(dz, dy, dx) for dz in range(4) for dy in range(4) for dx in range(4)]
    random.Random(7).shuffle(left)
    hops, ordered = [0, 0, 0], []
    while left:
        def uneven(step):
            return sum((done + min(d, 4 - d) - len(ordered) - 1) ** 2 for done, d in zip(hops, step))

        best = min(left, key=uneven)
        left.remove(best)
        ordered.append(best)
        hops = [done + min(d, 4 - d) for done, d in zip(hops, best)]
    return ordered


def body(
    volt, wgt, flags, dm, chirps, dft, proto, recv2, tables, dftv, protov, product0, last0, power0,
    vin, give, send, recv, win, chv, flagv, dmv, beams, give2, send2, keep, ordered, padded, even, odd, acc,
    load_sem, plane_sem, given, given2, sent, sent2, sibling_sem, sibling_sem2, recv_sem, recv_sem2, pack_sem, packs_sent, relays_sent, *stages,
):
    x = lax.rem(lax.axis_index("chan"), 4)
    y = lax.axis_index("chan") // 4
    z = lax.axis_index("stn") // 2
    core = lax.rem(lax.axis_index("stn"), 2)
    chip = z * CHAN_AXIS + lax.axis_index("chan")
    sibling = (z * 2 + 1 - core, lax.axis_index("chan"))

    turn = 1 + 2 * core
    zs = [lax.rem(z + dz * turn, 4) for dz in range(4)]
    xs = [lax.rem(x + dx * turn, 4) for dx in range(4)]
    ys = [lax.rem(y + dy * turn, 4) * 4 for dy in range(4)]

    flag_load = pltpu.make_async_copy(flags, flagv, load_sem.at[0])
    flag_load.start()
    volt_loads = [
        pltpu.make_async_copy(volt.at[:, :, number], vin.at[:, :, number], load_sem.at[n])
        for n, number in ((1, 1 - core), (2, core))
    ]
    for load in volt_loads:
        load.start()

    barrier = pltpu.get_barrier_semaphore()
    line = [(zs[dz] * 2 + core, ys[0] + x) for dz in range(1, 4)]
    plane = [(z * 2 + core, ys[dy] + xs[dx]) for dy in range(4) for dx in range(4) if (dy, dx) != (0, 0)]
    greeted = [sibling] + line + plane
    for peer in greeted:
        pl.semaphore_signal(barrier, inc=1, device_id=peer, device_id_type=MESH)

    def hand_over(part, give, send, given, sibling_sem):
        pltpu.make_async_remote_copy(
            src_ref=give.at[part],
            dst_ref=send.at[part, :, :, :, core] if len(send.shape) == 8 else send.at[part, :, core],
            send_sem=given,
            recv_sem=sibling_sem.at[part],
            device_id=sibling,
            device_id_type=MESH,
        ).start()

    def exchange(part, send, landing, sibling_sem, sent, recv_sem):
        share = send.at[part, :, 1 - core]
        pltpu.make_async_copy(share, share, sibling_sem.at[part]).wait()
        pltpu.make_async_copy(send.at[part, chip], landing, recv_sem.at[part]).start()
        for dz, dy, dx in exchange_order():
            if (dz, dy, dx) != (0, 0, 0):
                chan = ys[dy] + xs[dx]
                pltpu.make_async_remote_copy(
                    src_ref=send.at[part, zs[dz] * CHAN_AXIS + chan],
                    dst_ref=landing,
                    send_sem=sent.at[part],
                    recv_sem=recv_sem.at[part],
                    device_id=(zs[dz] * 2 + core, chan),
                    device_id_type=MESH,
                ).start()

    by_z, by_x, by_y, by_xz, by_yz, by_xy, by_xyz = stages

    def place(steps):
        dz, dy, dx = steps
        return zs[dz % 4] * 2 + core, ys[dy % 4] + xs[dx % 4]

    def packs(part):
        near = (-1, 0, 1)
        listed = []
        for m in range(3):
            listed.append(((3, m, slice(0, 3)), by_z.at[part, m], (1, 0, 0), [(1, m - 1, d) for d in near]))
            listed.append(((m, slice(0, 3), 3), by_x.at[part, m], (0, 0, 1), [(m - 1, d, 1) for d in near]))
            listed.append(((m, 3, slice(0, 3)), by_y.at[part, m], (0, 1, 0), [(m - 1, 1, d) for d in near]))
            listed.append(((m, 3, 3), by_xy.at[part, m], (0, 1, 1), [(m - 1, 1, 1)]))
        listed.append(((3, slice(0, 3), 3), by_xz.at[part], (1, 0, 1), [(1, d, 1) for d in near]))
        listed.append(((3, 3, slice(0, 3)), by_yz.at[part], (1, 1, 0), [(1, 1, d) for d in near]))
        listed.append(((3, 3, 3), by_xyz.at[part], (1, 1, 1), [(1, 1, 1)]))
        return [(15 * part + n, *pack) for n, pack in enumerate(listed)]

    def send_packs(part):
        share = send.at[part, :, :, :, 1 - core]
        pltpu.make_async_copy(share, share, sibling_sem.at[part]).wait()
        for n, at, stage, steps, _ in packs(part):
            pltpu.make_async_remote_copy(
                src_ref=send.at[part, at[0], at[1], at[2]],
                dst_ref=stage,
                send_sem=packs_sent,
                recv_sem=pack_sem.at[n],
                device_id=place(steps),
                device_id_type=MESH,
            ).start()

    def send_direct(part):
        pltpu.make_async_copy(send.at[part, 1, 1, 1], recv.at[part, chip], recv_sem.at[part, 0]).start()
        for steps in exchange_order():
            if 2 not in steps and steps != (0, 0, 0):
                at = [(d + 1) % 4 for d in steps]
                pltpu.make_async_remote_copy(
                    src_ref=send.at[part, at[0], at[1], at[2]],
                    dst_ref=recv.at[part, chip],
                    send_sem=sent.at[part],
                    recv_sem=recv_sem.at[part, steps[0]],
                    device_id=place(steps),
                    device_id_type=MESH,
                ).start()

    def relay_packs(part):
        for n, _, stage, steps, onward in packs(part):
            pltpu.make_async_copy(stage, stage, pack_sem.at[n]).wait()
            dz, dy, dx = (-d % 4 for d in steps)
            origin = zs[dz] * CHAN_AXIS + ys[dy] + xs[dx]
            for m, further in enumerate(onward):
                pltpu.make_async_remote_copy(
                    src_ref=stage.at[m] if len(onward) > 1 else stage,
                    dst_ref=recv.at[part, origin],
                    send_sem=relays_sent,
                    recv_sem=recv_sem.at[part, (steps[0] + further[0]) % 4],
                    device_id=place(further),
                    device_id_type=MESH,
                ).start()

    flag_load.wait()
    row, col = iota(0), iota(1)
    hits = ones_where(iota(0, (256, 64)) == flagv[...])
    count = dot(hits, jnp.ones((64, 256), BF16))
    keep_rows = ones_where((count < 0.5) & (row % 16 == col % 16))
    keep[...] = dot(ones_where(iota(1, (16, 256)) // 16 == iota(0, (16, 256))), keep_rows)

    def sort_out(number):
        way = 1 + 2 * number
        there = (row // 128) * 8 + ((x + (row // 32 + 3) % 4 * way) % 4) * 2 + (row // 8) % 2
        swap = jnp.where((col // 16 == ((row // 16) % 2) * 8 + row % 8) & (col % 16 == there), 1.0, 0.0)
        for zz in range(4):
            for half in range(2):
                block = vin[:, zz, number, half].reshape(256, 256)
                mine = (swap * keep[pl.ds((zz * 2 + number) * 2 + half, 1), :]).astype(BF16)
                sorted_block = dot(mine, block).astype(BF16)
                for one in range(2):
                    mz = lax.rem((zz + 4 - z) * way + 1, 4)
                    my = lax.rem((half * 2 + one + 4 - y) * way + 1, 4)
                    yield mz, my, sorted_block[one * 128 : one * 128 + 128].reshape(4, 4, 8, 256)

    volt_loads[0].wait()
    for mz, my, block in sort_out(1 - core):
        for part in range(PARTS):
            give[part, mz, my] = block[..., part * SPAN : part * SPAN + SPAN]
    pl.semaphore_wait(barrier, len(greeted))
    for peer in line:
        pl.semaphore_signal(plane_sem, inc=1, device_id=peer, device_id_type=MESH)
    for part in range(PARTS):
        hand_over(part, give, send, given, sibling_sem)
    volt_loads[1].wait()
    for mz, my, block in sort_out(core):
        for part in range(PARTS):
            send[part, mz, my, :, core] = block[..., part * SPAN : part * SPAN + SPAN]
    loads = [
        pltpu.make_async_copy(source, target, load_sem.at[n])
        for n, (source, target) in enumerate(
            ((wgt, win), (dm, dmv), (chirps, chv), (dft, dftv), (proto, protov)), 3
        )
    ]
    for load in loads:
        load.start()
    pl.semaphore_wait(plane_sem, len(line))
    send_packs(0)
    send_packs(1)
    send_direct(0)
    relay_packs(0)
    send_direct(1)
    relay_packs(1)
    for load in loads:
        load.wait()

    def toeplitz(n, carry):
        b, block = n // NBLOCK, lax.rem(n, NBLOCK)
        for part in range(2):
            wide = jnp.broadcast_to(chv[dmv[b], pl.ds(part * NBLOCK + block, 1), :], (8, 2 * CHANNELS))
            eight = pltpu.roll(wide, CHANNELS + 1, 1, stride=1, stride_axis=0)
            for k in range(0, CHANNELS, 16):
                both = [pltpu.roll(eight, k + i, 1)[:, :CHANNELS] if k + i else eight[:, :CHANNELS] for i in (0, 8)]
                rows = pl.ds(pl.multiple_of(block * CHANNELS + k, 16), 16)
                tables[b, rows, part * CHANNELS : (part + 1) * CHANNELS] = jnp.concatenate(both, axis=0).astype(BF16)
        return carry


    to_device = lax.rem(core + row // 128, 2) * 16 + (row // 8) % 16
    order = ones_where(
        (col // 128 == row % 2) & ((col // 64) % 2 == (row // 2) % 2) & (col % 64 == to_device * 2 + (row // 4) % 2)
    )
    for part in range(PARTS):
        for n, dz in enumerate((3, 0, 1, 2)):
            source = zs[-dz % 4]
            arrived = recv.at[part, pl.ds(pl.multiple_of(source * 16, 16), 16)]
            pltpu.make_async_copy(arrived, arrived, recv_sem.at[part, dz]).wait()
            for c in range(2):
                real, imag, weight_real, weight_imag = [], [], [], []
                for number in range(2):
                    chips = pl.ds(pl.multiple_of(source * 16, 16), 16)
                    inputs = pl.ds(pl.multiple_of((source * 2 + number) * 128, 128), 128)
                    real.append(recv[part, chips, number, c].reshape(128, SPAN))
                    imag.append(recv[part, chips, number, 2 + c].reshape(128, SPAN))
                    weight_real.append(win[0, c, :, inputs])
                    weight_imag.append(win[1, c, :, inputs])
                parts = jnp.concatenate(
                    [
                        jnp.concatenate(real + [-half for half in imag], axis=0),
                        jnp.concatenate(imag + real, axis=0),
                    ],
                    axis=1,
                )
                product = dot(jnp.concatenate(weight_real + weight_imag, axis=1), parts)
                if n == 0:
                    acc[c] = product
                elif n < 3:
                    acc[c] += product
                else:
                    beams[c] = (acc[c] + product).astype(BF16)
        for zz in range(4):
            rows = slice(zz * 64, zz * 64 + 64)
            block = jnp.concatenate([beams[c, rows, q * SPAN : q * SPAN + SPAN] for c in range(2) for q in range(2)], axis=0)
            block = dot(order, block).astype(BF16)
            send2[part, zz * 16 : zz * 16 + 16, core] = block[:128].reshape(16, 8, SPAN)
            give2[part, zz * 16 : zz * 16 + 16] = block[128:].reshape(16, 8, SPAN)
        hand_over(part, give2, send2, given2, sibling_sem2)
        if part == 0:
            lax.fori_loop(0, 2 * NBLOCK, toeplitz, 0)
        exchange(part, send2, recv2.at[part, chip], sibling_sem2, sent2, recv_sem2)

    arrived = recv2.at[0]
    pltpu.make_async_copy(arrived, arrived, recv_sem2.at[0]).wait()
    for b, power, last in front(
        lambda n: recv2[0, n * 16 : n * 16 + 16].reshape(256, SPAN), lambda b: 0.0, dftv, protov, ordered, padded
    ):
        power0[b : b + 1, :] = power
        last0[b] = last
    for b in range(2):
        for n in range(4):
            lanes, series = synthesise(b, n, protov, padded)
            store_shifted(series, lanes, even, odd)
        product0[b] = chirped(stacked_shifts(even, odd), tables[b])

    for blocks, sem in ((give, given), (give2, given2)):
        pltpu.make_async_copy(blocks, blocks, sem).wait()
    for sem in (packs_sent, relays_sent):
        for part in range(PARTS):
            blocks = recv.at[part, 0:37]
            pltpu.make_async_copy(blocks, blocks, sem).wait()
    for part in range(PARTS):
        for blocks, sem in ((recv.at[part, 0:26], sent), (send2.at[part, 0:63], sent2)):
            pltpu.make_async_copy(blocks, blocks, sem.at[part]).wait()
    arrived = recv2.at[1]
    pltpu.make_async_copy(arrived, arrived, recv_sem2.at[1]).wait()


def front(chunk, before_first, dftv, protov, xs, padded):
    row, col = iota(0), iota(1)
    sort = ones_where(col == ((row % 32) // 2 * 2 + (row % 64) // 32) * 8 + (row // 64) * 2 + row % 2)
    spread = ones_where(iota(1, (SPAN, SPAN)) == (iota(0, (SPAN, SPAN)) % 8) * 16 + iota(0, (SPAN, SPAN)) // 8)
    for n in range(4):
        block = dot(sort, chunk(n)).astype(BF16)
        for k in range(4):
            xs[k // 2, (k % 2) * 256 + n * 64 : (k % 2) * 256 + n * 64 + 64, :] = block[k * 64 : k * 64 + 64]
    for b in range(2):
        turned = lax.dot_general(spread, xs[b], (((1,), (1,)), ((), ())), preferred_element_type=F32)
        power = jnp.sum(turned * turned, axis=0, keepdims=True)
        spectra = dot(turned.astype(BF16), dftv[...])
        last = spectra[SPAN - 88 :]
        first = iota(0, (88, 512)) % 8 == 0
        padded[b, 0:88, :] = jnp.where(first, before_first(b), pltpu.roll(last, 1, 0))
        padded[b, 88 : 88 + SPAN, :] = spectra
        yield b, power, pltpu.roll(last, 81, 0)


def synthesise(b, n, protov, padded):
    lanes = slice(n * 128, n * 128 + 128)
    series = protov[0:1, lanes] * padded[b, 88 : 88 + SPAN, lanes]
    for tap in range(1, TAPS):
        series = series + protov[tap : tap + 1, lanes] * padded[b, 88 - 8 * tap : 88 - 8 * tap + SPAN, lanes]
    return lanes, series


def store_shifted(series, lanes, even, odd):
    after = jnp.where(iota(0, (32, 128)) % 8 == 7, 0.0, pltpu.roll(series[:32], 31, 0))
    even[0:SPAN, lanes] = series.astype(BF16)
    even[SPAN : SPAN + 32, lanes] = after.astype(BF16)
    odd[0 : SPAN + 16, lanes] = jnp.concatenate([series[8:], after[:24]], axis=0).astype(BF16)


def stacked_shifts(even, odd):
    shifted = [even[0:SPAN], odd[0:SPAN], even[16 : 16 + SPAN], odd[16 : 16 + SPAN], even[32 : 32 + SPAN]]
    return [jnp.concatenate([block[:, p * 256 : p * 256 + 256] for block in shifted], axis=1) for p in range(2)]


def chirped(parts, table):
    product = dot(jnp.concatenate(parts, axis=0), table)
    rows = product.shape[0] // 2
    real = product[:rows, :256] + product[rows:, 256:]
    imag = product[rows:, :256] - product[:rows, 256:]
    return jnp.concatenate([real, imag], axis=1)


def tail(
    xv, tv, dftv, protov, product0, last0, power0, out, band,
    xs, padded, even0, even1, odd0, odd1, over0, over1, outv, bandv, out_sem,
):
    band_copy = pltpu.make_async_copy(bandv, band, out_sem.at[2])
    for b, power, _ in front(lambda n: xv[1, n * 256 : n * 256 + 256, :], lambda b: last0[b], dftv, protov, xs, padded):
        power = (power + power0[b : b + 1, :]) * (1.0 / TIME)
        bandv[b : b + 1, :] = power[:, :256] + power[:, 256:]
    band_copy.start()
    results = []
    for b, (even, odd, over) in enumerate(((even0, odd0, over0), (even1, odd1, over1))):
        for n in range(4):
            lanes, series = synthesise(b, n, protov, padded)
            store_shifted(series, lanes, even, odd)
            over_edge = jnp.where(iota(0, (32, 128)) % 8 == 7, pltpu.roll(series[:32], 7, 0), 0.0)
            for blk in range(NBLOCK):
                seen = [over_edge[: 8 * blk]] if blk else []
                unseen = [jnp.zeros((32 - 8 * blk, 128), F32)] if blk < 4 else []
                over[blk, :, lanes] = jnp.concatenate(unseen + seen, axis=0).astype(BF16)
        edges = [
            jnp.concatenate([over[blk, :, p * 256 : p * 256 + 256] for blk in range(NBLOCK)], axis=1) for p in range(2)
        ]
        parts = [jnp.concatenate(pair, axis=0) for pair in zip(stacked_shifts(even, odd), edges)]
        product = chirped(parts, tv[b])
        results.append(
            jnp.concatenate([product0[b, :96], product0[b, 96:] + product[SPAN:], product[:SPAN]], axis=0).astype(BF16)
        )
    row, col = iota(0), iota(1)
    final = ones_where(col == (row % 4) * 64 + ((row // 4) % 8) * 8 + row // 32)
    copies = []
    for h in range(2):
        for j in range(2):
            rows = slice(128 * h + 64 * j, 128 * h + 64 * j + 64)
            block = jnp.concatenate(
                [
                    jnp.concatenate([results[b][rows, half * 128 + q * 256 : half * 128 + q * 256 + 128] for q in range(2)], axis=1)
                    for half in range(2) for b in range(2)
                ],
                axis=0,
            )
            block = dot(final, block).astype(BF16)
            for q in range(2):
                for k in range(8):
                    start = 512 * h + 64 * k + 32 * j
                    outv[q, start : start + 32, :] = block[32 * k : 32 * k + 32, q * 128 : q * 128 + 128]
        done = pl.ds(512 * h, 512)
        copies.append(pltpu.make_async_copy(outv.at[:, done], out.at[:, done], out_sem.at[h]))
        copies[-1].start()
    for copy in copies + [band_copy]:
        copy.wait()


def in_hbm(array):
    return pltpu.with_memory_space_constraint(array, pltpu.HBM)


def on_device(voltages, weights, flags, dm_index):
    hbm = pl.BlockSpec(memory_space=pl.ANY)
    vmem = pl.BlockSpec(memory_space=pltpu.VMEM)
    dma = pltpu.SemaphoreType.DMA
    params = dict(vmem_limit_bytes=24 * 1024 * 1024)
    beams, tables, dft, proto, product0, last0, power0 = pl.pallas_call(
        body,
        out_shape=(
            jax.ShapeDtypeStruct((PARTS, 64, 2, 8, SPAN), BF16),
            jax.ShapeDtypeStruct((2, NBLOCK * CHANNELS, 512), BF16),
            jax.ShapeDtypeStruct((512, 512), BF16),
            jax.ShapeDtypeStruct((TAPS, 512), F32),
            jax.ShapeDtypeStruct((2, SPAN, 512), F32),
            jax.ShapeDtypeStruct((2, 88, 512), F32),
            jax.ShapeDtypeStruct((2, 512), F32),
        ),
        in_specs=[hbm] * 7,
        out_specs=(vmem,) * 7,
        scratch_shapes=[
            pltpu.VMEM((16, 4, 2, 2, 16, 256), BF16),
            pltpu.VMEM((PARTS, 4, 4, 4, 4, 8, SPAN), BF16),
            pltpu.VMEM((PARTS, 4, 4, 4, 2, 4, 8, SPAN), BF16),
            pltpu.VMEM((PARTS, 64, 2, 4, 8, SPAN), BF16),
            pltpu.VMEM((2, 2, 256, 1024), BF16),
            pltpu.VMEM((DMS, 16, 512), F32),
            pltpu.VMEM((1, 64), jnp.int32),
            pltpu.SMEM((2,), jnp.int32),
            pltpu.VMEM((2, 256, 2 * SPAN), BF16),
            pltpu.VMEM((PARTS, 64, 8, SPAN), BF16),
            pltpu.VMEM((PARTS, 64, 2, 8, SPAN), BF16),
            pltpu.VMEM((16, 256), F32),
            pltpu.VMEM((2, 512, SPAN), BF16),
            pltpu.VMEM((2, 88 + SPAN, 512), F32),
            pltpu.VMEM((SPAN + 32, 512), BF16),
            pltpu.VMEM((SPAN + 16, 512), BF16),
            pltpu.VMEM((2, 256, 2 * SPAN), F32),
            dma((8,)),
            pltpu.SemaphoreType.REGULAR,
            dma,
            dma,
            *[dma((PARTS,)) for _ in range(4)],
            dma((PARTS, 4)),
            dma((PARTS,)),
            dma((30,)),
            dma,
            dma,
            *[
                pltpu.VMEM((PARTS,) + shape + (2, 4, 8, SPAN), BF16)
                for shape in [(3, 3), (3, 3), (3, 3), (3,), (3,), (3,), ()]
            ],
        ],
        compiler_params=pltpu.CompilerParams(collective_id=0, has_side_effects=True, **params),
        name="beamform",
    )(
        in_hbm(voltages.reshape(16, 4, 2, 2, 16, TIME)),
        in_hbm(weights),
        in_hbm(flags),
        in_hbm(dm_index),
        in_hbm(jnp.asarray(chirp_rows()).astype(BF16).astype(F32)),
        in_hbm(jnp.asarray(dft_rows()).astype(BF16)),
        in_hbm(jnp.asarray(prototype())),
    )
    dedispersed, bandpass = pl.pallas_call(
        tail,
        out_shape=(
            jax.ShapeDtypeStruct((2, 2 * TIME * 2, 128), BF16),
            jax.ShapeDtypeStruct((2, CHANNELS), F32),
        ),
        in_specs=[vmem] * 7,
        out_specs=(hbm, hbm),
        scratch_shapes=[
            pltpu.VMEM((2, 512, SPAN), BF16),
            pltpu.VMEM((2, 88 + SPAN, 512), F32),
            *[pltpu.VMEM((SPAN + 32, 512), BF16) for _ in range(2)],
            *[pltpu.VMEM((SPAN + 16, 512), BF16) for _ in range(2)],
            *[pltpu.VMEM((NBLOCK, 32, 512), BF16) for _ in range(2)],
            pltpu.VMEM((2, 2 * TIME * 2, 128), BF16),
            pltpu.VMEM((2, CHANNELS), F32),
            dma((3,)),
        ],
        compiler_params=pltpu.CompilerParams(**params),
        name="synthesis",
    )(
        beams.reshape(PARTS, 1024, SPAN),
        tables,
        dft,
        proto,
        product0,
        last0,
        power0,
    )
    dedispersed = dedispersed.reshape(2, 512, 2, 128).transpose(0, 2, 1, 3).reshape(2, 2, TIME * CHANNELS)
    return dedispersed, bandpass


def solution(mesh):
    return jax.shard_map(
        on_device,
        mesh=mesh,
        in_specs=(
            P(None, ("stn", "chan"), None, None),
            P(None, ("stn", "chan"), None, None),
            P(("stn", "chan"), None),
            P(("stn", "chan")),
        ),
        out_specs=(P(None, ("stn", "chan"), None), P(("stn", "chan"), None)),
        check_vma=False,
    )
```

```python
import math
import random

import jax
import jax.numpy as jnp
import numpy as np
from jax import lax
from jax.experimental import pallas as pl
from jax.experimental.pallas import tpu as pltpu
from jax.sharding import PartitionSpec as P

CHANNELS = 256
BEAMS = 256
INPUTS = 1024
TIME = 256
TAPS = 12
CHIRP = 1024
DMS = 16
NBLOCK = CHIRP // CHANNELS + 1
DEVICES = 128
CHAN_AXIS = 16
PARTS = 2
SPAN = TIME // PARTS
MESH = pl.DeviceIdType.MESH
BF16 = jnp.bfloat16
F32 = jnp.float32


def dft_rows():
    order = np.arange(CHANNELS)
    angle = 2.0 * math.pi / CHANNELS * (order[:, None] * order[None, :] % CHANNELS)
    cosine = np.cos(angle) / math.sqrt(CHANNELS)
    sine = np.sin(angle) / math.sqrt(CHANNELS)
    return np.block([[cosine, sine], [-sine, cosine]]).astype(np.float32)


def prototype():
    counter = np.arange(TAPS * CHANNELS, dtype=np.float64)
    offset = (counter + 0.5) / CHANNELS - TAPS / 2.0
    window = 0.54 + 0.46 * np.cos(math.pi * offset / (TAPS / 2.0))
    taps = (np.sinc(offset) * window).reshape(TAPS, CHANNELS)
    return np.concatenate([taps, taps], axis=1).astype(np.float32)


def chirp_rows():
    dms = np.arange(DMS, dtype=np.int64)[:, None, None]
    lag = np.arange(NBLOCK)[None, :, None] * CHANNELS + CHANNELS - 1 - np.arange(2 * CHANNELS)[None, None, :]
    valid = (lag >= 0) & (lag < CHIRP)
    lag = np.clip(lag, 0, CHIRP - 1)
    angle = math.pi * ((dms + 1) * lag * lag % (2 * DMS * CHIRP)) / (DMS * CHIRP)
    real = np.where(valid, np.cos(angle), 0.0) / math.sqrt(CHIRP)
    imag = np.where(valid, np.sin(angle), 0.0) / math.sqrt(CHIRP)
    rows = np.concatenate([real, imag, np.zeros((DMS, 6, 2 * CHANNELS))], axis=1)
    return rows.astype(np.float32)


def iota(axis, shape=(256, 256)):
    return lax.broadcasted_iota(jnp.int32, shape, axis)


def ones_where(condition):
    return jnp.where(condition, 1.0, 0.0).astype(BF16)


def dot(a, b):
    return jnp.dot(a, b, preferred_element_type=F32)


def exchange_order():
    left = [(dz, dy, dx) for dz in range(4) for dy in range(4) for dx in range(4)]
    random.Random(7).shuffle(left)
    hops, ordered = [0, 0, 0], []
    while left:
        def uneven(step):
            return sum((done + min(d, 4 - d) - len(ordered) - 1) ** 2 for done, d in zip(hops, step))

        best = min(left, key=uneven)
        left.remove(best)
        ordered.append(best)
        hops = [done + min(d, 4 - d) for done, d in zip(hops, best)]
    return ordered


def body(
    volt, wgt, flags, dm, chirps, dft, proto, recv2, tables, dftv, protov, product0, last0, power0,
    vin, give, send, recv, win, chv, flagv, dmv, beams, give2, send2, keep, ordered, padded, even, odd, acc,
    load_sem, plane_sem, given, given2, sent, sent2, sibling_sem, sibling_sem2, recv_sem, recv_sem2, pack_sem, packs_sent, relays_sent, *stages,
):
    x = lax.rem(lax.axis_index("chan"), 4)
    y = lax.axis_index("chan") // 4
    z = lax.axis_index("stn") // 2
    core = lax.rem(lax.axis_index("stn"), 2)
    chip = z * CHAN_AXIS + lax.axis_index("chan")
    sibling = (z * 2 + 1 - core, lax.axis_index("chan"))

    turn = 1 + 2 * core
    zs = [lax.rem(z + dz * turn, 4) for dz in range(4)]
    xs = [lax.rem(x + dx * turn, 4) for dx in range(4)]
    ys = [lax.rem(y + dy * turn, 4) * 4 for dy in range(4)]

    flag_load = pltpu.make_async_copy(flags, flagv, load_sem.at[0])
    flag_load.start()
    volt_loads = [
        pltpu.make_async_copy(volt.at[:, :, number], vin.at[:, :, number], load_sem.at[n])
        for n, number in ((1, 1 - core), (2, core))
    ]
    for load in volt_loads:
        load.start()

    barrier = pltpu.get_barrier_semaphore()
    line = [(zs[dz] * 2 + core, ys[0] + x) for dz in range(1, 4)]
    plane = [(z * 2 + core, ys[dy] + xs[dx]) for dy in range(4) for dx in range(4) if (dy, dx) != (0, 0)]
    greeted = [sibling] + line + plane
    for peer in greeted:
        pl.semaphore_signal(barrier, inc=1, device_id=peer, device_id_type=MESH)

    def hand_over(part, give, send, given, sibling_sem):
        pltpu.make_async_remote_copy(
            src_ref=give.at[part],
            dst_ref=send.at[part, :, :, :, core] if len(send.shape) == 8 else send.at[part, :, core],
            send_sem=given,
            recv_sem=sibling_sem.at[part],
            device_id=sibling,
            device_id_type=MESH,
        ).start()

    def exchange(part, send, landing, sibling_sem, sent, recv_sem):
        share = send.at[part, :, 1 - core]
        pltpu.make_async_copy(share, share, sibling_sem.at[part]).wait()
        pltpu.make_async_copy(send.at[part, chip], landing, recv_sem.at[part]).start()
        for dz, dy, dx in exchange_order():
            if (dz, dy, dx) != (0, 0, 0):
                chan = ys[dy] + xs[dx]
                pltpu.make_async_remote_copy(
                    src_ref=send.at[part, zs[dz] * CHAN_AXIS + chan],
                    dst_ref=landing,
                    send_sem=sent.at[part],
                    recv_sem=recv_sem.at[part],
                    device_id=(zs[dz] * 2 + core, chan),
                    device_id_type=MESH,
                ).start()

    by_z, by_x, by_y, by_xz, by_yz, by_xy, by_xyz = stages

    def place(steps):
        dz, dy, dx = steps
        return zs[dz % 4] * 2 + core, ys[dy % 4] + xs[dx % 4]

    def packs(part):
        near = (-1, 0, 1)
        listed = []
        for m in range(3):
            listed.append(((3, m, slice(0, 3)), by_z.at[part, m], (1, 0, 0), [(1, m - 1, d) for d in near]))
            listed.append(((m, slice(0, 3), 3), by_x.at[part, m], (0, 0, 1), [(m - 1, d, 1) for d in near]))
            listed.append(((m, 3, slice(0, 3)), by_y.at[part, m], (0, 1, 0), [(m - 1, 1, d) for d in near]))
            listed.append(((m, 3, 3), by_xy.at[part, m], (0, 1, 1), [(m - 1, 1, 1)]))
        listed.append(((3, slice(0, 3), 3), by_xz.at[part], (1, 0, 1), [(1, d, 1) for d in near]))
        listed.append(((3, 3, slice(0, 3)), by_yz.at[part], (1, 1, 0), [(1, 1, d) for d in near]))
        listed.append(((3, 3, 3), by_xyz.at[part], (1, 1, 1), [(1, 1, 1)]))
        return [(15 * part + n, *pack) for n, pack in enumerate(listed)]

    def send_packs(part):
        share = send.at[part, :, :, :, 1 - core]
        pltpu.make_async_copy(share, share, sibling_sem.at[part]).wait()
        for n, at, stage, steps, _ in packs(part):
            pltpu.make_async_remote_copy(
                src_ref=send.at[part, at[0], at[1], at[2]],
                dst_ref=stage,
                send_sem=packs_sent,
                recv_sem=pack_sem.at[n],
                device_id=place(steps),
                device_id_type=MESH,
            ).start()

    def send_direct(part):
        pltpu.make_async_copy(send.at[part, 1, 1, 1], recv.at[part, chip], recv_sem.at[part, 0]).start()
        for steps in exchange_order():
            if 2 not in steps and steps != (0, 0, 0):
                at = [(d + 1) % 4 for d in steps]
                pltpu.make_async_remote_copy(
                    src_ref=send.at[part, at[0], at[1], at[2]],
                    dst_ref=recv.at[part, chip],
                    send_sem=sent.at[part],
                    recv_sem=recv_sem.at[part, steps[0]],
                    device_id=place(steps),
                    device_id_type=MESH,
                ).start()

    def relay_packs(part):
        for n, _, stage, steps, onward in packs(part):
            pltpu.make_async_copy(stage, stage, pack_sem.at[n]).wait()
            dz, dy, dx = (-d % 4 for d in steps)
            origin = zs[dz] * CHAN_AXIS + ys[dy] + xs[dx]
            for m, further in enumerate(onward):
                pltpu.make_async_remote_copy(
                    src_ref=stage.at[m] if len(onward) > 1 else stage,
                    dst_ref=recv.at[part, origin],
                    send_sem=relays_sent,
                    recv_sem=recv_sem.at[part, (steps[0] + further[0]) % 4],
                    device_id=place(further),
                    device_id_type=MESH,
                ).start()

    flag_load.wait()
    row, col = iota(0), iota(1)
    hits = ones_where(iota(0, (256, 64)) == flagv[...])
    count = dot(hits, jnp.ones((64, 256), BF16))
    keep_rows = ones_where((count < 0.5) & (row % 16 == col % 16))
    keep[...] = dot(ones_where(iota(1, (16, 256)) // 16 == iota(0, (16, 256))), keep_rows)

    def sort_out(number):
        way = 1 + 2 * number
        there = (row // 128) * 8 + ((x + (row // 32 + 3) % 4 * way) % 4) * 2 + (row // 8) % 2
        swap = jnp.where((col // 16 == ((row // 16) % 2) * 8 + row % 8) & (col % 16 == there), 1.0, 0.0)
        for zz in range(4):
            for half in range(2):
                block = vin[:, zz, number, half].reshape(256, 256)
                mine = (swap * keep[pl.ds((zz * 2 + number) * 2 + half, 1), :]).astype(BF16)
                sorted_block = dot(mine, block).astype(BF16)
                for one in range(2):
                    mz = lax.rem((zz + 4 - z) * way + 1, 4)
                    my = lax.rem((half * 2 + one + 4 - y) * way + 1, 4)
                    yield mz, my, sorted_block[one * 128 : one * 128 + 128].reshape(4, 4, 8, 256)

    volt_loads[0].wait()
    for mz, my, block in sort_out(1 - core):
        for part in range(PARTS):
            give[part, mz, my] = block[..., part * SPAN : part * SPAN + SPAN]
    pl.semaphore_wait(barrier, len(greeted))
    for peer in line:
        pl.semaphore_signal(plane_sem, inc=1, device_id=peer, device_id_type=MESH)
    for part in range(PARTS):
        hand_over(part, give, send, given, sibling_sem)
    volt_loads[1].wait()
    for mz, my, block in sort_out(core):
        for part in range(PARTS):
            send[part, mz, my, :, core] = block[..., part * SPAN : part * SPAN + SPAN]
    loads = [
        pltpu.make_async_copy(source, target, load_sem.at[n])
        for n, (source, target) in enumerate(
            ((wgt, win), (dm, dmv), (chirps, chv), (dft, dftv), (proto, protov)), 3
        )
    ]
    for load in loads:
        load.start()
    pl.semaphore_wait(plane_sem, len(line))
    send_packs(0)
    send_direct(0)
    send_packs(1)
    relay_packs(0)
    relay_packs(1)
    send_direct(1)
    for load in loads:
        load.wait()

    def toeplitz(n, carry):
        b, block = n // NBLOCK, lax.rem(n, NBLOCK)
        for part in range(2):
            wide = jnp.broadcast_to(chv[dmv[b], pl.ds(part * NBLOCK + block, 1), :], (8, 2 * CHANNELS))
            eight = pltpu.roll(wide, CHANNELS + 1, 1, stride=1, stride_axis=0)
            for k in range(0, CHANNELS, 16):
                both = [pltpu.roll(eight, k + i, 1)[:, :CHANNELS] if k + i else eight[:, :CHANNELS] for i in (0, 8)]
                rows = pl.ds(pl.multiple_of(block * CHANNELS + k, 16), 16)
                tables[b, rows, part * CHANNELS : (part + 1) * CHANNELS] = jnp.concatenate(both, axis=0).astype(BF16)
        return carry


    to_device = lax.rem(core + row // 128, 2) * 16 + (row // 8) % 16
    order = ones_where(
        (col // 128 == row % 2) & ((col // 64) % 2 == (row // 2) % 2) & (col % 64 == to_device * 2 + (row // 4) % 2)
    )
    for part in range(PARTS):
        for n, dz in enumerate((3, 0, 1, 2)):
            source = zs[-dz % 4]
            arrived = recv.at[part, pl.ds(pl.multiple_of(source * 16, 16), 16)]
            pltpu.make_async_copy(arrived, arrived, recv_sem.at[part, dz]).wait()
            for c in range(2):
                real, imag, weight_real, weight_imag = [], [], [], []
                for number in range(2):
                    chips = pl.ds(pl.multiple_of(source * 16, 16), 16)
                    inputs = pl.ds(pl.multiple_of((source * 2 + number) * 128, 128), 128)
                    real.append(recv[part, chips, number, c].reshape(128, SPAN))
                    imag.append(recv[part, chips, number, 2 + c].reshape(128, SPAN))
                    weight_real.append(win[0, c, :, inputs])
                    weight_imag.append(win[1, c, :, inputs])
                parts = jnp.concatenate(
                    [
                        jnp.concatenate(real + [-half for half in imag], axis=0),
                        jnp.concatenate(imag + real, axis=0),
                    ],
                    axis=1,
                )
                product = dot(jnp.concatenate(weight_real + weight_imag, axis=1), parts)
                if n == 0:
                    acc[c] = product
                elif n < 3:
                    acc[c] += product
                else:
                    beams[c] = (acc[c] + product).astype(BF16)
        for zz in range(4):
            rows = slice(zz * 64, zz * 64 + 64)
            block = jnp.concatenate([beams[c, rows, q * SPAN : q * SPAN + SPAN] for c in range(2) for q in range(2)], axis=0)
            block = dot(order, block).astype(BF16)
            send2[part, zz * 16 : zz * 16 + 16, core] = block[:128].reshape(16, 8, SPAN)
            give2[part, zz * 16 : zz * 16 + 16] = block[128:].reshape(16, 8, SPAN)
        hand_over(part, give2, send2, given2, sibling_sem2)
        if part == 0:
            lax.fori_loop(0, 2 * NBLOCK, toeplitz, 0)
        exchange(part, send2, recv2.at[part, chip], sibling_sem2, sent2, recv_sem2)

    arrived = recv2.at[0]
    pltpu.make_async_copy(arrived, arrived, recv_sem2.at[0]).wait()
    for b, power, last in front(
        lambda n: recv2[0, n * 16 : n * 16 + 16].reshape(256, SPAN), lambda b: 0.0, dftv, protov, ordered, padded
    ):
        power0[b : b + 1, :] = power
        last0[b] = last
    for b in range(2):
        for n in range(4):
            lanes, series = synthesise(b, n, protov, padded)
            store_shifted(series, lanes, even, odd)
        product0[b] = chirped(stacked_shifts(even, odd), tables[b])

    for blocks, sem in ((give, given), (give2, given2)):
        pltpu.make_async_copy(blocks, blocks, sem).wait()
    for sem in (packs_sent, relays_sent):
        for part in range(PARTS):
            blocks = recv.at[part, 0:37]
            pltpu.make_async_copy(blocks, blocks, sem).wait()
    for part in range(PARTS):
        for blocks, sem in ((recv.at[part, 0:26], sent), (send2.at[part, 0:63], sent2)):
            pltpu.make_async_copy(blocks, blocks, sem.at[part]).wait()
    arrived = recv2.at[1]
    pltpu.make_async_copy(arrived, arrived, recv_sem2.at[1]).wait()


def front(chunk, before_first, dftv, protov, xs, padded):
    row, col = iota(0), iota(1)
    sort = ones_where(col == ((row % 32) // 2 * 2 + (row % 64) // 32) * 8 + (row // 64) * 2 + row % 2)
    spread = ones_where(iota(1, (SPAN, SPAN)) == (iota(0, (SPAN, SPAN)) % 8) * 16 + iota(0, (SPAN, SPAN)) // 8)
    for n in range(4):
        block = dot(sort, chunk(n)).astype(BF16)
        for k in range(4):
            xs[k // 2, (k % 2) * 256 + n * 64 : (k % 2) * 256 + n * 64 + 64, :] = block[k * 64 : k * 64 + 64]
    for b in range(2):
        turned = lax.dot_general(spread, xs[b], (((1,), (1,)), ((), ())), preferred_element_type=F32)
        power = jnp.sum(turned * turned, axis=0, keepdims=True)
        spectra = dot(turned.astype(BF16), dftv[...])
        last = spectra[SPAN - 88 :]
        first = iota(0, (88, 512)) % 8 == 0
        padded[b, 0:88, :] = jnp.where(first, before_first(b), pltpu.roll(last, 1, 0))
        padded[b, 88 : 88 + SPAN, :] = spectra
        yield b, power, pltpu.roll(last, 81, 0)


def synthesise(b, n, protov, padded):
    lanes = slice(n * 128, n * 128 + 128)
    series = protov[0:1, lanes] * padded[b, 88 : 88 + SPAN, lanes]
    for tap in range(1, TAPS):
        series = series + protov[tap : tap + 1, lanes] * padded[b, 88 - 8 * tap : 88 - 8 * tap + SPAN, lanes]
    return lanes, series


def store_shifted(series, lanes, even, odd):
    after = jnp.where(iota(0, (32, 128)) % 8 == 7, 0.0, pltpu.roll(series[:32], 31, 0))
    even[0:SPAN, lanes] = series.astype(BF16)
    even[SPAN : SPAN + 32, lanes] = after.astype(BF16)
    odd[0 : SPAN + 16, lanes] = jnp.concatenate([series[8:], after[:24]], axis=0).astype(BF16)


def stacked_shifts(even, odd):
    shifted = [even[0:SPAN], odd[0:SPAN], even[16 : 16 + SPAN], odd[16 : 16 + SPAN], even[32 : 32 + SPAN]]
    return [jnp.concatenate([block[:, p * 256 : p * 256 + 256] for block in shifted], axis=1) for p in range(2)]


def chirped(parts, table):
    product = dot(jnp.concatenate(parts, axis=0), table)
    rows = product.shape[0] // 2
    real = product[:rows, :256] + product[rows:, 256:]
    imag = product[rows:, :256] - product[:rows, 256:]
    return jnp.concatenate([real, imag], axis=1)


def tail(
    xv, tv, dftv, protov, product0, last0, power0, out, band,
    xs, padded, even0, even1, odd0, odd1, over0, over1, outv, bandv, out_sem,
):
    band_copy = pltpu.make_async_copy(bandv, band, out_sem.at[2])
    for b, power, _ in front(lambda n: xv[1, n * 256 : n * 256 + 256, :], lambda b: last0[b], dftv, protov, xs, padded):
        power = (power + power0[b : b + 1, :]) * (1.0 / TIME)
        bandv[b : b + 1, :] = power[:, :256] + power[:, 256:]
    band_copy.start()
    results = []
    for b, (even, odd, over) in enumerate(((even0, odd0, over0), (even1, odd1, over1))):
        for n in range(4):
            lanes, series = synthesise(b, n, protov, padded)
            store_shifted(series, lanes, even, odd)
            over_edge = jnp.where(iota(0, (32, 128)) % 8 == 7, pltpu.roll(series[:32], 7, 0), 0.0)
            for blk in range(NBLOCK):
                seen = [over_edge[: 8 * blk]] if blk else []
                unseen = [jnp.zeros((32 - 8 * blk, 128), F32)] if blk < 4 else []
                over[blk, :, lanes] = jnp.concatenate(unseen + seen, axis=0).astype(BF16)
        edges = [
            jnp.concatenate([over[blk, :, p * 256 : p * 256 + 256] for blk in range(NBLOCK)], axis=1) for p in range(2)
        ]
        parts = [jnp.concatenate(pair, axis=0) for pair in zip(stacked_shifts(even, odd), edges)]
        product = chirped(parts, tv[b])
        results.append(
            jnp.concatenate([product0[b, :96], product0[b, 96:] + product[SPAN:], product[:SPAN]], axis=0).astype(BF16)
        )
    row, col = iota(0), iota(1)
    final = ones_where(col == (row % 4) * 64 + ((row // 4) % 8) * 8 + row // 32)
    copies = []
    for h in range(2):
        for j in range(2):
            rows = slice(128 * h + 64 * j, 128 * h + 64 * j + 64)
            block = jnp.concatenate(
                [
                    jnp.concatenate([results[b][rows, half * 128 + q * 256 : half * 128 + q * 256 + 128] for q in range(2)], axis=1)
                    for half in range(2) for b in range(2)
                ],
                axis=0,
            )
            block = dot(final, block).astype(BF16)
            for q in range(2):
                for k in range(8):
                    start = 512 * h + 64 * k + 32 * j
                    outv[q, start : start + 32, :] = block[32 * k : 32 * k + 32, q * 128 : q * 128 + 128]
        done = pl.ds(512 * h, 512)
        copies.append(pltpu.make_async_copy(outv.at[:, done], out.at[:, done], out_sem.at[h]))
        copies[-1].start()
    for copy in copies + [band_copy]:
        copy.wait()


def in_hbm(array):
    return pltpu.with_memory_space_constraint(array, pltpu.HBM)


def on_device(voltages, weights, flags, dm_index):
    hbm = pl.BlockSpec(memory_space=pl.ANY)
    vmem = pl.BlockSpec(memory_space=pltpu.VMEM)
    dma = pltpu.SemaphoreType.DMA
    params = dict(vmem_limit_bytes=24 * 1024 * 1024)
    beams, tables, dft, proto, product0, last0, power0 = pl.pallas_call(
        body,
        out_shape=(
            jax.ShapeDtypeStruct((PARTS, 64, 2, 8, SPAN), BF16),
            jax.ShapeDtypeStruct((2, NBLOCK * CHANNELS, 512), BF16),
            jax.ShapeDtypeStruct((512, 512), BF16),
            jax.ShapeDtypeStruct((TAPS, 512), F32),
            jax.ShapeDtypeStruct((2, SPAN, 512), F32),
            jax.ShapeDtypeStruct((2, 88, 512), F32),
            jax.ShapeDtypeStruct((2, 512), F32),
        ),
        in_specs=[hbm] * 7,
        out_specs=(vmem,) * 7,
        scratch_shapes=[
            pltpu.VMEM((16, 4, 2, 2, 16, 256), BF16),
            pltpu.VMEM((PARTS, 4, 4, 4, 4, 8, SPAN), BF16),
            pltpu.VMEM((PARTS, 4, 4, 4, 2, 4, 8, SPAN), BF16),
            pltpu.VMEM((PARTS, 64, 2, 4, 8, SPAN), BF16),
            pltpu.VMEM((2, 2, 256, 1024), BF16),
            pltpu.VMEM((DMS, 16, 512), F32),
            pltpu.VMEM((1, 64), jnp.int32),
            pltpu.SMEM((2,), jnp.int32),
            pltpu.VMEM((2, 256, 2 * SPAN), BF16),
            pltpu.VMEM((PARTS, 64, 8, SPAN), BF16),
            pltpu.VMEM((PARTS, 64, 2, 8, SPAN), BF16),
            pltpu.VMEM((16, 256), F32),
            pltpu.VMEM((2, 512, SPAN), BF16),
            pltpu.VMEM((2, 88 + SPAN, 512), F32),
            pltpu.VMEM((SPAN + 32, 512), BF16),
            pltpu.VMEM((SPAN + 16, 512), BF16),
            pltpu.VMEM((2, 256, 2 * SPAN), F32),
            dma((8,)),
            pltpu.SemaphoreType.REGULAR,
            dma,
            dma,
            *[dma((PARTS,)) for _ in range(4)],
            dma((PARTS, 4)),
            dma((PARTS,)),
            dma((30,)),
            dma,
            dma,
            *[
                pltpu.VMEM((PARTS,) + shape + (2, 4, 8, SPAN), BF16)
                for shape in [(3, 3), (3, 3), (3, 3), (3,), (3,), (3,), ()]
            ],
        ],
        compiler_params=pltpu.CompilerParams(collective_id=0, has_side_effects=True, **params),
        name="beamform",
    )(
        in_hbm(voltages.reshape(16, 4, 2, 2, 16, TIME)),
        in_hbm(weights),
        in_hbm(flags),
        in_hbm(dm_index),
        in_hbm(jnp.asarray(chirp_rows()).astype(BF16).astype(F32)),
        in_hbm(jnp.asarray(dft_rows()).astype(BF16)),
        in_hbm(jnp.asarray(prototype())),
    )
    dedispersed, bandpass = pl.pallas_call(
        tail,
        out_shape=(
            jax.ShapeDtypeStruct((2, 2 * TIME * 2, 128), BF16),
            jax.ShapeDtypeStruct((2, CHANNELS), F32),
        ),
        in_specs=[vmem] * 7,
        out_specs=(hbm, hbm),
        scratch_shapes=[
            pltpu.VMEM((2, 512, SPAN), BF16),
            pltpu.VMEM((2, 88 + SPAN, 512), F32),
            *[pltpu.VMEM((SPAN + 32, 512), BF16) for _ in range(2)],
            *[pltpu.VMEM((SPAN + 16, 512), BF16) for _ in range(2)],
            *[pltpu.VMEM((NBLOCK, 32, 512), BF16) for _ in range(2)],
            pltpu.VMEM((2, 2 * TIME * 2, 128), BF16),
            pltpu.VMEM((2, CHANNELS), F32),
            dma((3,)),
        ],
        compiler_params=pltpu.CompilerParams(**params),
        name="synthesis",
    )(
        beams.reshape(PARTS, 1024, SPAN),
        tables,
        dft,
        proto,
        product0,
        last0,
        power0,
    )
    dedispersed = dedispersed.reshape(2, 512, 2, 128).transpose(0, 2, 1, 3).reshape(2, 2, TIME * CHANNELS)
    return dedispersed, bandpass


def solution(mesh):
    return jax.shard_map(
        on_device,
        mesh=mesh,
        in_specs=(
            P(None, ("stn", "chan"), None, None),
            P(None, ("stn", "chan"), None, None),
            P(("stn", "chan"), None),
            P(("stn", "chan")),
        ),
        out_specs=(P(None, ("stn", "chan"), None), P(("stn", "chan"), None)),
        check_vma=False,
    )
```

```python
import math
import random

import jax
import jax.numpy as jnp
import numpy as np
from jax import lax
from jax.experimental import pallas as pl
from jax.experimental.pallas import tpu as pltpu
from jax.sharding import PartitionSpec as P

CHANNELS = 256
BEAMS = 256
INPUTS = 1024
TIME = 256
TAPS = 12
CHIRP = 1024
DMS = 16
NBLOCK = CHIRP // CHANNELS + 1
DEVICES = 128
CHAN_AXIS = 16
PARTS = 2
SPAN = TIME // PARTS
MESH = pl.DeviceIdType.MESH
BF16 = jnp.bfloat16
F32 = jnp.float32


def dft_rows():
    order = np.arange(CHANNELS)
    angle = 2.0 * math.pi / CHANNELS * (order[:, None] * order[None, :] % CHANNELS)
    cosine = np.cos(angle) / math.sqrt(CHANNELS)
    sine = np.sin(angle) / math.sqrt(CHANNELS)
    return np.block([[cosine, sine], [-sine, cosine]]).astype(np.float32)


def prototype():
    counter = np.arange(TAPS * CHANNELS, dtype=np.float64)
    offset = (counter + 0.5) / CHANNELS - TAPS / 2.0
    window = 0.54 + 0.46 * np.cos(math.pi * offset / (TAPS / 2.0))
    taps = (np.sinc(offset) * window).reshape(TAPS, CHANNELS)
    return np.concatenate([taps, taps], axis=1).astype(np.float32)


def chirp_rows():
    dms = np.arange(DMS, dtype=np.int64)[:, None, None]
    lag = np.arange(NBLOCK)[None, :, None] * CHANNELS + CHANNELS - 1 - np.arange(2 * CHANNELS)[None, None, :]
    valid = (lag >= 0) & (lag < CHIRP)
    lag = np.clip(lag, 0, CHIRP - 1)
    angle = math.pi * ((dms + 1) * lag * lag % (2 * DMS * CHIRP)) / (DMS * CHIRP)
    real = np.where(valid, np.cos(angle), 0.0) / math.sqrt(CHIRP)
    imag = np.where(valid, np.sin(angle), 0.0) / math.sqrt(CHIRP)
    rows = np.concatenate([real, imag, np.zeros((DMS, 6, 2 * CHANNELS))], axis=1)
    return rows.astype(np.float32)


def iota(axis, shape=(256, 256)):
    return lax.broadcasted_iota(jnp.int32, shape, axis)


def ones_where(condition):
    return jnp.where(condition, 1.0, 0.0).astype(BF16)


def dot(a, b):
    return jnp.dot(a, b, preferred_element_type=F32)


def exchange_order():
    left = [(dz, dy, dx) for dz in range(4) for dy in range(4) for dx in range(4)]
    random.Random(7).shuffle(left)
    hops, ordered = [0, 0, 0], []
    while left:
        def uneven(step):
            return sum((done + min(d, 4 - d) - len(ordered) - 1) ** 2 for done, d in zip(hops, step))

        best = min(left, key=uneven)
        left.remove(best)
        ordered.append(best)
        hops = [done + min(d, 4 - d) for done, d in zip(hops, best)]
    return ordered


def body(
    volt, wgt, flags, dm, chirps, dft, proto, recv2, tables, dftv, protov, product0, last0, power0,
    vin, give, send, recv, win, chv, flagv, dmv, beams, give2, send2, keep, ordered, padded, even, odd, acc,
    load_sem, plane_sem, given, given2, sent, sent2, sibling_sem, sibling_sem2, recv_sem, recv_sem2, pack_sem, packs_sent, relays_sent, *stages,
):
    x = lax.rem(lax.axis_index("chan"), 4)
    y = lax.axis_index("chan") // 4
    z = lax.axis_index("stn") // 2
    core = lax.rem(lax.axis_index("stn"), 2)
    chip = z * CHAN_AXIS + lax.axis_index("chan")
    sibling = (z * 2 + 1 - core, lax.axis_index("chan"))

    turn = 1 + 2 * core
    zs = [lax.rem(z + dz * turn, 4) for dz in range(4)]
    xs = [lax.rem(x + dx * turn, 4) for dx in range(4)]
    ys = [lax.rem(y + dy * turn, 4) * 4 for dy in range(4)]

    flag_load = pltpu.make_async_copy(flags, flagv, load_sem.at[0])
    flag_load.start()
    volt_loads = [
        pltpu.make_async_copy(volt.at[:, :, number], vin.at[:, :, number], load_sem.at[n])
        for n, number in ((1, 1 - core), (2, core))
    ]
    for load in volt_loads:
        load.start()

    barrier = pltpu.get_barrier_semaphore()
    line = [(zs[dz] * 2 + core, ys[0] + x) for dz in range(1, 4)]
    plane = [(z * 2 + core, ys[dy] + xs[dx]) for dy in range(4) for dx in range(4) if (dy, dx) != (0, 0)]
    greeted = [sibling] + line + plane
    for peer in greeted:
        pl.semaphore_signal(barrier, inc=1, device_id=peer, device_id_type=MESH)

    def hand_over(part, give, send, given, sibling_sem):
        pltpu.make_async_remote_copy(
            src_ref=give.at[part],
            dst_ref=send.at[part, :, :, :, core] if len(send.shape) == 8 else send.at[part, :, core],
            send_sem=given,
            recv_sem=sibling_sem.at[part],
            device_id=sibling,
            device_id_type=MESH,
        ).start()

    def exchange(part, send, landing, sibling_sem, sent, recv_sem):
        for zz in range(4):
            share = send.at[part, zz * 16 : zz * 16 + 16, 1 - core]
            pltpu.make_async_copy(share, share, sibling_sem.at[part, zz]).wait()
        pltpu.make_async_copy(send.at[part, chip], landing, recv_sem.at[part]).start()
        for dz, dy, dx in exchange_order():
            if (dz, dy, dx) != (0, 0, 0):
                chan = ys[dy] + xs[dx]
                pltpu.make_async_remote_copy(
                    src_ref=send.at[part, zs[dz] * CHAN_AXIS + chan],
                    dst_ref=landing,
                    send_sem=sent.at[part],
                    recv_sem=recv_sem.at[part],
                    device_id=(zs[dz] * 2 + core, chan),
                    device_id_type=MESH,
                ).start()

    by_z, by_x, by_y, by_xz, by_yz, by_xy, by_xyz = stages

    def place(steps):
        dz, dy, dx = steps
        return zs[dz % 4] * 2 + core, ys[dy % 4] + xs[dx % 4]

    def packs(part):
        near = (-1, 0, 1)
        listed = []
        for m in range(3):
            listed.append(((3, m, slice(0, 3)), by_z.at[part, m], (1, 0, 0), [(1, m - 1, d) for d in near]))
            listed.append(((m, slice(0, 3), 3), by_x.at[part, m], (0, 0, 1), [(m - 1, d, 1) for d in near]))
            listed.append(((m, 3, slice(0, 3)), by_y.at[part, m], (0, 1, 0), [(m - 1, 1, d) for d in near]))
            listed.append(((m, 3, 3), by_xy.at[part, m], (0, 1, 1), [(m - 1, 1, 1)]))
        listed.append(((3, slice(0, 3), 3), by_xz.at[part], (1, 0, 1), [(1, d, 1) for d in near]))
        listed.append(((3, 3, slice(0, 3)), by_yz.at[part], (1, 1, 0), [(1, 1, d) for d in near]))
        listed.append(((3, 3, 3), by_xyz.at[part], (1, 1, 1), [(1, 1, 1)]))
        return [(15 * part + n, *pack) for n, pack in enumerate(listed)]

    def send_packs(part):
        share = send.at[part, :, :, :, 1 - core]
        pltpu.make_async_copy(share, share, sibling_sem.at[part]).wait()
        for n, at, stage, steps, _ in packs(part):
            pltpu.make_async_remote_copy(
                src_ref=send.at[part, at[0], at[1], at[2]],
                dst_ref=stage,
                send_sem=packs_sent,
                recv_sem=pack_sem.at[n],
                device_id=place(steps),
                device_id_type=MESH,
            ).start()

    def send_direct(part):
        pltpu.make_async_copy(send.at[part, 1, 1, 1], recv.at[part, chip], recv_sem.at[part, 0]).start()
        for steps in exchange_order():
            if 2 not in steps and steps != (0, 0, 0):
                at = [(d + 1) % 4 for d in steps]
                pltpu.make_async_remote_copy(
                    src_ref=send.at[part, at[0], at[1], at[2]],
                    dst_ref=recv.at[part, chip],
                    send_sem=sent.at[part],
                    recv_sem=recv_sem.at[part, steps[0]],
                    device_id=place(steps),
                    device_id_type=MESH,
                ).start()

    def relay_packs(part):
        for n, _, stage, steps, onward in packs(part):
            pltpu.make_async_copy(stage, stage, pack_sem.at[n]).wait()
            dz, dy, dx = (-d % 4 for d in steps)
            origin = zs[dz] * CHAN_AXIS + ys[dy] + xs[dx]
            for m, further in enumerate(onward):
                pltpu.make_async_remote_copy(
                    src_ref=stage.at[m] if len(onward) > 1 else stage,
                    dst_ref=recv.at[part, origin],
                    send_sem=relays_sent,
                    recv_sem=recv_sem.at[part, (steps[0] + further[0]) % 4],
                    device_id=place(further),
                    device_id_type=MESH,
                ).start()

    flag_load.wait()
    row, col = iota(0), iota(1)
    hits = ones_where(iota(0, (256, 64)) == flagv[...])
    count = dot(hits, jnp.ones((64, 256), BF16))
    keep_rows = ones_where((count < 0.5) & (row % 16 == col % 16))
    keep[...] = dot(ones_where(iota(1, (16, 256)) // 16 == iota(0, (16, 256))), keep_rows)

    def sort_out(number):
        way = 1 + 2 * number
        there = (row // 128) * 8 + ((x + (row // 32 + 3) % 4 * way) % 4) * 2 + (row // 8) % 2
        swap = jnp.where((col // 16 == ((row // 16) % 2) * 8 + row % 8) & (col % 16 == there), 1.0, 0.0)
        for zz in range(4):
            for half in range(2):
                block = vin[:, zz, number, half].reshape(256, 256)
                mine = (swap * keep[pl.ds((zz * 2 + number) * 2 + half, 1), :]).astype(BF16)
                sorted_block = dot(mine, block).astype(BF16)
                for one in range(2):
                    mz = lax.rem((zz + 4 - z) * way + 1, 4)
                    my = lax.rem((half * 2 + one + 4 - y) * way + 1, 4)
                    yield mz, my, sorted_block[one * 128 : one * 128 + 128].reshape(4, 4, 8, 256)

    volt_loads[0].wait()
    for mz, my, block in sort_out(1 - core):
        for part in range(PARTS):
            give[part, mz, my] = block[..., part * SPAN : part * SPAN + SPAN]
    pl.semaphore_wait(barrier, len(greeted))
    for peer in line:
        pl.semaphore_signal(plane_sem, inc=1, device_id=peer, device_id_type=MESH)
    for part in range(PARTS):
        hand_over(part, give, send, given, sibling_sem)
    volt_loads[1].wait()
    for mz, my, block in sort_out(core):
        for part in range(PARTS):
            send[part, mz, my, :, core] = block[..., part * SPAN : part * SPAN + SPAN]
    loads = [
        pltpu.make_async_copy(source, target, load_sem.at[n])
        for n, (source, target) in enumerate(
            ((wgt, win), (dm, dmv), (chirps, chv), (dft, dftv), (proto, protov)), 3
        )
    ]
    for load in loads:
        load.start()
    pl.semaphore_wait(plane_sem, len(line))
    send_packs(0)
    send_direct(0)
    send_packs(1)
    relay_packs(0)
    send_direct(1)
    relay_packs(1)
    for load in loads:
        load.wait()

    def toeplitz(n, carry):
        b, block = n // NBLOCK, lax.rem(n, NBLOCK)
        for part in range(2):
            wide = jnp.broadcast_to(chv[dmv[b], pl.ds(part * NBLOCK + block, 1), :], (8, 2 * CHANNELS))
            eight = pltpu.roll(wide, CHANNELS + 1, 1, stride=1, stride_axis=0)
            for k in range(0, CHANNELS, 16):
                both = [pltpu.roll(eight, k + i, 1)[:, :CHANNELS] if k + i else eight[:, :CHANNELS] for i in (0, 8)]
                rows = pl.ds(pl.multiple_of(block * CHANNELS + k, 16), 16)
                tables[b, rows, part * CHANNELS : (part + 1) * CHANNELS] = jnp.concatenate(both, axis=0).astype(BF16)
        return carry


    to_device = lax.rem(core + row // 128, 2) * 16 + (row // 8) % 16
    order = ones_where(
        (col // 128 == row % 2) & ((col // 64) % 2 == (row // 2) % 2) & (col % 64 == to_device * 2 + (row // 4) % 2)
    )
    for part in range(PARTS):
        for n, dz in enumerate((3, 0, 1, 2)):
            source = zs[-dz % 4]
            arrived = recv.at[part, pl.ds(pl.multiple_of(source * 16, 16), 16)]
            pltpu.make_async_copy(arrived, arrived, recv_sem.at[part, dz]).wait()
            for c in range(2):
                real, imag, weight_real, weight_imag = [], [], [], []
                for number in range(2):
                    chips = pl.ds(pl.multiple_of(source * 16, 16), 16)
                    inputs = pl.ds(pl.multiple_of((source * 2 + number) * 128, 128), 128)
                    real.append(recv[part, chips, number, c].reshape(128, SPAN))
                    imag.append(recv[part, chips, number, 2 + c].reshape(128, SPAN))
                    weight_real.append(win[0, c, :, inputs])
                    weight_imag.append(win[1, c, :, inputs])
                parts = jnp.concatenate(
                    [
                        jnp.concatenate(real + [-half for half in imag], axis=0),
                        jnp.concatenate(imag + real, axis=0),
                    ],
                    axis=1,
                )
                product = dot(jnp.concatenate(weight_real + weight_imag, axis=1), parts)
                if n == 0:
                    acc[c] = product
                elif n < 3:
                    acc[c] += product
                else:
                    beams[c] = (acc[c] + product).astype(BF16)
        for zz in range(4):
            rows = slice(zz * 64, zz * 64 + 64)
            block = jnp.concatenate([beams[c, rows, q * SPAN : q * SPAN + SPAN] for c in range(2) for q in range(2)], axis=0)
            block = dot(order, block).astype(BF16)
            chips = pl.ds(zz * 16, 16)
            give2[part, chips] = block[128:].reshape(16, 8, SPAN)
            pltpu.make_async_remote_copy(
                src_ref=give2.at[part, chips],
                dst_ref=send2.at[part, chips, core],
                send_sem=given2,
                recv_sem=sibling_sem2.at[part, zz],
                device_id=sibling,
                device_id_type=MESH,
            ).start()
            send2[part, chips, core] = block[:128].reshape(16, 8, SPAN)
        if part == 0:
            lax.fori_loop(0, 2 * NBLOCK, toeplitz, 0)
        exchange(part, send2, recv2.at[part, chip], sibling_sem2, sent2, recv_sem2)

    arrived = recv2.at[0]
    pltpu.make_async_copy(arrived, arrived, recv_sem2.at[0]).wait()
    for b, power, last in front(
        lambda n: recv2[0, n * 16 : n * 16 + 16].reshape(256, SPAN), lambda b: 0.0, dftv, protov, ordered, padded
    ):
        power0[b : b + 1, :] = power
        last0[b] = last
    for b in range(2):
        for n in range(4):
            lanes, series = synthesise(b, n, protov, padded)
            store_shifted(series, lanes, even, odd)
        product0[b] = chirped(stacked_shifts(even, odd), tables[b])

    for blocks, sem in ((give, given), (give2, given2)):
        pltpu.make_async_copy(blocks, blocks, sem).wait()
    for sem in (packs_sent, relays_sent):
        for part in range(PARTS):
            blocks = recv.at[part, 0:37]
            pltpu.make_async_copy(blocks, blocks, sem).wait()
    for part in range(PARTS):
        for blocks, sem in ((recv.at[part, 0:26], sent), (send2.at[part, 0:63], sent2)):
            pltpu.make_async_copy(blocks, blocks, sem.at[part]).wait()
    arrived = recv2.at[1]
    pltpu.make_async_copy(arrived, arrived, recv_sem2.at[1]).wait()


def front(chunk, before_first, dftv, protov, xs, padded):
    row, col = iota(0), iota(1)
    sort = ones_where(col == ((row % 32) // 2 * 2 + (row % 64) // 32) * 8 + (row // 64) * 2 + row % 2)
    spread = ones_where(iota(1, (SPAN, SPAN)) == (iota(0, (SPAN, SPAN)) % 8) * 16 + iota(0, (SPAN, SPAN)) // 8)
    for n in range(4):
        block = dot(sort, chunk(n)).astype(BF16)
        for k in range(4):
            xs[k // 2, (k % 2) * 256 + n * 64 : (k % 2) * 256 + n * 64 + 64, :] = block[k * 64 : k * 64 + 64]
    for b in range(2):
        turned = lax.dot_general(spread, xs[b], (((1,), (1,)), ((), ())), preferred_element_type=F32)
        power = jnp.sum(turned * turned, axis=0, keepdims=True)
        spectra = dot(turned.astype(BF16), dftv[...])
        last = spectra[SPAN - 88 :]
        first = iota(0, (88, 512)) % 8 == 0
        padded[b, 0:88, :] = jnp.where(first, before_first(b), pltpu.roll(last, 1, 0))
        padded[b, 88 : 88 + SPAN, :] = spectra
        yield b, power, pltpu.roll(last, 81, 0)


def synthesise(b, n, protov, padded):
    lanes = slice(n * 128, n * 128 + 128)
    series = protov[0:1, lanes] * padded[b, 88 : 88 + SPAN, lanes]
    for tap in range(1, TAPS):
        series = series + protov[tap : tap + 1, lanes] * padded[b, 88 - 8 * tap : 88 - 8 * tap + SPAN, lanes]
    return lanes, series


def store_shifted(series, lanes, even, odd):
    after = jnp.where(iota(0, (32, 128)) % 8 == 7, 0.0, pltpu.roll(series[:32], 31, 0))
    even[0:SPAN, lanes] = series.astype(BF16)
    even[SPAN : SPAN + 32, lanes] = after.astype(BF16)
    odd[0 : SPAN + 16, lanes] = jnp.concatenate([series[8:], after[:24]], axis=0).astype(BF16)


def stacked_shifts(even, odd):
    shifted = [even[0:SPAN], odd[0:SPAN], even[16 : 16 + SPAN], odd[16 : 16 + SPAN], even[32 : 32 + SPAN]]
    return [jnp.concatenate([block[:, p * 256 : p * 256 + 256] for block in shifted], axis=1) for p in range(2)]


def chirped(parts, table):
    product = dot(jnp.concatenate(parts, axis=0), table)
    rows = product.shape[0] // 2
    real = product[:rows, :256] + product[rows:, 256:]
    imag = product[rows:, :256] - product[:rows, 256:]
    return jnp.concatenate([real, imag], axis=1)


def tail(
    xv, tv, dftv, protov, product0, last0, power0, out, band,
    xs, padded, even0, even1, odd0, odd1, over0, over1, outv, bandv, out_sem,
):
    band_copy = pltpu.make_async_copy(bandv, band, out_sem.at[2])
    for b, power, _ in front(lambda n: xv[1, n * 256 : n * 256 + 256, :], lambda b: last0[b], dftv, protov, xs, padded):
        power = (power + power0[b : b + 1, :]) * (1.0 / TIME)
        bandv[b : b + 1, :] = power[:, :256] + power[:, 256:]
    band_copy.start()
    results = []
    for b, (even, odd, over) in enumerate(((even0, odd0, over0), (even1, odd1, over1))):
        for n in range(4):
            lanes, series = synthesise(b, n, protov, padded)
            store_shifted(series, lanes, even, odd)
            over_edge = jnp.where(iota(0, (32, 128)) % 8 == 7, pltpu.roll(series[:32], 7, 0), 0.0)
            for blk in range(NBLOCK):
                seen = [over_edge[: 8 * blk]] if blk else []
                unseen = [jnp.zeros((32 - 8 * blk, 128), F32)] if blk < 4 else []
                over[blk, :, lanes] = jnp.concatenate(unseen + seen, axis=0).astype(BF16)
        edges = [
            jnp.concatenate([over[blk, :, p * 256 : p * 256 + 256] for blk in range(NBLOCK)], axis=1) for p in range(2)
        ]
        parts = [jnp.concatenate(pair, axis=0) for pair in zip(stacked_shifts(even, odd), edges)]
        product = chirped(parts, tv[b])
        results.append(
            jnp.concatenate([product0[b, :96], product0[b, 96:] + product[SPAN:], product[:SPAN]], axis=0).astype(BF16)
        )
    row, col = iota(0), iota(1)
    final = ones_where(col == (row % 4) * 64 + ((row // 4) % 8) * 8 + row // 32)
    copies = []
    for h in range(2):
        for j in range(2):
            rows = slice(128 * h + 64 * j, 128 * h + 64 * j + 64)
            block = jnp.concatenate(
                [
                    jnp.concatenate([results[b][rows, half * 128 + q * 256 : half * 128 + q * 256 + 128] for q in range(2)], axis=1)
                    for half in range(2) for b in range(2)
                ],
                axis=0,
            )
            block = dot(final, block).astype(BF16)
            for q in range(2):
                for k in range(8):
                    start = 512 * h + 64 * k + 32 * j
                    outv[q, start : start + 32, :] = block[32 * k : 32 * k + 32, q * 128 : q * 128 + 128]
        done = pl.ds(512 * h, 512)
        copies.append(pltpu.make_async_copy(outv.at[:, done], out.at[:, done], out_sem.at[h]))
        copies[-1].start()
    for copy in copies + [band_copy]:
        copy.wait()


def in_hbm(array):
    return pltpu.with_memory_space_constraint(array, pltpu.HBM)


def on_device(voltages, weights, flags, dm_index):
    hbm = pl.BlockSpec(memory_space=pl.ANY)
    vmem = pl.BlockSpec(memory_space=pltpu.VMEM)
    dma = pltpu.SemaphoreType.DMA
    params = dict(vmem_limit_bytes=24 * 1024 * 1024)
    beams, tables, dft, proto, product0, last0, power0 = pl.pallas_call(
        body,
        out_shape=(
            jax.ShapeDtypeStruct((PARTS, 64, 2, 8, SPAN), BF16),
            jax.ShapeDtypeStruct((2, NBLOCK * CHANNELS, 512), BF16),
            jax.ShapeDtypeStruct((512, 512), BF16),
            jax.ShapeDtypeStruct((TAPS, 512), F32),
            jax.ShapeDtypeStruct((2, SPAN, 512), F32),
            jax.ShapeDtypeStruct((2, 88, 512), F32),
            jax.ShapeDtypeStruct((2, 512), F32),
        ),
        in_specs=[hbm] * 7,
        out_specs=(vmem,) * 7,
        scratch_shapes=[
            pltpu.VMEM((16, 4, 2, 2, 16, 256), BF16),
            pltpu.VMEM((PARTS, 4, 4, 4, 4, 8, SPAN), BF16),
            pltpu.VMEM((PARTS, 4, 4, 4, 2, 4, 8, SPAN), BF16),
            pltpu.VMEM((PARTS, 64, 2, 4, 8, SPAN), BF16),
            pltpu.VMEM((2, 2, 256, 1024), BF16),
            pltpu.VMEM((DMS, 16, 512), F32),
            pltpu.VMEM((1, 64), jnp.int32),
            pltpu.SMEM((2,), jnp.int32),
            pltpu.VMEM((2, 256, 2 * SPAN), BF16),
            pltpu.VMEM((PARTS, 64, 8, SPAN), BF16),
            pltpu.VMEM((PARTS, 64, 2, 8, SPAN), BF16),
            pltpu.VMEM((16, 256), F32),
            pltpu.VMEM((2, 512, SPAN), BF16),
            pltpu.VMEM((2, 88 + SPAN, 512), F32),
            pltpu.VMEM((SPAN + 32, 512), BF16),
            pltpu.VMEM((SPAN + 16, 512), BF16),
            pltpu.VMEM((2, 256, 2 * SPAN), F32),
            dma((8,)),
            pltpu.SemaphoreType.REGULAR,
            dma,
            dma,
            *[dma((PARTS,)) for _ in range(3)],
            dma((PARTS, 4)),
            dma((PARTS, 4)),
            dma((PARTS,)),
            dma((30,)),
            dma,
            dma,
            *[
                pltpu.VMEM((PARTS,) + shape + (2, 4, 8, SPAN), BF16)
                for shape in [(3, 3), (3, 3), (3, 3), (3,), (3,), (3,), ()]
            ],
        ],
        compiler_params=pltpu.CompilerParams(collective_id=0, has_side_effects=True, **params),
        name="beamform",
    )(
        in_hbm(voltages.reshape(16, 4, 2, 2, 16, TIME)),
        in_hbm(weights),
        in_hbm(flags),
        in_hbm(dm_index),
        in_hbm(jnp.asarray(chirp_rows()).astype(BF16).astype(F32)),
        in_hbm(jnp.asarray(dft_rows()).astype(BF16)),
        in_hbm(jnp.asarray(prototype())),
    )
    dedispersed, bandpass = pl.pallas_call(
        tail,
        out_shape=(
            jax.ShapeDtypeStruct((2, 2 * TIME * 2, 128), BF16),
            jax.ShapeDtypeStruct((2, CHANNELS), F32),
        ),
        in_specs=[vmem] * 7,
        out_specs=(hbm, hbm),
        scratch_shapes=[
            pltpu.VMEM((2, 512, SPAN), BF16),
            pltpu.VMEM((2, 88 + SPAN, 512), F32),
            *[pltpu.VMEM((SPAN + 32, 512), BF16) for _ in range(2)],
            *[pltpu.VMEM((SPAN + 16, 512), BF16) for _ in range(2)],
            *[pltpu.VMEM((NBLOCK, 32, 512), BF16) for _ in range(2)],
            pltpu.VMEM((2, 2 * TIME * 2, 128), BF16),
            pltpu.VMEM((2, CHANNELS), F32),
            dma((3,)),
        ],
        compiler_params=pltpu.CompilerParams(**params),
        name="synthesis",
    )(
        beams.reshape(PARTS, 1024, SPAN),
        tables,
        dft,
        proto,
        product0,
        last0,
        power0,
    )
    dedispersed = dedispersed.reshape(2, 512, 2, 128).transpose(0, 2, 1, 3).reshape(2, 2, TIME * CHANNELS)
    return dedispersed, bandpass


def solution(mesh):
    return jax.shard_map(
        on_device,
        mesh=mesh,
        in_specs=(
            P(None, ("stn", "chan"), None, None),
            P(None, ("stn", "chan"), None, None),
            P(("stn", "chan"), None),
            P(("stn", "chan")),
        ),
        out_specs=(P(None, ("stn", "chan"), None), P(("stn", "chan"), None)),
        check_vma=False,
    )
```
